32 devices in a mesh: gx: 8 (over z, y), gy: 4 (over x, core).
Axes of the slice: x: 2, y: 2, z: 4, core: 2. Of those that a mesh axis runs over, the one named last changes fastest.
Arguments:
- density_init: float32 [2, 256, 256, 128], P(None, 'gx', 'gy'), may hold values from 0.2 to 1.5
- solid_mask: int32 [256, 256, 128], P('gx', 'gy'), may hold values from 0 to 1
- loadings: float32 [2], replicated, may hold values from 0.3 to 1
Outputs:
- density: float32 [2, 256, 256, 128], P(None, 'gx', 'gy')
The draws below stay inside these ranges and needn't reach their ends.
All inputs are finite; a program needn't handle non-finite values.
Results may differ from the reference program's by a relative error of at most 0.0001.
Values sent between devices are 32-bit elements; how exact they have to be, the bound alone decides.
No kernel may reach another device: no remote copies, remote signals or barrier semaphores. Data moves between devices by JAX's collectives and lax.ppermute only.
A program may use at most 128 MiB of HBM per device.

```python
import math
import jax
import jax.numpy as jnp
import numpy as np
from jax import lax

NZ = 128
ITERS = 2
NX = 256
NY = 256


def draw_solid_mask(key, part):
    rows = jnp.arange(NX, dtype=jnp.int32)[:, None, None]
    levels = jax.random.randint(key, (NX, NY, NZ), 0, 4, dtype=jnp.int32)
    limits = 1 + 3 * rows // NX
    return (levels >= limits).astype(jnp.int32)


def block_levels(rng, extent, shards, smallest, high):
    def one(position, shards_of):
        steps = jax.random.uniform(jax.random.fold_in(jax.random.fold_in(rng, 6), position), (shards_of,), jnp.float32, smallest / len(shards), high / len(shards))
        return jnp.repeat(jnp.exp(steps), extent[position] // shards_of).reshape((-1,) + (1,) * (len(extent) - position - 1))

    factor_of = one(*shards[0])
    for cut in shards[1:]:
        factor_of = factor_of * one(*cut)
    return factor_of


def setup_inputs(seed: int = 0) -> dict:
    keys = jax.random.split(jax.random.key(seed), 4)
    density_init = jnp.clip(0.2 + 1.3 * jax.random.uniform(keys[0], (2, NX, NY, NZ), jnp.float32) ** block_levels(keys[0], (2, NX, NY, NZ), ((1, 8), (2, 4)), -0.2, 0.2), 0.2, 1.5)
    solid_mask = draw_solid_mask(jax.random.fold_in(keys[3], 71), 0)
    loadings = jnp.clip(jnp.exp(jax.random.uniform(keys[2], (2,), jnp.float32, math.log(0.3), math.log(1.0))), 0.3, 1.0)
    return {"density_init": density_init, "solid_mask": solid_mask, "loadings": loadings}


SEGMENTS = (1.5131, 1.0)
RADII = (6.0, 8.0)
CROSS = 0.25
DAMPING = 0.3
ATTRACT = ((0.30, 0.22), (0.22, 0.16))


def profile(kind, radius):
    offset = np.arange(17) - 8.0
    if kind == 0:
        values = np.maximum(radius * radius - offset * offset, 0.0)
    elif kind == 1:
        values = offset * offset * np.maximum(radius * radius - offset * offset, 0.0)
    else:
        values = np.exp(-np.abs(offset) / 4.0)
    return values / values.sum()


def smooth_axis(field, taps_row, axis):
    widths = [(0, 0), (0, 0), (0, 0)]
    widths[axis] = (8, 8)
    padded = jnp.pad(field, widths)
    length = field.shape[axis]
    total = jnp.zeros_like(field)
    for offset in range(17):
        total = total + float(taps_row[offset]) * lax.slice_in_dim(padded, offset, offset + length, axis=axis)
    return total


def convolve(field, taps_row):
    return smooth_axis(smooth_axis(smooth_axis(field, taps_row, 0), taps_row, 1), taps_row, 2)


def reference(density_init, solid_mask, loadings):
    pore_mask = (solid_mask == 0).astype(jnp.float32)
    density = density_init * pore_mask[None]
    total_cells = float(NX * NY * NZ)
    for iteration in range(ITERS):
        packing = SEGMENTS[0] * convolve(density[0], profile(0, RADII[0])) + SEGMENTS[1] * convolve(density[1], profile(0, RADII[1]))
        surface = convolve(density[0], profile(1, RADII[0])) + convolve(density[1], profile(1, RADII[1]))
        attraction = [convolve(density[0], profile(2, 0.0)), convolve(density[1], profile(2, 0.0))]
        deriv_two = jnp.log(1.0 + packing) + 2.0 * CROSS * surface * (1.0 + packing)
        deriv_three = surface / (1.0 + packing) + CROSS * surface * surface
        proposals = []
        for comp in range(2):
            potential = SEGMENTS[comp] * convolve(deriv_three, profile(0, RADII[comp])) + convolve(deriv_two, profile(1, RADII[comp]))
            potential = potential - ATTRACT[comp][0] * attraction[0] - ATTRACT[comp][1] * attraction[1]
            proposals.append(pore_mask * jnp.exp(-potential))
        proposal = jnp.stack(proposals)
        totals = jnp.sum(proposal, axis=(1, 2, 3))
        scales = loadings * total_cells / totals
        density = (1.0 - DAMPING) * density + DAMPING * scales[:, None, None, None] * proposal
    return density
```

```python
import functools

import jax
import jax.numpy as jnp
import ml_dtypes
import numpy as np
from jax import lax
from jax.experimental import pallas as pl
from jax.experimental.pallas import tpu as pltpu
from jax.sharding import PartitionSpec as P

ITERS = 2
SEGMENTS = (1.5131, 1.0)
RADII = (6.0, 8.0)
CROSS = 0.25
DAMPING = 0.3
ATTRACT = ((0.3, 0.22), (0.22, 0.16))
HALO = 8
AXES = ("gx", "gy")
BF16 = jnp.bfloat16
F32 = jnp.float32


def raw_profile(kind, radius):
    offset = np.arange(17) - 8.0
    if kind == 0:
        return np.maximum(radius * radius - offset * offset, 0.0)
    if kind == 1:
        return offset * offset * np.maximum(radius * radius - offset * offset, 0.0)
    return np.exp(-np.abs(offset) / 4.0)


def split_bf16(table):
    high = table.astype(np.float32).astype(ml_dtypes.bfloat16)
    low = (table - high.astype(np.float64)).astype(np.float32).astype(ml_dtypes.bfloat16)
    return high, low


def column_table(kinds, cols):
    parts = []
    for kind, radius in kinds:
        taps = raw_profile(kind, radius)
        band = np.zeros((cols, cols + 16))
        for row in range(cols):
            band[row, row : row + 17] = taps
        parts.append(band)
    high, low = split_bf16(np.concatenate(parts))
    return np.concatenate([high, high, low], axis=1)


def depth_table(kinds, depth):
    parts = []
    for kind, radius in kinds:
        taps = raw_profile(kind, radius)
        band = np.zeros((depth, depth))
        for column in range(depth):
            for offset in range(17):
                source = column + offset - 8
                if 0 <= source < depth:
                    band[source, column] = taps[offset]
        parts.append(band)
    high, low = split_bf16(np.concatenate(parts))
    return np.concatenate([high, low], axis=1)


def row_taps(kind, radius, scale):
    taps = raw_profile(kind, radius)
    return [float(v) for v in taps * (scale / taps.sum() ** 3)]


def smooth_columns(pieces, table, rows):
    field = jnp.concatenate(pieces, axis=1)
    high = field.astype(BF16)
    low = (field - high.astype(F32)).astype(BF16)
    stacked = jnp.concatenate([high, low, high], axis=0)
    return jnp.dot(table, stacked, preferred_element_type=F32)


def smooth_rows(values, taps, count):
    out = []
    for i in range(count):
        total = None
        for k in range(9):
            if taps[8 + k] == 0.0:
                continue
            pair = values[i + 8] if k == 0 else values[i + 8 - k] + values[i + 8 + k]
            term = taps[8 + k] * pair
            total = term if total is None else total + term
        out.append(total)
    return out


def smooth_rows_exp(values, taps, count):
    q = float(np.exp(-0.25))
    q9 = q**9
    up = values[0]
    for j in range(1, 9):
        up = up * q + values[j]
    ups = [up]
    for i in range(1, count):
        up = up * q + (values[i + 8] - q9 * values[i - 1])
        ups.append(up)
    down = values[count + 15]
    for j in range(1, 8):
        down = down * q + values[count + 15 - j]
    down = down * q
    out = [None] * count
    out[count - 1] = taps[8] * (ups[count - 1] + down)
    for i in range(count - 2, -1, -1):
        down = down * q + (q * values[i + 9] - q9 * values[i + 17])
        out[i] = taps[8] * (ups[i] + down)
    return out


def split_dot(pair, table):
    high = pair.astype(BF16)
    low = (pair - high.astype(F32)).astype(BF16)
    depth = table.shape[1] // 2
    both = jnp.dot(high, table, preferred_element_type=F32)
    rest = jnp.dot(low, table[:, :depth], preferred_element_type=F32)
    return both[:, :depth] + both[:, depth:] + rest


STAGE1 = (((0, RADII[0]), (1, RADII[0]), (2, 0.0)), ((0, RADII[1]), (1, RADII[1]), (2, 0.0)))
STAGE2 = (((0, RADII[0]), (0, RADII[1])), ((1, RADII[0]), (1, RADII[1])))


def columns_pass(own, left, right, top, bottom, tables, rows, cols, scratch, per):
    def store(result, comp, row):
        for p in range(per):
            scratch[comp * per + p, row] = result[p * cols : (p + 1) * cols, :128]
            scratch[comp * per + p, row + 1] = result[p * cols : (p + 1) * cols, 128:]

    for comp in range(2):
        table = tables[comp]

        @pl.loop(0, rows // 2)
        def _(i):
            pieces = []
            for j in range(2):
                x = 2 * i + j
                pieces.append(jnp.concatenate([left[comp, x], own[comp, x], right[comp, x]], axis=0))
            store(smooth_columns(pieces, table[...], rows), comp, HALO + 2 * i)

        for halo, start in ((top, 0), (bottom, HALO + rows)):

            @pl.loop(0, HALO // 2)
            def _(i, halo=halo, start=start):
                pieces = [halo[comp, 2 * i], halo[comp, 2 * i + 1]]
                store(smooth_columns(pieces, table[...], rows), comp, start + 2 * i)


def rows_pass(scratch, fields, rows, cols, out):
    @pl.loop(0, cols // 8)
    def _(t):
        window = pl.ds(pl.multiple_of(t * 8, 8), 8)
        for index, kind, radius, scale in fields:
            taps = row_taps(kind, radius, scale)
            values = [scratch[index, x, window, :] for x in range(rows + 16)]
            smooth = smooth_rows_exp if kind == 2 else smooth_rows
            for x, value in enumerate(smooth(values, taps, rows)):
                out[index, x, window, :] = value


def stage1_kernel(own, left, right, top, bottom, wy0, wy1, wz3, wz2, wza, deriv, attraction, ys, xs):
    _, rows, cols, depth = own.shape
    columns_pass(own, left, right, top, bottom, (wy0, wy1), rows, cols, ys, 3)
    fields = []
    for comp in range(2):
        for p, (kind, radius) in enumerate(STAGE1[comp]):
            fields.append((comp * 3 + p, kind, radius, SEGMENTS[comp] if kind == 0 else 1.0))
    rows_pass(ys, fields, rows, cols, xs)

    @pl.loop(0, rows // 2)
    def _(i):
        x = pl.ds(2 * i, 2)
        flat = lambda p: xs[p, x].reshape(2 * cols, depth)
        n3 = split_dot(jnp.concatenate([flat(0), flat(3)], axis=1), wz3[...])
        n2 = split_dot(jnp.concatenate([flat(1), flat(4)], axis=1), wz2[...])
        for comp in range(2):
            a = split_dot(flat(3 * comp + 2), wza[...])
            attraction[comp, x] = a.reshape(2, cols, depth)
        one = 1.0 + n3
        deriv[0, x] = (jnp.log(one) + 2.0 * CROSS * n2 * one).reshape(2, cols, depth)
        deriv[1, x] = (n2 / one + CROSS * n2 * n2).reshape(2, cols, depth)


def stage2_kernel(own, left, right, top, bottom, solid, attraction, wy0, wy1, wz0, wz1, proposal, sums, ys, xs):
    _, rows, cols, depth = own.shape
    columns_pass(own, left, right, top, bottom, (wy0, wy1), rows, cols, ys, 2)
    fields = []
    for d in range(2):
        for comp, (kind, radius) in enumerate(STAGE2[1 - d]):
            fields.append((d * 2 + comp, kind, radius, SEGMENTS[comp] if kind == 0 else 1.0))
    rows_pass(ys, fields, rows, cols, xs)
    sums[...] = jnp.zeros_like(sums)

    @pl.loop(0, rows // 2)
    def _(i):
        x = pl.ds(2 * i, 2)
        flat = lambda p: xs[p, x].reshape(2 * cols, depth)
        pore = solid[x].reshape(2 * cols, depth) == 0
        a0 = attraction[0, x].reshape(2 * cols, depth)
        a1 = attraction[1, x].reshape(2 * cols, depth)
        for comp, wz in ((0, wz0), (1, wz1)):
            mu = split_dot(jnp.concatenate([flat(2 + comp), flat(comp)], axis=1), wz[...])
            mu = mu - ATTRACT[comp][0] * a0 - ATTRACT[comp][1] * a1
            value = jnp.where(pore, jnp.exp(-mu), 0.0)
            proposal[comp, x] = value.reshape(2, cols, depth)
            sums[comp] += value.reshape(2 * cols // 8, 8, depth).sum(0)


def in_vmem(count):
    return [pl.BlockSpec(memory_space=pltpu.VMEM)] * count


PARAMS = pltpu.CompilerParams(vmem_limit_bytes=56 * 1024 * 1024)


def stage1(own, left, right, top, bottom):
    _, rows, cols, depth = own.shape
    tables = [jnp.asarray(column_table(STAGE1[c], cols)) for c in range(2)]
    depths = [
        jnp.asarray(depth_table([STAGE1[0][0], STAGE1[1][0]], depth)),
        jnp.asarray(depth_table([STAGE1[0][1], STAGE1[1][1]], depth)),
        jnp.asarray(depth_table([STAGE1[0][2]], depth)),
    ]
    block = jax.ShapeDtypeStruct(own.shape, F32)
    return pl.pallas_call(
        stage1_kernel,
        out_shape=(block, block),
        in_specs=in_vmem(10),
        out_specs=tuple(in_vmem(2)),
        scratch_shapes=[pltpu.VMEM((6, rows + 16, cols, depth), F32), pltpu.VMEM((6, rows, cols, depth), F32)],
        compiler_params=PARAMS,
        name="stage1",
    )(own, left, right, top, bottom, *tables, *depths)


def stage2(own, left, right, top, bottom, solid, attraction):
    _, rows, cols, depth = own.shape
    tables = [jnp.asarray(column_table(STAGE2[1 - d], cols)) for d in range(2)]
    depths = [jnp.asarray(depth_table([STAGE2[0][c], STAGE2[1][c]], depth)) for c in range(2)]
    return pl.pallas_call(
        stage2_kernel,
        out_shape=(jax.ShapeDtypeStruct(own.shape, F32), jax.ShapeDtypeStruct((2, 8, depth), F32)),
        in_specs=in_vmem(11),
        out_specs=tuple(in_vmem(2)),
        scratch_shapes=[pltpu.VMEM((4, rows + 16, cols, depth), F32), pltpu.VMEM((4, rows, cols, depth), F32)],
        compiler_params=PARAMS,
        name="stage2",
    )(own, left, right, top, bottom, solid, attraction, *tables, *depths)


def shift(value, axis, step):
    count = lax.axis_size(axis)
    return lax.ppermute(value, axis, [(i, i + step) for i in range(count) if 0 <= i + step < count])


def exchange(own):
    rows, cols = own.shape[1:3]
    left = shift(own[:, :, cols - HALO :], "gy", 1)
    right = shift(own[:, :, :HALO], "gy", -1)

    def edge(start):
        part = slice(start, start + HALO)
        return jnp.concatenate([left[:, part], own[:, part], right[:, part]], axis=2)

    top = shift(edge(rows - HALO), "gx", 1)
    bottom = shift(edge(0), "gx", -1)
    return left, right, top, bottom


def total_over(sums, axes):
    for axis in reversed(axes):
        count = lax.axis_size(axis)
        if count & (count - 1):
            sums = lax.psum(sums, axis)
            continue
        bit = 1
        while bit < count:
            sums = sums + lax.ppermute(sums, axis, [(i, i ^ bit) for i in range(count)])
            bit *= 2
    return sums


def body(density_init, solid_mask, loadings):
    rows, cols, depth = solid_mask.shape
    total_cells = float(rows * lax.axis_size("gx") * cols * lax.axis_size("gy") * depth)
    density = density_init * (solid_mask == 0).astype(F32)[None]
    halos = exchange(density)
    for iteration in range(ITERS):
        deriv, attraction = stage1(density, *halos)
        proposal, sums = stage2(deriv, *exchange(deriv), solid_mask, attraction)
        totals = total_over(sums.sum(axis=1), AXES).sum(axis=1)
        scales = DAMPING * loadings * total_cells / totals
        mix = lambda old, new: (1.0 - DAMPING) * old + scales[:, None, None, None] * new
        if iteration + 1 < ITERS:
            halos = [mix(old, new) for old, new in zip(halos, exchange(proposal))]
        density = mix(density, proposal)
    return density


def solution(mesh):
    in_specs = (P(None, "gx", "gy", None), P("gx", "gy", None), P())
    out_specs = P(None, "gx", "gy", None)
    return jax.shard_map(body, mesh=mesh, in_specs=in_specs, out_specs=out_specs, check_vma=False)
```

```python
import functools

import jax
import jax.numpy as jnp
import ml_dtypes
import numpy as np
from jax import lax
from jax.experimental import pallas as pl
from jax.experimental.pallas import tpu as pltpu
from jax.sharding import PartitionSpec as P

ITERS = 2
SEGMENTS = (1.5131, 1.0)
RADII = (6.0, 8.0)
CROSS = 0.25
DAMPING = 0.3
ATTRACT = ((0.3, 0.22), (0.22, 0.16))
REACH = (5, 7)
FAR = 8
DERIV = REACH[1]
DEEP = tuple(DERIV + r for r in REACH)
WIDE = 8
AXES = ("gx", "gy")
BF16 = jnp.bfloat16
F32 = jnp.float32


def raw_profile(kind, radius):
    offset = np.arange(17) - 8.0
    if kind == 0:
        return np.maximum(radius * radius - offset * offset, 0.0)
    if kind == 1:
        return offset * offset * np.maximum(radius * radius - offset * offset, 0.0)
    return np.exp(-np.abs(offset) / 4.0)


def split_bf16(table):
    high = table.astype(np.float32).astype(ml_dtypes.bfloat16)
    low = (table - high.astype(np.float64)).astype(np.float32).astype(ml_dtypes.bfloat16)
    return high, low


def column_band(kind, radius, count, columns, first):
    band = np.zeros((count, columns))
    for o in range(count):
        band[o, first + o : first + o + 17] = raw_profile(kind, radius)
    return band


def depth_band(kind, radius, depth):
    taps = raw_profile(kind, radius)
    band = np.zeros((depth, depth))
    for column in range(depth):
        for offset in range(17):
            source = column + offset - 8
            if 0 <= source < depth:
                band[source, column] = taps[offset]
    return band


def stage1_tables(comp, cols):
    wide = cols + 2 * WIDE
    pack = column_band(0, RADII[comp], wide, wide + 16, 0)
    rest = np.concatenate(
        [column_band(1, RADII[comp], wide, wide + 16, 0), column_band(2, 0.0, cols, wide + 16, WIDE)]
    )
    high, low = split_bf16(np.concatenate([pack, rest]))
    return [jnp.asarray(np.concatenate([high, high], axis=1)), jnp.asarray(low[wide:])]


def stage2_table(kind, cols):
    high, low = split_bf16(np.concatenate([column_band(kind, r, cols, cols + 16, 0) for r in RADII]))
    return jnp.asarray(np.concatenate([high, high] if kind == 0 else [high, high, low], axis=1))


def depth_table(kinds, depth):
    high, low = split_bf16(np.concatenate([depth_band(kind, radius, depth) for kind, radius in kinds]))
    return jnp.asarray(np.concatenate([high, low], axis=1))


def attraction_table(depth):
    band = depth_band(2, 0.0, depth)
    high, low = split_bf16(-np.concatenate([np.concatenate([ATTRACT[i][j] * band for i in range(2)], axis=1) for j in range(2)]))
    return jnp.asarray(np.concatenate([high, low], axis=1))


def row_taps(kind, radius, scale):
    taps = raw_profile(kind, radius)
    return [float(v) for v in taps * (scale / taps.sum() ** 3)]


def split(field):
    high = field.astype(BF16)
    return high, (field - high.astype(F32)).astype(BF16)


def smooth_rows(values, taps, count, reach):
    out = []
    for i in range(count):
        total = None
        for k in range(reach + 1):
            if taps[8 + k] == 0.0:
                continue
            pair = values[i + reach] if k == 0 else values[i + reach - k] + values[i + reach + k]
            term = taps[8 + k] * pair
            total = term if total is None else total + term
        out.append(total)
    return out


def smooth_rows_exp(values, scale, count):
    q = float(np.exp(-0.25))
    q9 = q**9
    up = values[0]
    for j in range(1, 9):
        up = up * q + values[j]
    ups = [up]
    for i in range(1, count):
        up = up * q + (values[i + 8] - q9 * values[i - 1])
        ups.append(up)
    down = values[count + 15]
    for j in range(1, 8):
        down = down * q + values[count + 15 - j]
    down = down * q
    out = [None] * count
    out[count - 1] = scale * (ups[count - 1] + down)
    for i in range(count - 2, -1, -1):
        down = down * q + (q * values[i + 9] - q9 * values[i + 17])
        out[i] = scale * (ups[i] + down)
    return out


def split_dot(pair, table):
    high, low = split(pair)
    width = table.shape[1] // 2
    both = jnp.dot(high, table, preferred_element_type=F32)
    rest = jnp.dot(low, table[:, :width], preferred_element_type=F32)
    return both[:, :width] + both[:, width:] + rest


def stage1_columns(load, pairs, comp, tables, near, far, cols, unroll):
    wide = cols + 2 * WIDE

    @pl.loop(0, pairs, unroll=unroll)
    def _(i):
        high, low = split(jnp.concatenate([load(2 * i), load(2 * i + 1)], axis=1))
        first = jnp.dot(tables[0][...], jnp.concatenate([high, low], axis=0), preferred_element_type=F32)
        rest = first[wide:] + jnp.dot(tables[1][...], high, preferred_element_type=F32)
        depth = high.shape[1] // 2
        for j in range(2):
            lanes = slice(j * depth, (j + 1) * depth)
            near[2 * comp, 2 * i + j] = first[:wide, lanes]
            near[2 * comp + 1, 2 * i + j] = rest[:wide, lanes]
            far[comp, 2 * i + j] = rest[wide:, lanes]


def stage1_rows(load, first, count, out):
    wide = out.shape[2]

    @pl.loop(0, wide // 8)
    def _(t):
        window = pl.ds(pl.multiple_of(t * 8, 8), 8)
        for comp in range(2):
            reach = REACH[comp]
            for kind in range(2):
                field = 2 * comp + kind
                taps = row_taps(kind, RADII[comp], SEGMENTS[comp] if kind == 0 else 1.0)
                values = [load(field, row, window) for row in range(first - reach, first + count + reach)]
                for i, value in enumerate(smooth_rows(values, taps, count, reach)):
                    out[field, i, window, :] = value


def stage1_depth(xs, count, step, wz3, wz2, deriv, inside, gates):
    wide, depth = xs.shape[2:]
    for i, start in enumerate(range(0, count, step)):
        rows = slice(start, start + step)
        pair = lambda p: jnp.concatenate([xs[q, rows].reshape(step * wide, depth) for q in (p, p + 2)], axis=1)
        n3 = split_dot(pair(0), wz3[...])
        n2 = split_dot(pair(1), wz2[...])
        one = 1.0 + n3
        two = (jnp.log(one) + 2.0 * CROSS * n2 * one).reshape(step, wide, depth)
        three = (n2 / one + CROSS * n2 * n2).reshape(step, wide, depth)
        for which, value in enumerate((two, three)):
            if gates[i] is not None:
                value = value * gates[i]
            deriv[which, rows, :WIDE] = value[:, :WIDE] * inside[2]
            deriv[which, rows, WIDE : wide - WIDE] = value[:, WIDE : wide - WIDE]
            deriv[which, rows, wide - WIDE :] = value[:, wide - WIDE :] * inside[3]


def stage2_columns(deriv, count, wy2, wy3, out, unroll):
    cols = out.shape[2]

    @pl.loop(0, count // 2, unroll=unroll)
    def _(i):
        for which, table in ((0, wy2), (1, wy3)):
            high, low = split(jnp.concatenate([deriv[which, 2 * i], deriv[which, 2 * i + 1]], axis=1))
            stacked = [high, low, high] if which == 0 else [high, low]
            result = jnp.dot(table[...], jnp.concatenate(stacked, axis=0), preferred_element_type=F32)
            depth = high.shape[1] // 2
            for comp in range(2):
                for j in range(2):
                    out[2 * which + comp, 2 * i + j] = result[comp * cols : (comp + 1) * cols, j * depth : (j + 1) * depth]


def mid_kernel(inside, own, left, right, ta0, tb0, ta1, tb1, wz3, wz2, wy2, wy3, near, far, y2, xs, deriv):
    _, rows, cols, depth = own.shape
    tables = ((ta0, tb0), (ta1, tb1))
    for comp in range(2):
        load = lambda row: jnp.concatenate([left[comp, row], own[comp, row], right[comp, row]], axis=0)
        stage1_columns(load, rows // 2, comp, tables[comp], near, far, cols, 4)
    count = rows - 2 * DERIV
    stage1_rows(lambda field, row, window: near[field, row, window, :], DERIV, count, xs)
    stage1_depth(xs, count, count // 3, wz3, wz2, deriv, inside, [None] * 3)
    stage2_columns(deriv, count, wy2, wy3, y2, 3)


def edge_kernel(top, inside, halo, left, right, near, far, y2, solid, ta0, tb0, ta1, tb1, wz3, wz2, wy2, wy3, wzm0, wzm1, wza,
                proposal, sums, near_h, far_h, xs, deriv, y2_h, xm, xa):
    _, rows, cols, depth = far.shape
    half = rows // 2
    tables = ((ta0, tb0), (ta1, tb1))
    for comp in range(2):
        base = 0 if comp == 0 else DEEP[0]
        load = lambda row: jnp.concatenate([left[base + row], halo[base + row], right[base + row]], axis=0)
        stage1_columns(load, DEEP[comp] // 2, comp, tables[comp], near_h, far_h, cols, 3)

    def pick(own, edge, index, row, window):
        comp = index // 2 if own is near else index
        if 0 <= row < rows:
            return own[index, row, window, :]
        return edge[index, row + DEEP[comp] if top else row - rows, window, :]

    first = -DERIV if top else rows - DERIV
    stage1_rows(lambda f, row, window: pick(near, near_h, f, row, window), first, 2 * DERIV, xs)
    stage1_depth(xs, 2 * DERIV, DERIV, wz3, wz2, deriv, inside, [inside[0], None] if top else [None, inside[1]])
    stage2_columns(deriv, 2 * DERIV, wy2, wy3, y2_h, 7)

    start = 0 if top else half

    @pl.loop(0, cols // 8)
    def _(t):
        window = pl.ds(pl.multiple_of(t * 8, 8), 8)

        def second(index, row):
            if DERIV <= row < rows - DERIV:
                return y2[index, row - DERIV, window, :]
            return y2_h[index, row - first, window, :]

        for which, kind in ((0, 1), (1, 0)):
            for comp in range(2):
                reach = REACH[comp]
                taps = row_taps(kind, RADII[comp], SEGMENTS[comp] if kind == 0 else 1.0)
                values = [second(2 * which + comp, row) for row in range(start - reach, start + half + reach)]
                for i, value in enumerate(smooth_rows(values, taps, half, reach)):
                    xm[2 * which + comp, i, window, :] = value
        scale = row_taps(2, 0.0, 1.0)[8]
        for comp in range(2):
            values = [pick(far, far_h, comp, row, window) for row in range(start - FAR, start + half + FAR)]
            for i, value in enumerate(smooth_rows_exp(values, scale, half)):
                xa[comp, i, window, :] = value

    sums[...] = jnp.zeros_like(sums)
    step = half // 2
    for i in range(0, half, step):
        part = slice(i, i + step)
        flat = lambda ref, p: ref[p, part].reshape(step * cols, depth)
        pore = solid[start + i : start + i + step].reshape(step * cols, depth) == 0
        pull = split_dot(jnp.concatenate([flat(xa, 0), flat(xa, 1)], axis=1), wza[...])
        for comp, wz in ((0, wzm0), (1, wzm1)):
            mu = split_dot(jnp.concatenate([flat(xm, 2 + comp), flat(xm, comp)], axis=1), wz[...])
            mu = mu + pull[:, comp * depth : (comp + 1) * depth]
            value = jnp.where(pore, jnp.exp(-mu), 0.0)
            proposal[comp, part] = value.reshape(step, cols, depth)
            sums[comp] += value.reshape(step * cols // 8, 8, depth).sum(0)


def in_vmem(count):
    return [pl.BlockSpec(memory_space=pltpu.VMEM)] * count


def params(mebibytes):
    return pltpu.CompilerParams(vmem_limit_bytes=mebibytes * 1024 * 1024)


def tables_for(cols, depth):
    first = [t for comp in range(2) for t in stage1_tables(comp, cols)]
    first += [depth_table([(kind, r) for r in RADII], depth) for kind in range(2)]
    first += [stage2_table(1, cols), stage2_table(0, cols)]
    second = [depth_table([(0, r), (1, r)], depth) for r in RADII] + [attraction_table(depth)]
    return first, second


def mid(inside, own, left, right, tables):
    _, rows, cols, depth = own.shape
    wide, count = cols + 2 * WIDE, rows - 2 * DERIV
    shape = lambda *s: jax.ShapeDtypeStruct(s, F32)
    return pl.pallas_call(
        mid_kernel,
        out_shape=(shape(4, rows, wide, depth), shape(2, rows, cols, depth), shape(4, count, cols, depth)),
        in_specs=[pl.BlockSpec(memory_space=pltpu.SMEM)] + in_vmem(3 + len(tables)),
        out_specs=tuple(in_vmem(3)),
        scratch_shapes=[pltpu.VMEM((4, count, wide, depth), F32), pltpu.VMEM((2, count, wide, depth), F32)],
        compiler_params=params(24),
        cost_estimate=pl.CostEstimate(flops=4 * 10**9, bytes_accessed=15 * 2**20, transcendentals=0),
        name="mid",
    )(inside, own, left, right, *tables)


def edge(top, inside, halo, left, right, near, far, y2, solid, tables):
    _, rows, cols, depth = far.shape
    wide, half = cols + 2 * WIDE, rows // 2
    f32 = lambda *s: pltpu.VMEM(s, F32)
    return pl.pallas_call(
        functools.partial(edge_kernel, top),
        out_shape=(jax.ShapeDtypeStruct((2, half, cols, depth), F32), jax.ShapeDtypeStruct((2, 8, depth), F32)),
        in_specs=[pl.BlockSpec(memory_space=pltpu.SMEM)] + in_vmem(7 + len(tables)),
        out_specs=tuple(in_vmem(2)),
        scratch_shapes=[
            f32(4, DEEP[1], wide, depth),
            f32(2, DEEP[1], cols, depth),
            f32(4, 2 * DERIV, wide, depth),
            f32(2, 2 * DERIV, wide, depth),
            f32(4, 2 * DERIV, cols, depth),
            f32(4, half, cols, depth),
            f32(2, half, cols, depth),
        ],
        compiler_params=params(32),
        cost_estimate=pl.CostEstimate(flops=4 * 10**9, bytes_accessed=15 * 2**20, transcendentals=0),
        name="edge_top" if top else "edge_bottom",
    )(inside, halo, left, right, near, far, y2, solid, *tables)


def shift(value, axis, step):
    count = lax.axis_size(axis)
    return lax.ppermute(value, axis, [(i, i + step) for i in range(count) if 0 <= i + step < count])


def rows_out(top_half, bottom_half):
    last = bottom_half.shape[1]
    lower = jnp.concatenate([bottom_half[c, last - DEEP[c] :] for c in range(2)])
    upper = jnp.concatenate([top_half[c, : DEEP[c]] for c in range(2)])
    return shift(lower, "gx", 1), shift(upper, "gx", -1)


def columns_out(value, dim):
    width = 2 * WIDE
    count = value.shape[dim]
    left = shift(lax.slice_in_dim(value, count - width, count, axis=dim), "gy", 1)
    right = shift(lax.slice_in_dim(value, 0, width, axis=dim), "gy", -1)
    return left, right


def total_over(sums, axes):
    for axis in reversed(axes):
        count = lax.axis_size(axis)
        if count & (count - 1):
            sums = lax.psum(sums, axis)
            continue
        bit = 1
        while bit < count:
            sums = sums + lax.ppermute(sums, axis, [(i, i ^ bit) for i in range(count)])
            bit *= 2
    return sums


def body(density_init, solid_mask, loadings):
    rows, cols, depth = solid_mask.shape
    total_cells = float(rows * lax.axis_size("gx") * cols * lax.axis_size("gy") * depth)
    first, second = tables_for(cols, depth)
    place = [(lax.axis_index(a), lax.axis_size(a)) for a in AXES]
    inside = jnp.stack([v for i, n in place for v in (i > 0, i + 1 < n)]).astype(F32)
    density = density_init * (solid_mask == 0).astype(F32)[None]
    above, below = rows_out(density, density)
    left, right = columns_out(density, 2)
    for iteration in range(ITERS):
        corners_left, corners_right = columns_out(jnp.concatenate([above, below]), 1)
        deep = above.shape[0]
        near, far, y2 = mid(inside, density, left, right, first)
        halves, sums = [], 0.0
        for top, halo in ((True, above), (False, below)):
            part = slice(0, deep) if top else slice(deep, 2 * deep)
            half, half_sums = edge(
                top, inside, halo, corners_left[part], corners_right[part], near, far, y2, solid_mask, first + second
            )
            halves.append(half)
            sums = sums + half_sums
        if iteration + 1 < ITERS:
            new_above, new_below = rows_out(*halves)
            proposal = jnp.concatenate(halves, axis=1)
            new_left, new_right = columns_out(proposal, 2)
        else:
            proposal = jnp.concatenate(halves, axis=1)
        totals = total_over(sums.sum(axis=1), AXES).sum(axis=1)
        scales = DAMPING * loadings * total_cells / totals
        mix = lambda old, new: (1.0 - DAMPING) * old + scales[:, None, None, None] * new
        if iteration + 1 < ITERS:
            by_row = jnp.concatenate([jnp.broadcast_to(scales[c], (DEEP[c],)) for c in range(2)])[:, None, None]
            above = (1.0 - DAMPING) * above + by_row * new_above
            below = (1.0 - DAMPING) * below + by_row * new_below
            left, right = mix(left, new_left), mix(right, new_right)
        density = mix(density, proposal)
    return density


def solution(mesh):
    in_specs = (P(None, "gx", "gy", None), P("gx", "gy", None), P())
    out_specs = P(None, "gx", "gy", None)
    return jax.shard_map(body, mesh=mesh, in_specs=in_specs, out_specs=out_specs, check_vma=False)
```

```python
import functools

import jax
import jax.numpy as jnp
import ml_dtypes
import numpy as np
from jax import lax
from jax.experimental import pallas as pl
from jax.experimental.pallas import tpu as pltpu
from jax.sharding import PartitionSpec as P

ITERS = 2
SEGMENTS = (1.5131, 1.0)
RADII = (6.0, 8.0)
CROSS = 0.25
DAMPING = 0.3
ATTRACT = ((0.3, 0.22), (0.22, 0.16))
REACH = (5, 7)
FAR = 8
DERIV = REACH[1]
DEEP = tuple(DERIV + r for r in REACH)
WIDE = 8
AXES = ("gx", "gy")
BF16 = jnp.bfloat16
F32 = jnp.float32


def raw_profile(kind, radius):
    offset = np.arange(17) - 8.0
    if kind == 0:
        return np.maximum(radius * radius - offset * offset, 0.0)
    if kind == 1:
        return offset * offset * np.maximum(radius * radius - offset * offset, 0.0)
    return np.exp(-np.abs(offset) / 4.0)


def split_bf16(table):
    high = table.astype(np.float32).astype(ml_dtypes.bfloat16)
    low = (table - high.astype(np.float64)).astype(np.float32).astype(ml_dtypes.bfloat16)
    return high, low


def column_band(kind, radius, count, columns, first):
    band = np.zeros((count, columns))
    for o in range(count):
        band[o, first + o : first + o + 17] = raw_profile(kind, radius)
    return band


def depth_band(kind, radius, depth):
    taps = raw_profile(kind, radius)
    band = np.zeros((depth, depth))
    for column in range(depth):
        for offset in range(17):
            source = column + offset - 8
            if 0 <= source < depth:
                band[source, column] = taps[offset]
    return band


def stage1_tables(comp, cols):
    wide = cols + 2 * WIDE
    pack = column_band(0, RADII[comp], wide, wide + 16, 0)
    rest = np.concatenate(
        [column_band(1, RADII[comp], wide, wide + 16, 0), column_band(2, 0.0, cols, wide + 16, WIDE)]
    )
    high, low = split_bf16(np.concatenate([pack, rest]))
    return [jnp.asarray(np.concatenate([high, high], axis=1)), jnp.asarray(low[wide:])]


def stage2_table(kind, cols):
    high, low = split_bf16(np.concatenate([column_band(kind, r, cols, cols + 16, 0) for r in RADII]))
    return jnp.asarray(np.concatenate([high, high] if kind == 0 else [high, high, low], axis=1))


def depth_table(kinds, depth):
    high, low = split_bf16(np.concatenate([depth_band(kind, radius, depth) for kind, radius in kinds]))
    return jnp.asarray(np.concatenate([high, low], axis=1))


def attraction_table(depth):
    band = depth_band(2, 0.0, depth)
    high, low = split_bf16(-np.concatenate([np.concatenate([ATTRACT[i][j] * band for i in range(2)], axis=1) for j in range(2)]))
    return jnp.asarray(np.concatenate([high, low], axis=1))


def row_taps(kind, radius, scale):
    taps = raw_profile(kind, radius)
    return [float(v) for v in taps * (scale / taps.sum() ** 3)]


def split(field):
    high = field.astype(BF16)
    return high, (field - high.astype(F32)).astype(BF16)


def smooth_rows(values, taps, count, reach):
    out = []
    for i in range(count):
        total = None
        for k in range(reach + 1):
            if taps[8 + k] == 0.0:
                continue
            pair = values[i + reach] if k == 0 else values[i + reach - k] + values[i + reach + k]
            term = taps[8 + k] * pair
            total = term if total is None else total + term
        out.append(total)
    return out


def smooth_rows_exp(values, scale, count):
    q = float(np.exp(-0.25))
    q9 = q**9
    up = values[0]
    for j in range(1, 9):
        up = up * q + values[j]
    ups = [up]
    for i in range(1, count):
        up = up * q + (values[i + 8] - q9 * values[i - 1])
        ups.append(up)
    down = values[count + 15]
    for j in range(1, 8):
        down = down * q + values[count + 15 - j]
    down = down * q
    out = [None] * count
    out[count - 1] = scale * (ups[count - 1] + down)
    for i in range(count - 2, -1, -1):
        down = down * q + (q * values[i + 9] - q9 * values[i + 17])
        out[i] = scale * (ups[i] + down)
    return out


def split_dot(pair, table):
    high, low = split(pair)
    width = table.shape[1] // 2
    both = jnp.dot(high, table, preferred_element_type=F32)
    rest = jnp.dot(low, table[:, :width], preferred_element_type=F32)
    return both[:, :width] + both[:, width:] + rest


def stage1_columns(load, pairs, comp, tables, near, far, cols, unroll, begin):
    wide = cols + 2 * WIDE

    @pl.loop(0, pairs, unroll=unroll)
    def _(i):
        high, low = split(jnp.concatenate([load(2 * i), load(2 * i + 1)], axis=1))
        first = jnp.dot(tables[0][...], jnp.concatenate([high, low], axis=0), preferred_element_type=F32)
        rest = first[wide:] + jnp.dot(tables[1][...], high, preferred_element_type=F32)
        depth = high.shape[1] // 2
        for j in range(2):
            lanes = slice(j * depth, (j + 1) * depth)
            row = begin + 2 * i + j
            near[2 * comp, row] = first[:wide, lanes]
            near[2 * comp + 1, row] = rest[:wide, lanes]
            far[comp, row] = rest[wide:, lanes]


def stage1_rows(load, first, count, out):
    wide = out.shape[2]

    @pl.loop(0, wide // 8)
    def _(t):
        window = pl.ds(pl.multiple_of(t * 8, 8), 8)
        for comp in range(2):
            reach = REACH[comp]
            for kind in range(2):
                field = 2 * comp + kind
                taps = row_taps(kind, RADII[comp], SEGMENTS[comp] if kind == 0 else 1.0)
                values = [load(field, row, window) for row in range(first - reach, first + count + reach)]
                for i, value in enumerate(smooth_rows(values, taps, count, reach)):
                    out[field, i, window, :] = value


def stage1_depth(xs, count, step, wz3, wz2, deriv, inside, gates):
    wide, depth = xs.shape[2:]
    for i, start in enumerate(range(0, count, step)):
        rows = slice(start, start + step)
        pair = lambda p: jnp.concatenate([xs[q, rows].reshape(step * wide, depth) for q in (p, p + 2)], axis=1)
        n3 = split_dot(pair(0), wz3[...])
        n2 = split_dot(pair(1), wz2[...])
        one = 1.0 + n3
        two = (jnp.log(one) + 2.0 * CROSS * n2 * one).reshape(step, wide, depth)
        three = (n2 / one + CROSS * n2 * n2).reshape(step, wide, depth)
        for which, value in enumerate((two, three)):
            if gates[i] is not None:
                value = value * gates[i]
            deriv[which, rows, :WIDE] = value[:, :WIDE] * inside[2]
            deriv[which, rows, WIDE : wide - WIDE] = value[:, WIDE : wide - WIDE]
            deriv[which, rows, wide - WIDE :] = value[:, wide - WIDE :] * inside[3]


def stage2_columns(deriv, count, wy2, wy3, out, unroll):
    cols = out.shape[2]

    @pl.loop(0, count // 2, unroll=unroll)
    def _(i):
        for which, table in ((0, wy2), (1, wy3)):
            high, low = split(jnp.concatenate([deriv[which, 2 * i], deriv[which, 2 * i + 1]], axis=1))
            stacked = [high, low, high] if which == 0 else [high, low]
            result = jnp.dot(table[...], jnp.concatenate(stacked, axis=0), preferred_element_type=F32)
            depth = high.shape[1] // 2
            for comp in range(2):
                for j in range(2):
                    out[2 * which + comp, 2 * i + j] = result[comp * cols : (comp + 1) * cols, j * depth : (j + 1) * depth]


def blend(first, second, scale):
    return first if scale is None else (1.0 - DAMPING) * first + scale * second


def mid_kernel(later, inside, *refs):
    if later:
        scales, own, solid, top, bottom, left, right, left_new, right_new, *refs = refs
    else:
        own, solid, left, right, *refs = refs
    ta0, tb0, ta1, tb1, wz3, wz2, wy2, wy3, near, far, y2, *refs = refs
    _, rows, cols, depth = own.shape
    half = rows // 2
    tables = ((ta0, tb0), (ta1, tb1))
    if not later:
        upper, *refs = refs
        base = 0
        for comp in range(2):
            part = slice(0, DEEP[comp])
            upper[base : base + DEEP[comp]] = jnp.where(solid[part] == 0, own[comp, part], 0.0)
            base += DEEP[comp]
    xs, deriv = refs
    for comp in range(2):
        scale = scales[comp] if later else None
        for begin, ref in ((0, top), (half, bottom)) if later else ((0, None),):

            def load(row):
                row = begin + row
                value = jnp.where(solid[row] == 0, own[comp, row], 0.0)
                value = blend(value, ref[comp, row - begin] if later else None, scale)
                sides = [blend(a[comp, row], b[comp, row] if later else None, scale) for a, b in
                         (((left, left_new), (right, right_new)) if later else ((left, None), (right, None)))]
                return jnp.concatenate([sides[0], value, sides[1]], axis=0)

            count = half if later else rows
            stage1_columns(load, count // 2, comp, tables[comp], near, far, cols, 4, begin)
    count = rows - 2 * DERIV
    stage1_rows(lambda field, row, window: near[field, row, window, :], DERIV, count, xs)
    stage1_depth(xs, count, count // 3, wz3, wz2, deriv, inside, [None] * 3)
    stage2_columns(deriv, count, wy2, wy3, y2, 3)


def edge_kernel(top, later, last, inside, *refs):
    if later:
        scales, halo, left, right, halo_new, left_new, right_new, *refs = refs
    else:
        halo, left, right, *refs = refs
    near, far, y2, solid, ta0, tb0, ta1, tb1, wz3, wz2, wy2, wy3, wzm0, wzm1, wza, proposal, sums, *refs = refs
    if not last:
        packed, *refs = refs
    near_h, far_h, xs, deriv, y2_h, xm, xa = refs
    _, rows, cols, depth = far.shape
    half = rows // 2
    tables = ((ta0, tb0), (ta1, tb1))
    for comp in range(2):
        base = 0 if comp == 0 else DEEP[0]
        scale = scales[comp] if later else None

        def load(row):
            pairs = ((left, left_new), (halo, halo_new), (right, right_new)) if later else ((left, None), (halo, None), (right, None))
            return jnp.concatenate(
                [blend(a[base + row], b[base + row] if later else None, scale) for a, b in pairs], axis=0
            )

        stage1_columns(load, DEEP[comp] // 2, comp, tables[comp], near_h, far_h, cols, 3, 0)

    def pick(own, edge, index, row, window):
        comp = index // 2 if own is near else index
        if 0 <= row < rows:
            return own[index, row, window, :]
        return edge[index, row + DEEP[comp] if top else row - rows, window, :]

    first = -DERIV if top else rows - DERIV
    stage1_rows(lambda f, row, window: pick(near, near_h, f, row, window), first, 2 * DERIV, xs)
    gates = [inside[0], None] if top else [None, inside[1]]
    stage1_depth(xs, 2 * DERIV, DERIV, wz3, wz2, deriv, inside, gates)
    stage2_columns(deriv, 2 * DERIV, wy2, wy3, y2_h, 7)

    start = 0 if top else half

    @pl.loop(0, cols // 8)
    def _(t):
        window = pl.ds(pl.multiple_of(t * 8, 8), 8)

        def second(index, row):
            if DERIV <= row < rows - DERIV:
                return y2[index, row - DERIV, window, :]
            return y2_h[index, row - first, window, :]

        for which, kind in ((0, 1), (1, 0)):
            for comp in range(2):
                reach = REACH[comp]
                taps = row_taps(kind, RADII[comp], SEGMENTS[comp] if kind == 0 else 1.0)
                values = [second(2 * which + comp, row) for row in range(start - reach, start + half + reach)]
                for i, value in enumerate(smooth_rows(values, taps, half, reach)):
                    xm[2 * which + comp, i, window, :] = value
        scale = row_taps(2, 0.0, 1.0)[8]
        for comp in range(2):
            values = [pick(far, far_h, comp, row, window) for row in range(start - FAR, start + half + FAR)]
            for i, value in enumerate(smooth_rows_exp(values, scale, half)):
                xa[comp, i, window, :] = value

    sums[...] = jnp.zeros_like(sums)
    step = half // 2
    for i in range(0, half, step):
        part = slice(i, i + step)
        flat = lambda ref, p: ref[p, part].reshape(step * cols, depth)
        pore = solid[start + i : start + i + step].reshape(step * cols, depth) == 0
        pull = split_dot(jnp.concatenate([flat(xa, 0), flat(xa, 1)], axis=1), wza[...])
        for comp, wz in ((0, wzm0), (1, wzm1)):
            mu = split_dot(jnp.concatenate([flat(xm, 2 + comp), flat(xm, comp)], axis=1), wz[...])
            mu = mu + pull[:, comp * depth : (comp + 1) * depth]
            value = jnp.where(pore, jnp.exp(-mu), 0.0)
            proposal[comp, part] = value.reshape(step, cols, depth)
            sums[comp] += value.reshape(step * cols // 8, 8, depth).sum(0)
    if not last:
        base = 0
        for comp in range(2):
            part = slice(0, DEEP[comp]) if top else slice(half - DEEP[comp], half)
            packed[base : base + DEEP[comp]] = proposal[comp, part]
            base += DEEP[comp]


def in_vmem(count):
    return [pl.BlockSpec(memory_space=pltpu.VMEM)] * count


def params(mebibytes):
    return pltpu.CompilerParams(vmem_limit_bytes=mebibytes * 1024 * 1024)


def shape(*sizes):
    return jax.ShapeDtypeStruct(sizes, F32)


def tables_for(cols, depth):
    first = [t for comp in range(2) for t in stage1_tables(comp, cols)]
    first += [depth_table([(kind, r) for r in RADII], depth) for kind in range(2)]
    first += [stage2_table(1, cols), stage2_table(0, cols)]
    second = [depth_table([(0, r), (1, r)], depth) for r in RADII] + [attraction_table(depth)]
    return first, second


COST = pl.CostEstimate(flops=1000, bytes_accessed=1000, transcendentals=0)


def mid(later, scalars, blocks, tables):
    rows, cols, depth = blocks[1].shape
    wide, count = cols + 2 * WIDE, rows - 2 * DERIV
    outs = [shape(4, rows, wide, depth), shape(2, rows, cols, depth), shape(4, count, cols, depth)]
    if not later:
        outs.append(shape(sum(DEEP), cols, depth))
    return pl.pallas_call(
        functools.partial(mid_kernel, later),
        out_shape=tuple(outs),
        in_specs=[pl.BlockSpec(memory_space=pltpu.SMEM)] * len(scalars) + in_vmem(len(blocks) + len(tables)),
        out_specs=tuple(in_vmem(len(outs))),
        scratch_shapes=[pltpu.VMEM((4, count, wide, depth), F32), pltpu.VMEM((2, count, wide, depth), F32)],
        compiler_params=params(24),
        cost_estimate=COST,
        name="mid",
    )(*scalars, *blocks, *tables)


def edge(top, later, last, scalars, blocks, tables):
    rows, cols, depth = blocks[-1].shape
    wide, half = cols + 2 * WIDE, rows // 2
    f32 = lambda *s: pltpu.VMEM(s, F32)
    outs = [shape(2, half, cols, depth), shape(2, 8, depth)]
    if not last:
        outs.append(shape(sum(DEEP), cols, depth))
    return pl.pallas_call(
        functools.partial(edge_kernel, top, later, last),
        out_shape=tuple(outs),
        in_specs=[pl.BlockSpec(memory_space=pltpu.SMEM)] * len(scalars) + in_vmem(len(blocks) + len(tables)),
        out_specs=tuple(in_vmem(len(outs))),
        scratch_shapes=[
            f32(4, DEEP[1], wide, depth),
            f32(2, DEEP[1], cols, depth),
            f32(4, 2 * DERIV, wide, depth),
            f32(2, 2 * DERIV, wide, depth),
            f32(4, 2 * DERIV, cols, depth),
            f32(4, half, cols, depth),
            f32(2, half, cols, depth),
        ],
        compiler_params=params(32),
        cost_estimate=COST,
        name="edge_top" if top else "edge_bottom",
    )(*scalars, *blocks, *tables)


def shift(value, axis, step):
    count = lax.axis_size(axis)
    return lax.ppermute(value, axis, [(i, i + step) for i in range(count) if 0 <= i + step < count])


def columns_out(last, first):
    return shift(last, "gy", 1), shift(first, "gy", -1)


def start_kernel(own, solid, lower, last, first):
    _, rows, cols, _ = own.shape
    width = 2 * WIDE
    base = 0
    for comp in range(2):
        part = slice(rows - DEEP[comp], rows)
        lower[base : base + DEEP[comp]] = jnp.where(solid[part] == 0, own[comp, part], 0.0)
        base += DEEP[comp]
        last[comp] = jnp.where(solid[:, cols - width :] == 0, own[comp, :, cols - width :], 0.0)
        first[comp] = jnp.where(solid[:, :width] == 0, own[comp, :, :width], 0.0)


def start_pack(own, solid):
    _, rows, cols, depth = own.shape
    side = shape(2, rows, 2 * WIDE, depth)
    return pl.pallas_call(
        start_kernel,
        out_shape=(shape(sum(DEEP), cols, depth), side, side),
        in_specs=in_vmem(2),
        out_specs=tuple(in_vmem(3)),
        compiler_params=params(12),
        cost_estimate=COST,
        name="start_pack",
    )(own, solid)


def sides_kernel(after, value, last, first):
    cols, width = value.shape[1], 2 * WIDE
    last[...] = value[:, cols - width :]
    first[...] = value[:, :width]


def sides_pack(after, value):
    count, _, depth = value.shape
    side = shape(count, 2 * WIDE, depth)
    return pl.pallas_call(
        sides_kernel,
        out_shape=(side, side),
        in_specs=[pl.BlockSpec(memory_space=pl.ANY)] + in_vmem(1),
        out_specs=tuple(in_vmem(2)),
        compiler_params=params(6),
        cost_estimate=COST,
        name="sides_pack",
    )(after, value)


def columns_kernel(top, bottom, last, first):
    half, cols, width = top.shape[1], top.shape[2], 2 * WIDE
    for ref, part in ((top, slice(0, half)), (bottom, slice(half, 2 * half))):
        last[:, part] = ref[:, :, cols - width :]
        first[:, part] = ref[:, :, :width]


def columns_pack(top, bottom):
    _, half, _, depth = top.shape
    side = shape(2, 2 * half, 2 * WIDE, depth)
    return pl.pallas_call(
        columns_kernel,
        out_shape=(side, side),
        in_specs=in_vmem(2),
        out_specs=tuple(in_vmem(2)),
        compiler_params=params(12),
        cost_estimate=COST,
        name="columns_pack",
    )(top, bottom)


def sum_kernel(after, one, two, out):
    out[...] = one[...] + two[...]


def sum_after(after, one, two):
    return pl.pallas_call(
        sum_kernel,
        out_shape=shape(*one.shape),
        in_specs=[pl.BlockSpec(memory_space=pl.ANY)] + in_vmem(2),
        out_specs=in_vmem(1)[0],
        compiler_params=params(2),
        cost_estimate=COST,
        name="sum_after",
    )(after, one, two)


def copy_kernel(after, value, out):
    out[...] = value[...]


def copy_after(after, value):
    return pl.pallas_call(
        copy_kernel,
        out_shape=shape(*value.shape),
        in_specs=[pl.BlockSpec(memory_space=pl.ANY)] + in_vmem(1),
        out_specs=in_vmem(1)[0],
        compiler_params=params(6),
        cost_estimate=COST,
        name="copy_after",
    )(after, value)


def add_partners(sums, axis, first, end):
    count = lax.axis_size(axis)
    for bit in range(first, end):
        sums = sums + lax.ppermute(sums, axis, [(i, i ^ (1 << bit)) for i in range(count)])
    return sums


def bits(axis):
    count = lax.axis_size(axis)
    assert count & (count - 1) == 0
    return count.bit_length() - 1


def body(density_init, solid_mask, loadings):
    rows, cols, depth = solid_mask.shape
    total_cells = float(rows * lax.axis_size("gx") * cols * lax.axis_size("gy") * depth)
    first, second = tables_for(cols, depth)
    place = [(lax.axis_index(a), lax.axis_size(a)) for a in AXES]
    inside = jnp.stack([v for i, n in place for v in (i > 0, i + 1 < n)]).astype(F32)

    def scale_of(sums):
        return DAMPING * loadings * total_cells / sums.sum(axis=(1, 2))

    both = first + second
    lower, last, head = start_pack(density_init, solid_mask)
    above = shift(lower, "gx", 1)
    left, right = columns_out(last, head)
    near, far, y2, upper = mid(False, [inside], [density_init, solid_mask, left, right], first)
    below = shift(upper, "gx", -1)
    top_sides = columns_out(*sides_pack(far, above))
    top, top_sums, upper = edge(True, False, False, [inside], [above, *top_sides, near, far, y2, solid_mask], both)
    below_new = shift(upper, "gx", -1)
    bottom_sides = columns_out(*sides_pack(top_sums, below))
    bottom, bottom_sums, lower = edge(False, False, False, [inside], [below, *bottom_sides, near, far, y2, solid_mask], both)
    left_new, right_new = columns_out(*columns_pack(top, bottom))
    sides_new = columns_out(*sides_pack(bottom_sums, below_new))
    sums = add_partners(sum_after(below_new, top_sums, bottom_sums), "gx", 0, 1)
    above_new = shift(copy_after(sums, lower), "gx", 1)
    scale = scale_of(add_partners(add_partners(sums, "gy", 0, bits("gy")), "gx", 1, bits("gx")))
    near, far, y2 = mid(True, [inside, scale], [density_init, solid_mask, top, bottom, left, right, left_new, right_new], first)
    old, new = [below, *bottom_sides], [below_new, *sides_new]
    last_bottom, bottom_sums = edge(False, True, True, [inside, scale], [*old, *new, near, far, y2, solid_mask], both)
    sides_new = columns_out(*sides_pack(far, above_new))
    old, new = [above, *top_sides], [above_new, *sides_new]
    last_top, top_sums = edge(True, True, True, [inside, scale], [*old, *new, near, far, y2, solid_mask], both)
    sums = top_sums + bottom_sums
    for axis in reversed(AXES):
        sums = add_partners(sums, axis, 0, bits(axis))
    last_scale = scale_of(sums)
    keep = 1.0 - DAMPING
    spread = lambda value: value[:, None, None, None]
    start = jnp.where(solid_mask[None] == 0, density_init, 0.0)
    once = keep * start + spread(scale) * jnp.concatenate([top, bottom], axis=1)
    return keep * once + spread(last_scale) * jnp.concatenate([last_top, last_bottom], axis=1)


def solution(mesh):
    in_specs = (P(None, "gx", "gy", None), P("gx", "gy", None), P())
    out_specs = P(None, "gx", "gy", None)
    return jax.shard_map(body, mesh=mesh, in_specs=in_specs, out_specs=out_specs, check_vma=False)
```

```python
import functools

import jax
import jax.numpy as jnp
import ml_dtypes
import numpy as np
from jax import lax
from jax.experimental import pallas as pl
from jax.experimental.pallas import tpu as pltpu
from jax.sharding import PartitionSpec as P

ITERS = 2
SEGMENTS = (1.5131, 1.0)
RADII = (6.0, 8.0)
CROSS = 0.25
DAMPING = 0.3
ATTRACT = ((0.3, 0.22), (0.22, 0.16))
REACH = (5, 7)
FAR = 8
DERIV = REACH[1]
DEEP = tuple(DERIV + r for r in REACH)
WIDE = 8
AXES = ("gx", "gy")
BF16 = jnp.bfloat16
F32 = jnp.float32


def raw_profile(kind, radius):
    offset = np.arange(17) - 8.0
    if kind == 0:
        return np.maximum(radius * radius - offset * offset, 0.0)
    if kind == 1:
        return offset * offset * np.maximum(radius * radius - offset * offset, 0.0)
    return np.exp(-np.abs(offset) / 4.0)


def split_bf16(table):
    high = table.astype(np.float32).astype(ml_dtypes.bfloat16)
    low = (table - high.astype(np.float64)).astype(np.float32).astype(ml_dtypes.bfloat16)
    return high, low


def column_band(kind, radius, count, columns, first):
    band = np.zeros((count, columns))
    for o in range(count):
        band[o, first + o : first + o + 17] = raw_profile(kind, radius)
    return band


def depth_band(kind, radius, depth):
    taps = raw_profile(kind, radius)
    band = np.zeros((depth, depth))
    for column in range(depth):
        for offset in range(17):
            source = column + offset - 8
            if 0 <= source < depth:
                band[source, column] = taps[offset]
    return band


def stage1_tables(comp, cols):
    wide = cols + 2 * WIDE
    pack = column_band(0, RADII[comp], wide, wide + 16, 0)
    rest = np.concatenate(
        [column_band(1, RADII[comp], wide, wide + 16, 0), column_band(2, 0.0, cols, wide + 16, WIDE)]
    )
    high, low = split_bf16(np.concatenate([pack, rest]))
    return {f"first{comp}": np.concatenate([high, high], axis=1), f"rest{comp}": low[wide:]}


def stage2_table(kind, cols):
    high, low = split_bf16(np.concatenate([column_band(kind, r, cols, cols + 16, 0) for r in RADII]))
    return np.concatenate([high, high] if kind == 0 else [high, high, low], axis=1)


def depth_table(kinds, depth):
    high, low = split_bf16(np.concatenate([depth_band(kind, radius, depth) for kind, radius in kinds]))
    return np.concatenate([high, low], axis=1)


def attraction_tables(depth):
    band = depth_band(2, 0.0, depth)
    high, low = split_bf16(-np.concatenate([np.concatenate([ATTRACT[i][j] * band for i in range(2)], axis=1) for j in range(2)]))
    return {"pull_high": high, "pull_low": low}


@functools.lru_cache
def packed_tables(cols, depth):
    tables = {**stage1_tables(0, cols), **stage1_tables(1, cols), **attraction_tables(depth)}
    tables |= {f"depth{kind}": depth_table([(kind, r) for r in RADII], depth) for kind in range(2)}
    tables |= {f"last{comp}": depth_table([(0, r), (1, r)], depth) for comp, r in enumerate(RADII)}
    tables |= {f"second{kind}": stage2_table(kind, cols) for kind in range(2)}
    width = max(t.shape[1] for t in tables.values())
    places, start = {}, 0
    for name, table in tables.items():
        places[name] = (start, *table.shape)
        start += table.shape[0]
    whole = np.zeros((start, width), ml_dtypes.bfloat16)
    for name, table in tables.items():
        whole[places[name][0] : places[name][0] + table.shape[0], : table.shape[1]] = table
    return whole, places


class Tables:
    def __init__(self, ref, cols, depth):
        self.ref, self.places = ref, packed_tables(cols, depth)[1]

    def __getitem__(self, name):
        start, rows, columns = self.places[name]
        return self.ref[start : start + rows, :columns]


def row_taps(kind, radius, scale):
    taps = raw_profile(kind, radius)
    return [float(v) for v in taps * (scale / taps.sum() ** 3)]


def split(field):
    high = field.astype(BF16)
    return high, (field - high.astype(F32)).astype(BF16)


def smooth_rows(values, taps, count, reach):
    out = []
    for i in range(count):
        total = None
        for k in range(reach + 1):
            if taps[8 + k] == 0.0:
                continue
            pair = values[i + reach] if k == 0 else values[i + reach - k] + values[i + reach + k]
            term = taps[8 + k] * pair
            total = term if total is None else total + term
        out.append(total)
    return out


def smooth_rows_exp(values, scale, count):
    q = float(np.exp(-0.25))
    q9 = q**9
    up = values[0]
    for j in range(1, 9):
        up = up * q + values[j]
    ups = [up]
    for i in range(1, count):
        up = up * q + (values[i + 8] - q9 * values[i - 1])
        ups.append(up)
    down = values[count + 15]
    for j in range(1, 8):
        down = down * q + values[count + 15 - j]
    down = down * q
    out = [None] * count
    out[count - 1] = scale * (ups[count - 1] + down)
    for i in range(count - 2, -1, -1):
        down = down * q + (q * values[i + 9] - q9 * values[i + 17])
        out[i] = scale * (ups[i] + down)
    return out


def split_dot(pair, table):
    high, low = split(pair)
    width = table.shape[1] // 2
    both = jnp.dot(high, table, preferred_element_type=F32)
    rest = jnp.dot(low, table[:, :width], preferred_element_type=F32)
    return both[:, :width] + both[:, width:] + rest


def stage1_columns(load, pairs, comp, tables, near, far, cols, unroll, begin):
    wide = cols + 2 * WIDE

    @pl.loop(0, pairs, unroll=unroll)
    def _(i):
        high, low = split(jnp.concatenate([load(2 * i), load(2 * i + 1)], axis=1))
        first = jnp.dot(tables[f"first{comp}"], jnp.concatenate([high, low], axis=0), preferred_element_type=F32)
        rest = first[wide:] + jnp.dot(tables[f"rest{comp}"], high, preferred_element_type=F32)
        depth = high.shape[1] // 2
        for j in range(2):
            lanes = slice(j * depth, (j + 1) * depth)
            row = begin + 2 * i + j
            near[2 * comp, row] = first[:wide, lanes]
            near[2 * comp + 1, row] = rest[:wide, lanes]
            far[comp, row] = rest[wide:, lanes]


def stage1_rows(load, first, count, out):
    wide = out.shape[2]

    @pl.loop(0, wide // 8)
    def _(t):
        window = pl.ds(pl.multiple_of(t * 8, 8), 8)
        for comp in range(2):
            reach = REACH[comp]
            for kind in range(2):
                field = 2 * comp + kind
                taps = row_taps(kind, RADII[comp], SEGMENTS[comp] if kind == 0 else 1.0)
                values = [load(field, row, window) for row in range(first - reach, first + count + reach)]
                for i, value in enumerate(smooth_rows(values, taps, count, reach)):
                    out[field, i, window, :] = value


def stage1_depth(xs, count, step, tables, deriv, place, gates):
    wide, depth = xs.shape[2:]
    for i, start in enumerate(range(0, count, step)):
        rows = slice(start, start + step)
        pair = lambda p: jnp.concatenate([xs[q, rows].reshape(step * wide, depth) for q in (p, p + 2)], axis=1)
        n3 = split_dot(pair(0), tables["depth0"])
        n2 = split_dot(pair(1), tables["depth1"])
        one = 1.0 + n3
        two = (jnp.log(one) + 2.0 * CROSS * n2 * one).reshape(step, wide, depth)
        three = (n2 / one + CROSS * n2 * n2).reshape(step, wide, depth)
        for which, value in enumerate((two, three)):
            if gates[i] is not None:
                value = value * place[gates[i]].astype(F32)
            deriv[which, rows, :WIDE] = value[:, :WIDE] * place[2].astype(F32)
            deriv[which, rows, WIDE : wide - WIDE] = value[:, WIDE : wide - WIDE]
            deriv[which, rows, wide - WIDE :] = value[:, wide - WIDE :] * place[3].astype(F32)


def stage2_columns(deriv, count, tables, out, unroll):
    cols = out.shape[2]

    @pl.loop(0, count // 2, unroll=unroll)
    def _(i):
        for which, kind in ((0, 1), (1, 0)):
            high, low = split(jnp.concatenate([deriv[which, 2 * i], deriv[which, 2 * i + 1]], axis=1))
            stacked = [high, low, high] if which == 0 else [high, low]
            result = jnp.dot(tables[f"second{kind}"], jnp.concatenate(stacked, axis=0), preferred_element_type=F32)
            depth = high.shape[1] // 2
            for comp in range(2):
                for j in range(2):
                    out[2 * which + comp, 2 * i + j] = result[comp * cols : (comp + 1) * cols, j * depth : (j + 1) * depth]


def blend(first, second, scale):
    return first if scale is None else (1.0 - DAMPING) * first + scale * second


def side_rows(pair, index, odd):
    one, two = pair[0][index], pair[1][index]
    return jnp.where(odd, one, two), jnp.where(odd, two, one)


def mid_kernel(later, place, *refs):
    if later:
        scales, own, solid, top, bottom, *refs = refs
        sides, sides_new, refs = refs[:2], refs[2:4], refs[4:]
    else:
        own, solid, *refs = refs
        sides, refs = refs[:2], refs[2:]
    table_ref, near, far, y2, extra, xs, deriv = refs
    _, rows, cols, depth = own.shape
    half = rows // 2
    tables = Tables(table_ref, cols, depth)
    odd = place[4] == 1
    if not later:
        base = 0
        for comp in range(2):
            part = slice(0, DEEP[comp])
            extra[base : base + DEEP[comp]] = jnp.where(solid[part] == 0, own[comp, part], 0.0)
            base += DEEP[comp]
    for comp in range(2):
        scale = scales[comp] if later else None
        for begin, ref in ((0, top), (half, bottom)) if later else ((0, None),):

            def load(row):
                row = begin + row
                value = jnp.where(solid[row] == 0, own[comp, row], 0.0)
                left, right = side_rows(sides, (comp, row), odd)
                if later:
                    value = blend(value, ref[comp, row - begin], scale)
                    extra[comp, row] = (1.0 - DAMPING) * value
                    left_new, right_new = side_rows(sides_new, (comp, row), odd)
                    left, right = blend(left, left_new, scale), blend(right, right_new, scale)
                return jnp.concatenate([left, value, right], axis=0)

            count = half if later else rows
            stage1_columns(load, count // 2, comp, tables, near, far, cols, 4, begin)
    count = rows - 2 * DERIV
    stage1_rows(lambda field, row, window: near[field, row, window, :], DERIV, count, xs)
    stage1_depth(xs, count, count // 3, tables, deriv, place, [None] * 3)
    stage2_columns(deriv, count, tables, y2, 3)


def edge_kernel(top, later, last, place, *refs):
    if later:
        scales, halo, *refs = refs
        sides, halo_new, sides_new, refs = refs[:2], refs[2], refs[3:5], refs[5:]
    else:
        halo, *refs = refs
        sides, refs = refs[:2], refs[2:]
    near, far, y2, solid, table_ref, proposal, sums, *refs = refs
    if not last:
        packed, *refs = refs
    near_h, far_h, xs, deriv, y2_h, xm, xa = refs
    _, rows, cols, depth = far.shape
    half = rows // 2
    tables = Tables(table_ref, cols, depth)
    odd = place[4] == 1
    for comp in range(2):
        base = 0 if comp == 0 else DEEP[0]
        scale = scales[comp] if later else None

        def load(row):
            value = halo[base + row]
            left, right = side_rows(sides, base + row, odd)
            if later:
                value = blend(value, halo_new[base + row], scale)
                left_new, right_new = side_rows(sides_new, base + row, odd)
                left, right = blend(left, left_new, scale), blend(right, right_new, scale)
            return jnp.concatenate([left, value, right], axis=0)

        stage1_columns(load, DEEP[comp] // 2, comp, tables, near_h, far_h, cols, 3, 0)

    def pick(own, edge, index, row, window):
        comp = index // 2 if own is near else index
        if 0 <= row < rows:
            return own[index, row, window, :]
        return edge[index, row + DEEP[comp] if top else row - rows, window, :]

    first = -DERIV if top else rows - DERIV
    stage1_rows(lambda f, row, window: pick(near, near_h, f, row, window), first, 2 * DERIV, xs)
    gates = [0, None] if top else [None, 1]
    stage1_depth(xs, 2 * DERIV, DERIV, tables, deriv, place, gates)
    stage2_columns(deriv, 2 * DERIV, tables, y2_h, 7)

    start = 0 if top else half

    @pl.loop(0, cols // 8)
    def _(t):
        window = pl.ds(pl.multiple_of(t * 8, 8), 8)

        def second(index, row):
            if DERIV <= row < rows - DERIV:
                return y2[index, row - DERIV, window, :]
            return y2_h[index, row - first, window, :]

        for which, kind in ((0, 1), (1, 0)):
            for comp in range(2):
                reach = REACH[comp]
                taps = row_taps(kind, RADII[comp], SEGMENTS[comp] if kind == 0 else 1.0)
                values = [second(2 * which + comp, row) for row in range(start - reach, start + half + reach)]
                for i, value in enumerate(smooth_rows(values, taps, half, reach)):
                    xm[2 * which + comp, i, window, :] = value
        scale = row_taps(2, 0.0, 1.0)[8]
        for comp in range(2):
            values = [pick(far, far_h, comp, row, window) for row in range(start - FAR, start + half + FAR)]
            for i, value in enumerate(smooth_rows_exp(values, scale, half)):
                xa[comp, i, window, :] = value

    sums[...] = jnp.zeros_like(sums)
    step = half // 2
    for i in range(0, half, step):
        part = slice(i, i + step)
        flat = lambda ref, p: ref[p, part].reshape(step * cols, depth)
        pore = solid[start + i : start + i + step].reshape(step * cols, depth) == 0
        high, low = split(jnp.concatenate([flat(xa, 0), flat(xa, 1)], axis=1))
        pull = jnp.dot(high, tables["pull_high"], preferred_element_type=F32)
        pull += jnp.dot(high, tables["pull_low"], preferred_element_type=F32)
        pull += jnp.dot(low, tables["pull_high"], preferred_element_type=F32)
        for comp in range(2):
            mu = split_dot(jnp.concatenate([flat(xm, 2 + comp), flat(xm, comp)], axis=1), tables[f"last{comp}"])
            mu = mu + pull[:, comp * depth : (comp + 1) * depth]
            value = jnp.where(pore, jnp.exp(-mu), 0.0)
            proposal[comp, part] = value.reshape(step, cols, depth)
            sums[comp] += value.reshape(step * cols // 8, 8, depth).sum(0)
    if not last:
        base = 0
        for comp in range(2):
            part = slice(0, DEEP[comp]) if top else slice(half - DEEP[comp], half)
            packed[base : base + DEEP[comp]] = proposal[comp, part]
            base += DEEP[comp]


def in_vmem(count):
    return [pl.BlockSpec(memory_space=pltpu.VMEM)] * count


def params(mebibytes):
    return pltpu.CompilerParams(vmem_limit_bytes=mebibytes * 1024 * 1024)


def shape(*sizes):
    return jax.ShapeDtypeStruct(sizes, F32)


COST = pl.CostEstimate(flops=1000, bytes_accessed=1000, transcendentals=0)


def mid(later, scalars, blocks, table):
    rows, cols, depth = blocks[1].shape
    wide, count = cols + 2 * WIDE, rows - 2 * DERIV
    outs = [shape(4, rows, wide, depth), shape(2, rows, cols, depth), shape(4, count, cols, depth)]
    outs.append(shape(2, rows, cols, depth) if later else shape(sum(DEEP), cols, depth))
    return pl.pallas_call(
        functools.partial(mid_kernel, later),
        out_shape=tuple(outs),
        in_specs=[pl.BlockSpec(memory_space=pltpu.SMEM)] * len(scalars) + in_vmem(len(blocks) + 1),
        out_specs=tuple(in_vmem(len(outs))),
        scratch_shapes=[pltpu.VMEM((4, count, wide, depth), F32), pltpu.VMEM((2, count, wide, depth), F32)],
        compiler_params=params(24),
        cost_estimate=COST,
        name="mid",
    )(*scalars, *blocks, table)


def edge(top, later, last, scalars, blocks, table):
    rows, cols, depth = blocks[-1].shape
    wide, half = cols + 2 * WIDE, rows // 2
    f32 = lambda *s: pltpu.VMEM(s, F32)
    outs = [shape(2, half, cols, depth), shape(2, 8, depth)]
    if not last:
        outs.append(shape(sum(DEEP), cols, depth))
    return pl.pallas_call(
        functools.partial(edge_kernel, top, later, last),
        out_shape=tuple(outs),
        in_specs=[pl.BlockSpec(memory_space=pltpu.SMEM)] * len(scalars) + in_vmem(len(blocks) + 1),
        out_specs=tuple(in_vmem(len(outs))),
        scratch_shapes=[
            f32(4, DEEP[1], wide, depth),
            f32(2, DEEP[1], cols, depth),
            f32(4, 2 * DERIV, wide, depth),
            f32(2, 2 * DERIV, wide, depth),
            f32(4, 2 * DERIV, cols, depth),
            f32(4, half, cols, depth),
            f32(2, half, cols, depth),
        ],
        compiler_params=params(32),
        cost_estimate=COST,
        name="edge_top" if top else "edge_bottom",
    )(*scalars, *blocks, table)


def shift(value, axis, step):
    count = lax.axis_size(axis)
    return lax.ppermute(value, axis, [(i, i + step) for i in range(count) if 0 <= i + step < count])


def swap_columns(even, odd):
    count = lax.axis_size("gy")
    pairs = lambda first: [p for i in range(first, count - 1, 2) for p in ((i, i + 1), (i + 1, i))]
    return lax.ppermute(even, "gy", pairs(0)), lax.ppermute(odd, "gy", pairs(1))


def side_starts(place, cols):
    right, left = cols - 2 * WIDE, 0
    odd = place[4]
    return pl.multiple_of(right * (1 - odd), 8), pl.multiple_of(right * odd, 8)


def first_rows_kernel(own, solid, out, density, mask, sems):
    rows = own.shape[1]
    most = max(DEEP)
    copies = [
        pltpu.make_async_copy(own.at[:, rows - most :], density, sems.at[0]),
        pltpu.make_async_copy(solid.at[rows - most :], mask, sems.at[1]),
    ]
    for copy in copies:
        copy.start()
    for copy in copies:
        copy.wait()
    base = 0
    for comp in range(2):
        out[base : base + DEEP[comp]] = jnp.where(mask[most - DEEP[comp] :] == 0, density[comp, most - DEEP[comp] :], 0.0)
        base += DEEP[comp]


def first_rows(own, solid):
    _, _, cols, depth = own.shape
    return pl.pallas_call(
        first_rows_kernel,
        out_shape=shape(sum(DEEP), cols, depth),
        in_specs=[pl.BlockSpec(memory_space=pltpu.HBM)] * 2,
        out_specs=in_vmem(1)[0],
        scratch_shapes=[
            pltpu.VMEM((2, max(DEEP), cols, depth), F32),
            pltpu.VMEM((max(DEEP), cols, depth), jnp.int32),
            pltpu.SemaphoreType.DMA((2,)),
        ],
        compiler_params=params(56),
        cost_estimate=COST,
        name="first_rows",
    )(own, solid)


def first_columns_kernel(place, own, solid, even, odd, density, mask, sems):
    copies = []
    for i, start in enumerate(side_starts(place, own.shape[2])):
        window = pl.ds(start, 2 * WIDE)
        copies.append(pltpu.make_async_copy(own.at[:, :, window], density.at[i], sems.at[i]))
        copies.append(pltpu.make_async_copy(solid.at[:, window], mask.at[i], sems.at[2 + i]))
    for copy in copies:
        copy.start()
    for copy in copies:
        copy.wait()
    for i, out in enumerate((even, odd)):
        for comp in range(2):
            out[comp] = jnp.where(mask[i] == 0, density[i, comp], 0.0)


def first_columns(place, own, solid):
    _, rows, _, depth = own.shape
    side = shape(2, rows, 2 * WIDE, depth)
    return pl.pallas_call(
        first_columns_kernel,
        out_shape=(side, side),
        in_specs=[pl.BlockSpec(memory_space=pltpu.SMEM)] + [pl.BlockSpec(memory_space=pltpu.HBM)] * 2,
        out_specs=tuple(in_vmem(2)),
        scratch_shapes=[
            pltpu.VMEM((2, 2, rows, 2 * WIDE, depth), F32),
            pltpu.VMEM((2, rows, 2 * WIDE, depth), jnp.int32),
            pltpu.SemaphoreType.DMA((4,)),
        ],
        compiler_params=params(56),
        cost_estimate=COST,
        name="first_columns",
    )(place, own, solid)


def sides_kernel(place, after, value, even, odd, sems):
    copies = []
    for i, (start, out) in enumerate(zip(side_starts(place, value.shape[1]), (even, odd))):
        copies.append(pltpu.make_async_copy(value.at[:, pl.ds(start, 2 * WIDE)], out, sems.at[i]))
    for copy in copies:
        copy.start()
    for copy in copies:
        copy.wait()


def sides_pack(place, after, value):
    count, _, depth = value.shape
    side = shape(count, 2 * WIDE, depth)
    return pl.pallas_call(
        sides_kernel,
        out_shape=(side, side),
        in_specs=[pl.BlockSpec(memory_space=pltpu.SMEM)] + [pl.BlockSpec(memory_space=pl.ANY)] * 2,
        out_specs=tuple(in_vmem(2)),
        scratch_shapes=[pltpu.SemaphoreType.DMA((2,))],
        compiler_params=params(4),
        cost_estimate=COST,
        name="sides_pack",
    )(place, after, value)


def columns_kernel(place, top, bottom, even, odd):
    half, cols = top.shape[1:3]
    for start, out in zip(side_starts(place, cols), (even, odd)):
        out[:, :half] = top[:, :, pl.ds(start, 2 * WIDE)]
        out[:, half:] = bottom[:, :, pl.ds(start, 2 * WIDE)]


def columns_pack(place, top, bottom):
    _, half, _, depth = top.shape
    side = shape(2, 2 * half, 2 * WIDE, depth)
    return pl.pallas_call(
        columns_kernel,
        out_shape=(side, side),
        in_specs=[pl.BlockSpec(memory_space=pltpu.SMEM)] + in_vmem(2),
        out_specs=tuple(in_vmem(2)),
        compiler_params=params(8),
        cost_estimate=COST,
        name="columns_pack",
    )(place, top, bottom)


def sum_kernel(after, one, two, out):
    out[...] = one[...] + two[...]


def sum_after(after, one, two):
    return pl.pallas_call(
        sum_kernel,
        out_shape=shape(*one.shape),
        in_specs=[pl.BlockSpec(memory_space=pl.ANY)] + in_vmem(2),
        out_specs=in_vmem(1)[0],
        compiler_params=params(2),
        cost_estimate=COST,
        name="sum_after",
    )(after, one, two)


def copy_kernel(after, value, out):
    out[...] = value[...]


def copy_after(after, value):
    return pl.pallas_call(
        copy_kernel,
        out_shape=shape(*value.shape),
        in_specs=[pl.BlockSpec(memory_space=pl.ANY)] + in_vmem(1),
        out_specs=in_vmem(1)[0],
        compiler_params=params(6),
        cost_estimate=COST,
        name="copy_after",
    )(after, value)


def add_partners(sums, axis, first, end):
    count = lax.axis_size(axis)
    for bit in range(first, end):
        sums = sums + lax.ppermute(sums, axis, [(i, i ^ (1 << bit)) for i in range(count)])
    return sums


def bits(axis):
    count = lax.axis_size(axis)
    assert count & (count - 1) == 0
    return count.bit_length() - 1


def body(density_init, solid_mask, loadings):
    rows, cols, depth = solid_mask.shape
    total_cells = float(rows * lax.axis_size("gx") * cols * lax.axis_size("gy") * depth)
    table = jnp.asarray(packed_tables(cols, depth)[0])
    places = [(lax.axis_index(a), lax.axis_size(a)) for a in AXES]
    place = jnp.stack([v for i, n in places for v in (i > 0, i + 1 < n)] + [places[1][0] % 2 == 1]).astype(jnp.int32)

    def scale_of(sums):
        return DAMPING * loadings * total_cells / sums.sum(axis=(1, 2))

    above = shift(first_rows(density_init, solid_mask), "gx", 1)
    columns = swap_columns(*first_columns(place, density_init, solid_mask))
    near, far, y2, upper = mid(False, [place], [density_init, solid_mask, *columns], table)
    below = shift(upper, "gx", -1)
    top_sides = swap_columns(*sides_pack(place, far, above))
    top, top_sums, upper = edge(True, False, False, [place], [above, *top_sides, near, far, y2, solid_mask], table)
    below_new = shift(upper, "gx", -1)
    bottom_sides = swap_columns(*sides_pack(place, top_sums, below))
    bottom, bottom_sums, lower = edge(False, False, False, [place], [below, *bottom_sides, near, far, y2, solid_mask], table)
    columns_new = swap_columns(*columns_pack(place, top, bottom))
    sides_new = swap_columns(*sides_pack(place, bottom_sums, below_new))
    sums = add_partners(sum_after(below_new, top_sums, bottom_sums), "gx", 0, 1)
    above_new = shift(copy_after(sums, lower), "gx", 1)
    scale = scale_of(add_partners(add_partners(sums, "gy", 0, bits("gy")), "gx", 1, bits("gx")))
    blocks = [density_init, solid_mask, top, bottom, *columns, *columns_new]
    near, far, y2, kept = mid(True, [place, scale], blocks, table)
    blocks = [below, *bottom_sides, below_new, *sides_new, near, far, y2, solid_mask]
    bottom, bottom_sums = edge(False, True, True, [place, scale], blocks, table)
    sides_new = swap_columns(*sides_pack(place, far, above_new))
    blocks = [above, *top_sides, above_new, *sides_new, near, far, y2, solid_mask]
    top, top_sums = edge(True, True, True, [place, scale], blocks, table)
    sums = top_sums + bottom_sums
    for axis in reversed(AXES):
        sums = add_partners(sums, axis, 0, bits(axis))
    return kept + scale_of(sums)[:, None, None, None] * jnp.concatenate([top, bottom], axis=1)


def solution(mesh):
    in_specs = (P(None, "gx", "gy", None), P("gx", "gy", None), P())
    out_specs = P(None, "gx", "gy", None)
    return jax.shard_map(body, mesh=mesh, in_specs=in_specs, out_specs=out_specs, check_vma=False)
```

```python
import functools

import jax
import jax.numpy as jnp
import ml_dtypes
import numpy as np
from jax import lax
from jax.experimental import pallas as pl
from jax.experimental.pallas import tpu as pltpu
from jax.sharding import PartitionSpec as P

ITERS = 2
SEGMENTS = (1.5131, 1.0)
RADII = (6.0, 8.0)
CROSS = 0.25
DAMPING = 0.3
ATTRACT = ((0.3, 0.22), (0.22, 0.16))
REACH = (5, 7)
FAR = 8
DERIV = REACH[1]
DEEP = tuple(DERIV + r for r in REACH)
WIDE = 8
AXES = ("gx", "gy")
BF16 = jnp.bfloat16
F32 = jnp.float32


def raw_profile(kind, radius):
    offset = np.arange(17) - 8.0
    if kind == 0:
        return np.maximum(radius * radius - offset * offset, 0.0)
    if kind == 1:
        return offset * offset * np.maximum(radius * radius - offset * offset, 0.0)
    return np.exp(-np.abs(offset) / 4.0)


def split_bf16(table):
    high = table.astype(np.float32).astype(ml_dtypes.bfloat16)
    low = (table - high.astype(np.float64)).astype(np.float32).astype(ml_dtypes.bfloat16)
    return high, low


def column_band(kind, radius, count, columns, first):
    band = np.zeros((count, columns))
    for o in range(count):
        band[o, first + o : first + o + 17] = raw_profile(kind, radius)
    return band


def depth_band(kind, radius, depth):
    taps = raw_profile(kind, radius)
    band = np.zeros((depth, depth))
    for column in range(depth):
        for offset in range(17):
            source = column + offset - 8
            if 0 <= source < depth:
                band[source, column] = taps[offset]
    return band


def stage1_tables(comp, cols):
    wide = cols + 2 * WIDE
    pack = column_band(0, RADII[comp], wide, wide + 16, 0)
    rest = np.concatenate(
        [column_band(1, RADII[comp], wide, wide + 16, 0), column_band(2, 0.0, cols, wide + 16, WIDE)]
    )
    high, low = split_bf16(np.concatenate([pack, rest]))
    return {f"first{comp}": np.concatenate([high, high], axis=1), f"rest{comp}": low[wide:]}


def stage2_table(kind, cols):
    high, low = split_bf16(np.concatenate([column_band(kind, r, cols, cols + 16, 0) for r in RADII]))
    return np.concatenate([high, high] if kind == 0 else [high, high, low], axis=1)


def depth_table(kinds, depth):
    high, low = split_bf16(np.concatenate([depth_band(kind, radius, depth) for kind, radius in kinds]))
    return np.concatenate([high, low], axis=1)


def attraction_tables(depth):
    band = depth_band(2, 0.0, depth)
    high, low = split_bf16(-np.concatenate([np.concatenate([ATTRACT[i][j] * band for i in range(2)], axis=1) for j in range(2)]))
    return {"pull_high": high, "pull_low": low}


@functools.lru_cache
def packed_tables(cols, depth):
    tables = {**stage1_tables(0, cols), **stage1_tables(1, cols), **attraction_tables(depth)}
    tables |= {f"depth{kind}": depth_table([(kind, r) for r in RADII], depth) for kind in range(2)}
    tables |= {f"last{comp}": depth_table([(0, r), (1, r)], depth) for comp, r in enumerate(RADII)}
    tables |= {f"second{kind}": stage2_table(kind, cols) for kind in range(2)}
    width = max(t.shape[1] for t in tables.values())
    places, start = {}, 0
    for name, table in tables.items():
        places[name] = (start, *table.shape)
        start += table.shape[0]
    whole = np.zeros((start, width), ml_dtypes.bfloat16)
    for name, table in tables.items():
        whole[places[name][0] : places[name][0] + table.shape[0], : table.shape[1]] = table
    return whole, places


class Tables:
    def __init__(self, ref, cols, depth):
        self.ref, self.places = ref, packed_tables(cols, depth)[1]

    def __getitem__(self, name):
        start, rows, columns = self.places[name]
        return self.ref[start : start + rows, :columns]


def row_taps(kind, radius, scale):
    taps = raw_profile(kind, radius)
    return [float(v) for v in taps * (scale / taps.sum() ** 3)]


def split(field):
    high = field.astype(BF16)
    return high, (field - high.astype(F32)).astype(BF16)


def smooth_rows(values, taps, count, reach):
    out = []
    for i in range(count):
        total = None
        for k in range(reach + 1):
            if taps[8 + k] == 0.0:
                continue
            pair = values[i + reach] if k == 0 else values[i + reach - k] + values[i + reach + k]
            term = taps[8 + k] * pair
            total = term if total is None else total + term
        out.append(total)
    return out


def smooth_rows_exp(values, scale, count):
    q = float(np.exp(-0.25))
    q9 = q**9
    up = values[0]
    for j in range(1, 9):
        up = up * q + values[j]
    ups = [up]
    for i in range(1, count):
        up = up * q + (values[i + 8] - q9 * values[i - 1])
        ups.append(up)
    down = values[count + 15]
    for j in range(1, 8):
        down = down * q + values[count + 15 - j]
    down = down * q
    out = [None] * count
    out[count - 1] = scale * (ups[count - 1] + down)
    for i in range(count - 2, -1, -1):
        down = down * q + (q * values[i + 9] - q9 * values[i + 17])
        out[i] = scale * (ups[i] + down)
    return out


def split_dot(pair, table):
    high, low = split(pair)
    width = table.shape[1] // 2
    both = jnp.dot(high, table, preferred_element_type=F32)
    rest = jnp.dot(low, table[:, :width], preferred_element_type=F32)
    return both[:, :width] + both[:, width:] + rest


def stage1_columns(load, pairs, comp, tables, near, far, cols, unroll, begin):
    wide = cols + 2 * WIDE

    @pl.loop(0, pairs, unroll=unroll)
    def _(i):
        high, low = split(jnp.concatenate([load(2 * i), load(2 * i + 1)], axis=1))
        first = jnp.dot(tables[f"first{comp}"], jnp.concatenate([high, low], axis=0), preferred_element_type=F32)
        rest = first[wide:] + jnp.dot(tables[f"rest{comp}"], high, preferred_element_type=F32)
        depth = high.shape[1] // 2
        for j in range(2):
            lanes = slice(j * depth, (j + 1) * depth)
            row = begin + 2 * i + j
            near[2 * comp, row] = first[:wide, lanes]
            near[2 * comp + 1, row] = rest[:wide, lanes]
            far[comp, row] = rest[wide:, lanes]


def stage1_rows(load, first, count, out):
    wide = out.shape[2]

    @pl.loop(0, wide // 8)
    def _(t):
        window = pl.ds(pl.multiple_of(t * 8, 8), 8)
        for comp in range(2):
            reach = REACH[comp]
            for kind in range(2):
                field = 2 * comp + kind
                taps = row_taps(kind, RADII[comp], SEGMENTS[comp] if kind == 0 else 1.0)
                values = [load(field, row, window) for row in range(first - reach, first + count + reach)]
                for i, value in enumerate(smooth_rows(values, taps, count, reach)):
                    out[field, i, window, :] = value


def stage1_depth(xs, count, step, tables, deriv, place, gates):
    wide, depth = xs.shape[2:]
    for i, start in enumerate(range(0, count, step)):
        rows = slice(start, start + step)
        pair = lambda p: jnp.concatenate([xs[q, rows].reshape(step * wide, depth) for q in (p, p + 2)], axis=1)
        n3 = split_dot(pair(0), tables["depth0"])
        n2 = split_dot(pair(1), tables["depth1"])
        one = 1.0 + n3
        two = (jnp.log(one) + 2.0 * CROSS * n2 * one).reshape(step, wide, depth)
        three = (n2 / one + CROSS * n2 * n2).reshape(step, wide, depth)
        for which, value in enumerate((two, three)):
            if gates[i] is not None:
                value = value * place[gates[i]].astype(F32)
            deriv[which, rows, :WIDE] = value[:, :WIDE] * place[2].astype(F32)
            deriv[which, rows, WIDE : wide - WIDE] = value[:, WIDE : wide - WIDE]
            deriv[which, rows, wide - WIDE :] = value[:, wide - WIDE :] * place[3].astype(F32)


def stage2_columns(deriv, count, tables, out, unroll):
    cols = out.shape[2]

    @pl.loop(0, count // 2, unroll=unroll)
    def _(i):
        for which, kind in ((0, 1), (1, 0)):
            high, low = split(jnp.concatenate([deriv[which, 2 * i], deriv[which, 2 * i + 1]], axis=1))
            stacked = [high, low, high] if which == 0 else [high, low]
            result = jnp.dot(tables[f"second{kind}"], jnp.concatenate(stacked, axis=0), preferred_element_type=F32)
            depth = high.shape[1] // 2
            for comp in range(2):
                for j in range(2):
                    out[2 * which + comp, 2 * i + j] = result[comp * cols : (comp + 1) * cols, j * depth : (j + 1) * depth]


def position():
    flags = []
    for axis in AXES:
        index = lax.axis_index(axis)
        flags += [(index > 0).astype(jnp.int32), (index + 1 < lax.axis_size(axis)).astype(jnp.int32)]
    return flags + [lax.rem(lax.axis_index("gy"), 2)]


def blend(first, second, scale):
    return first if scale is None else (1.0 - DAMPING) * first + scale * second


def side_rows(pair, index, odd):
    one, two = pair[0][index], pair[1][index]
    return jnp.where(odd, one, two), jnp.where(odd, two, one)


def mid_kernel(later, *refs):
    if later:
        scales, own, solid, top, bottom, *refs = refs
        sides, sides_new, refs = refs[:2], refs[2:4], refs[4:]
    else:
        own, solid, *refs = refs
        sides, refs = refs[:2], refs[2:]
    if later:
        table_ref, near, far, extra, y2, xs, deriv = refs
    else:
        table_ref, near, far, extra = refs
    _, rows, cols, depth = own.shape
    half = rows // 2
    tables = Tables(table_ref, cols, depth)
    place = position()
    odd = place[4] == 1
    if not later:
        base = 0
        for comp in range(2):
            part = slice(0, DEEP[comp])
            extra[base : base + DEEP[comp]] = jnp.where(solid[part] == 0, own[comp, part], 0.0)
            base += DEEP[comp]
    for comp in range(2):
        scale = scales[comp] if later else None
        for begin, ref in ((0, top), (half, bottom)) if later else ((0, None),):

            def load(row):
                row = begin + row
                value = jnp.where(solid[row] == 0, own[comp, row], 0.0)
                left, right = side_rows(sides, (comp, row), odd)
                if later:
                    value = blend(value, ref[comp, row - begin], scale)
                    extra[comp, row] = (1.0 - DAMPING) * value
                    left_new, right_new = side_rows(sides_new, (comp, row), odd)
                    left, right = blend(left, left_new, scale), blend(right, right_new, scale)
                return jnp.concatenate([left, value, right], axis=0)

            count = half if later else rows
            stage1_columns(load, count // 2, comp, tables, near, far, cols, 16, begin)
    if later:
        mid_derivatives(near, y2, xs, deriv, tables, place)


def mid_derivatives(near, y2, xs, deriv, tables, place):
    count = y2.shape[1]
    stage1_rows(lambda field, row, window: near[field, row, window, :], DERIV, count, xs)
    stage1_depth(xs, count, count // 3, tables, deriv, place, [None] * 3)
    stage2_columns(deriv, count, tables, y2, count // 2)


def rest_kernel(after, near, table_ref, y2, xs, deriv):
    cols, depth = y2.shape[2:]
    mid_derivatives(near, y2, xs, deriv, Tables(table_ref, cols, depth), position())


def edge_kernel(top, later, last, *refs):
    if later:
        scales, halo, *refs = refs
        sides, halo_new, sides_new, refs = refs[:2], refs[2], refs[3:5], refs[5:]
    else:
        halo, *refs = refs
        sides, refs = refs[:2], refs[2:]
    near, far, y2, solid, table_ref, proposal, sums, *refs = refs
    if not last:
        packed, *refs = refs
    near_h, far_h, xs, deriv, y2_h, xm, xa = refs
    _, rows, cols, depth = far.shape
    half = rows // 2
    tables = Tables(table_ref, cols, depth)
    place = position()
    odd = place[4] == 1
    for comp in range(2):
        base = 0 if comp == 0 else DEEP[0]
        scale = scales[comp] if later else None

        def load(row):
            value = halo[base + row]
            left, right = side_rows(sides, base + row, odd)
            if later:
                value = blend(value, halo_new[base + row], scale)
                left_new, right_new = side_rows(sides_new, base + row, odd)
                left, right = blend(left, left_new, scale), blend(right, right_new, scale)
            return jnp.concatenate([left, value, right], axis=0)

        stage1_columns(load, DEEP[comp] // 2, comp, tables, near_h, far_h, cols, DEEP[comp] // 2, 0)

    def pick(own, edge, index, row, window):
        comp = index // 2 if own is near else index
        if 0 <= row < rows:
            return own[index, row, window, :]
        return edge[index, row + DEEP[comp] if top else row - rows, window, :]

    first = -DERIV if top else rows - DERIV
    stage1_rows(lambda f, row, window: pick(near, near_h, f, row, window), first, 2 * DERIV, xs)
    gates = [0, None] if top else [None, 1]
    stage1_depth(xs, 2 * DERIV, DERIV, tables, deriv, place, gates)
    stage2_columns(deriv, 2 * DERIV, tables, y2_h, 7)

    start = 0 if top else half

    @pl.loop(0, cols // 8)
    def _(t):
        window = pl.ds(pl.multiple_of(t * 8, 8), 8)

        def second(index, row):
            if DERIV <= row < rows - DERIV:
                return y2[index, row - DERIV, window, :]
            return y2_h[index, row - first, window, :]

        for which, kind in ((0, 1), (1, 0)):
            for comp in range(2):
                reach = REACH[comp]
                taps = row_taps(kind, RADII[comp], SEGMENTS[comp] if kind == 0 else 1.0)
                values = [second(2 * which + comp, row) for row in range(start - reach, start + half + reach)]
                for i, value in enumerate(smooth_rows(values, taps, half, reach)):
                    xm[2 * which + comp, i, window, :] = value
        scale = row_taps(2, 0.0, 1.0)[8]
        for comp in range(2):
            values = [pick(far, far_h, comp, row, window) for row in range(start - FAR, start + half + FAR)]
            for i, value in enumerate(smooth_rows_exp(values, scale, half)):
                xa[comp, i, window, :] = value

    sums[...] = jnp.zeros_like(sums)
    step = half // 2
    for i in range(0, half, step):
        part = slice(i, i + step)
        flat = lambda ref, p: ref[p, part].reshape(step * cols, depth)
        pore = solid[start + i : start + i + step].reshape(step * cols, depth) == 0
        high, low = split(jnp.concatenate([flat(xa, 0), flat(xa, 1)], axis=1))
        pull = jnp.dot(high, tables["pull_high"], preferred_element_type=F32)
        pull += jnp.dot(high, tables["pull_low"], preferred_element_type=F32)
        pull += jnp.dot(low, tables["pull_high"], preferred_element_type=F32)
        for comp in range(2):
            mu = split_dot(jnp.concatenate([flat(xm, 2 + comp), flat(xm, comp)], axis=1), tables[f"last{comp}"])
            mu = mu + pull[:, comp * depth : (comp + 1) * depth]
            value = jnp.where(pore, jnp.exp(-mu), 0.0)
            proposal[comp, part] = value.reshape(step, cols, depth)
            sums[comp] += value.reshape(step * cols // 8, 8, depth).sum(0)
    if not last:
        base = 0
        for comp in range(2):
            part = slice(0, DEEP[comp]) if top else slice(half - DEEP[comp], half)
            packed[base : base + DEEP[comp]] = proposal[comp, part]
            base += DEEP[comp]


def in_vmem(count):
    return [pl.BlockSpec(memory_space=pltpu.VMEM)] * count


def params(mebibytes):
    return pltpu.CompilerParams(vmem_limit_bytes=mebibytes * 1024 * 1024)


def shape(*sizes):
    return jax.ShapeDtypeStruct(sizes, F32)


COST = pl.CostEstimate(flops=1000, bytes_accessed=1000, transcendentals=0)


def derivative_scratch(count, wide, depth):
    return [pltpu.VMEM((4, count, wide, depth), F32), pltpu.VMEM((2, count, wide, depth), F32)]


def mid(later, scalars, blocks, table):
    rows, cols, depth = blocks[1].shape
    wide, count = cols + 2 * WIDE, rows - 2 * DERIV
    outs = [shape(4, rows, wide, depth), shape(2, rows, cols, depth)]
    if later:
        outs += [shape(2, rows, cols, depth), shape(4, count, cols, depth)]
    else:
        outs += [shape(sum(DEEP), cols, depth)]
    return pl.pallas_call(
        functools.partial(mid_kernel, later),
        out_shape=tuple(outs),
        in_specs=[pl.BlockSpec(memory_space=pltpu.SMEM)] * len(scalars) + in_vmem(len(blocks) + 1),
        out_specs=tuple(in_vmem(len(outs))),
        scratch_shapes=derivative_scratch(count, wide, depth) if later else [],
        compiler_params=params(24),
        cost_estimate=COST,
        name="mid",
    )(*scalars, *blocks, table)


def rest(after, near, table):
    _, rows, wide, depth = near.shape
    count = rows - 2 * DERIV
    return pl.pallas_call(
        rest_kernel,
        out_shape=shape(4, count, wide - 2 * WIDE, depth),
        in_specs=[pl.BlockSpec(memory_space=pl.ANY)] + in_vmem(2),
        out_specs=in_vmem(1)[0],
        scratch_shapes=derivative_scratch(count, wide, depth),
        compiler_params=params(24),
        cost_estimate=COST,
        name="rest",
    )(after, near, table)


def edge(top, later, last, scalars, blocks, table):
    rows, cols, depth = blocks[-1].shape
    wide, half = cols + 2 * WIDE, rows // 2
    f32 = lambda *s: pltpu.VMEM(s, F32)
    outs = [shape(2, half, cols, depth), shape(2, 8, depth)]
    if not last:
        outs.append(shape(sum(DEEP), cols, depth))
    return pl.pallas_call(
        functools.partial(edge_kernel, top, later, last),
        out_shape=tuple(outs),
        in_specs=[pl.BlockSpec(memory_space=pltpu.SMEM)] * len(scalars) + in_vmem(len(blocks) + 1),
        out_specs=tuple(in_vmem(len(outs))),
        scratch_shapes=[
            f32(4, DEEP[1], wide, depth),
            f32(2, DEEP[1], cols, depth),
            f32(4, 2 * DERIV, wide, depth),
            f32(2, 2 * DERIV, wide, depth),
            f32(4, 2 * DERIV, cols, depth),
            f32(4, half, cols, depth),
            f32(2, half, cols, depth),
        ],
        compiler_params=params(32),
        cost_estimate=COST,
        name="edge_top" if top else "edge_bottom",
    )(*scalars, *blocks, table)


def shift(value, axis, step):
    count = lax.axis_size(axis)
    return lax.ppermute(value, axis, [(i, i + step) for i in range(count) if 0 <= i + step < count])


def swap_columns(even, odd):
    count = lax.axis_size("gy")
    pairs = lambda first: [p for i in range(first, count - 1, 2) for p in ((i, i + 1), (i + 1, i))]
    return lax.ppermute(even, "gy", pairs(0)), lax.ppermute(odd, "gy", pairs(1))


def side_starts(cols):
    right, left = cols - 2 * WIDE, 0
    odd = position()[4]
    return pl.multiple_of(right * (1 - odd), 8), pl.multiple_of(right * odd, 8)


def first_rows_kernel(own, solid, out, density, mask, sems):
    rows = own.shape[1]
    most = max(DEEP)
    half = most // 2
    copies = []
    for part, begin in enumerate((0, half)):
        source, target = pl.ds(rows - most + begin, half), pl.ds(begin, half)
        copies.append(pltpu.make_async_copy(solid.at[source], mask.at[target], sems.at[part]))
        for comp in range(2):
            copies.append(pltpu.make_async_copy(own.at[comp, source], density.at[comp, target], sems.at[2 + 2 * part + comp]))
    for copy in copies:
        copy.start()
    for copy in copies:
        copy.wait()
    base = 0
    for comp in range(2):
        out[base : base + DEEP[comp]] = jnp.where(mask[most - DEEP[comp] :] == 0, density[comp, most - DEEP[comp] :], 0.0)
        base += DEEP[comp]


def first_rows(own, solid):
    _, _, cols, depth = own.shape
    return pl.pallas_call(
        first_rows_kernel,
        out_shape=shape(sum(DEEP), cols, depth),
        in_specs=[pl.BlockSpec(memory_space=pl.ANY)] * 2,
        out_specs=in_vmem(1)[0],
        scratch_shapes=[
            pltpu.VMEM((2, max(DEEP), cols, depth), F32),
            pltpu.VMEM((max(DEEP), cols, depth), jnp.int32),
            pltpu.SemaphoreType.DMA((6,)),
        ],
        compiler_params=params(56),
        cost_estimate=COST,
        name="first_rows",
    )(own, solid)


def first_columns_kernel(own, solid, even, odd):
    for start, out in zip(side_starts(own.shape[2]), (even, odd)):
        window = pl.ds(start, 2 * WIDE)
        for comp in range(2):
            out[comp] = jnp.where(solid[:, window] == 0, own[comp, :, window], 0.0)


def first_columns(own, solid):
    _, rows, _, depth = own.shape
    side = shape(2, rows, 2 * WIDE, depth)
    return pl.pallas_call(
        first_columns_kernel,
        out_shape=(side, side),
        in_specs=in_vmem(2),
        out_specs=tuple(in_vmem(2)),
        compiler_params=params(8),
        cost_estimate=COST,
        name="first_columns",
    )(own, solid)


def sides_kernel(after, value, even, odd, sems):
    copies = []
    for i, (start, out) in enumerate(zip(side_starts(value.shape[1]), (even, odd))):
        copies.append(pltpu.make_async_copy(value.at[:, pl.ds(start, 2 * WIDE)], out, sems.at[i]))
    for copy in copies:
        copy.start()
    for copy in copies:
        copy.wait()


def sides_pack(after, value):
    count, _, depth = value.shape
    side = shape(count, 2 * WIDE, depth)
    return pl.pallas_call(
        sides_kernel,
        out_shape=(side, side),
        in_specs=[pl.BlockSpec(memory_space=pl.ANY)] * 2,
        out_specs=tuple(in_vmem(2)),
        scratch_shapes=[pltpu.SemaphoreType.DMA((2,))],
        compiler_params=params(4),
        cost_estimate=COST,
        name="sides_pack",
    )(after, value)


def columns_kernel(top, bottom, even, odd):
    half, cols = top.shape[1:3]
    for start, out in zip(side_starts(cols), (even, odd)):
        out[:, :half] = top[:, :, pl.ds(start, 2 * WIDE)]
        out[:, half:] = bottom[:, :, pl.ds(start, 2 * WIDE)]


def columns_pack(top, bottom):
    _, half, _, depth = top.shape
    side = shape(2, 2 * half, 2 * WIDE, depth)
    return pl.pallas_call(
        columns_kernel,
        out_shape=(side, side),
        in_specs=in_vmem(2),
        out_specs=tuple(in_vmem(2)),
        compiler_params=params(8),
        cost_estimate=COST,
        name="columns_pack",
    )(top, bottom)


def sum_kernel(after, one, two, out):
    out[...] = one[...] + two[...]


def sum_after(after, one, two):
    return pl.pallas_call(
        sum_kernel,
        out_shape=shape(*one.shape),
        in_specs=[pl.BlockSpec(memory_space=pl.ANY)] + in_vmem(2),
        out_specs=in_vmem(1)[0],
        compiler_params=params(2),
        cost_estimate=COST,
        name="sum_after",
    )(after, one, two)


def copy_kernel(after, value, out):
    out[...] = value[...]


def copy_after(after, value):
    return pl.pallas_call(
        copy_kernel,
        out_shape=shape(*value.shape),
        in_specs=[pl.BlockSpec(memory_space=pl.ANY)] + in_vmem(1),
        out_specs=in_vmem(1)[0],
        compiler_params=params(6),
        cost_estimate=COST,
        name="copy_after",
    )(after, value)


def add_partners(sums, axis, first, end):
    count = lax.axis_size(axis)
    for bit in range(first, end):
        sums = sums + lax.ppermute(sums, axis, [(i, i ^ (1 << bit)) for i in range(count)])
    return sums


def spread_kernel(one, two, out):
    total = (one[...] + two[...]).sum(axis=1)
    out[...] = jnp.broadcast_to(total[None], out.shape)


def total_over_all(one, two):
    devices = lax.axis_size(AXES)
    copies = pl.pallas_call(
        spread_kernel,
        out_shape=shape(devices, 2, one.shape[2]),
        in_specs=in_vmem(2),
        out_specs=in_vmem(1)[0],
        compiler_params=params(4),
        cost_estimate=COST,
        name="spread",
    )(one, two)
    return lax.all_to_all(copies, AXES, 0, 0, tiled=True).transpose(1, 0, 2)


def bits(axis):
    count = lax.axis_size(axis)
    assert count & (count - 1) == 0
    return count.bit_length() - 1


def body(density_init, solid_mask, loadings):
    rows, cols, depth = solid_mask.shape
    total_cells = float(rows * lax.axis_size("gx") * cols * lax.axis_size("gy") * depth)
    table = jnp.asarray(packed_tables(cols, depth)[0])

    def scale_of(sums):
        return DAMPING * loadings * total_cells / sums.sum(axis=tuple(range(sums.ndim))[1:])

    above = shift(first_rows(density_init, solid_mask), "gx", 1)
    columns = swap_columns(*first_columns(density_init, solid_mask))
    near, far, upper = mid(False, [], [density_init, solid_mask, *columns], table)
    below = shift(upper, "gx", -1)
    to_sides = sides_pack(far, above)
    top_sides = swap_columns(*to_sides)
    y2 = rest(to_sides[0], near, table)
    top, top_sums, upper = edge(True, False, False, [], [above, *top_sides, near, far, y2, solid_mask], table)
    below_new = shift(upper, "gx", -1)
    bottom_sides = swap_columns(*sides_pack(top_sums, below))
    bottom, bottom_sums, lower = edge(False, False, False, [], [below, *bottom_sides, near, far, y2, solid_mask], table)
    columns_new = swap_columns(*columns_pack(top, bottom))
    sides_new = swap_columns(*sides_pack(bottom_sums, below_new))
    sums = add_partners(sum_after(below_new, top_sums, bottom_sums), "gx", 0, 1)
    above_new = shift(copy_after(sums, lower), "gx", 1)
    scale = scale_of(add_partners(add_partners(sums, "gy", 0, bits("gy")), "gx", 1, bits("gx")))
    blocks = [density_init, solid_mask, top, bottom, *columns, *columns_new]
    near, far, kept, y2 = mid(True, [scale], blocks, table)
    blocks = [below, *bottom_sides, below_new, *sides_new, near, far, y2, solid_mask]
    bottom, bottom_sums = edge(False, True, True, [scale], blocks, table)
    sides_new = swap_columns(*sides_pack(far, above_new))
    blocks = [above, *top_sides, above_new, *sides_new, near, far, y2, solid_mask]
    top, top_sums = edge(True, True, True, [scale], blocks, table)
    scale = scale_of(total_over_all(top_sums, bottom_sums))
    return kept + scale[:, None, None, None] * jnp.concatenate([top, bottom], axis=1)


def solution(mesh):
    in_specs = (P(None, "gx", "gy", None), P("gx", "gy", None), P())
    out_specs = P(None, "gx", "gy", None)
    return jax.shard_map(body, mesh=mesh, in_specs=in_specs, out_specs=out_specs, check_vma=False)
```

```python
import functools

import jax
import jax.numpy as jnp
import ml_dtypes
import numpy as np
from jax import lax
from jax.experimental import pallas as pl
from jax.experimental.pallas import tpu as pltpu
from jax.sharding import PartitionSpec as P

ITERS = 2
SEGMENTS = (1.5131, 1.0)
RADII = (6.0, 8.0)
CROSS = 0.25
DAMPING = 0.3
ATTRACT = ((0.3, 0.22), (0.22, 0.16))
REACH = (5, 7)
FAR = 8
DERIV = REACH[1]
DEEP = tuple(DERIV + r for r in REACH)
WIDE = 8
AXES = ("gx", "gy")
BF16 = jnp.bfloat16
F32 = jnp.float32


def raw_profile(kind, radius):
    offset = np.arange(17) - 8.0
    if kind == 0:
        return np.maximum(radius * radius - offset * offset, 0.0)
    if kind == 1:
        return offset * offset * np.maximum(radius * radius - offset * offset, 0.0)
    return np.exp(-np.abs(offset) / 4.0)


def split_bf16(table):
    high = table.astype(np.float32).astype(ml_dtypes.bfloat16)
    low = (table - high.astype(np.float64)).astype(np.float32).astype(ml_dtypes.bfloat16)
    return high, low


def column_band(kind, radius, count, columns, first):
    band = np.zeros((count, columns))
    for o in range(count):
        band[o, first + o : first + o + 17] = raw_profile(kind, radius)
    return band


def depth_band(kind, radius, depth):
    taps = raw_profile(kind, radius)
    band = np.zeros((depth, depth))
    for column in range(depth):
        for offset in range(17):
            source = column + offset - 8
            if 0 <= source < depth:
                band[source, column] = taps[offset]
    return band


def stage1_tables(comp, cols):
    wide = cols + 2 * WIDE
    pack = column_band(0, RADII[comp], wide, wide + 16, 0)
    rest = np.concatenate(
        [column_band(1, RADII[comp], wide, wide + 16, 0), column_band(2, 0.0, cols, wide + 16, WIDE)]
    )
    high, low = split_bf16(np.concatenate([pack, rest]))
    return {f"first{comp}": np.concatenate([high, high], axis=1), f"rest{comp}": low[wide:]}


def stage2_table(kind, cols):
    high, low = split_bf16(np.concatenate([column_band(kind, r, cols, cols + 16, 0) for r in RADII]))
    return np.concatenate([high, high] if kind == 0 else [high, high, low], axis=1)


def depth_table(kinds, depth):
    high, low = split_bf16(np.concatenate([depth_band(kind, radius, depth) for kind, radius in kinds]))
    return np.concatenate([high, low], axis=1)


def attraction_tables(depth):
    band = depth_band(2, 0.0, depth)
    high, low = split_bf16(-np.concatenate([np.concatenate([ATTRACT[i][j] * band for i in range(2)], axis=1) for j in range(2)]))
    return {"pull_high": high, "pull_low": low}


@functools.lru_cache
def packed_tables(cols, depth):
    tables = {**stage1_tables(0, cols), **stage1_tables(1, cols), **attraction_tables(depth)}
    tables |= {f"depth{kind}": depth_table([(kind, r) for r in RADII], depth) for kind in range(2)}
    tables |= {f"last{comp}": depth_table([(0, r), (1, r)], depth) for comp, r in enumerate(RADII)}
    tables |= {f"second{kind}": stage2_table(kind, cols) for kind in range(2)}
    width = max(t.shape[1] for t in tables.values())
    places, start = {}, 0
    for name, table in tables.items():
        places[name] = (start, *table.shape)
        start += table.shape[0]
    whole = np.zeros((start, width), ml_dtypes.bfloat16)
    for name, table in tables.items():
        whole[places[name][0] : places[name][0] + table.shape[0], : table.shape[1]] = table
    return whole, places


class Tables:
    def __init__(self, ref, cols, depth):
        self.ref, self.places = ref, packed_tables(cols, depth)[1]

    def __getitem__(self, name):
        start, rows, columns = self.places[name]
        return self.ref[start : start + rows, :columns]


def row_taps(kind, radius, scale):
    taps = raw_profile(kind, radius)
    return [float(v) for v in taps * (scale / taps.sum() ** 3)]


def split(field):
    high = field.astype(BF16)
    return high, (field - high.astype(F32)).astype(BF16)


def smooth_rows(values, taps, count, reach):
    out = []
    for i in range(count):
        total = None
        for k in range(reach + 1):
            if taps[8 + k] == 0.0:
                continue
            pair = values[i + reach] if k == 0 else values[i + reach - k] + values[i + reach + k]
            term = taps[8 + k] * pair
            total = term if total is None else total + term
        out.append(total)
    return out


def smooth_rows_exp(values, scale, count):
    q = float(np.exp(-0.25))
    q9 = q**9
    up = values[0]
    for j in range(1, 9):
        up = up * q + values[j]
    ups = [up]
    for i in range(1, count):
        up = up * q + (values[i + 8] - q9 * values[i - 1])
        ups.append(up)
    down = values[count + 15]
    for j in range(1, 8):
        down = down * q + values[count + 15 - j]
    down = down * q
    out = [None] * count
    out[count - 1] = scale * (ups[count - 1] + down)
    for i in range(count - 2, -1, -1):
        down = down * q + (q * values[i + 9] - q9 * values[i + 17])
        out[i] = scale * (ups[i] + down)
    return out


def split_dot(pair, table):
    high, low = split(pair)
    width = table.shape[1] // 2
    both = jnp.dot(high, table, preferred_element_type=F32)
    rest = jnp.dot(low, table[:, :width], preferred_element_type=F32)
    return both[:, :width] + both[:, width:] + rest


def stage1_columns(load, pairs, comp, tables, near, far, cols, unroll, begin):
    wide = cols + 2 * WIDE

    @pl.loop(0, pairs, unroll=unroll)
    def _(i):
        high, low = split(jnp.concatenate([load(2 * i), load(2 * i + 1)], axis=1))
        first = jnp.dot(tables[f"first{comp}"], jnp.concatenate([high, low], axis=0), preferred_element_type=F32)
        rest = first[wide:] + jnp.dot(tables[f"rest{comp}"], high, preferred_element_type=F32)
        depth = high.shape[1] // 2
        for j in range(2):
            lanes = slice(j * depth, (j + 1) * depth)
            row = begin + 2 * i + j
            near[2 * comp, row] = first[:wide, lanes]
            near[2 * comp + 1, row] = rest[:wide, lanes]
            far[comp, row] = rest[wide:, lanes]


def stage1_rows(load, first, count, out):
    wide = out.shape[2]

    @pl.loop(0, wide // 8)
    def _(t):
        window = pl.ds(pl.multiple_of(t * 8, 8), 8)
        for comp in range(2):
            reach = REACH[comp]
            for kind in range(2):
                field = 2 * comp + kind
                taps = row_taps(kind, RADII[comp], SEGMENTS[comp] if kind == 0 else 1.0)
                values = [load(field, row, window) for row in range(first - reach, first + count + reach)]
                for i, value in enumerate(smooth_rows(values, taps, count, reach)):
                    out[field, i, window, :] = value


def stage1_depth(xs, count, step, tables, deriv, place, gates):
    wide, depth = xs.shape[2:]
    for i, start in enumerate(range(0, count, step)):
        rows = slice(start, start + step)
        pair = lambda p: jnp.concatenate([xs[q, rows].reshape(step * wide, depth) for q in (p, p + 2)], axis=1)
        n3 = split_dot(pair(0), tables["depth0"])
        n2 = split_dot(pair(1), tables["depth1"])
        one = 1.0 + n3
        two = (jnp.log(one) + 2.0 * CROSS * n2 * one).reshape(step, wide, depth)
        three = (n2 / one + CROSS * n2 * n2).reshape(step, wide, depth)
        for which, value in enumerate((two, three)):
            if gates[i] is not None:
                value = value * place[gates[i]].astype(F32)
            deriv[which, rows, :WIDE] = value[:, :WIDE] * place[2].astype(F32)
            deriv[which, rows, WIDE : wide - WIDE] = value[:, WIDE : wide - WIDE]
            deriv[which, rows, wide - WIDE :] = value[:, wide - WIDE :] * place[3].astype(F32)


def stage2_columns(deriv, count, tables, out, unroll):
    cols = out.shape[2]

    @pl.loop(0, count // 2, unroll=unroll)
    def _(i):
        for which, kind in ((0, 1), (1, 0)):
            high, low = split(jnp.concatenate([deriv[which, 2 * i], deriv[which, 2 * i + 1]], axis=1))
            stacked = [high, low, high] if which == 0 else [high, low]
            result = jnp.dot(tables[f"second{kind}"], jnp.concatenate(stacked, axis=0), preferred_element_type=F32)
            depth = high.shape[1] // 2
            for comp in range(2):
                for j in range(2):
                    out[2 * which + comp, 2 * i + j] = result[comp * cols : (comp + 1) * cols, j * depth : (j + 1) * depth]


def position():
    flags = []
    for axis in AXES:
        index = lax.axis_index(axis)
        flags += [(index > 0).astype(jnp.int32), (index + 1 < lax.axis_size(axis)).astype(jnp.int32)]
    return flags + [lax.rem(lax.axis_index("gy"), 2)]


def blend(first, second, scale):
    return first if scale is None else (1.0 - DAMPING) * first + scale * second


def side_rows(pair, index, odd):
    one, two = pair[0][index], pair[1][index]
    return jnp.where(odd, one, two), jnp.where(odd, two, one)


def mid_kernel(later, *refs):
    own, solid, *refs = refs
    sides, table_ref, near, far, refs = refs[:2], *refs[2:5], refs[5:]
    rows, cols, depth = far.shape[1:]
    tables = Tables(table_ref, cols, depth)
    odd = position()[4] == 1
    if not later:
        (upper,) = refs
        base = 0
        for comp in range(2):
            part = slice(0, DEEP[comp])
            upper[base : base + DEEP[comp]] = jnp.where(solid[part] == 0, own[comp, part], 0.0)
            base += DEEP[comp]
    parts = ((0, own), (rows // 2, solid)) if later else ((0, own),)
    for comp in range(2):
        for begin, ref in parts:

            def load(row):
                left, right = side_rows(sides, (comp, begin + row), odd)
                value = ref[comp, row] if later else jnp.where(solid[row] == 0, ref[comp, row], 0.0)
                return jnp.concatenate([left, value, right], axis=0)

            count = rows // len(parts) // 2
            stage1_columns(load, count, comp, tables, near, far, cols, count, begin)


def rest_kernel(later, *refs):
    if later:
        scales, near_old, near, own, solid, top, bottom, table_ref, y2, kept, xs, deriv = refs
        half = top.shape[1]
        for comp in range(2):
            for begin, ref in ((0, top), (half, bottom)):
                part = slice(begin, begin + half)
                start = jnp.where(solid[part] == 0, own[comp, part], 0.0)
                kept[comp, part] = (1.0 - DAMPING) * blend(start, ref[comp], scales[comp])
    else:
        after, near, table_ref, y2, xs, deriv = refs
    count, cols, depth = y2.shape[1:]
    tables, place = Tables(table_ref, cols, depth), position()

    def load(field, row, window):
        value = near[field, row, window, :]
        return blend(near_old[field, row, window, :], value, scales[field // 2]) if later else value

    stage1_rows(load, DERIV, count, xs)
    stage1_depth(xs, count, count // 3, tables, deriv, place, [None] * 3)
    stage2_columns(deriv, count, tables, y2, count // 2)


def edge_kernel(top, later, last, *refs):
    if later:
        scales, halo, *refs = refs
        sides, halo_new, sides_new, near_old, far_old, refs = refs[:2], refs[2], refs[3:5], *refs[5:7], refs[7:]
    else:
        halo, *refs = refs
        sides, refs = refs[:2], refs[2:]
    near, far, y2, solid, table_ref, proposal, sums, *refs = refs
    if not last:
        packed, *refs = refs
    near_h, far_h, xs, deriv, y2_h, xm, xa = refs
    _, rows, cols, depth = far.shape
    half = rows // 2
    tables = Tables(table_ref, cols, depth)
    place = position()
    odd = place[4] == 1
    for comp in range(2):
        base = 0 if comp == 0 else DEEP[0]
        scale = scales[comp] if later else None

        def load(row):
            value = halo[base + row]
            left, right = side_rows(sides, base + row, odd)
            if later:
                value = blend(value, halo_new[base + row], scale)
                left_new, right_new = side_rows(sides_new, base + row, odd)
                left, right = blend(left, left_new, scale), blend(right, right_new, scale)
            return jnp.concatenate([left, value, right], axis=0)

        stage1_columns(load, DEEP[comp] // 2, comp, tables, near_h, far_h, cols, DEEP[comp] // 2, 0)

    if not later:
        near_old = far_old = None

    def pick(own, edge, index, row, window):
        comp = index // 2 if own is near else index
        if 0 <= row < rows:
            value = own[index, row, window, :]
            old = near_old if own is near else far_old
            return blend(old[index, row, window, :], value, scales[comp]) if later else value
        return edge[index, row + DEEP[comp] if top else row - rows, window, :]

    first = -DERIV if top else rows - DERIV
    stage1_rows(lambda f, row, window: pick(near, near_h, f, row, window), first, 2 * DERIV, xs)
    gates = [0, None] if top else [None, 1]
    stage1_depth(xs, 2 * DERIV, DERIV, tables, deriv, place, gates)
    stage2_columns(deriv, 2 * DERIV, tables, y2_h, 7)

    start = 0 if top else half

    @pl.loop(0, cols // 8)
    def _(t):
        window = pl.ds(pl.multiple_of(t * 8, 8), 8)

        def second(index, row):
            if DERIV <= row < rows - DERIV:
                return y2[index, row - DERIV, window, :]
            return y2_h[index, row - first, window, :]

        for which, kind in ((0, 1), (1, 0)):
            for comp in range(2):
                reach = REACH[comp]
                taps = row_taps(kind, RADII[comp], SEGMENTS[comp] if kind == 0 else 1.0)
                values = [second(2 * which + comp, row) for row in range(start - reach, start + half + reach)]
                for i, value in enumerate(smooth_rows(values, taps, half, reach)):
                    xm[2 * which + comp, i, window, :] = value
        scale = row_taps(2, 0.0, 1.0)[8]
        for comp in range(2):
            values = [pick(far, far_h, comp, row, window) for row in range(start - FAR, start + half + FAR)]
            for i, value in enumerate(smooth_rows_exp(values, scale, half)):
                xa[comp, i, window, :] = value

    sums[...] = jnp.zeros_like(sums)
    step = half // 2
    for i in range(0, half, step):
        part = slice(i, i + step)
        flat = lambda ref, p: ref[p, part].reshape(step * cols, depth)
        pore = solid[start + i : start + i + step].reshape(step * cols, depth) == 0
        high, low = split(jnp.concatenate([flat(xa, 0), flat(xa, 1)], axis=1))
        pull = jnp.dot(high, tables["pull_high"], preferred_element_type=F32)
        pull += jnp.dot(high, tables["pull_low"], preferred_element_type=F32)
        pull += jnp.dot(low, tables["pull_high"], preferred_element_type=F32)
        for comp in range(2):
            mu = split_dot(jnp.concatenate([flat(xm, 2 + comp), flat(xm, comp)], axis=1), tables[f"last{comp}"])
            mu = mu + pull[:, comp * depth : (comp + 1) * depth]
            value = jnp.where(pore, jnp.exp(-mu), 0.0)
            proposal[comp, part] = value.reshape(step, cols, depth)
            sums[comp] += value.reshape(step * cols // 8, 8, depth).sum(0)
    if not last:
        base = 0
        for comp in range(2):
            part = slice(0, DEEP[comp]) if top else slice(half - DEEP[comp], half)
            packed[base : base + DEEP[comp]] = proposal[comp, part]
            base += DEEP[comp]


def in_vmem(count):
    return [pl.BlockSpec(memory_space=pltpu.VMEM)] * count


def params(mebibytes):
    return pltpu.CompilerParams(vmem_limit_bytes=mebibytes * 1024 * 1024)


def shape(*sizes):
    return jax.ShapeDtypeStruct(sizes, F32)


COST = pl.CostEstimate(flops=1000, bytes_accessed=1000, transcendentals=0)


def derivative_scratch(count, wide, depth):
    return [pltpu.VMEM((4, count, wide, depth), F32), pltpu.VMEM((2, count, wide, depth), F32)]


def mid(later, blocks, table):
    _, rows, _, depth = blocks[2].shape
    cols = blocks[0].shape[2]
    outs = [shape(4, rows, cols + 2 * WIDE, depth), shape(2, rows, cols, depth)]
    if not later:
        outs += [shape(sum(DEEP), cols, depth)]
    return pl.pallas_call(
        functools.partial(mid_kernel, later),
        out_shape=tuple(outs),
        in_specs=in_vmem(len(blocks) + 1),
        out_specs=tuple(in_vmem(len(outs))),
        compiler_params=params(6),
        cost_estimate=COST,
        name="mid",
    )(*blocks, table)


def rest(later, first, blocks, table):
    _, rows, wide, depth = blocks[0].shape
    count, cols = rows - 2 * DERIV, wide - 2 * WIDE
    outs = [shape(4, count, cols, depth)]
    if later:
        outs += [shape(2, rows, cols, depth)]
    return pl.pallas_call(
        functools.partial(rest_kernel, later),
        out_shape=tuple(outs),
        in_specs=[pl.BlockSpec(memory_space=pltpu.SMEM if later else pl.ANY)] + in_vmem(len(blocks) + 1),
        out_specs=tuple(in_vmem(len(outs))),
        scratch_shapes=[pltpu.VMEM((4, count, wide, depth), F32), pltpu.VMEM((2, count, wide, depth), F32)],
        compiler_params=params(8),
        cost_estimate=COST,
        name="rest",
    )(first, *blocks, table)


def edge(top, later, last, scalars, blocks, table):
    rows, cols, depth = blocks[-1].shape
    wide, half = cols + 2 * WIDE, rows // 2
    f32 = lambda *s: pltpu.VMEM(s, F32)
    outs = [shape(2, half, cols, depth), shape(2, 8, depth)]
    if not last:
        outs.append(shape(sum(DEEP), cols, depth))
    return pl.pallas_call(
        functools.partial(edge_kernel, top, later, last),
        out_shape=tuple(outs),
        in_specs=[pl.BlockSpec(memory_space=pltpu.SMEM)] * len(scalars) + in_vmem(len(blocks) + 1),
        out_specs=tuple(in_vmem(len(outs))),
        scratch_shapes=[
            f32(4, DEEP[1], wide, depth),
            f32(2, DEEP[1], cols, depth),
            f32(4, 2 * DERIV, wide, depth),
            f32(2, 2 * DERIV, wide, depth),
            f32(4, 2 * DERIV, cols, depth),
            f32(4, half, cols, depth),
            f32(2, half, cols, depth),
        ],
        compiler_params=params(16),
        cost_estimate=COST,
        name="edge_top" if top else "edge_bottom",
    )(*scalars, *blocks, table)


def shift(value, axis, step):
    count = lax.axis_size(axis)
    return lax.ppermute(value, axis, [(i, i + step) for i in range(count) if 0 <= i + step < count])


def swap_columns(even, odd):
    count = lax.axis_size("gy")
    pairs = lambda first: [p for i in range(first, count - 1, 2) for p in ((i, i + 1), (i + 1, i))]
    return lax.ppermute(even, "gy", pairs(0)), lax.ppermute(odd, "gy", pairs(1))


def side_starts(cols):
    right, left = cols - 2 * WIDE, 0
    odd = position()[4]
    return pl.multiple_of(right * (1 - odd), 8), pl.multiple_of(right * odd, 8)


def first_rows_kernel(own, solid, out, density, mask, sems):
    rows = own.shape[1]
    most = max(DEEP)
    half = most // 2
    copies = []
    for part, begin in enumerate((0, half)):
        source, target = pl.ds(rows - most + begin, half), pl.ds(begin, half)
        copies.append(pltpu.make_async_copy(solid.at[source], mask.at[target], sems.at[part]))
        for comp in range(2):
            copies.append(pltpu.make_async_copy(own.at[comp, source], density.at[comp, target], sems.at[2 + 2 * part + comp]))
    for copy in copies:
        copy.start()
    for copy in copies:
        copy.wait()
    base = 0
    for comp in range(2):
        out[base : base + DEEP[comp]] = jnp.where(mask[most - DEEP[comp] :] == 0, density[comp, most - DEEP[comp] :], 0.0)
        base += DEEP[comp]


def first_rows(own, solid):
    _, _, cols, depth = own.shape
    return pl.pallas_call(
        first_rows_kernel,
        out_shape=shape(sum(DEEP), cols, depth),
        in_specs=[pl.BlockSpec(memory_space=pl.ANY)] * 2,
        out_specs=in_vmem(1)[0],
        scratch_shapes=[
            pltpu.VMEM((2, max(DEEP), cols, depth), F32),
            pltpu.VMEM((max(DEEP), cols, depth), jnp.int32),
            pltpu.SemaphoreType.DMA((6,)),
        ],
        compiler_params=params(56),
        cost_estimate=COST,
        name="first_rows",
    )(own, solid)


def first_columns_kernel(own, solid, even, odd):
    for start, out in zip(side_starts(own.shape[2]), (even, odd)):
        window = pl.ds(start, 2 * WIDE)
        for comp in range(2):
            out[comp] = jnp.where(solid[:, window] == 0, own[comp, :, window], 0.0)


def first_columns(own, solid):
    _, rows, _, depth = own.shape
    side = shape(2, rows, 2 * WIDE, depth)
    return pl.pallas_call(
        first_columns_kernel,
        out_shape=(side, side),
        in_specs=in_vmem(2),
        out_specs=tuple(in_vmem(2)),
        compiler_params=params(8),
        cost_estimate=COST,
        name="first_columns",
    )(own, solid)


def sides_kernel(after, value, even, odd, sems):
    copies = []
    for i, (start, out) in enumerate(zip(side_starts(value.shape[1]), (even, odd))):
        copies.append(pltpu.make_async_copy(value.at[:, pl.ds(start, 2 * WIDE)], out, sems.at[i]))
    for copy in copies:
        copy.start()
    for copy in copies:
        copy.wait()


def sides_pack(after, value):
    count, _, depth = value.shape
    side = shape(count, 2 * WIDE, depth)
    return pl.pallas_call(
        sides_kernel,
        out_shape=(side, side),
        in_specs=[pl.BlockSpec(memory_space=pl.ANY)] * 2,
        out_specs=tuple(in_vmem(2)),
        scratch_shapes=[pltpu.SemaphoreType.DMA((2,))],
        compiler_params=params(4),
        cost_estimate=COST,
        name="sides_pack",
    )(after, value)


def columns_kernel(top, bottom, even, odd):
    half, cols = top.shape[1:3]
    for start, out in zip(side_starts(cols), (even, odd)):
        out[:, :half] = top[:, :, pl.ds(start, 2 * WIDE)]
        out[:, half:] = bottom[:, :, pl.ds(start, 2 * WIDE)]


def columns_pack(top, bottom):
    _, half, _, depth = top.shape
    side = shape(2, 2 * half, 2 * WIDE, depth)
    return pl.pallas_call(
        columns_kernel,
        out_shape=(side, side),
        in_specs=in_vmem(2),
        out_specs=tuple(in_vmem(2)),
        compiler_params=params(8),
        cost_estimate=COST,
        name="columns_pack",
    )(top, bottom)


def sum_kernel(after, one, two, out):
    out[...] = one[...] + two[...]


def sum_after(after, one, two):
    return pl.pallas_call(
        sum_kernel,
        out_shape=shape(*one.shape),
        in_specs=[pl.BlockSpec(memory_space=pl.ANY)] + in_vmem(2),
        out_specs=in_vmem(1)[0],
        compiler_params=params(2),
        cost_estimate=COST,
        name="sum_after",
    )(after, one, two)


def copy_kernel(after, value, out):
    out[...] = value[...]


def copy_after(after, value):
    return pl.pallas_call(
        copy_kernel,
        out_shape=shape(*value.shape),
        in_specs=[pl.BlockSpec(memory_space=pl.ANY)] + in_vmem(1),
        out_specs=in_vmem(1)[0],
        compiler_params=params(6),
        cost_estimate=COST,
        name="copy_after",
    )(after, value)


def add_partners(sums, axis, first, end):
    count = lax.axis_size(axis)
    for bit in range(first, end):
        sums = sums + lax.ppermute(sums, axis, [(i, i ^ (1 << bit)) for i in range(count)])
    return sums


def spread_kernel(one, two, out):
    total = (one[...] + two[...]).sum(axis=1)
    out[...] = jnp.broadcast_to(total[None], out.shape)


def total_over_all(one, two):
    devices = lax.axis_size(AXES)
    copies = pl.pallas_call(
        spread_kernel,
        out_shape=shape(devices, 2, one.shape[2]),
        in_specs=in_vmem(2),
        out_specs=in_vmem(1)[0],
        compiler_params=params(4),
        cost_estimate=COST,
        name="spread",
    )(one, two)
    return lax.all_to_all(copies, AXES, 0, 0, tiled=True).transpose(1, 0, 2)


def bits(axis):
    count = lax.axis_size(axis)
    assert count & (count - 1) == 0
    return count.bit_length() - 1


def body(density_init, solid_mask, loadings):
    rows, cols, depth = solid_mask.shape
    total_cells = float(rows * lax.axis_size("gx") * cols * lax.axis_size("gy") * depth)
    table = jnp.asarray(packed_tables(cols, depth)[0])

    def scale_of(sums):
        return DAMPING * loadings * total_cells / sums.sum(axis=tuple(range(sums.ndim))[1:])

    above = shift(first_rows(density_init, solid_mask), "gx", 1)
    columns = swap_columns(*first_columns(density_init, solid_mask))
    near, far, upper = mid(False, [density_init, solid_mask, *columns], table)
    below = shift(copy_after(above, upper), "gx", -1)
    to_sides = sides_pack(far, above)
    top_sides = swap_columns(*to_sides)
    (y2,) = rest(False, to_sides[0], [near], table)
    top, top_sums, upper = edge(True, False, False, [], [above, *top_sides, near, far, y2, solid_mask], table)
    below_new = shift(upper, "gx", -1)
    bottom_sides = swap_columns(*sides_pack(top_sums, below))
    bottom, bottom_sums, lower = edge(False, False, False, [], [below, *bottom_sides, near, far, y2, solid_mask], table)
    columns = swap_columns(*columns_pack(top, bottom))
    sides_new = swap_columns(*sides_pack(bottom_sums, below_new))
    sums = add_partners(sum_after(below_new, top_sums, bottom_sums), "gx", 0, 1)
    above_new = shift(copy_after(sums, lower), "gx", 1)
    near_new, far_new = mid(True, [top, bottom, *columns], table)
    scale = scale_of(add_partners(add_partners(sums, "gy", 0, bits("gy")), "gx", 1, bits("gx")))
    y2, kept = rest(True, scale, [near, near_new, density_init, solid_mask, top, bottom], table)
    common = [near, far, near_new, far_new, y2, solid_mask]
    bottom, bottom_sums = edge(False, True, True, [scale], [below, *bottom_sides, below_new, *sides_new, *common], table)
    sides_new = swap_columns(*sides_pack(y2, above_new))
    top, top_sums = edge(True, True, True, [scale], [above, *top_sides, above_new, *sides_new, *common], table)
    scale = scale_of(total_over_all(top_sums, bottom_sums))
    return kept + scale[:, None, None, None] * jnp.concatenate([top, bottom], axis=1)


def solution(mesh):
    in_specs = (P(None, "gx", "gy", None), P("gx", "gy", None), P())
    out_specs = P(None, "gx", "gy", None)
    return jax.shard_map(body, mesh=mesh, in_specs=in_specs, out_specs=out_specs, check_vma=False)
```

```python
import functools

import jax
import jax.numpy as jnp
import ml_dtypes
import numpy as np
from jax import lax
from jax.experimental import pallas as pl
from jax.experimental.pallas import tpu as pltpu
from jax.sharding import PartitionSpec as P

ITERS = 2
SEGMENTS = (1.5131, 1.0)
RADII = (6.0, 8.0)
CROSS = 0.25
DAMPING = 0.3
ATTRACT = ((0.3, 0.22), (0.22, 0.16))
REACH = (5, 7)
FAR = 8
DERIV = REACH[1]
DEEP = tuple(DERIV + r for r in REACH)
WIDE = 8
AXES = ("gx", "gy")
BF16 = jnp.bfloat16
F32 = jnp.float32


def raw_profile(kind, radius):
    offset = np.arange(17) - 8.0
    if kind == 0:
        return np.maximum(radius * radius - offset * offset, 0.0)
    if kind == 1:
        return offset * offset * np.maximum(radius * radius - offset * offset, 0.0)
    return np.exp(-np.abs(offset) / 4.0)


def split_bf16(table):
    high = table.astype(np.float32).astype(ml_dtypes.bfloat16)
    low = (table - high.astype(np.float64)).astype(np.float32).astype(ml_dtypes.bfloat16)
    return high, low


def column_band(kind, radius, count, columns, first):
    band = np.zeros((count, columns))
    for o in range(count):
        band[o, first + o : first + o + 17] = raw_profile(kind, radius)
    return band


def depth_band(kind, radius, depth):
    taps = raw_profile(kind, radius)
    band = np.zeros((depth, depth))
    for column in range(depth):
        for offset in range(17):
            source = column + offset - 8
            if 0 <= source < depth:
                band[source, column] = taps[offset]
    return band


def stage1_tables(comp, cols):
    wide = cols + 2 * WIDE
    pack = column_band(0, RADII[comp], wide, wide + 16, 0)
    rest = np.concatenate(
        [column_band(1, RADII[comp], wide, wide + 16, 0), column_band(2, 0.0, cols, wide + 16, WIDE)]
    )
    high, low = split_bf16(np.concatenate([pack, rest]))
    return {f"first{comp}": np.concatenate([high, high], axis=1), f"rest{comp}": low[wide:]}


def stage2_table(kind, cols):
    high, low = split_bf16(np.concatenate([column_band(kind, r, cols, cols + 16, 0) for r in RADII]))
    return np.concatenate([high, high] if kind == 0 else [high, high, low], axis=1)


def depth_table(kinds, depth):
    high, low = split_bf16(np.concatenate([depth_band(kind, radius, depth) for kind, radius in kinds]))
    return np.concatenate([high, low], axis=1)


def attraction_tables(depth):
    band = depth_band(2, 0.0, depth)
    high, low = split_bf16(-np.concatenate([np.concatenate([ATTRACT[i][j] * band for i in range(2)], axis=1) for j in range(2)]))
    return {"pull_high": high, "pull_low": low}


@functools.lru_cache
def packed_tables(cols, depth):
    tables = {**stage1_tables(0, cols), **stage1_tables(1, cols), **attraction_tables(depth)}
    tables |= {f"depth{kind}": depth_table([(kind, r) for r in RADII], depth) for kind in range(2)}
    tables |= {f"last{comp}": depth_table([(0, r), (1, r)], depth) for comp, r in enumerate(RADII)}
    tables |= {f"second{kind}": stage2_table(kind, cols) for kind in range(2)}
    width = max(t.shape[1] for t in tables.values())
    places, start = {}, 0
    for name, table in tables.items():
        places[name] = (start, *table.shape)
        start += table.shape[0]
    whole = np.zeros((start, width), ml_dtypes.bfloat16)
    for name, table in tables.items():
        whole[places[name][0] : places[name][0] + table.shape[0], : table.shape[1]] = table
    return whole, places


class Tables:
    def __init__(self, ref, cols, depth):
        self.ref, self.places = ref, packed_tables(cols, depth)[1]

    def __getitem__(self, name):
        start, rows, columns = self.places[name]
        return self.ref[start : start + rows, :columns]


def row_taps(kind, radius, scale):
    taps = raw_profile(kind, radius)
    return [float(v) for v in taps * (scale / taps.sum() ** 3)]


def split(field):
    high = field.astype(BF16)
    return high, (field - high.astype(F32)).astype(BF16)


def smooth_rows(values, taps, count, reach):
    out = []
    for i in range(count):
        total = None
        for k in range(reach + 1):
            if taps[8 + k] == 0.0:
                continue
            pair = values[i + reach] if k == 0 else values[i + reach - k] + values[i + reach + k]
            term = taps[8 + k] * pair
            total = term if total is None else total + term
        out.append(total)
    return out


def smooth_rows_exp(values, scale, count):
    q = float(np.exp(-0.25))
    q9 = q**9
    up = values[0]
    for j in range(1, 9):
        up = up * q + values[j]
    ups = [up]
    for i in range(1, count):
        up = up * q + (values[i + 8] - q9 * values[i - 1])
        ups.append(up)
    down = values[count + 15]
    for j in range(1, 8):
        down = down * q + values[count + 15 - j]
    down = down * q
    out = [None] * count
    out[count - 1] = scale * (ups[count - 1] + down)
    for i in range(count - 2, -1, -1):
        down = down * q + (q * values[i + 9] - q9 * values[i + 17])
        out[i] = scale * (ups[i] + down)
    return out


def split_dot(pair, table):
    high, low = split(pair)
    width = table.shape[1] // 2
    both = jnp.dot(high, table, preferred_element_type=F32)
    rest = jnp.dot(low, table[:, :width], preferred_element_type=F32)
    return both[:, :width] + both[:, width:] + rest


def stage1_columns(load, pairs, comp, tables, near, far, cols, unroll, begin):
    wide = cols + 2 * WIDE

    @pl.loop(0, pairs, unroll=unroll)
    def _(i):
        high, low = split(jnp.concatenate([load(2 * i), load(2 * i + 1)], axis=1))
        first = jnp.dot(tables[f"first{comp}"], jnp.concatenate([high, low], axis=0), preferred_element_type=F32)
        rest = first[wide:] + jnp.dot(tables[f"rest{comp}"], high, preferred_element_type=F32)
        depth = high.shape[1] // 2
        for j in range(2):
            lanes = slice(j * depth, (j + 1) * depth)
            row = begin + 2 * i + j
            near[2 * comp, row] = first[:wide, lanes]
            near[2 * comp + 1, row] = rest[:wide, lanes]
            far[comp, row] = rest[wide:, lanes]


def stage1_rows(load, first, count, out):
    wide = out.shape[2]

    @pl.loop(0, wide // 8)
    def _(t):
        window = pl.ds(pl.multiple_of(t * 8, 8), 8)
        for comp in range(2):
            reach = REACH[comp]
            for kind in range(2):
                field = 2 * comp + kind
                taps = row_taps(kind, RADII[comp], SEGMENTS[comp] if kind == 0 else 1.0)
                values = [load(field, row, window) for row in range(first - reach, first + count + reach)]
                for i, value in enumerate(smooth_rows(values, taps, count, reach)):
                    out[field, i, window, :] = value


def stage1_depth(xs, count, step, tables, deriv, place, gates):
    wide, depth = xs.shape[2:]
    for i, start in enumerate(range(0, count, step)):
        rows = slice(start, start + step)
        pair = lambda p: jnp.concatenate([xs[q, rows].reshape(step * wide, depth) for q in (p, p + 2)], axis=1)
        n3 = split_dot(pair(0), tables["depth0"])
        n2 = split_dot(pair(1), tables["depth1"])
        one = 1.0 + n3
        two = (jnp.log(one) + 2.0 * CROSS * n2 * one).reshape(step, wide, depth)
        three = (n2 / one + CROSS * n2 * n2).reshape(step, wide, depth)
        for which, value in enumerate((two, three)):
            if gates[i] is not None:
                value = value * place[gates[i]].astype(F32)
            deriv[which, rows, :WIDE] = value[:, :WIDE] * place[2].astype(F32)
            deriv[which, rows, WIDE : wide - WIDE] = value[:, WIDE : wide - WIDE]
            deriv[which, rows, wide - WIDE :] = value[:, wide - WIDE :] * place[3].astype(F32)


def stage2_columns(deriv, count, tables, out, unroll):
    cols = out.shape[2]

    @pl.loop(0, count // 2, unroll=unroll)
    def _(i):
        for which, kind in ((0, 1), (1, 0)):
            high, low = split(jnp.concatenate([deriv[which, 2 * i], deriv[which, 2 * i + 1]], axis=1))
            stacked = [high, low, high] if which == 0 else [high, low]
            result = jnp.dot(tables[f"second{kind}"], jnp.concatenate(stacked, axis=0), preferred_element_type=F32)
            depth = high.shape[1] // 2
            for comp in range(2):
                for j in range(2):
                    out[2 * which + comp, 2 * i + j] = result[comp * cols : (comp + 1) * cols, j * depth : (j + 1) * depth]


def position():
    flags = []
    for axis in AXES:
        index = lax.axis_index(axis)
        flags += [(index > 0).astype(jnp.int32), (index + 1 < lax.axis_size(axis)).astype(jnp.int32)]
    return flags + [lax.rem(lax.axis_index("gy"), 2)]


def blend(first, second, scale):
    return first if scale is None else (1.0 - DAMPING) * first + scale * second


def side_rows(pair, index, odd):
    one, two = pair[0][index], pair[1][index]
    return jnp.where(odd, one, two), jnp.where(odd, two, one)


def mid_kernel(later, *refs):
    own, solid, *refs = refs
    sides, table_ref, near, far, refs = refs[:2], *refs[2:5], refs[5:]
    rows, cols, depth = far.shape[1:]
    tables = Tables(table_ref, cols, depth)
    odd = position()[4] == 1
    if not later:
        (upper,) = refs
        base = 0
        for comp in range(2):
            part = slice(0, DEEP[comp])
            upper[base : base + DEEP[comp]] = jnp.where(solid[part] == 0, own[comp, part], 0.0)
            base += DEEP[comp]
    parts = ((0, own), (rows // 2, solid)) if later else ((0, own),)
    for comp in range(2):
        for begin, ref in parts:

            def load(row):
                left, right = side_rows(sides, (comp, begin + row), odd)
                value = ref[comp, row] if later else jnp.where(solid[row] == 0, ref[comp, row], 0.0)
                return jnp.concatenate([left, value, right], axis=0)

            count = rows // len(parts) // 2
            stage1_columns(load, count, comp, tables, near, far, cols, count, begin)


def rest_kernel(later, *refs):
    if later:
        scales, near_old, near, table_ref, y2, xs, deriv = refs
    else:
        near, table_ref, y2, xs, deriv = refs
    count, cols, depth = y2.shape[1:]
    tables, place = Tables(table_ref, cols, depth), position()

    def load(field, row, window):
        value = near[field, row, window, :]
        return blend(near_old[field, row, window, :], value, scales[field // 2]) if later else value

    stage1_rows(load, DERIV, count, xs)
    stage1_depth(xs, count, count // 3, tables, deriv, place, [None] * 3)
    stage2_columns(deriv, count, tables, y2, count // 2)


def edge_kernel(top, later, last, *refs):
    if later:
        scales, halo, *refs = refs
        sides, halo_new, sides_new, near_old, far_old, refs = refs[:2], refs[2], refs[3:5], *refs[5:7], refs[7:]
    else:
        halo, *refs = refs
        sides, refs = refs[:2], refs[2:]
    near, far, y2, solid, table_ref, proposal, sums, *refs = refs
    if not last:
        packed, *refs = refs
    near_h, far_h, xs, deriv, y2_h, xm, xa = refs
    _, rows, cols, depth = far.shape
    half = rows // 2
    tables = Tables(table_ref, cols, depth)
    place = position()
    odd = place[4] == 1
    for comp in range(2):
        base = 0 if comp == 0 else DEEP[0]
        scale = scales[comp] if later else None

        def load(row):
            value = halo[base + row]
            left, right = side_rows(sides, base + row, odd)
            if later:
                value = blend(value, halo_new[base + row], scale)
                left_new, right_new = side_rows(sides_new, base + row, odd)
                left, right = blend(left, left_new, scale), blend(right, right_new, scale)
            return jnp.concatenate([left, value, right], axis=0)

        stage1_columns(load, DEEP[comp] // 2, comp, tables, near_h, far_h, cols, DEEP[comp] // 2, 0)

    if not later:
        near_old = far_old = None

    def pick(own, edge, index, row, window):
        comp = index // 2 if own is near else index
        if 0 <= row < rows:
            value = own[index, row, window, :]
            old = near_old if own is near else far_old
            return blend(old[index, row, window, :], value, scales[comp]) if later else value
        return edge[index, row + DEEP[comp] if top else row - rows, window, :]

    first = -DERIV if top else rows - DERIV
    stage1_rows(lambda f, row, window: pick(near, near_h, f, row, window), first, 2 * DERIV, xs)
    gates = [0, None] if top else [None, 1]
    stage1_depth(xs, 2 * DERIV, DERIV, tables, deriv, place, gates)
    stage2_columns(deriv, 2 * DERIV, tables, y2_h, 7)

    start = 0 if top else half

    @pl.loop(0, cols // 8)
    def _(t):
        window = pl.ds(pl.multiple_of(t * 8, 8), 8)

        def second(index, row):
            if DERIV <= row < rows - DERIV:
                return y2[index, row - DERIV, window, :]
            return y2_h[index, row - first, window, :]

        for which, kind in ((0, 1), (1, 0)):
            for comp in range(2):
                reach = REACH[comp]
                taps = row_taps(kind, RADII[comp], SEGMENTS[comp] if kind == 0 else 1.0)
                values = [second(2 * which + comp, row) for row in range(start - reach, start + half + reach)]
                for i, value in enumerate(smooth_rows(values, taps, half, reach)):
                    xm[2 * which + comp, i, window, :] = value
        scale = row_taps(2, 0.0, 1.0)[8]
        for comp in range(2):
            values = [pick(far, far_h, comp, row, window) for row in range(start - FAR, start + half + FAR)]
            for i, value in enumerate(smooth_rows_exp(values, scale, half)):
                xa[comp, i, window, :] = value

    sums[...] = jnp.zeros_like(sums)
    step = half // 2
    for i in range(0, half, step):
        part = slice(i, i + step)
        flat = lambda ref, p: ref[p, part].reshape(step * cols, depth)
        pore = solid[start + i : start + i + step].reshape(step * cols, depth) == 0
        high, low = split(jnp.concatenate([flat(xa, 0), flat(xa, 1)], axis=1))
        pull = jnp.dot(high, tables["pull_high"], preferred_element_type=F32)
        pull += jnp.dot(high, tables["pull_low"], preferred_element_type=F32)
        pull += jnp.dot(low, tables["pull_high"], preferred_element_type=F32)
        for comp in range(2):
            mu = split_dot(jnp.concatenate([flat(xm, 2 + comp), flat(xm, comp)], axis=1), tables[f"last{comp}"])
            mu = mu + pull[:, comp * depth : (comp + 1) * depth]
            value = jnp.where(pore, jnp.exp(-mu), 0.0)
            proposal[comp, part] = value.reshape(step, cols, depth)
            sums[comp] += value.reshape(step * cols // 8, 8, depth).sum(0)
    if not last:
        base = 0
        for comp in range(2):
            part = slice(0, DEEP[comp]) if top else slice(half - DEEP[comp], half)
            packed[base : base + DEEP[comp]] = proposal[comp, part]
            base += DEEP[comp]


def in_vmem(count):
    return [pl.BlockSpec(memory_space=pltpu.VMEM)] * count


def params(mebibytes):
    return pltpu.CompilerParams(vmem_limit_bytes=mebibytes * 1024 * 1024)


def shape(*sizes):
    return jax.ShapeDtypeStruct(sizes, F32)


COST = pl.CostEstimate(flops=1000, bytes_accessed=1000, transcendentals=0)


def derivative_scratch(count, wide, depth):
    return [pltpu.VMEM((4, count, wide, depth), F32), pltpu.VMEM((2, count, wide, depth), F32)]


def mid(later, blocks, table):
    _, rows, _, depth = blocks[2].shape
    cols = blocks[0].shape[2]
    outs = [shape(4, rows, cols + 2 * WIDE, depth), shape(2, rows, cols, depth)]
    if not later:
        outs += [shape(sum(DEEP), cols, depth)]
    return pl.pallas_call(
        functools.partial(mid_kernel, later),
        out_shape=tuple(outs),
        in_specs=in_vmem(len(blocks) + 1),
        out_specs=tuple(in_vmem(len(outs))),
        compiler_params=params(6),
        cost_estimate=COST,
        name="mid",
    )(*blocks, table)


def rest(later, scalars, blocks, table):
    _, rows, wide, depth = blocks[0].shape
    count, cols = rows - 2 * DERIV, wide - 2 * WIDE
    return pl.pallas_call(
        functools.partial(rest_kernel, later),
        out_shape=shape(4, count, cols, depth),
        in_specs=[pl.BlockSpec(memory_space=pltpu.SMEM)] * len(scalars) + in_vmem(len(blocks) + 1),
        out_specs=in_vmem(1)[0],
        scratch_shapes=[pltpu.VMEM((4, count, wide, depth), F32), pltpu.VMEM((2, count, wide, depth), F32)],
        compiler_params=params(8),
        cost_estimate=COST,
        name="rest",
    )(*scalars, *blocks, table)


def edge(top, later, last, scalars, blocks, table):
    rows, cols, depth = blocks[-1].shape
    wide, half = cols + 2 * WIDE, rows // 2
    f32 = lambda *s: pltpu.VMEM(s, F32)
    outs = [shape(2, half, cols, depth), shape(2, 8, depth)]
    if not last:
        outs.append(shape(sum(DEEP), cols, depth))
    return pl.pallas_call(
        functools.partial(edge_kernel, top, later, last),
        out_shape=tuple(outs),
        in_specs=[pl.BlockSpec(memory_space=pltpu.SMEM)] * len(scalars) + in_vmem(len(blocks) + 1),
        out_specs=tuple(in_vmem(len(outs))),
        scratch_shapes=[
            f32(4, DEEP[1], wide, depth),
            f32(2, DEEP[1], cols, depth),
            f32(4, 2 * DERIV, wide, depth),
            f32(2, 2 * DERIV, wide, depth),
            f32(4, 2 * DERIV, cols, depth),
            f32(4, half, cols, depth),
            f32(2, half, cols, depth),
        ],
        compiler_params=params(16),
        cost_estimate=COST,
        name="edge_top" if top else "edge_bottom",
    )(*scalars, *blocks, table)


def shift(value, axis, step):
    count = lax.axis_size(axis)
    return lax.ppermute(value, axis, [(i, i + step) for i in range(count) if 0 <= i + step < count])


def swap_columns(even, odd):
    count = lax.axis_size("gy")
    pairs = lambda first: [p for i in range(first, count - 1, 2) for p in ((i, i + 1), (i + 1, i))]
    return lax.ppermute(even, "gy", pairs(0)), lax.ppermute(odd, "gy", pairs(1))


def side_starts(cols):
    right, left = cols - 2 * WIDE, 0
    odd = position()[4]
    return pl.multiple_of(right * (1 - odd), 8), pl.multiple_of(right * odd, 8)


def first_rows_kernel(own, solid, out, density, mask, sems):
    rows = own.shape[1]
    most = max(DEEP)
    half = most // 2
    copies = []
    for part, begin in enumerate((0, half)):
        source, target = pl.ds(rows - most + begin, half), pl.ds(begin, half)
        copies.append(pltpu.make_async_copy(solid.at[source], mask.at[target], sems.at[part]))
        for comp in range(2):
            copies.append(pltpu.make_async_copy(own.at[comp, source], density.at[comp, target], sems.at[2 + 2 * part + comp]))
    for copy in copies:
        copy.start()
    for copy in copies:
        copy.wait()
    base = 0
    for comp in range(2):
        out[base : base + DEEP[comp]] = jnp.where(mask[most - DEEP[comp] :] == 0, density[comp, most - DEEP[comp] :], 0.0)
        base += DEEP[comp]


def first_rows(own, solid):
    _, _, cols, depth = own.shape
    return pl.pallas_call(
        first_rows_kernel,
        out_shape=shape(sum(DEEP), cols, depth),
        in_specs=[pl.BlockSpec(memory_space=pl.ANY)] * 2,
        out_specs=in_vmem(1)[0],
        scratch_shapes=[
            pltpu.VMEM((2, max(DEEP), cols, depth), F32),
            pltpu.VMEM((max(DEEP), cols, depth), jnp.int32),
            pltpu.SemaphoreType.DMA((6,)),
        ],
        compiler_params=params(56),
        cost_estimate=COST,
        name="first_rows",
    )(own, solid)


def first_columns_kernel(own, solid, even, odd):
    for start, out in zip(side_starts(own.shape[2]), (even, odd)):
        window = pl.ds(start, 2 * WIDE)
        for comp in range(2):
            out[comp] = jnp.where(solid[:, window] == 0, own[comp, :, window], 0.0)


def first_columns(own, solid):
    _, rows, _, depth = own.shape
    side = shape(2, rows, 2 * WIDE, depth)
    return pl.pallas_call(
        first_columns_kernel,
        out_shape=(side, side),
        in_specs=in_vmem(2),
        out_specs=tuple(in_vmem(2)),
        compiler_params=params(8),
        cost_estimate=COST,
        name="first_columns",
    )(own, solid)


def sides_kernel(after, value, even, odd, sems):
    copies = []
    for i, (start, out) in enumerate(zip(side_starts(value.shape[1]), (even, odd))):
        copies.append(pltpu.make_async_copy(value.at[:, pl.ds(start, 2 * WIDE)], out, sems.at[i]))
    for copy in copies:
        copy.start()
    for copy in copies:
        copy.wait()


def sides_pack(after, value):
    count, _, depth = value.shape
    side = shape(count, 2 * WIDE, depth)
    return pl.pallas_call(
        sides_kernel,
        out_shape=(side, side),
        in_specs=[pl.BlockSpec(memory_space=pl.ANY)] * 2,
        out_specs=tuple(in_vmem(2)),
        scratch_shapes=[pltpu.SemaphoreType.DMA((2,))],
        compiler_params=params(4),
        cost_estimate=COST,
        name="sides_pack",
    )(after, value)


def columns_kernel(top, bottom, even, odd):
    half, cols = top.shape[1:3]
    for start, out in zip(side_starts(cols), (even, odd)):
        out[:, :half] = top[:, :, pl.ds(start, 2 * WIDE)]
        out[:, half:] = bottom[:, :, pl.ds(start, 2 * WIDE)]


def columns_pack(top, bottom):
    _, half, _, depth = top.shape
    side = shape(2, 2 * half, 2 * WIDE, depth)
    return pl.pallas_call(
        columns_kernel,
        out_shape=(side, side),
        in_specs=in_vmem(2),
        out_specs=tuple(in_vmem(2)),
        compiler_params=params(8),
        cost_estimate=COST,
        name="columns_pack",
    )(top, bottom)


def copy_kernel(after, value, out):
    out[...] = value[...]


def copy_after(after, value):
    return pl.pallas_call(
        copy_kernel,
        out_shape=shape(*value.shape),
        in_specs=[pl.BlockSpec(memory_space=pl.ANY)] + in_vmem(1),
        out_specs=in_vmem(1)[0],
        compiler_params=params(6),
        cost_estimate=COST,
        name="copy_after",
    )(after, value)


def add_partners(sums, axis, first, end):
    count = lax.axis_size(axis)
    for bit in range(first, end):
        sums = sums + lax.ppermute(sums, axis, [(i, i ^ (1 << bit)) for i in range(count)])
    return sums


def spread_kernel(one, two, out):
    total = (one[...] + two[...]).sum(axis=1)
    out[...] = jnp.broadcast_to(total[None], out.shape)


def total_over_all(one, two):
    devices = lax.axis_size(AXES)
    copies = pl.pallas_call(
        spread_kernel,
        out_shape=shape(devices, 2, one.shape[2]),
        in_specs=in_vmem(2),
        out_specs=in_vmem(1)[0],
        compiler_params=params(4),
        cost_estimate=COST,
        name="spread",
    )(one, two)
    return lax.all_to_all(copies, AXES, 0, 0, tiled=True)


def last_kernel(total_cells, scales, loadings, totals, own, solid, old_top, old_bottom, top, bottom, out):
    comp, lower = pl.program_id(0), pl.program_id(1)
    half = top.shape[1]
    total = jnp.where(comp == 0, jnp.sum(totals[:, 0]), jnp.sum(totals[:, 1]))
    factor = jnp.full((1, 1, 1), DAMPING * loadings[comp] * total_cells, F32) / total
    part = pl.ds(lower * half, half)
    start = jnp.where(solid[part] == 0, own[comp, part], 0.0)
    pick = lambda one, two: jnp.where(lower == 0, one[comp], two[comp])
    kept = (1.0 - DAMPING) * blend(start, pick(old_top, old_bottom), scales[comp])
    out[0] = kept + factor * pick(top, bottom)


def last_update(total_cells, scalars, blocks):
    own = blocks[1]
    _, rows, cols, depth = own.shape
    return pl.pallas_call(
        functools.partial(last_kernel, total_cells),
        grid=(2, 2),
        out_shape=shape(*own.shape),
        in_specs=[pl.BlockSpec(memory_space=pltpu.SMEM)] * len(scalars) + in_vmem(len(blocks)),
        out_specs=pl.BlockSpec((1, rows // 2, cols, depth), lambda comp, lower: (comp, lower, 0, 0)),
        compiler_params=params(6),
        cost_estimate=COST,
        name="last_update",
    )(*scalars, *blocks)


def bits(axis):
    count = lax.axis_size(axis)
    assert count & (count - 1) == 0
    return count.bit_length() - 1


def body(density_init, solid_mask, loadings):
    rows, cols, depth = solid_mask.shape
    total_cells = float(rows * lax.axis_size("gx") * cols * lax.axis_size("gy") * depth)
    table = jnp.asarray(packed_tables(cols, depth)[0])

    def scale_of(sums):
        return DAMPING * loadings * total_cells / sums.sum(axis=tuple(range(sums.ndim))[1:])

    above = shift(first_rows(density_init, solid_mask), "gx", 1)
    columns = swap_columns(*first_columns(density_init, solid_mask))
    near, far, upper = mid(False, [density_init, solid_mask, *columns], table)
    y2 = rest(False, [], [near], table)
    below = shift(copy_after(y2, upper), "gx", -1)
    top_sides = swap_columns(*sides_pack(y2, above))
    top, top_sums, upper = edge(True, False, False, [], [above, *top_sides, near, far, y2, solid_mask], table)
    below_new = shift(upper, "gx", -1)
    bottom_sides = swap_columns(*sides_pack(top_sums, below))
    bottom, bottom_sums, lower = edge(False, False, False, [], [below, *bottom_sides, near, far, y2, solid_mask], table)
    old = [density_init, solid_mask, top, bottom]
    columns = swap_columns(*columns_pack(top, bottom))
    sums = add_partners(top_sums + bottom_sums, "gy", 0, bits("gy"))
    sides_new = swap_columns(*sides_pack(sums, below_new))
    sums = add_partners(copy_after(below_new, sums), "gx", 0, 1)
    above_new = shift(copy_after(sums, lower), "gx", 1)
    near_new, far_new = mid(True, [top, bottom, *columns], table)
    scale = scale_of(add_partners(sums, "gx", 1, bits("gx")))
    y2 = rest(True, [scale], [near, near_new], table)
    common = [near, far, near_new, far_new, y2, solid_mask]
    bottom, bottom_sums = edge(False, True, True, [scale], [below, *bottom_sides, below_new, *sides_new, *common], table)
    sides_new = swap_columns(*sides_pack(y2, above_new))
    top, top_sums = edge(True, True, True, [scale], [above, *top_sides, above_new, *sides_new, *common], table)
    totals = total_over_all(top_sums, bottom_sums)
    return last_update(total_cells, [scale, loadings], [totals, *old, top, bottom])


def solution(mesh):
    in_specs = (P(None, "gx", "gy", None), P("gx", "gy", None), P())
    out_specs = P(None, "gx", "gy", None)
    return jax.shard_map(body, mesh=mesh, in_specs=in_specs, out_specs=out_specs, check_vma=False)
```

```python
import functools

import jax
import jax.numpy as jnp
import ml_dtypes
import numpy as np
from jax import lax
from jax.experimental import pallas as pl
from jax.experimental.pallas import tpu as pltpu
from jax.sharding import PartitionSpec as P

ITERS = 2
SEGMENTS = (1.5131, 1.0)
RADII = (6.0, 8.0)
CROSS = 0.25
DAMPING = 0.3
ATTRACT = ((0.3, 0.22), (0.22, 0.16))
REACH = (5, 7)
FAR = 8
DERIV = REACH[1]
DEEP = tuple(DERIV + r for r in REACH)
WIDE = 8
AXES = ("gx", "gy")
BF16 = jnp.bfloat16
F32 = jnp.float32


def raw_profile(kind, radius):
    offset = np.arange(17) - 8.0
    if kind == 0:
        return np.maximum(radius * radius - offset * offset, 0.0)
    if kind == 1:
        return offset * offset * np.maximum(radius * radius - offset * offset, 0.0)
    return np.exp(-np.abs(offset) / 4.0)


def split_bf16(table):
    high = table.astype(np.float32).astype(ml_dtypes.bfloat16)
    low = (table - high.astype(np.float64)).astype(np.float32).astype(ml_dtypes.bfloat16)
    return high, low


def column_band(kind, radius, count, columns, first):
    band = np.zeros((count, columns))
    for o in range(count):
        band[o, first + o : first + o + 17] = raw_profile(kind, radius)
    return band


def depth_band(kind, radius, depth):
    taps = raw_profile(kind, radius)
    band = np.zeros((depth, depth))
    for column in range(depth):
        for offset in range(17):
            source = column + offset - 8
            if 0 <= source < depth:
                band[source, column] = taps[offset]
    return band


def stage1_tables(comp, cols):
    wide = cols + 2 * WIDE
    pack = column_band(0, RADII[comp], wide, wide + 16, 0)
    rest = np.concatenate(
        [column_band(1, RADII[comp], wide, wide + 16, 0), column_band(2, 0.0, cols, wide + 16, WIDE)]
    )
    high, low = split_bf16(np.concatenate([pack, rest]))
    return {f"first{comp}": np.concatenate([high, high], axis=1), f"rest{comp}": low[wide:]}


def stage2_table(kind, cols):
    high, low = split_bf16(np.concatenate([column_band(kind, r, cols, cols + 16, 0) for r in RADII]))
    return np.concatenate([high, high] if kind == 0 else [high, high, low], axis=1)


def depth_table(kinds, depth):
    high, low = split_bf16(np.concatenate([depth_band(kind, radius, depth) for kind, radius in kinds]))
    return np.concatenate([high, low], axis=1)


def attraction_tables(depth):
    band = depth_band(2, 0.0, depth)
    high, low = split_bf16(-np.concatenate([np.concatenate([ATTRACT[i][j] * band for i in range(2)], axis=1) for j in range(2)]))
    return {"pull_high": high, "pull_low": low}


@functools.lru_cache
def packed_tables(cols, depth):
    tables = {**stage1_tables(0, cols), **stage1_tables(1, cols), **attraction_tables(depth)}
    tables |= {f"depth{kind}": depth_table([(kind, r) for r in RADII], depth) for kind in range(2)}
    tables |= {f"last{comp}": depth_table([(0, r), (1, r)], depth) for comp, r in enumerate(RADII)}
    tables |= {f"second{kind}": stage2_table(kind, cols) for kind in range(2)}
    width = max(t.shape[1] for t in tables.values())
    places, start = {}, 0
    for name, table in tables.items():
        places[name] = (start, *table.shape)
        start += table.shape[0]
    whole = np.zeros((start, width), ml_dtypes.bfloat16)
    for name, table in tables.items():
        whole[places[name][0] : places[name][0] + table.shape[0], : table.shape[1]] = table
    return whole, places


class Tables:
    def __init__(self, ref, cols, depth):
        self.ref, self.places = ref, packed_tables(cols, depth)[1]

    def __getitem__(self, name):
        start, rows, columns = self.places[name]
        return self.ref[start : start + rows, :columns]


def row_taps(kind, radius, scale):
    taps = raw_profile(kind, radius)
    return [float(v) for v in taps * (scale / taps.sum() ** 3)]


def split(field):
    high = field.astype(BF16)
    return high, (field - high.astype(F32)).astype(BF16)


def smooth_rows(values, taps, count, reach):
    out = []
    for i in range(count):
        total = None
        for k in range(reach + 1):
            if taps[8 + k] == 0.0:
                continue
            pair = values[i + reach] if k == 0 else values[i + reach - k] + values[i + reach + k]
            term = taps[8 + k] * pair
            total = term if total is None else total + term
        out.append(total)
    return out


def smooth_rows_exp(values, scale, count):
    q = float(np.exp(-0.25))
    q9 = q**9
    up = values[0]
    for j in range(1, 9):
        up = up * q + values[j]
    ups = [up]
    for i in range(1, count):
        up = up * q + (values[i + 8] - q9 * values[i - 1])
        ups.append(up)
    down = values[count + 15]
    for j in range(1, 8):
        down = down * q + values[count + 15 - j]
    down = down * q
    out = [None] * count
    out[count - 1] = scale * (ups[count - 1] + down)
    for i in range(count - 2, -1, -1):
        down = down * q + (q * values[i + 9] - q9 * values[i + 17])
        out[i] = scale * (ups[i] + down)
    return out


def split_dot(pair, table):
    high, low = split(pair)
    width = table.shape[1] // 2
    both = jnp.dot(high, table, preferred_element_type=F32)
    rest = jnp.dot(low, table[:, :width], preferred_element_type=F32)
    return both[:, :width] + both[:, width:] + rest


def stage1_columns(load, pairs, comp, tables, near, far, cols, unroll, begin):
    wide = cols + 2 * WIDE

    @pl.loop(0, pairs, unroll=unroll)
    def _(i):
        high, low = split(jnp.concatenate([load(2 * i), load(2 * i + 1)], axis=1))
        first = jnp.dot(tables[f"first{comp}"], jnp.concatenate([high, low], axis=0), preferred_element_type=F32)
        rest = first[wide:] + jnp.dot(tables[f"rest{comp}"], high, preferred_element_type=F32)
        depth = high.shape[1] // 2
        for j in range(2):
            lanes = slice(j * depth, (j + 1) * depth)
            row = begin + 2 * i + j
            near[2 * comp, row] = first[:wide, lanes]
            near[2 * comp + 1, row] = rest[:wide, lanes]
            far[comp, row] = rest[wide:, lanes]


def stage1_rows(load, first, count, out):
    wide = out.shape[2]

    @pl.loop(0, wide // 8)
    def _(t):
        window = pl.ds(pl.multiple_of(t * 8, 8), 8)
        for comp in range(2):
            reach = REACH[comp]
            for kind in range(2):
                field = 2 * comp + kind
                taps = row_taps(kind, RADII[comp], SEGMENTS[comp] if kind == 0 else 1.0)
                values = [load(field, row, window) for row in range(first - reach, first + count + reach)]
                for i, value in enumerate(smooth_rows(values, taps, count, reach)):
                    out[field, i, window, :] = value


def stage1_depth(xs, count, step, tables, deriv, place, gates):
    wide, depth = xs.shape[2:]
    for i, start in enumerate(range(0, count, step)):
        rows = slice(start, start + step)
        pair = lambda p: jnp.concatenate([xs[q, rows].reshape(step * wide, depth) for q in (p, p + 2)], axis=1)
        n3 = split_dot(pair(0), tables["depth0"])
        n2 = split_dot(pair(1), tables["depth1"])
        one = 1.0 + n3
        two = (jnp.log(one) + 2.0 * CROSS * n2 * one).reshape(step, wide, depth)
        three = (n2 / one + CROSS * n2 * n2).reshape(step, wide, depth)
        for which, value in enumerate((two, three)):
            if gates[i] is not None:
                value = value * place[gates[i]].astype(F32)
            deriv[which, rows, :WIDE] = value[:, :WIDE] * place[2].astype(F32)
            deriv[which, rows, WIDE : wide - WIDE] = value[:, WIDE : wide - WIDE]
            deriv[which, rows, wide - WIDE :] = value[:, wide - WIDE :] * place[3].astype(F32)


def stage2_columns(deriv, count, tables, out, unroll):
    cols = out.shape[2]

    @pl.loop(0, count // 2, unroll=unroll)
    def _(i):
        for which, kind in ((0, 1), (1, 0)):
            high, low = split(jnp.concatenate([deriv[which, 2 * i], deriv[which, 2 * i + 1]], axis=1))
            stacked = [high, low, high] if which == 0 else [high, low]
            result = jnp.dot(tables[f"second{kind}"], jnp.concatenate(stacked, axis=0), preferred_element_type=F32)
            depth = high.shape[1] // 2
            for comp in range(2):
                for j in range(2):
                    out[2 * which + comp, 2 * i + j] = result[comp * cols : (comp + 1) * cols, j * depth : (j + 1) * depth]


def position():
    flags = []
    for axis in AXES:
        index = lax.axis_index(axis)
        flags += [(index > 0).astype(jnp.int32), (index + 1 < lax.axis_size(axis)).astype(jnp.int32)]
    return flags + [lax.rem(lax.axis_index("gy"), 2)]


def blend(first, second, scale):
    return first if scale is None else (1.0 - DAMPING) * first + scale * second


def side_rows(pair, index, odd):
    one, two = pair[0][index], pair[1][index]
    return jnp.where(odd, one, two), jnp.where(odd, two, one)


def mid_kernel(later, *refs):
    own, solid, *refs = refs
    sides, table_ref, near, far, refs = refs[:2], *refs[2:5], refs[5:]
    rows, cols, depth = far.shape[1:]
    tables = Tables(table_ref, cols, depth)
    odd = position()[4] == 1
    if not later:
        (upper,) = refs
        base = 0
        for comp in range(2):
            part = slice(0, DEEP[comp])
            upper[base : base + DEEP[comp]] = jnp.where(solid[part] == 0, own[comp, part], 0.0)
            base += DEEP[comp]
    parts = ((0, own), (rows // 2, solid)) if later else ((0, own),)
    for comp in range(2):
        for begin, ref in parts:

            def load(row):
                left, right = side_rows(sides, (comp, begin + row), odd)
                value = ref[comp, row] if later else jnp.where(solid[row] == 0, ref[comp, row], 0.0)
                return jnp.concatenate([left, value, right], axis=0)

            count = rows // len(parts) // 2
            stage1_columns(load, count, comp, tables, near, far, cols, count, begin)


def rest_kernel(later, *refs):
    if later:
        scales, near_old, far_old, near_new, far_new, table_ref, y2, near, far, xs, deriv = refs
        for old, new, out in ((near_old, near_new, near), (far_old, far_new, far)):
            fields, rows = out.shape[:2]

            @pl.loop(0, rows)
            def _(row):
                for field in range(fields):
                    out[field, row] = blend(old[field, row], new[field, row], scales[2 * field // fields])
    else:
        after, near, table_ref, y2, xs, deriv = refs
    count, cols, depth = y2.shape[1:]
    tables, place = Tables(table_ref, cols, depth), position()
    stage1_rows(lambda field, row, window: near[field, row, window, :], DERIV, count, xs)
    stage1_depth(xs, count, count // 3, tables, deriv, place, [None] * 3)
    stage2_columns(deriv, count, tables, y2, count // 2)


def edge_kernel(top, later, last, *refs):
    if later:
        scales, halo, *refs = refs
        sides, halo_new, sides_new, refs = refs[:2], refs[2], refs[3:5], refs[5:]
    else:
        halo, *refs = refs
        sides, refs = refs[:2], refs[2:]
    near, far, y2, solid, table_ref, proposal, sums, *refs = refs
    if not last:
        packed, *refs = refs
    near_h, far_h, xs, deriv, y2_h, xm, xa = refs
    _, rows, cols, depth = far.shape
    half = rows // 2
    tables = Tables(table_ref, cols, depth)
    place = position()
    odd = place[4] == 1
    for comp in range(2):
        base = 0 if comp == 0 else DEEP[0]
        scale = scales[comp] if later else None

        def load(row):
            value = halo[base + row]
            left, right = side_rows(sides, base + row, odd)
            if later:
                value = blend(value, halo_new[base + row], scale)
                left_new, right_new = side_rows(sides_new, base + row, odd)
                left, right = blend(left, left_new, scale), blend(right, right_new, scale)
            return jnp.concatenate([left, value, right], axis=0)

        stage1_columns(load, DEEP[comp] // 2, comp, tables, near_h, far_h, cols, DEEP[comp] // 2, 0)

    def pick(own, edge, index, row, window):
        comp = index // 2 if own is near else index
        if 0 <= row < rows:
            return own[index, row, window, :]
        return edge[index, row + DEEP[comp] if top else row - rows, window, :]

    first = -DERIV if top else rows - DERIV
    stage1_rows(lambda f, row, window: pick(near, near_h, f, row, window), first, 2 * DERIV, xs)
    gates = [0, None] if top else [None, 1]
    stage1_depth(xs, 2 * DERIV, DERIV, tables, deriv, place, gates)
    stage2_columns(deriv, 2 * DERIV, tables, y2_h, 7)

    start = 0 if top else half

    @pl.loop(0, cols // 8)
    def _(t):
        window = pl.ds(pl.multiple_of(t * 8, 8), 8)

        def second(index, row):
            if DERIV <= row < rows - DERIV:
                return y2[index, row - DERIV, window, :]
            return y2_h[index, row - first, window, :]

        for which, kind in ((0, 1), (1, 0)):
            for comp in range(2):
                reach = REACH[comp]
                taps = row_taps(kind, RADII[comp], SEGMENTS[comp] if kind == 0 else 1.0)
                values = [second(2 * which + comp, row) for row in range(start - reach, start + half + reach)]
                for i, value in enumerate(smooth_rows(values, taps, half, reach)):
                    xm[2 * which + comp, i, window, :] = value
        scale = row_taps(2, 0.0, 1.0)[8]
        for comp in range(2):
            values = [pick(far, far_h, comp, row, window) for row in range(start - FAR, start + half + FAR)]
            for i, value in enumerate(smooth_rows_exp(values, scale, half)):
                xa[comp, i, window, :] = value

    sums[...] = jnp.zeros_like(sums)
    step = half // 2
    for i in range(0, half, step):
        part = slice(i, i + step)
        flat = lambda ref, p: ref[p, part].reshape(step * cols, depth)
        pore = solid[start + i : start + i + step].reshape(step * cols, depth) == 0
        high, low = split(jnp.concatenate([flat(xa, 0), flat(xa, 1)], axis=1))
        pull = jnp.dot(high, tables["pull_high"], preferred_element_type=F32)
        pull += jnp.dot(high, tables["pull_low"], preferred_element_type=F32)
        pull += jnp.dot(low, tables["pull_high"], preferred_element_type=F32)
        for comp in range(2):
            mu = split_dot(jnp.concatenate([flat(xm, 2 + comp), flat(xm, comp)], axis=1), tables[f"last{comp}"])
            mu = mu + pull[:, comp * depth : (comp + 1) * depth]
            value = jnp.where(pore, jnp.exp(-mu), 0.0)
            proposal[comp, part] = value.reshape(step, cols, depth)
            sums[comp] += value.reshape(step * cols // 8, 8, depth).sum(0)
    if not last:
        base = 0
        for comp in range(2):
            part = slice(0, DEEP[comp]) if top else slice(half - DEEP[comp], half)
            packed[base : base + DEEP[comp]] = proposal[comp, part]
            base += DEEP[comp]


def in_vmem(count):
    return [pl.BlockSpec(memory_space=pltpu.VMEM)] * count


def params(mebibytes):
    return pltpu.CompilerParams(vmem_limit_bytes=mebibytes * 1024 * 1024)


def shape(*sizes):
    return jax.ShapeDtypeStruct(sizes, F32)


COST = pl.CostEstimate(flops=1000, bytes_accessed=1000, transcendentals=0)


def derivative_scratch(count, wide, depth):
    return [pltpu.VMEM((4, count, wide, depth), F32), pltpu.VMEM((2, count, wide, depth), F32)]


def mid(later, blocks, table):
    _, rows, _, depth = blocks[2].shape
    cols = blocks[0].shape[2]
    outs = [shape(4, rows, cols + 2 * WIDE, depth), shape(2, rows, cols, depth)]
    if not later:
        outs += [shape(sum(DEEP), cols, depth)]
    return pl.pallas_call(
        functools.partial(mid_kernel, later),
        out_shape=tuple(outs),
        in_specs=in_vmem(len(blocks) + 1),
        out_specs=tuple(in_vmem(len(outs))),
        compiler_params=params(6),
        cost_estimate=COST,
        name="mid",
    )(*blocks, table)


def rest(later, first, blocks, table):
    _, rows, wide, depth = blocks[0].shape
    count, cols = rows - 2 * DERIV, wide - 2 * WIDE
    outs = [shape(4, count, cols, depth)]
    if later:
        outs += [shape(*block.shape) for block in blocks[:2]]
    return pl.pallas_call(
        functools.partial(rest_kernel, later),
        out_shape=tuple(outs),
        in_specs=[pl.BlockSpec(memory_space=pltpu.SMEM if later else pl.ANY)] + in_vmem(len(blocks) + 1),
        out_specs=tuple(in_vmem(len(outs))),
        scratch_shapes=[pltpu.VMEM((4, count, wide, depth), F32), pltpu.VMEM((2, count, wide, depth), F32)],
        compiler_params=params(8),
        cost_estimate=COST,
        name="rest",
    )(first, *blocks, table)


def edge(top, later, last, scalars, blocks, table):
    rows, cols, depth = blocks[-1].shape
    wide, half = cols + 2 * WIDE, rows // 2
    f32 = lambda *s: pltpu.VMEM(s, F32)
    outs = [shape(2, half, cols, depth), shape(2, 8, depth)]
    if not last:
        outs.append(shape(sum(DEEP), cols, depth))
    return pl.pallas_call(
        functools.partial(edge_kernel, top, later, last),
        out_shape=tuple(outs),
        in_specs=[pl.BlockSpec(memory_space=pltpu.SMEM)] * len(scalars) + in_vmem(len(blocks) + 1),
        out_specs=tuple(in_vmem(len(outs))),
        scratch_shapes=[
            f32(4, DEEP[1], wide, depth),
            f32(2, DEEP[1], cols, depth),
            f32(4, 2 * DERIV, wide, depth),
            f32(2, 2 * DERIV, wide, depth),
            f32(4, 2 * DERIV, cols, depth),
            f32(4, half, cols, depth),
            f32(2, half, cols, depth),
        ],
        compiler_params=params(16),
        cost_estimate=COST,
        name="edge_top" if top else "edge_bottom",
    )(*scalars, *blocks, table)


def shift(value, axis, step):
    count = lax.axis_size(axis)
    return lax.ppermute(value, axis, [(i, i + step) for i in range(count) if 0 <= i + step < count])


def swap_columns(even, odd):
    count = lax.axis_size("gy")
    pairs = lambda first: [p for i in range(first, count - 1, 2) for p in ((i, i + 1), (i + 1, i))]
    return lax.ppermute(even, "gy", pairs(0)), lax.ppermute(odd, "gy", pairs(1))


def side_starts(cols):
    right, left = cols - 2 * WIDE, 0
    odd = position()[4]
    return pl.multiple_of(right * (1 - odd), 8), pl.multiple_of(right * odd, 8)


def first_rows_kernel(own, solid, out, density, mask, sems):
    rows = own.shape[1]
    most = max(DEEP)
    half = most // 2
    copies = []
    for part, begin in enumerate((0, half)):
        source, target = pl.ds(rows - most + begin, half), pl.ds(begin, half)
        copies.append(pltpu.make_async_copy(solid.at[source], mask.at[target], sems.at[part]))
        for comp in range(2):
            copies.append(pltpu.make_async_copy(own.at[comp, source], density.at[comp, target], sems.at[2 + 2 * part + comp]))
    for copy in copies:
        copy.start()
    for copy in copies:
        copy.wait()
    base = 0
    for comp in range(2):
        out[base : base + DEEP[comp]] = jnp.where(mask[most - DEEP[comp] :] == 0, density[comp, most - DEEP[comp] :], 0.0)
        base += DEEP[comp]


def first_rows(own, solid):
    _, _, cols, depth = own.shape
    return pl.pallas_call(
        first_rows_kernel,
        out_shape=shape(sum(DEEP), cols, depth),
        in_specs=[pl.BlockSpec(memory_space=pl.ANY)] * 2,
        out_specs=in_vmem(1)[0],
        scratch_shapes=[
            pltpu.VMEM((2, max(DEEP), cols, depth), F32),
            pltpu.VMEM((max(DEEP), cols, depth), jnp.int32),
            pltpu.SemaphoreType.DMA((6,)),
        ],
        compiler_params=params(56),
        cost_estimate=COST,
        name="first_rows",
    )(own, solid)


def first_columns_kernel(own, solid, even, odd):
    for start, out in zip(side_starts(own.shape[2]), (even, odd)):
        window = pl.ds(start, 2 * WIDE)
        for comp in range(2):
            out[comp] = jnp.where(solid[:, window] == 0, own[comp, :, window], 0.0)


def first_columns(own, solid):
    _, rows, _, depth = own.shape
    side = shape(2, rows, 2 * WIDE, depth)
    return pl.pallas_call(
        first_columns_kernel,
        out_shape=(side, side),
        in_specs=in_vmem(2),
        out_specs=tuple(in_vmem(2)),
        compiler_params=params(8),
        cost_estimate=COST,
        name="first_columns",
    )(own, solid)


def sides_kernel(after, value, even, odd, sems):
    copies = []
    for i, (start, out) in enumerate(zip(side_starts(value.shape[1]), (even, odd))):
        copies.append(pltpu.make_async_copy(value.at[:, pl.ds(start, 2 * WIDE)], out, sems.at[i]))
    for copy in copies:
        copy.start()
    for copy in copies:
        copy.wait()


def sides_pack(after, value):
    count, _, depth = value.shape
    side = shape(count, 2 * WIDE, depth)
    return pl.pallas_call(
        sides_kernel,
        out_shape=(side, side),
        in_specs=[pl.BlockSpec(memory_space=pl.ANY)] * 2,
        out_specs=tuple(in_vmem(2)),
        scratch_shapes=[pltpu.SemaphoreType.DMA((2,))],
        compiler_params=params(4),
        cost_estimate=COST,
        name="sides_pack",
    )(after, value)


def columns_kernel(top, bottom, even, odd):
    half, cols = top.shape[1:3]
    for start, out in zip(side_starts(cols), (even, odd)):
        out[:, :half] = top[:, :, pl.ds(start, 2 * WIDE)]
        out[:, half:] = bottom[:, :, pl.ds(start, 2 * WIDE)]


def columns_pack(top, bottom):
    _, half, _, depth = top.shape
    side = shape(2, 2 * half, 2 * WIDE, depth)
    return pl.pallas_call(
        columns_kernel,
        out_shape=(side, side),
        in_specs=in_vmem(2),
        out_specs=tuple(in_vmem(2)),
        compiler_params=params(8),
        cost_estimate=COST,
        name="columns_pack",
    )(top, bottom)


def copy_kernel(after, value, out):
    out[...] = value[...]


def copy_after(after, value):
    return pl.pallas_call(
        copy_kernel,
        out_shape=shape(*value.shape),
        in_specs=[pl.BlockSpec(memory_space=pl.ANY)] + in_vmem(1),
        out_specs=in_vmem(1)[0],
        compiler_params=params(6),
        cost_estimate=COST,
        name="copy_after",
    )(after, value)


def add_partners(sums, axis, first, end):
    count = lax.axis_size(axis)
    for bit in range(first, end):
        sums = sums + lax.ppermute(sums, axis, [(i, i ^ (1 << bit)) for i in range(count)])
    return sums


def spread_kernel(one, two, out):
    total = (one[...] + two[...]).sum(axis=1)
    out[...] = jnp.broadcast_to(total[None], out.shape)


def total_over_all(one, two):
    devices = lax.axis_size(AXES)
    copies = pl.pallas_call(
        spread_kernel,
        out_shape=shape(devices, 2, one.shape[2]),
        in_specs=in_vmem(2),
        out_specs=in_vmem(1)[0],
        compiler_params=params(4),
        cost_estimate=COST,
        name="spread",
    )(one, two)
    return lax.all_to_all(copies, AXES, 0, 0, tiled=True)


def last_kernel(total_cells, scales, loadings, totals, own, solid, old_top, old_bottom, top, bottom, out, ready, sems):
    half = top.shape[1]
    copies = []
    for comp in range(2):
        total = jnp.sum(totals[:, comp], keepdims=True)
        factor = DAMPING * loadings[comp] * total_cells / total
        for i, (old, new) in enumerate(((old_top, top), (old_bottom, bottom))):
            part = slice(i * half, (i + 1) * half)
            start = jnp.where(solid[part] == 0, own[comp, part], 0.0)
            kept = (1.0 - DAMPING) * blend(start, old[comp], scales[comp])
            ready[comp, part] = kept + factor[None] * new[comp]
            copies.append(pltpu.make_async_copy(ready.at[comp, part], out.at[comp, part], sems.at[2 * comp + i]))
            copies[-1].start()
    for copy in copies:
        copy.wait()


def last_update(total_cells, scalars, blocks):
    own = blocks[1]
    return pl.pallas_call(
        functools.partial(last_kernel, total_cells),
        out_shape=shape(*own.shape),
        in_specs=[pl.BlockSpec(memory_space=pltpu.SMEM)] * len(scalars) + in_vmem(len(blocks)),
        out_specs=pl.BlockSpec(memory_space=pl.ANY),
        scratch_shapes=[pltpu.VMEM(own.shape, F32), pltpu.SemaphoreType.DMA((4,))],
        compiler_params=params(4),
        cost_estimate=COST,
        name="last_update",
    )(*scalars, *blocks)


def bits(axis):
    count = lax.axis_size(axis)
    assert count & (count - 1) == 0
    return count.bit_length() - 1


def body(density_init, solid_mask, loadings):
    rows, cols, depth = solid_mask.shape
    total_cells = float(rows * lax.axis_size("gx") * cols * lax.axis_size("gy") * depth)
    table = jnp.asarray(packed_tables(cols, depth)[0])

    def scale_of(sums):
        return DAMPING * loadings * total_cells / sums.sum(axis=tuple(range(sums.ndim))[1:])

    above = shift(first_rows(density_init, solid_mask), "gx", 1)
    columns = swap_columns(*first_columns(density_init, solid_mask))
    near, far, upper = mid(False, [density_init, solid_mask, *columns], table)
    below = shift(copy_after(above, upper), "gx", -1)
    to_sides = sides_pack(far, above)
    top_sides = swap_columns(*to_sides)
    (y2,) = rest(False, to_sides[0], [near], table)
    top, top_sums, upper = edge(True, False, False, [], [above, *top_sides, near, far, y2, solid_mask], table)
    below_new = shift(upper, "gx", -1)
    bottom_sides = swap_columns(*sides_pack(top_sums, below))
    bottom, bottom_sums, lower = edge(False, False, False, [], [below, *bottom_sides, near, far, y2, solid_mask], table)
    old = [density_init, solid_mask, top, bottom]
    columns = swap_columns(*columns_pack(top, bottom))
    sums = add_partners(top_sums + bottom_sums, "gy", 0, bits("gy"))
    sides_new = swap_columns(*sides_pack(sums, below_new))
    sums = add_partners(copy_after(below_new, sums), "gx", 0, 1)
    above_new = shift(copy_after(sums, lower), "gx", 1)
    near_new, far_new = mid(True, [top, bottom, *columns], table)
    scale = scale_of(add_partners(sums, "gx", 1, bits("gx")))
    y2, near, far = rest(True, scale, [near, far, near_new, far_new], table)
    common = [near, far, y2, solid_mask]
    bottom, bottom_sums = edge(False, True, True, [scale], [below, *bottom_sides, below_new, *sides_new, *common], table)
    sides_new = swap_columns(*sides_pack(y2, above_new))
    top, top_sums = edge(True, True, True, [scale], [above, *top_sides, above_new, *sides_new, *common], table)
    totals = total_over_all(top_sums, bottom_sums)
    return last_update(total_cells, [scale, loadings], [totals, *old, top, bottom])


def solution(mesh):
    in_specs = (P(None, "gx", "gy", None), P("gx", "gy", None), P())
    out_specs = P(None, "gx", "gy", None)
    return jax.shard_map(body, mesh=mesh, in_specs=in_specs, out_specs=out_specs, check_vma=False)
```

```python
import functools

import jax
import jax.numpy as jnp
import ml_dtypes
import numpy as np
from jax import lax
from jax.experimental import pallas as pl
from jax.experimental.pallas import tpu as pltpu
from jax.sharding import PartitionSpec as P

ITERS = 2
SEGMENTS = (1.5131, 1.0)
RADII = (6.0, 8.0)
CROSS = 0.25
DAMPING = 0.3
ATTRACT = ((0.3, 0.22), (0.22, 0.16))
REACH = (5, 7)
FAR = 8
DERIV = REACH[1]
DEEP = tuple(DERIV + r for r in REACH)
WIDE = 8
AXES = ("gx", "gy")
BF16 = jnp.bfloat16
F32 = jnp.float32


def raw_profile(kind, radius):
    offset = np.arange(17) - 8.0
    if kind == 0:
        return np.maximum(radius * radius - offset * offset, 0.0)
    if kind == 1:
        return offset * offset * np.maximum(radius * radius - offset * offset, 0.0)
    return np.exp(-np.abs(offset) / 4.0)


def split_bf16(table):
    high = table.astype(np.float32).astype(ml_dtypes.bfloat16)
    low = (table - high.astype(np.float64)).astype(np.float32).astype(ml_dtypes.bfloat16)
    return high, low


def column_band(kind, radius, count, columns, first):
    band = np.zeros((count, columns))
    for o in range(count):
        band[o, first + o : first + o + 17] = raw_profile(kind, radius)
    return band


def depth_band(kind, radius, depth):
    taps = raw_profile(kind, radius)
    band = np.zeros((depth, depth))
    for column in range(depth):
        for offset in range(17):
            source = column + offset - 8
            if 0 <= source < depth:
                band[source, column] = taps[offset]
    return band


def stage1_tables(comp, cols):
    wide = cols + 2 * WIDE
    pack = column_band(0, RADII[comp], wide, wide + 16, 0)
    rest = np.concatenate(
        [column_band(1, RADII[comp], wide, wide + 16, 0), column_band(2, 0.0, cols, wide + 16, WIDE)]
    )
    high, low = split_bf16(np.concatenate([pack, rest]))
    return {f"first{comp}": np.concatenate([high, high], axis=1), f"rest{comp}": low[wide:]}


def stage2_table(kind, cols):
    high, low = split_bf16(np.concatenate([column_band(kind, r, cols, cols + 16, 0) for r in RADII]))
    return np.concatenate([high, high] if kind == 0 else [high, high, low], axis=1)


def depth_table(kinds, depth):
    high, low = split_bf16(np.concatenate([depth_band(kind, radius, depth) for kind, radius in kinds]))
    return np.concatenate([high, low], axis=1)


def attraction_tables(depth):
    band = depth_band(2, 0.0, depth)
    high, low = split_bf16(-np.concatenate([np.concatenate([ATTRACT[i][j] * band for i in range(2)], axis=1) for j in range(2)]))
    return {"pull_high": high, "pull_low": low}


@functools.lru_cache
def packed_tables(cols, depth):
    tables = {**stage1_tables(0, cols), **stage1_tables(1, cols), **attraction_tables(depth)}
    tables |= {f"depth{kind}": depth_table([(kind, r) for r in RADII], depth) for kind in range(2)}
    tables |= {f"last{comp}": depth_table([(0, r), (1, r)], depth) for comp, r in enumerate(RADII)}
    tables |= {f"second{kind}": stage2_table(kind, cols) for kind in range(2)}
    width = max(t.shape[1] for t in tables.values())
    places, start = {}, 0
    for name, table in tables.items():
        places[name] = (start, *table.shape)
        start += table.shape[0]
    whole = np.zeros((start, width), ml_dtypes.bfloat16)
    for name, table in tables.items():
        whole[places[name][0] : places[name][0] + table.shape[0], : table.shape[1]] = table
    return whole, places


class Tables:
    def __init__(self, ref, cols, depth):
        self.ref, self.places = ref, packed_tables(cols, depth)[1]

    def __getitem__(self, name):
        start, rows, columns = self.places[name]
        return self.ref[start : start + rows, :columns]


def row_taps(kind, radius, scale):
    taps = raw_profile(kind, radius)
    return [float(v) for v in taps * (scale / taps.sum() ** 3)]


def split(field):
    high = field.astype(BF16)
    return high, (field - high.astype(F32)).astype(BF16)


def smooth_rows(values, taps, count, reach):
    out = []
    for i in range(count):
        total = None
        for k in range(reach + 1):
            if taps[8 + k] == 0.0:
                continue
            pair = values[i + reach] if k == 0 else values[i + reach - k] + values[i + reach + k]
            term = taps[8 + k] * pair
            total = term if total is None else total + term
        out.append(total)
    return out


def smooth_rows_exp(values, scale, count):
    q = float(np.exp(-0.25))
    q9 = q**9
    up = values[0]
    for j in range(1, 9):
        up = up * q + values[j]
    ups = [up]
    for i in range(1, count):
        up = up * q + (values[i + 8] - q9 * values[i - 1])
        ups.append(up)
    down = values[count + 15]
    for j in range(1, 8):
        down = down * q + values[count + 15 - j]
    down = down * q
    out = [None] * count
    out[count - 1] = scale * (ups[count - 1] + down)
    for i in range(count - 2, -1, -1):
        down = down * q + (q * values[i + 9] - q9 * values[i + 17])
        out[i] = scale * (ups[i] + down)
    return out


def split_dot(pair, table):
    high, low = split(pair)
    width = table.shape[1] // 2
    both = jnp.dot(high, table, preferred_element_type=F32)
    rest = jnp.dot(low, table[:, :width], preferred_element_type=F32)
    return both[:, :width] + both[:, width:] + rest


def stage1_columns(load, pairs, comp, tables, near, far, cols, unroll, begin):
    wide = cols + 2 * WIDE

    @pl.loop(0, pairs, unroll=unroll)
    def _(i):
        high, low = split(jnp.concatenate([load(2 * i), load(2 * i + 1)], axis=1))
        first = jnp.dot(tables[f"first{comp}"], jnp.concatenate([high, low], axis=0), preferred_element_type=F32)
        rest = first[wide:] + jnp.dot(tables[f"rest{comp}"], high, preferred_element_type=F32)
        depth = high.shape[1] // 2
        for j in range(2):
            lanes = slice(j * depth, (j + 1) * depth)
            row = begin + 2 * i + j
            near[2 * comp, row] = first[:wide, lanes]
            near[2 * comp + 1, row] = rest[:wide, lanes]
            far[comp, row] = rest[wide:, lanes]


def stage1_rows(load, first, count, out):
    wide = out.shape[2]

    @pl.loop(0, wide // 8)
    def _(t):
        window = pl.ds(pl.multiple_of(t * 8, 8), 8)
        for comp in range(2):
            reach = REACH[comp]
            for kind in range(2):
                field = 2 * comp + kind
                taps = row_taps(kind, RADII[comp], SEGMENTS[comp] if kind == 0 else 1.0)
                values = [load(field, row, window) for row in range(first - reach, first + count + reach)]
                for i, value in enumerate(smooth_rows(values, taps, count, reach)):
                    out[field, i, window, :] = value


def stage1_depth(xs, count, step, tables, deriv, place, gates):
    wide, depth = xs.shape[2:]
    for i, start in enumerate(range(0, count, step)):
        rows = slice(start, start + step)
        pair = lambda p: jnp.concatenate([xs[q, rows].reshape(step * wide, depth) for q in (p, p + 2)], axis=1)
        n3 = split_dot(pair(0), tables["depth0"])
        n2 = split_dot(pair(1), tables["depth1"])
        one = 1.0 + n3
        two = (jnp.log(one) + 2.0 * CROSS * n2 * one).reshape(step, wide, depth)
        three = (n2 / one + CROSS * n2 * n2).reshape(step, wide, depth)
        for which, value in enumerate((two, three)):
            if gates[i] is not None:
                value = value * place[gates[i]].astype(F32)
            deriv[which, rows, :WIDE] = value[:, :WIDE] * place[2].astype(F32)
            deriv[which, rows, WIDE : wide - WIDE] = value[:, WIDE : wide - WIDE]
            deriv[which, rows, wide - WIDE :] = value[:, wide - WIDE :] * place[3].astype(F32)


def stage2_columns(deriv, count, tables, out, unroll):
    cols = out.shape[2]

    @pl.loop(0, count // 2, unroll=unroll)
    def _(i):
        for which, kind in ((0, 1), (1, 0)):
            high, low = split(jnp.concatenate([deriv[which, 2 * i], deriv[which, 2 * i + 1]], axis=1))
            stacked = [high, low, high] if which == 0 else [high, low]
            result = jnp.dot(tables[f"second{kind}"], jnp.concatenate(stacked, axis=0), preferred_element_type=F32)
            depth = high.shape[1] // 2
            for comp in range(2):
                for j in range(2):
                    out[2 * which + comp, 2 * i + j] = result[comp * cols : (comp + 1) * cols, j * depth : (j + 1) * depth]


def position():
    flags = []
    for axis in AXES:
        index = lax.axis_index(axis)
        flags += [(index > 0).astype(jnp.int32), (index + 1 < lax.axis_size(axis)).astype(jnp.int32)]
    return flags + [lax.rem(lax.axis_index("gy"), 2)]


def blend(first, second, scale):
    return first if scale is None else (1.0 - DAMPING) * first + scale * second


def side_rows(pair, index, odd):
    one, two = pair[0][index], pair[1][index]
    return jnp.where(odd, one, two), jnp.where(odd, two, one)


def mid_kernel(later, *refs):
    own, solid, *refs = refs
    sides, table_ref, near, far, refs = refs[:2], *refs[2:5], refs[5:]
    rows, cols, depth = far.shape[1:]
    tables = Tables(table_ref, cols, depth)
    odd = position()[4] == 1
    if not later:
        (upper,) = refs
        base = 0
        for comp in range(2):
            part = slice(0, DEEP[comp])
            upper[base : base + DEEP[comp]] = jnp.where(solid[part] == 0, own[comp, part], 0.0)
            base += DEEP[comp]
    parts = ((0, own), (rows // 2, solid)) if later else ((0, own),)
    for comp in range(2):
        for begin, ref in parts:

            def load(row):
                left, right = side_rows(sides, (comp, begin + row), odd)
                value = ref[comp, row] if later else jnp.where(solid[row] == 0, ref[comp, row], 0.0)
                return jnp.concatenate([left, value, right], axis=0)

            count = rows // len(parts) // 2
            stage1_columns(load, count, comp, tables, near, far, cols, count, begin)


def rest_kernel(later, *refs):
    if later:
        scales, near_old, far_old, near_new, far_new, table_ref, y2, near, far, xs, deriv = refs
        for old, new, out in ((near_old, near_new, near), (far_old, far_new, far)):
            fields, rows = out.shape[:2]

            @pl.loop(0, rows)
            def _(row):
                for field in range(fields):
                    out[field, row] = blend(old[field, row], new[field, row], scales[2 * field // fields])
    else:
        after, near, table_ref, y2, xs, deriv = refs
    count, cols, depth = y2.shape[1:]
    tables, place = Tables(table_ref, cols, depth), position()
    stage1_rows(lambda field, row, window: near[field, row, window, :], DERIV, count, xs)
    stage1_depth(xs, count, count // 3, tables, deriv, place, [None] * 3)
    stage2_columns(deriv, count, tables, y2, count // 2)


def edge_kernel(top, later, last, *refs):
    if later:
        scales, halo, *refs = refs
        sides, halo_new, sides_new, refs = refs[:2], refs[2], refs[3:5], refs[5:]
    else:
        halo, *refs = refs
        sides, refs = refs[:2], refs[2:]
    near, far, y2, solid, table_ref, proposal, sums, *refs = refs
    if not last:
        packed, *refs = refs
    near_h, far_h, xs, deriv, y2_h, xm, xa = refs
    _, rows, cols, depth = far.shape
    half = rows // 2
    tables = Tables(table_ref, cols, depth)
    place = position()
    odd = place[4] == 1
    for comp in range(2):
        base = 0 if comp == 0 else DEEP[0]
        scale = scales[comp] if later else None

        def load(row):
            value = halo[base + row]
            left, right = side_rows(sides, base + row, odd)
            if later:
                value = blend(value, halo_new[base + row], scale)
                left_new, right_new = side_rows(sides_new, base + row, odd)
                left, right = blend(left, left_new, scale), blend(right, right_new, scale)
            return jnp.concatenate([left, value, right], axis=0)

        stage1_columns(load, DEEP[comp] // 2, comp, tables, near_h, far_h, cols, DEEP[comp] // 2, 0)

    def pick(own, edge, index, row, window):
        comp = index // 2 if own is near else index
        if 0 <= row < rows:
            return own[index, row, window, :]
        return edge[index, row + DEEP[comp] if top else row - rows, window, :]

    first = -DERIV if top else rows - DERIV
    stage1_rows(lambda f, row, window: pick(near, near_h, f, row, window), first, 2 * DERIV, xs)
    gates = [0, None] if top else [None, 1]
    stage1_depth(xs, 2 * DERIV, DERIV, tables, deriv, place, gates)
    stage2_columns(deriv, 2 * DERIV, tables, y2_h, 7)

    start = 0 if top else half

    @pl.loop(0, cols // 8)
    def _(t):
        window = pl.ds(pl.multiple_of(t * 8, 8), 8)

        def second(index, row):
            if DERIV <= row < rows - DERIV:
                return y2[index, row - DERIV, window, :]
            return y2_h[index, row - first, window, :]

        for which, kind in ((0, 1), (1, 0)):
            for comp in range(2):
                reach = REACH[comp]
                taps = row_taps(kind, RADII[comp], SEGMENTS[comp] if kind == 0 else 1.0)
                values = [second(2 * which + comp, row) for row in range(start - reach, start + half + reach)]
                for i, value in enumerate(smooth_rows(values, taps, half, reach)):
                    xm[2 * which + comp, i, window, :] = value
        scale = row_taps(2, 0.0, 1.0)[8]
        for comp in range(2):
            values = [pick(far, far_h, comp, row, window) for row in range(start - FAR, start + half + FAR)]
            for i, value in enumerate(smooth_rows_exp(values, scale, half)):
                xa[comp, i, window, :] = value

    sums[...] = jnp.zeros_like(sums)
    step = half // 2
    for i in range(0, half, step):
        part = slice(i, i + step)
        flat = lambda ref, p: ref[p, part].reshape(step * cols, depth)
        pore = solid[start + i : start + i + step].reshape(step * cols, depth) == 0
        high, low = split(jnp.concatenate([flat(xa, 0), flat(xa, 1)], axis=1))
        pull = jnp.dot(high, tables["pull_high"], preferred_element_type=F32)
        pull += jnp.dot(high, tables["pull_low"], preferred_element_type=F32)
        pull += jnp.dot(low, tables["pull_high"], preferred_element_type=F32)
        for comp in range(2):
            mu = split_dot(jnp.concatenate([flat(xm, 2 + comp), flat(xm, comp)], axis=1), tables[f"last{comp}"])
            mu = mu + pull[:, comp * depth : (comp + 1) * depth]
            value = jnp.where(pore, jnp.exp(-mu), 0.0)
            proposal[comp, part] = value.reshape(step, cols, depth)
            sums[comp] += value.reshape(step * cols // 8, 8, depth).sum(0)
    if not last:
        base = 0
        for comp in range(2):
            part = slice(0, DEEP[comp]) if top else slice(half - DEEP[comp], half)
            packed[base : base + DEEP[comp]] = proposal[comp, part]
            base += DEEP[comp]


def in_vmem(count):
    return [pl.BlockSpec(memory_space=pltpu.VMEM)] * count


def params(mebibytes):
    return pltpu.CompilerParams(vmem_limit_bytes=mebibytes * 1024 * 1024)


def shape(*sizes):
    return jax.ShapeDtypeStruct(sizes, F32)


COST = pl.CostEstimate(flops=1000, bytes_accessed=1000, transcendentals=0)


def derivative_scratch(count, wide, depth):
    return [pltpu.VMEM((4, count, wide, depth), F32), pltpu.VMEM((2, count, wide, depth), F32)]


def mid(later, blocks, table):
    _, rows, _, depth = blocks[2].shape
    cols = blocks[0].shape[2]
    outs = [shape(4, rows, cols + 2 * WIDE, depth), shape(2, rows, cols, depth)]
    if not later:
        outs += [shape(sum(DEEP), cols, depth)]
    return pl.pallas_call(
        functools.partial(mid_kernel, later),
        out_shape=tuple(outs),
        in_specs=in_vmem(len(blocks) + 1),
        out_specs=tuple(in_vmem(len(outs))),
        compiler_params=params(6),
        cost_estimate=COST,
        name="mid",
    )(*blocks, table)


def rest(later, first, blocks, table):
    _, rows, wide, depth = blocks[0].shape
    count, cols = rows - 2 * DERIV, wide - 2 * WIDE
    outs = [shape(4, count, cols, depth)]
    if later:
        outs += [shape(*block.shape) for block in blocks[:2]]
    return pl.pallas_call(
        functools.partial(rest_kernel, later),
        out_shape=tuple(outs),
        in_specs=[pl.BlockSpec(memory_space=pltpu.SMEM if later else pl.ANY)] + in_vmem(len(blocks) + 1),
        out_specs=tuple(in_vmem(len(outs))),
        scratch_shapes=[pltpu.VMEM((4, count, wide, depth), F32), pltpu.VMEM((2, count, wide, depth), F32)],
        compiler_params=params(8),
        cost_estimate=COST,
        name="rest",
    )(first, *blocks, table)


def edge(top, later, last, scalars, blocks, table):
    rows, cols, depth = blocks[-1].shape
    wide, half = cols + 2 * WIDE, rows // 2
    f32 = lambda *s: pltpu.VMEM(s, F32)
    outs = [shape(2, half, cols, depth), shape(2, 8, depth)]
    if not last:
        outs.append(shape(sum(DEEP), cols, depth))
    return pl.pallas_call(
        functools.partial(edge_kernel, top, later, last),
        out_shape=tuple(outs),
        in_specs=[pl.BlockSpec(memory_space=pltpu.SMEM)] * len(scalars) + in_vmem(len(blocks) + 1),
        out_specs=tuple(in_vmem(len(outs))),
        scratch_shapes=[
            f32(4, DEEP[1], wide, depth),
            f32(2, DEEP[1], cols, depth),
            f32(4, 2 * DERIV, wide, depth),
            f32(2, 2 * DERIV, wide, depth),
            f32(4, 2 * DERIV, cols, depth),
            f32(4, half, cols, depth),
            f32(2, half, cols, depth),
        ],
        compiler_params=params(16),
        cost_estimate=COST,
        name="edge_top" if top else "edge_bottom",
    )(*scalars, *blocks, table)


def shift(value, axis, step):
    count = lax.axis_size(axis)
    return lax.ppermute(value, axis, [(i, i + step) for i in range(count) if 0 <= i + step < count])


def swap_columns(even, odd):
    count = lax.axis_size("gy")
    pairs = lambda first: [p for i in range(first, count - 1, 2) for p in ((i, i + 1), (i + 1, i))]
    return lax.ppermute(even, "gy", pairs(0)), lax.ppermute(odd, "gy", pairs(1))


def side_starts(cols):
    right, left = cols - 2 * WIDE, 0
    odd = position()[4]
    return pl.multiple_of(right * (1 - odd), 8), pl.multiple_of(right * odd, 8)


def first_rows_kernel(own, solid, out, density, mask, sems):
    rows = own.shape[1]
    most = max(DEEP)
    half = most // 2
    copies = []
    for part, begin in enumerate((0, half)):
        source, target = pl.ds(rows - most + begin, half), pl.ds(begin, half)
        copies.append(pltpu.make_async_copy(solid.at[source], mask.at[target], sems.at[part]))
        for comp in range(2):
            copies.append(pltpu.make_async_copy(own.at[comp, source], density.at[comp, target], sems.at[2 + 2 * part + comp]))
    for copy in copies:
        copy.start()
    for copy in copies:
        copy.wait()
    base = 0
    for comp in range(2):
        out[base : base + DEEP[comp]] = jnp.where(mask[most - DEEP[comp] :] == 0, density[comp, most - DEEP[comp] :], 0.0)
        base += DEEP[comp]


def first_rows(own, solid):
    _, _, cols, depth = own.shape
    return pl.pallas_call(
        first_rows_kernel,
        out_shape=shape(sum(DEEP), cols, depth),
        in_specs=[pl.BlockSpec(memory_space=pl.ANY)] * 2,
        out_specs=in_vmem(1)[0],
        scratch_shapes=[
            pltpu.VMEM((2, max(DEEP), cols, depth), F32),
            pltpu.VMEM((max(DEEP), cols, depth), jnp.int32),
            pltpu.SemaphoreType.DMA((6,)),
        ],
        compiler_params=params(56),
        cost_estimate=COST,
        name="first_rows",
    )(own, solid)


def first_columns_kernel(own, solid, even, odd):
    for start, out in zip(side_starts(own.shape[2]), (even, odd)):
        window = pl.ds(start, 2 * WIDE)
        for comp in range(2):
            out[comp] = jnp.where(solid[:, window] == 0, own[comp, :, window], 0.0)


def first_columns(own, solid):
    _, rows, _, depth = own.shape
    side = shape(2, rows, 2 * WIDE, depth)
    return pl.pallas_call(
        first_columns_kernel,
        out_shape=(side, side),
        in_specs=in_vmem(2),
        out_specs=tuple(in_vmem(2)),
        compiler_params=params(8),
        cost_estimate=COST,
        name="first_columns",
    )(own, solid)


def sides_kernel(after, value, even, odd, sems):
    copies = []
    for i, (start, out) in enumerate(zip(side_starts(value.shape[1]), (even, odd))):
        copies.append(pltpu.make_async_copy(value.at[:, pl.ds(start, 2 * WIDE)], out, sems.at[i]))
    for copy in copies:
        copy.start()
    for copy in copies:
        copy.wait()


def sides_pack(after, value):
    count, _, depth = value.shape
    side = shape(count, 2 * WIDE, depth)
    return pl.pallas_call(
        sides_kernel,
        out_shape=(side, side),
        in_specs=[pl.BlockSpec(memory_space=pl.ANY)] * 2,
        out_specs=tuple(in_vmem(2)),
        scratch_shapes=[pltpu.SemaphoreType.DMA((2,))],
        compiler_params=params(4),
        cost_estimate=COST,
        name="sides_pack",
    )(after, value)


def columns_kernel(top, bottom, even, odd):
    half, cols = top.shape[1:3]
    for start, out in zip(side_starts(cols), (even, odd)):
        out[:, :half] = top[:, :, pl.ds(start, 2 * WIDE)]
        out[:, half:] = bottom[:, :, pl.ds(start, 2 * WIDE)]


def columns_pack(top, bottom):
    _, half, _, depth = top.shape
    side = shape(2, 2 * half, 2 * WIDE, depth)
    return pl.pallas_call(
        columns_kernel,
        out_shape=(side, side),
        in_specs=in_vmem(2),
        out_specs=tuple(in_vmem(2)),
        compiler_params=params(8),
        cost_estimate=COST,
        name="columns_pack",
    )(top, bottom)


def copy_kernel(after, value, out):
    out[...] = value[...]


def copy_after(after, value):
    return pl.pallas_call(
        copy_kernel,
        out_shape=shape(*value.shape),
        in_specs=[pl.BlockSpec(memory_space=pl.ANY)] + in_vmem(1),
        out_specs=in_vmem(1)[0],
        compiler_params=params(6),
        cost_estimate=COST,
        name="copy_after",
    )(after, value)


def add_partners(sums, axis, first, end):
    count = lax.axis_size(axis)
    for bit in range(first, end):
        sums = sums + lax.ppermute(sums, axis, [(i, i ^ (1 << bit)) for i in range(count)])
    return sums


def spread_kernel(one, two, out):
    total = (one[...] + two[...]).sum(axis=1)
    out[...] = jnp.broadcast_to(total[None], out.shape)


def total_over_all(one, two):
    devices = lax.axis_size(AXES)
    copies = pl.pallas_call(
        spread_kernel,
        out_shape=shape(devices, 2, one.shape[2]),
        in_specs=in_vmem(2),
        out_specs=in_vmem(1)[0],
        compiler_params=params(4),
        cost_estimate=COST,
        name="spread",
    )(one, two)
    return lax.all_to_all(copies, AXES, 0, 0, tiled=True)


def last_kernel(total_cells, scales, loadings, totals, own, solid, old_top, old_bottom, top, bottom, out, ready, sems):
    half = top.shape[1]
    copies = []
    for comp in range(2):
        total = jnp.sum(totals[:, comp], keepdims=True)
        factor = DAMPING * loadings[comp] * total_cells / total
        for i, (old, new) in enumerate(((old_top, top), (old_bottom, bottom))):
            part = slice(i * half, (i + 1) * half)
            start = jnp.where(solid[part] == 0, own[comp, part], 0.0)
            kept = (1.0 - DAMPING) * blend(start, old[comp], scales[comp])
            ready[comp, part] = kept + factor[None] * new[comp]
            copies.append(pltpu.make_async_copy(ready.at[comp, part], out.at[comp, part], sems.at[2 * comp + i]))
            copies[-1].start()
    for copy in copies:
        copy.wait()


def last_update(total_cells, scalars, blocks):
    own = blocks[1]
    return pl.pallas_call(
        functools.partial(last_kernel, total_cells),
        out_shape=shape(*own.shape),
        in_specs=[pl.BlockSpec(memory_space=pltpu.SMEM)] * len(scalars) + in_vmem(len(blocks)),
        out_specs=pl.BlockSpec(memory_space=pl.ANY),
        scratch_shapes=[pltpu.VMEM(own.shape, F32), pltpu.SemaphoreType.DMA((4,))],
        compiler_params=params(4),
        cost_estimate=COST,
        name="last_update",
    )(*scalars, *blocks)


def bits(axis):
    count = lax.axis_size(axis)
    assert count & (count - 1) == 0
    return count.bit_length() - 1


def body(density_init, solid_mask, loadings):
    rows, cols, depth = solid_mask.shape
    total_cells = float(rows * lax.axis_size("gx") * cols * lax.axis_size("gy") * depth)
    table = jnp.asarray(packed_tables(cols, depth)[0])

    def scale_of(sums):
        return DAMPING * loadings * total_cells / sums.sum(axis=tuple(range(sums.ndim))[1:])

    above = shift(first_rows(density_init, solid_mask), "gx", 1)
    columns = swap_columns(*first_columns(density_init, solid_mask))
    near, far, upper = mid(False, [density_init, solid_mask, *columns], table)
    below = shift(copy_after(above, upper), "gx", -1)
    to_sides = sides_pack(far, above)
    top_sides = swap_columns(*to_sides)
    (y2,) = rest(False, to_sides[0], [near], table)
    top, top_sums, upper = edge(True, False, False, [], [above, *top_sides, near, far, y2, solid_mask], table)
    below_new = shift(upper, "gx", -1)
    bottom_sides = swap_columns(*sides_pack(top_sums, below))
    bottom, bottom_sums, lower = edge(False, False, False, [], [below, *bottom_sides, near, far, y2, solid_mask], table)
    old = [density_init, solid_mask, top, bottom]
    columns = swap_columns(*columns_pack(top, bottom))
    sums = add_partners(top_sums + bottom_sums, "gy", 0, bits("gy"))
    sides_new = swap_columns(*sides_pack(sums, below_new))
    sums = add_partners(copy_after(below_new, sums), "gx", 0, bits("gx"))
    above_new = shift(copy_after(sums, lower), "gx", 1)
    near_new, far_new = mid(True, [top, bottom, *columns], table)
    scale = scale_of(sums)
    y2, near, far = rest(True, scale, [near, far, near_new, far_new], table)
    common = [near, far, y2, solid_mask]
    bottom, bottom_sums = edge(False, True, True, [scale], [below, *bottom_sides, below_new, *sides_new, *common], table)
    sides_new = swap_columns(*sides_pack(y2, above_new))
    top, top_sums = edge(True, True, True, [scale], [above, *top_sides, above_new, *sides_new, *common], table)
    totals = total_over_all(top_sums, bottom_sums)
    return last_update(total_cells, [scale, loadings], [totals, *old, top, bottom])


def solution(mesh):
    in_specs = (P(None, "gx", "gy", None), P("gx", "gy", None), P())
    out_specs = P(None, "gx", "gy", None)
    return jax.shard_map(body, mesh=mesh, in_specs=in_specs, out_specs=out_specs, check_vma=False)
```

```python
import functools

import jax
import jax.numpy as jnp
import ml_dtypes
import numpy as np
from jax import lax
from jax.experimental import pallas as pl
from jax.experimental.pallas import tpu as pltpu
from jax.sharding import PartitionSpec as P

ITERS = 2
SEGMENTS = (1.5131, 1.0)
RADII = (6.0, 8.0)
CROSS = 0.25
DAMPING = 0.3
ATTRACT = ((0.3, 0.22), (0.22, 0.16))
REACH = (5, 7)
FAR = 8
DERIV = REACH[1]
DEEP = tuple(DERIV + r for r in REACH)
WIDE = 8
AXES = ("gx", "gy")
BF16 = jnp.bfloat16
F32 = jnp.float32


def raw_profile(kind, radius):
    offset = np.arange(17) - 8.0
    if kind == 0:
        return np.maximum(radius * radius - offset * offset, 0.0)
    if kind == 1:
        return offset * offset * np.maximum(radius * radius - offset * offset, 0.0)
    return np.exp(-np.abs(offset) / 4.0)


def split_bf16(table):
    high = table.astype(np.float32).astype(ml_dtypes.bfloat16)
    low = (table - high.astype(np.float64)).astype(np.float32).astype(ml_dtypes.bfloat16)
    return high, low


def column_band(kind, radius, count, columns, first):
    band = np.zeros((count, columns))
    for o in range(count):
        band[o, first + o : first + o + 17] = raw_profile(kind, radius)
    return band


def depth_band(kind, radius, depth):
    taps = raw_profile(kind, radius)
    band = np.zeros((depth, depth))
    for column in range(depth):
        for offset in range(17):
            source = column + offset - 8
            if 0 <= source < depth:
                band[source, column] = taps[offset]
    return band


def stage1_tables(comp, cols):
    wide = cols + 2 * WIDE
    pack = column_band(0, RADII[comp], wide, wide + 16, 0)
    rest = np.concatenate(
        [column_band(1, RADII[comp], wide, wide + 16, 0), column_band(2, 0.0, cols, wide + 16, WIDE)]
    )
    high, low = split_bf16(np.concatenate([pack, rest]))
    return {f"first{comp}": np.concatenate([high, high], axis=1), f"rest{comp}": low[wide:]}


def stage2_table(kind, cols):
    high, low = split_bf16(np.concatenate([column_band(kind, r, cols, cols + 16, 0) for r in RADII]))
    return np.concatenate([high, high] if kind == 0 else [high, high, low], axis=1)


def depth_table(kinds, depth):
    high, low = split_bf16(np.concatenate([depth_band(kind, radius, depth) for kind, radius in kinds]))
    return np.concatenate([high, low], axis=1)


def attraction_tables(depth):
    band = depth_band(2, 0.0, depth)
    high, low = split_bf16(-np.concatenate([np.concatenate([ATTRACT[i][j] * band for i in range(2)], axis=1) for j in range(2)]))
    return {"pull_high": high, "pull_low": low}


@functools.lru_cache
def packed_tables(cols, depth):
    tables = {**stage1_tables(0, cols), **stage1_tables(1, cols), **attraction_tables(depth)}
    tables |= {f"depth{kind}": depth_table([(kind, r) for r in RADII], depth) for kind in range(2)}
    tables |= {f"last{comp}": depth_table([(0, r), (1, r)], depth) for comp, r in enumerate(RADII)}
    tables |= {f"second{kind}": stage2_table(kind, cols) for kind in range(2)}
    width = max(t.shape[1] for t in tables.values())
    places, start = {}, 0
    for name, table in tables.items():
        places[name] = (start, *table.shape)
        start += table.shape[0]
    whole = np.zeros((start, width), ml_dtypes.bfloat16)
    for name, table in tables.items():
        whole[places[name][0] : places[name][0] + table.shape[0], : table.shape[1]] = table
    return whole, places


class Tables:
    def __init__(self, ref, cols, depth):
        self.ref, self.places = ref, packed_tables(cols, depth)[1]

    def __getitem__(self, name):
        start, rows, columns = self.places[name]
        return self.ref[start : start + rows, :columns]


def row_taps(kind, radius, scale):
    taps = raw_profile(kind, radius)
    return [float(v) for v in taps * (scale / taps.sum() ** 3)]


def split(field):
    high = field.astype(BF16)
    return high, (field - high.astype(F32)).astype(BF16)


def smooth_rows(values, taps, count, reach):
    out = []
    for i in range(count):
        total = None
        for k in range(reach + 1):
            if taps[8 + k] == 0.0:
                continue
            pair = values[i + reach] if k == 0 else values[i + reach - k] + values[i + reach + k]
            term = taps[8 + k] * pair
            total = term if total is None else total + term
        out.append(total)
    return out


def smooth_rows_exp(values, scale, count):
    q = float(np.exp(-0.25))
    q9 = q**9
    up = values[0]
    for j in range(1, 9):
        up = up * q + values[j]
    ups = [up]
    for i in range(1, count):
        up = up * q + (values[i + 8] - q9 * values[i - 1])
        ups.append(up)
    down = values[count + 15]
    for j in range(1, 8):
        down = down * q + values[count + 15 - j]
    down = down * q
    out = [None] * count
    out[count - 1] = scale * (ups[count - 1] + down)
    for i in range(count - 2, -1, -1):
        down = down * q + (q * values[i + 9] - q9 * values[i + 17])
        out[i] = scale * (ups[i] + down)
    return out


def split_dot(pair, table):
    high, low = split(pair)
    width = table.shape[1] // 2
    both = jnp.dot(high, table, preferred_element_type=F32)
    rest = jnp.dot(low, table[:, :width], preferred_element_type=F32)
    return both[:, :width] + both[:, width:] + rest


def stage1_columns(load, pairs, comp, tables, near, far, cols, unroll, begin):
    wide = cols + 2 * WIDE

    @pl.loop(0, pairs, unroll=unroll)
    def _(i):
        high, low = split(jnp.concatenate([load(2 * i), load(2 * i + 1)], axis=1))
        first = jnp.dot(tables[f"first{comp}"], jnp.concatenate([high, low], axis=0), preferred_element_type=F32)
        rest = first[wide:] + jnp.dot(tables[f"rest{comp}"], high, preferred_element_type=F32)
        depth = high.shape[1] // 2
        for j in range(2):
            lanes = slice(j * depth, (j + 1) * depth)
            row = begin + 2 * i + j
            near[2 * comp, row] = first[:wide, lanes]
            near[2 * comp + 1, row] = rest[:wide, lanes]
            far[comp, row] = rest[wide:, lanes]


def stage1_rows(load, first, count, out):
    wide = out.shape[2]

    @pl.loop(0, wide // 8)
    def _(t):
        window = pl.ds(pl.multiple_of(t * 8, 8), 8)
        for comp in range(2):
            reach = REACH[comp]
            for kind in range(2):
                field = 2 * comp + kind
                taps = row_taps(kind, RADII[comp], SEGMENTS[comp] if kind == 0 else 1.0)
                values = [load(field, row, window) for row in range(first - reach, first + count + reach)]
                for i, value in enumerate(smooth_rows(values, taps, count, reach)):
                    out[field, i, window, :] = value


def stage1_depth(xs, count, step, tables, deriv, place, gates):
    wide, depth = xs.shape[2:]
    for i, start in enumerate(range(0, count, step)):
        rows = slice(start, start + step)
        pair = lambda p: jnp.concatenate([xs[q, rows].reshape(step * wide, depth) for q in (p, p + 2)], axis=1)
        n3 = split_dot(pair(0), tables["depth0"])
        n2 = split_dot(pair(1), tables["depth1"])
        one = 1.0 + n3
        two = (jnp.log(one) + 2.0 * CROSS * n2 * one).reshape(step, wide, depth)
        three = (n2 / one + CROSS * n2 * n2).reshape(step, wide, depth)
        for which, value in enumerate((two, three)):
            if gates[i] is not None:
                value = value * place[gates[i]].astype(F32)
            deriv[which, rows, :WIDE] = value[:, :WIDE] * place[2].astype(F32)
            deriv[which, rows, WIDE : wide - WIDE] = value[:, WIDE : wide - WIDE]
            deriv[which, rows, wide - WIDE :] = value[:, wide - WIDE :] * place[3].astype(F32)


def stage2_columns(deriv, count, tables, out, unroll):
    cols = out.shape[2]

    @pl.loop(0, count // 2, unroll=unroll)
    def _(i):
        for which, kind in ((0, 1), (1, 0)):
            high, low = split(jnp.concatenate([deriv[which, 2 * i], deriv[which, 2 * i + 1]], axis=1))
            stacked = [high, low, high] if which == 0 else [high, low]
            result = jnp.dot(tables[f"second{kind}"], jnp.concatenate(stacked, axis=0), preferred_element_type=F32)
            depth = high.shape[1] // 2
            for comp in range(2):
                for j in range(2):
                    out[2 * which + comp, 2 * i + j] = result[comp * cols : (comp + 1) * cols, j * depth : (j + 1) * depth]


def position():
    flags = []
    for axis in AXES:
        index = lax.axis_index(axis)
        flags += [(index > 0).astype(jnp.int32), (index + 1 < lax.axis_size(axis)).astype(jnp.int32)]
    return flags + [lax.rem(lax.axis_index("gy"), 2)]


def blend(first, second, scale):
    return first if scale is None else (1.0 - DAMPING) * first + scale * second


def side_rows(pair, index, odd):
    one, two = pair[0][index], pair[1][index]
    return jnp.where(odd, one, two), jnp.where(odd, two, one)


def mid_kernel(later, own, *refs):
    if later:
        sides, table_ref, near, far = refs[:2], *refs[2:]
    else:
        solid, *sides, table_ref, near, far, upper = refs
        base = 0
        for comp in range(2):
            part = slice(0, DEEP[comp])
            upper[base : base + DEEP[comp]] = jnp.where(solid[part] == 0, own[comp, part], 0.0)
            base += DEEP[comp]
    rows, cols, depth = far.shape[1:]
    tables = Tables(table_ref, cols, depth)
    odd = position()[4] == 1
    for comp in range(2):

        def load(row):
            left, right = side_rows(sides, (comp, row), odd)
            value = own[comp, row] if later else jnp.where(solid[row] == 0, own[comp, row], 0.0)
            return jnp.concatenate([left, value, right], axis=0)

        stage1_columns(load, rows // 2, comp, tables, near, far, cols, rows // 2, 0)


def rest_kernel(later, *refs):
    if later:
        scales, near_old, far_old, near_top, far_top, near_bottom, far_bottom, table_ref, y2, near, far, xs, deriv = refs
        half = near_top.shape[1]
        for old, halves, out in ((near_old, (near_top, near_bottom), near), (far_old, (far_top, far_bottom), far)):
            fields = out.shape[0]

            @pl.loop(0, half)
            def _(row):
                for field in range(fields):
                    for i, new in enumerate(halves):
                        at = row + i * half
                        out[field, at] = blend(old[field, at], new[field, row], scales[2 * field // fields])
    else:
        after, near, table_ref, y2, xs, deriv = refs
    count, cols, depth = y2.shape[1:]
    tables, place = Tables(table_ref, cols, depth), position()
    stage1_rows(lambda field, row, window: near[field, row, window, :], DERIV, count, xs)
    stage1_depth(xs, count, count // 3, tables, deriv, place, [None] * 3)
    stage2_columns(deriv, count, tables, y2, count // 2)


def edge_kernel(top, later, last, *refs):
    if later:
        scales, after, halo, *refs = refs
        sides, halo_new, sides_new, refs = refs[:2], refs[2], refs[3:5], refs[5:]
    else:
        after, halo, *refs = refs
        sides, refs = refs[:2], refs[2:]
    near, far, y2, solid, table_ref, proposal, sums, *refs = refs
    if not last:
        packed, *refs = refs
    near_h, far_h, xs, deriv, y2_h, xm, xa = refs
    _, rows, cols, depth = far.shape
    half = rows // 2
    tables = Tables(table_ref, cols, depth)
    place = position()
    odd = place[4] == 1
    for comp in range(2):
        base = 0 if comp == 0 else DEEP[0]
        scale = scales[comp] if later else None

        def load(row):
            value = halo[base + row]
            left, right = side_rows(sides, base + row, odd)
            if later:
                value = blend(value, halo_new[base + row], scale)
                left_new, right_new = side_rows(sides_new, base + row, odd)
                left, right = blend(left, left_new, scale), blend(right, right_new, scale)
            return jnp.concatenate([left, value, right], axis=0)

        stage1_columns(load, DEEP[comp] // 2, comp, tables, near_h, far_h, cols, DEEP[comp] // 2, 0)

    def pick(own, edge, index, row, window):
        comp = index // 2 if own is near else index
        if 0 <= row < rows:
            return own[index, row, window, :]
        return edge[index, row + DEEP[comp] if top else row - rows, window, :]

    first = -DERIV if top else rows - DERIV
    stage1_rows(lambda f, row, window: pick(near, near_h, f, row, window), first, 2 * DERIV, xs)
    gates = [0, None] if top else [None, 1]
    stage1_depth(xs, 2 * DERIV, DERIV, tables, deriv, place, gates)
    stage2_columns(deriv, 2 * DERIV, tables, y2_h, 7)

    start = 0 if top else half

    @pl.loop(0, cols // 8)
    def _(t):
        window = pl.ds(pl.multiple_of(t * 8, 8), 8)

        def second(index, row):
            if DERIV <= row < rows - DERIV:
                return y2[index, row - DERIV, window, :]
            return y2_h[index, row - first, window, :]

        for which, kind in ((0, 1), (1, 0)):
            for comp in range(2):
                reach = REACH[comp]
                taps = row_taps(kind, RADII[comp], SEGMENTS[comp] if kind == 0 else 1.0)
                values = [second(2 * which + comp, row) for row in range(start - reach, start + half + reach)]
                for i, value in enumerate(smooth_rows(values, taps, half, reach)):
                    xm[2 * which + comp, i, window, :] = value
        scale = row_taps(2, 0.0, 1.0)[8]
        for comp in range(2):
            values = [pick(far, far_h, comp, row, window) for row in range(start - FAR, start + half + FAR)]
            for i, value in enumerate(smooth_rows_exp(values, scale, half)):
                xa[comp, i, window, :] = value

    sums[...] = jnp.zeros_like(sums)
    step = half // 2
    for i in range(0, half, step):
        part = slice(i, i + step)
        flat = lambda ref, p: ref[p, part].reshape(step * cols, depth)
        pore = solid[start + i : start + i + step].reshape(step * cols, depth) == 0
        high, low = split(jnp.concatenate([flat(xa, 0), flat(xa, 1)], axis=1))
        pull = jnp.dot(high, tables["pull_high"], preferred_element_type=F32)
        pull += jnp.dot(high, tables["pull_low"], preferred_element_type=F32)
        pull += jnp.dot(low, tables["pull_high"], preferred_element_type=F32)
        for comp in range(2):
            mu = split_dot(jnp.concatenate([flat(xm, 2 + comp), flat(xm, comp)], axis=1), tables[f"last{comp}"])
            mu = mu + pull[:, comp * depth : (comp + 1) * depth]
            value = jnp.where(pore, jnp.exp(-mu), 0.0)
            proposal[comp, part] = value.reshape(step, cols, depth)
            sums[comp] += value.reshape(step * cols // 8, 8, depth).sum(0)
    if not last:
        base = 0
        for comp in range(2):
            part = slice(0, DEEP[comp]) if top else slice(half - DEEP[comp], half)
            packed[base : base + DEEP[comp]] = proposal[comp, part]
            base += DEEP[comp]


def in_vmem(count):
    return [pl.BlockSpec(memory_space=pltpu.VMEM)] * count


def params(mebibytes):
    return pltpu.CompilerParams(vmem_limit_bytes=mebibytes * 1024 * 1024)


def shape(*sizes):
    return jax.ShapeDtypeStruct(sizes, F32)


COST = pl.CostEstimate(flops=1000, bytes_accessed=1000, transcendentals=0)


def derivative_scratch(count, wide, depth):
    return [pltpu.VMEM((4, count, wide, depth), F32), pltpu.VMEM((2, count, wide, depth), F32)]


def mid(later, blocks, table):
    _, rows, cols, depth = blocks[0].shape
    outs = [shape(4, rows, cols + 2 * WIDE, depth), shape(2, rows, cols, depth)]
    if not later:
        outs += [shape(sum(DEEP), cols, depth)]
    return pl.pallas_call(
        functools.partial(mid_kernel, later),
        out_shape=tuple(outs),
        in_specs=in_vmem(len(blocks) + 1),
        out_specs=tuple(in_vmem(len(outs))),
        compiler_params=params(6),
        cost_estimate=COST,
        name="mid",
    )(*blocks, table)


def rest(later, first, blocks, table):
    _, rows, wide, depth = blocks[0].shape
    count, cols = rows - 2 * DERIV, wide - 2 * WIDE
    outs = [shape(4, count, cols, depth)]
    if later:
        outs += [shape(*block.shape) for block in blocks[:2]]
    return pl.pallas_call(
        functools.partial(rest_kernel, later),
        out_shape=tuple(outs),
        in_specs=[pl.BlockSpec(memory_space=pltpu.SMEM if later else pl.ANY)] + in_vmem(len(blocks) + 1),
        out_specs=tuple(in_vmem(len(outs))),
        scratch_shapes=[pltpu.VMEM((4, count, wide, depth), F32), pltpu.VMEM((2, count, wide, depth), F32)],
        compiler_params=params(8),
        cost_estimate=COST,
        name="rest",
    )(first, *blocks, table)


def edge(top, later, last, scalars, after, blocks, table):
    rows, cols, depth = blocks[-1].shape
    wide, half = cols + 2 * WIDE, rows // 2
    f32 = lambda *s: pltpu.VMEM(s, F32)
    outs = [shape(2, half, cols, depth), shape(2, 8, depth)]
    if not last:
        outs.append(shape(sum(DEEP), cols, depth))
    return pl.pallas_call(
        functools.partial(edge_kernel, top, later, last),
        out_shape=tuple(outs),
        in_specs=[pl.BlockSpec(memory_space=pltpu.SMEM)] * len(scalars) + [pl.BlockSpec(memory_space=pl.ANY)] + in_vmem(len(blocks) + 1),
        out_specs=tuple(in_vmem(len(outs))),
        scratch_shapes=[
            f32(4, DEEP[1], wide, depth),
            f32(2, DEEP[1], cols, depth),
            f32(4, 2 * DERIV, wide, depth),
            f32(2, 2 * DERIV, wide, depth),
            f32(4, 2 * DERIV, cols, depth),
            f32(4, half, cols, depth),
            f32(2, half, cols, depth),
        ],
        compiler_params=params(16),
        cost_estimate=COST,
        name="edge_top" if top else "edge_bottom",
    )(*scalars, after, *blocks, table)


def shift(value, axis, step):
    count = lax.axis_size(axis)
    return lax.ppermute(value, axis, [(i, i + step) for i in range(count) if 0 <= i + step < count])


def swap_columns(even, odd):
    count = lax.axis_size("gy")
    pairs = lambda first: [p for i in range(first, count - 1, 2) for p in ((i, i + 1), (i + 1, i))]
    return lax.ppermute(even, "gy", pairs(0)), lax.ppermute(odd, "gy", pairs(1))


def side_starts(cols):
    right, left = cols - 2 * WIDE, 0
    odd = position()[4]
    return pl.multiple_of(right * (1 - odd), 8), pl.multiple_of(right * odd, 8)


def first_rows_kernel(own, solid, out, density, mask, sems):
    rows = own.shape[1]
    most = max(DEEP)
    half = most // 2
    copies = []
    for part, begin in enumerate((0, half)):
        source, target = pl.ds(rows - most + begin, half), pl.ds(begin, half)
        copies.append(pltpu.make_async_copy(solid.at[source], mask.at[target], sems.at[part]))
        for comp in range(2):
            copies.append(pltpu.make_async_copy(own.at[comp, source], density.at[comp, target], sems.at[2 + 2 * part + comp]))
    for copy in copies:
        copy.start()
    for copy in copies:
        copy.wait()
    base = 0
    for comp in range(2):
        out[base : base + DEEP[comp]] = jnp.where(mask[most - DEEP[comp] :] == 0, density[comp, most - DEEP[comp] :], 0.0)
        base += DEEP[comp]


def first_rows(own, solid):
    _, _, cols, depth = own.shape
    return pl.pallas_call(
        first_rows_kernel,
        out_shape=shape(sum(DEEP), cols, depth),
        in_specs=[pl.BlockSpec(memory_space=pl.ANY)] * 2,
        out_specs=in_vmem(1)[0],
        scratch_shapes=[
            pltpu.VMEM((2, max(DEEP), cols, depth), F32),
            pltpu.VMEM((max(DEEP), cols, depth), jnp.int32),
            pltpu.SemaphoreType.DMA((6,)),
        ],
        compiler_params=params(56),
        cost_estimate=COST,
        name="first_rows",
    )(own, solid)


def first_columns_kernel(own, solid, even, odd):
    for start, out in zip(side_starts(own.shape[2]), (even, odd)):
        window = pl.ds(start, 2 * WIDE)
        for comp in range(2):
            out[comp] = jnp.where(solid[:, window] == 0, own[comp, :, window], 0.0)


def first_columns(own, solid):
    _, rows, _, depth = own.shape
    side = shape(2, rows, 2 * WIDE, depth)
    return pl.pallas_call(
        first_columns_kernel,
        out_shape=(side, side),
        in_specs=in_vmem(2),
        out_specs=tuple(in_vmem(2)),
        compiler_params=params(8),
        cost_estimate=COST,
        name="first_columns",
    )(own, solid)


def sides_kernel(after, value, even, odd, sems):
    copies = []
    for i, (start, out) in enumerate(zip(side_starts(value.shape[1]), (even, odd))):
        copies.append(pltpu.make_async_copy(value.at[:, pl.ds(start, 2 * WIDE)], out, sems.at[i]))
    for copy in copies:
        copy.start()
    for copy in copies:
        copy.wait()


def sides_pack(after, value):
    count, _, depth = value.shape
    side = shape(count, 2 * WIDE, depth)
    return pl.pallas_call(
        sides_kernel,
        out_shape=(side, side),
        in_specs=[pl.BlockSpec(memory_space=pl.ANY)] * 2,
        out_specs=tuple(in_vmem(2)),
        scratch_shapes=[pltpu.SemaphoreType.DMA((2,))],
        compiler_params=params(4),
        cost_estimate=COST,
        name="sides_pack",
    )(after, value)


def columns_kernel(value, even, odd):
    for start, out in zip(side_starts(value.shape[2]), (even, odd)):
        out[...] = value[:, :, pl.ds(start, 2 * WIDE)]


def columns_pack(value):
    _, count, _, depth = value.shape
    side = shape(2, count, 2 * WIDE, depth)
    return pl.pallas_call(
        columns_kernel,
        out_shape=(side, side),
        in_specs=in_vmem(1),
        out_specs=tuple(in_vmem(2)),
        compiler_params=params(8),
        cost_estimate=COST,
        name="columns_pack",
    )(value)


def ready_kernel(after, value, out):
    pass


def ready_after(after, value):
    return pl.pallas_call(
        ready_kernel,
        out_shape=shape(*value.shape),
        in_specs=[pl.BlockSpec(memory_space=pl.ANY)] * 2,
        out_specs=pl.BlockSpec(memory_space=pl.ANY),
        input_output_aliases={1: 0},
        compiler_params=params(2),
        cost_estimate=COST,
        name="ready_after",
    )(after, value)


def add_partners(sums, axis, first, end):
    count = lax.axis_size(axis)
    for bit in range(first, end):
        sums = sums + lax.ppermute(sums, axis, [(i, i ^ (1 << bit)) for i in range(count)])
    return sums


def spread_kernel(one, two, out):
    total = (one[...] + two[...]).sum(axis=1)
    out[...] = jnp.broadcast_to(total[None], out.shape)


def total_over_all(one, two):
    devices = lax.axis_size(AXES)
    copies = pl.pallas_call(
        spread_kernel,
        out_shape=shape(devices, 2, one.shape[2]),
        in_specs=in_vmem(2),
        out_specs=in_vmem(1)[0],
        compiler_params=params(4),
        cost_estimate=COST,
        name="spread",
    )(one, two)
    return lax.all_to_all(copies, AXES, 0, 0, tiled=True)


def last_kernel(total_cells, scales, loadings, totals, own, solid, old_top, old_bottom, top, bottom, out, ready, sems):
    half = top.shape[1]
    copies = []
    for comp in range(2):
        total = jnp.sum(totals[:, comp], keepdims=True)
        factor = DAMPING * loadings[comp] * total_cells / total
        for i, (old, new) in enumerate(((old_top, top), (old_bottom, bottom))):
            part = slice(i * half, (i + 1) * half)
            start = jnp.where(solid[part] == 0, own[comp, part], 0.0)
            kept = (1.0 - DAMPING) * blend(start, old[comp], scales[comp])
            ready[comp, part] = kept + factor[None] * new[comp]
            copies.append(pltpu.make_async_copy(ready.at[comp, part], out.at[comp, part], sems.at[2 * comp + i]))
            copies[-1].start()
    for copy in copies:
        copy.wait()


def last_update(total_cells, scalars, blocks):
    own = blocks[1]
    return pl.pallas_call(
        functools.partial(last_kernel, total_cells),
        out_shape=shape(*own.shape),
        in_specs=[pl.BlockSpec(memory_space=pltpu.SMEM)] * len(scalars) + in_vmem(len(blocks)),
        out_specs=pl.BlockSpec(memory_space=pl.ANY),
        scratch_shapes=[pltpu.VMEM(own.shape, F32), pltpu.SemaphoreType.DMA((4,))],
        compiler_params=params(4),
        cost_estimate=COST,
        name="last_update",
    )(*scalars, *blocks)


def bits(axis):
    count = lax.axis_size(axis)
    assert count & (count - 1) == 0
    return count.bit_length() - 1


def body(density_init, solid_mask, loadings):
    rows, cols, depth = solid_mask.shape
    total_cells = float(rows * lax.axis_size("gx") * cols * lax.axis_size("gy") * depth)
    table = jnp.asarray(packed_tables(cols, depth)[0])

    def scale_of(sums):
        return DAMPING * loadings * total_cells / sums.sum(axis=tuple(range(sums.ndim))[1:])

    above = shift(first_rows(density_init, solid_mask), "gx", 1)
    columns = swap_columns(*first_columns(density_init, solid_mask))
    near, far, upper = mid(False, [density_init, solid_mask, *columns], table)
    below = shift(ready_after(above, upper), "gx", -1)
    to_sides = sides_pack(far, above)
    top_sides = swap_columns(*to_sides)
    (y2,) = rest(False, to_sides[0], [near], table)
    top, top_sums, upper = edge(True, False, False, [], y2, [above, *top_sides, near, far, y2, solid_mask], table)
    below_new = shift(upper, "gx", -1)
    top_columns = swap_columns(*columns_pack(top))
    bottom_sides = swap_columns(*sides_pack(top_sums, below))
    near_top, far_top = mid(True, [top, *top_columns], table)
    blocks = [below, *bottom_sides, near, far, y2, solid_mask]
    bottom, bottom_sums, lower = edge(False, False, False, [], far_top, blocks, table)
    old = [density_init, solid_mask, top, bottom]
    sums = add_partners(top_sums + bottom_sums, "gy", 0, bits("gy"))
    sides_new = swap_columns(*sides_pack(sums, below_new))
    sums = add_partners(ready_after(below_new, sums), "gx", 0, bits("gx"))
    above_new = shift(ready_after(sums, lower), "gx", 1)
    near_bottom, far_bottom = mid(True, [bottom, *swap_columns(*columns_pack(bottom))], table)
    scale = scale_of(sums)
    y2, near, far = rest(True, scale, [near, far, near_top, far_top, near_bottom, far_bottom], table)
    common = [near, far, y2, solid_mask]
    bottom, bottom_sums = edge(False, True, True, [scale], y2, [below, *bottom_sides, below_new, *sides_new, *common], table)
    sides_new = swap_columns(*sides_pack(y2, above_new))
    top, top_sums = edge(True, True, True, [scale], y2, [above, *top_sides, above_new, *sides_new, *common], table)
    totals = total_over_all(top_sums, bottom_sums)
    return last_update(total_cells, [scale, loadings], [totals, *old, top, bottom])


def solution(mesh):
    in_specs = (P(None, "gx", "gy", None), P("gx", "gy", None), P())
    out_specs = P(None, "gx", "gy", None)
    return jax.shard_map(body, mesh=mesh, in_specs=in_specs, out_specs=out_specs, check_vma=False)
```

```python
import functools

import jax
import jax.numpy as jnp
import ml_dtypes
import numpy as np
from jax import lax
from jax.experimental import pallas as pl
from jax.experimental.pallas import tpu as pltpu
from jax.sharding import PartitionSpec as P

ITERS = 2
SEGMENTS = (1.5131, 1.0)
RADII = (6.0, 8.0)
CROSS = 0.25
DAMPING = 0.3
ATTRACT = ((0.3, 0.22), (0.22, 0.16))
REACH = (5, 7)
FAR = 8
DERIV = REACH[1]
DEEP = tuple(DERIV + r for r in REACH)
WIDE = 8
AXES = ("gx", "gy")
BF16 = jnp.bfloat16
F32 = jnp.float32


def raw_profile(kind, radius):
    offset = np.arange(17) - 8.0
    if kind == 0:
        return np.maximum(radius * radius - offset * offset, 0.0)
    if kind == 1:
        return offset * offset * np.maximum(radius * radius - offset * offset, 0.0)
    return np.exp(-np.abs(offset) / 4.0)


def split_bf16(table):
    high = table.astype(np.float32).astype(ml_dtypes.bfloat16)
    low = (table - high.astype(np.float64)).astype(np.float32).astype(ml_dtypes.bfloat16)
    return high, low


def column_band(kind, radius, count, columns, first):
    band = np.zeros((count, columns))
    for o in range(count):
        band[o, first + o : first + o + 17] = raw_profile(kind, radius)
    return band


def depth_band(kind, radius, depth):
    taps = raw_profile(kind, radius)
    band = np.zeros((depth, depth))
    for column in range(depth):
        for offset in range(17):
            source = column + offset - 8
            if 0 <= source < depth:
                band[source, column] = taps[offset]
    return band


def stage1_tables(comp, cols):
    wide = cols + 2 * WIDE
    pack = column_band(0, RADII[comp], wide, wide + 16, 0)
    rest = np.concatenate(
        [column_band(1, RADII[comp], wide, wide + 16, 0), column_band(2, 0.0, cols, wide + 16, WIDE)]
    )
    high, low = split_bf16(np.concatenate([pack, rest]))
    return {f"first{comp}": np.concatenate([high, high], axis=1), f"rest{comp}": low[wide:]}


def stage2_table(kind, cols):
    high, low = split_bf16(np.concatenate([column_band(kind, r, cols, cols + 16, 0) for r in RADII]))
    return np.concatenate([high, high] if kind == 0 else [high, high, low], axis=1)


def depth_table(kinds, depth):
    scale = lambda kind, comp: SEGMENTS[comp] / raw_profile(0, RADII[comp]).sum() ** 3 if kind == 0 else 1.0
    high, low = split_bf16(np.concatenate([scale(kind, c) * depth_band(kind, RADII[c], depth) for kind, c in kinds]))
    return np.concatenate([high, low], axis=1)


def attraction_tables(depth):
    band = depth_band(2, 0.0, depth)
    high, low = split_bf16(-np.concatenate([np.concatenate([ATTRACT[i][j] * band for i in range(2)], axis=1) for j in range(2)]))
    return {"pull_high": high, "pull_low": low}


@functools.lru_cache
def packed_tables(cols, depth):
    tables = {**stage1_tables(0, cols), **stage1_tables(1, cols), **attraction_tables(depth)}
    tables |= {f"depth{kind}": depth_table([(kind, comp) for comp in range(2)], depth) for kind in range(2)}
    tables |= {f"last{comp}": depth_table([(0, comp), (1, comp)], depth) for comp in range(2)}
    tables |= {f"second{kind}": stage2_table(kind, cols) for kind in range(2)}
    width = max(t.shape[1] for t in tables.values())
    places, start = {}, 0
    for name, table in tables.items():
        places[name] = (start, *table.shape)
        start += table.shape[0]
    whole = np.zeros((start, width), ml_dtypes.bfloat16)
    for name, table in tables.items():
        whole[places[name][0] : places[name][0] + table.shape[0], : table.shape[1]] = table
    return whole, places


class Tables:
    def __init__(self, ref, cols, depth):
        self.ref, self.places = ref, packed_tables(cols, depth)[1]

    def __getitem__(self, name):
        start, rows, columns = self.places[name]
        return self.ref[start : start + rows, :columns]


def row_taps(kind, radius, scale):
    taps = raw_profile(kind, radius)
    return [float(v) for v in taps * (scale / taps.sum() ** 3)]


def split(field):
    high = field.astype(BF16)
    return high, (field - high.astype(F32)).astype(BF16)


def smooth_rows(values, taps, count, reach):
    out = []
    for i in range(count):
        total = None
        for k in range(reach + 1):
            if taps[8 + k] == 0.0:
                continue
            pair = values[i + reach] if k == 0 else values[i + reach - k] + values[i + reach + k]
            term = taps[8 + k] * pair
            total = term if total is None else total + term
        out.append(total)
    return out


def smooth_rows_packing(values, radius, count):
    reach = radius - 1
    at = lambda x: values[x + reach]
    taps = raw_profile(0, radius)
    out = smooth_rows(values[: 2 + 2 * reach], [float(v) for v in taps], 2, reach)
    slope = out[1] - out[0]
    box = at(1)
    for j in range(1, radius):
        box = box + (at(1 - j) + at(1 + j))
    for x in range(1, count - 1):
        if x > 1:
            box = box + (at(x + reach) - at(x - radius))
        slope = slope + ((2 * radius - 1.0) * (at(x + radius) + at(x - radius)) - 2.0 * box)
        out.append(out[-1] + slope)
    return out


def smooth_rows_of(kind, comp, values, count):
    if kind == 0:
        return smooth_rows_packing(values, int(RADII[comp]), count)
    return smooth_rows(values, row_taps(kind, RADII[comp], 1.0), count, REACH[comp])


def smooth_rows_exp(values, scale, count):
    q = float(np.exp(-0.25))
    q9 = q**9
    up = values[0]
    for j in range(1, 9):
        up = up * q + values[j]
    ups = [up]
    for i in range(1, count):
        up = up * q + (values[i + 8] - q9 * values[i - 1])
        ups.append(up)
    down = values[count + 15]
    for j in range(1, 8):
        down = down * q + values[count + 15 - j]
    down = down * q
    out = [None] * count
    out[count - 1] = scale * (ups[count - 1] + down)
    for i in range(count - 2, -1, -1):
        down = down * q + (q * values[i + 9] - q9 * values[i + 17])
        out[i] = scale * (ups[i] + down)
    return out


def split_dot(pair, table):
    high, low = split(pair)
    width = table.shape[1] // 2
    both = jnp.dot(high, table, preferred_element_type=F32)
    rest = jnp.dot(low, table[:, :width], preferred_element_type=F32)
    return both[:, :width] + both[:, width:] + rest


def stage1_columns(load, pairs, comp, tables, near, far, cols, unroll, begin):
    wide = cols + 2 * WIDE

    @pl.loop(0, pairs, unroll=unroll)
    def _(i):
        high, low = split(jnp.concatenate([load(2 * i), load(2 * i + 1)], axis=1))
        first = jnp.dot(tables[f"first{comp}"], jnp.concatenate([high, low], axis=0), preferred_element_type=F32)
        rest = first[wide:] + jnp.dot(tables[f"rest{comp}"], high, preferred_element_type=F32)
        depth = high.shape[1] // 2
        for j in range(2):
            lanes = slice(j * depth, (j + 1) * depth)
            row = begin + 2 * i + j
            near[2 * comp, row] = first[:wide, lanes]
            near[2 * comp + 1, row] = rest[:wide, lanes]
            far[comp, row] = rest[wide:, lanes]


def stage1_rows(load, first, count, out):
    wide = out.shape[2]

    @pl.loop(0, wide // 8)
    def _(t):
        window = pl.ds(pl.multiple_of(t * 8, 8), 8)
        for comp in range(2):
            reach = REACH[comp]
            for kind in range(2):
                field = 2 * comp + kind
                values = [load(field, row, window) for row in range(first - reach, first + count + reach)]
                for i, value in enumerate(smooth_rows_of(kind, comp, values, count)):
                    out[field, i, window, :] = value


def stage1_depth(xs, count, step, tables, deriv, place, gates):
    wide, depth = xs.shape[2:]
    for i, start in enumerate(range(0, count, step)):
        rows = slice(start, start + step)
        pair = lambda p: jnp.concatenate([xs[q, rows].reshape(step * wide, depth) for q in (p, p + 2)], axis=1)
        n3 = split_dot(pair(0), tables["depth0"])
        n2 = split_dot(pair(1), tables["depth1"])
        one = 1.0 + n3
        two = (jnp.log(one) + 2.0 * CROSS * n2 * one).reshape(step, wide, depth)
        three = (n2 / one + CROSS * n2 * n2).reshape(step, wide, depth)
        for which, value in enumerate((two, three)):
            if gates[i] is not None:
                value = value * place[gates[i]].astype(F32)
            deriv[which, rows, :WIDE] = value[:, :WIDE] * place[2].astype(F32)
            deriv[which, rows, WIDE : wide - WIDE] = value[:, WIDE : wide - WIDE]
            deriv[which, rows, wide - WIDE :] = value[:, wide - WIDE :] * place[3].astype(F32)


def stage2_columns(deriv, count, tables, out, unroll):
    cols = out.shape[2]

    @pl.loop(0, count // 2, unroll=unroll)
    def _(i):
        for which, kind in ((0, 1), (1, 0)):
            high, low = split(jnp.concatenate([deriv[which, 2 * i], deriv[which, 2 * i + 1]], axis=1))
            stacked = [high, low, high] if which == 0 else [high, low]
            result = jnp.dot(tables[f"second{kind}"], jnp.concatenate(stacked, axis=0), preferred_element_type=F32)
            depth = high.shape[1] // 2
            for comp in range(2):
                for j in range(2):
                    out[2 * which + comp, 2 * i + j] = result[comp * cols : (comp + 1) * cols, j * depth : (j + 1) * depth]


def position():
    flags = []
    for axis in AXES:
        index = lax.axis_index(axis)
        flags += [(index > 0).astype(jnp.int32), (index + 1 < lax.axis_size(axis)).astype(jnp.int32)]
    return flags + [lax.rem(lax.axis_index("gy"), 2)]


def blend(first, second, scale):
    return first if scale is None else (1.0 - DAMPING) * first + scale * second


def side_rows(pair, index, odd):
    one, two = pair[0][index], pair[1][index]
    return jnp.where(odd, one, two), jnp.where(odd, two, one)


def mid_kernel(later, own, *refs):
    if later:
        sides, table_ref, near, far = refs[:2], *refs[2:]
    else:
        solid, *sides, table_ref, near, far, upper = refs
        base = 0
        for comp in range(2):
            part = slice(0, DEEP[comp])
            upper[base : base + DEEP[comp]] = jnp.where(solid[part] == 0, own[comp, part], 0.0)
            base += DEEP[comp]
    rows, cols, depth = far.shape[1:]
    tables = Tables(table_ref, cols, depth)
    odd = position()[4] == 1
    for comp in range(2):

        def load(row):
            index = (comp, row) if len(sides[0].shape) == 4 else sum(DEEP) + comp * rows + row
            left, right = side_rows(sides, index, odd)
            value = own[comp, row] if later else jnp.where(solid[row] == 0, own[comp, row], 0.0)
            return jnp.concatenate([left, value, right], axis=0)

        stage1_columns(load, rows // 2, comp, tables, near, far, cols, rows // 2, 0)


def rest_kernel(later, *refs):
    if later:
        scales, near_old, far_old, near_top, far_top, near_bottom, far_bottom, table_ref, y2, near, far, xs, deriv = refs
        half = near_top.shape[1]
        for old, halves, out in ((near_old, (near_top, near_bottom), near), (far_old, (far_top, far_bottom), far)):
            fields = out.shape[0]

            @pl.loop(0, half)
            def _(row):
                for field in range(fields):
                    for i, new in enumerate(halves):
                        at = row + i * half
                        out[field, at] = blend(old[field, at], new[field, row], scales[2 * field // fields])
    else:
        after, near, table_ref, y2, xs, deriv = refs
    count, cols, depth = y2.shape[1:]
    tables, place = Tables(table_ref, cols, depth), position()
    stage1_rows(lambda field, row, window: near[field, row, window, :], DERIV, count, xs)
    stage1_depth(xs, count, count // 3, tables, deriv, place, [None] * 3)
    stage2_columns(deriv, count, tables, y2, count // 2)


def edge_kernel(top, later, last, *refs):
    if later:
        scales, after, halo, *refs = refs
        sides, halo_new, sides_new, refs = refs[:2], refs[2], refs[3:5], refs[5:]
    else:
        after, halo, *refs = refs
        sides, refs = refs[:2], refs[2:]
    near, far, y2, solid, table_ref, proposal, sums, *refs = refs
    if not last:
        packed, *refs = refs
    near_h, far_h, xs, deriv, y2_h, xm, xa = refs
    _, rows, cols, depth = far.shape
    half = rows // 2
    tables = Tables(table_ref, cols, depth)
    place = position()
    odd = place[4] == 1
    for comp in range(2):
        base = 0 if comp == 0 else DEEP[0]
        scale = scales[comp] if later else None

        def load(row):
            value = halo[base + row]
            left, right = side_rows(sides, base + row, odd)
            if later:
                value = blend(value, halo_new[base + row], scale)
                left_new, right_new = side_rows(sides_new, base + row, odd)
                left, right = blend(left, left_new, scale), blend(right, right_new, scale)
            return jnp.concatenate([left, value, right], axis=0)

        stage1_columns(load, DEEP[comp] // 2, comp, tables, near_h, far_h, cols, DEEP[comp] // 2, 0)

    def pick(own, edge, index, row, window):
        comp = index // 2 if own is near else index
        if 0 <= row < rows:
            return own[index, row, window, :]
        return edge[index, row + DEEP[comp] if top else row - rows, window, :]

    first = -DERIV if top else rows - DERIV
    stage1_rows(lambda f, row, window: pick(near, near_h, f, row, window), first, 2 * DERIV, xs)
    gates = [0, None] if top else [None, 1]
    stage1_depth(xs, 2 * DERIV, DERIV, tables, deriv, place, gates)
    stage2_columns(deriv, 2 * DERIV, tables, y2_h, 7)

    start = 0 if top else half

    @pl.loop(0, cols // 8)
    def _(t):
        window = pl.ds(pl.multiple_of(t * 8, 8), 8)

        def second(index, row):
            if DERIV <= row < rows - DERIV:
                return y2[index, row - DERIV, window, :]
            return y2_h[index, row - first, window, :]

        for which, kind in ((0, 1), (1, 0)):
            for comp in range(2):
                reach = REACH[comp]
                values = [second(2 * which + comp, row) for row in range(start - reach, start + half + reach)]
                for i, value in enumerate(smooth_rows_of(kind, comp, values, half)):
                    xm[2 * which + comp, i, window, :] = value
        scale = row_taps(2, 0.0, 1.0)[8]
        for comp in range(2):
            values = [pick(far, far_h, comp, row, window) for row in range(start - FAR, start + half + FAR)]
            for i, value in enumerate(smooth_rows_exp(values, scale, half)):
                xa[comp, i, window, :] = value

    sums[...] = jnp.zeros_like(sums)
    step = half // 2
    for i in range(0, half, step):
        part = slice(i, i + step)
        flat = lambda ref, p: ref[p, part].reshape(step * cols, depth)
        pore = solid[start + i : start + i + step].reshape(step * cols, depth) == 0
        high, low = split(jnp.concatenate([flat(xa, 0), flat(xa, 1)], axis=1))
        pull = jnp.dot(high, tables["pull_high"], preferred_element_type=F32)
        pull += jnp.dot(high, tables["pull_low"], preferred_element_type=F32)
        pull += jnp.dot(low, tables["pull_high"], preferred_element_type=F32)
        for comp in range(2):
            mu = split_dot(jnp.concatenate([flat(xm, 2 + comp), flat(xm, comp)], axis=1), tables[f"last{comp}"])
            mu = mu + pull[:, comp * depth : (comp + 1) * depth]
            value = jnp.where(pore, jnp.exp(-mu), 0.0)
            proposal[comp, part] = value.reshape(step, cols, depth)
            sums[comp] += value.reshape(step * cols // 8, 8, depth).sum(0)
    if not last:
        base = 0
        for comp in range(2):
            part = slice(0, DEEP[comp]) if top else slice(half - DEEP[comp], half)
            packed[base : base + DEEP[comp]] = proposal[comp, part]
            base += DEEP[comp]


def in_vmem(count):
    return [pl.BlockSpec(memory_space=pltpu.VMEM)] * count


def params(mebibytes):
    return pltpu.CompilerParams(vmem_limit_bytes=mebibytes * 1024 * 1024)


def shape(*sizes):
    return jax.ShapeDtypeStruct(sizes, F32)


COST = pl.CostEstimate(flops=1000, bytes_accessed=1000, transcendentals=0)


def derivative_scratch(count, wide, depth):
    return [pltpu.VMEM((4, count, wide, depth), F32), pltpu.VMEM((2, count, wide, depth), F32)]


def mid(later, blocks, table):
    _, rows, cols, depth = blocks[0].shape
    outs = [shape(4, rows, cols + 2 * WIDE, depth), shape(2, rows, cols, depth)]
    if not later:
        outs += [shape(sum(DEEP), cols, depth)]
    return pl.pallas_call(
        functools.partial(mid_kernel, later),
        out_shape=tuple(outs),
        in_specs=in_vmem(len(blocks) + 1),
        out_specs=tuple(in_vmem(len(outs))),
        compiler_params=params(6),
        cost_estimate=COST,
        name="mid",
    )(*blocks, table)


def rest(later, first, blocks, table):
    _, rows, wide, depth = blocks[0].shape
    count, cols = rows - 2 * DERIV, wide - 2 * WIDE
    outs = [shape(4, count, cols, depth)]
    if later:
        outs += [shape(*block.shape) for block in blocks[:2]]
    return pl.pallas_call(
        functools.partial(rest_kernel, later),
        out_shape=tuple(outs),
        in_specs=[pl.BlockSpec(memory_space=pltpu.SMEM if later else pl.ANY)] + in_vmem(len(blocks) + 1),
        out_specs=tuple(in_vmem(len(outs))),
        scratch_shapes=[pltpu.VMEM((4, count, wide, depth), F32), pltpu.VMEM((2, count, wide, depth), F32)],
        compiler_params=params(8),
        cost_estimate=COST,
        name="rest",
    )(first, *blocks, table)


def edge(top, later, last, scalars, after, blocks, table):
    rows, cols, depth = blocks[-1].shape
    wide, half = cols + 2 * WIDE, rows // 2
    f32 = lambda *s: pltpu.VMEM(s, F32)
    outs = [shape(2, half, cols, depth), shape(2, 8, depth)]
    if not last:
        outs.append(shape(sum(DEEP), cols, depth))
    return pl.pallas_call(
        functools.partial(edge_kernel, top, later, last),
        out_shape=tuple(outs),
        in_specs=[pl.BlockSpec(memory_space=pltpu.SMEM)] * len(scalars) + [pl.BlockSpec(memory_space=pl.ANY)] + in_vmem(len(blocks) + 1),
        out_specs=tuple(in_vmem(len(outs))),
        scratch_shapes=[
            f32(4, DEEP[1], wide, depth),
            f32(2, DEEP[1], cols, depth),
            f32(4, 2 * DERIV, wide, depth),
            f32(2, 2 * DERIV, wide, depth),
            f32(4, 2 * DERIV, cols, depth),
            f32(4, half, cols, depth),
            f32(2, half, cols, depth),
        ],
        compiler_params=params(16),
        cost_estimate=COST,
        name="edge_top" if top else "edge_bottom",
    )(*scalars, after, *blocks, table)


def shift(value, axis, step):
    count = lax.axis_size(axis)
    return lax.ppermute(value, axis, [(i, i + step) for i in range(count) if 0 <= i + step < count])


def swap_columns(even, odd):
    count = lax.axis_size("gy")
    pairs = lambda first: [p for i in range(first, count - 1, 2) for p in ((i, i + 1), (i + 1, i))]
    return lax.ppermute(even, "gy", pairs(0)), lax.ppermute(odd, "gy", pairs(1))


def side_starts(cols):
    right, left = cols - 2 * WIDE, 0
    odd = position()[4]
    return pl.multiple_of(right * (1 - odd), 8), pl.multiple_of(right * odd, 8)


def first_rows_kernel(own, solid, out, density, mask, sems):
    rows = own.shape[1]
    most = max(DEEP)
    half = most // 2
    copies = []
    for part, begin in enumerate((0, half)):
        source, target = pl.ds(rows - most + begin, half), pl.ds(begin, half)
        copies.append(pltpu.make_async_copy(solid.at[source], mask.at[target], sems.at[part]))
        for comp in range(2):
            copies.append(pltpu.make_async_copy(own.at[comp, source], density.at[comp, target], sems.at[2 + 2 * part + comp]))
    for copy in copies:
        copy.start()
    for copy in copies:
        copy.wait()
    base = 0
    for comp in range(2):
        out[base : base + DEEP[comp]] = jnp.where(mask[most - DEEP[comp] :] == 0, density[comp, most - DEEP[comp] :], 0.0)
        base += DEEP[comp]


def first_rows(own, solid):
    _, _, cols, depth = own.shape
    return pl.pallas_call(
        first_rows_kernel,
        out_shape=shape(sum(DEEP), cols, depth),
        in_specs=[pl.BlockSpec(memory_space=pl.ANY)] * 2,
        out_specs=in_vmem(1)[0],
        scratch_shapes=[
            pltpu.VMEM((2, max(DEEP), cols, depth), F32),
            pltpu.VMEM((max(DEEP), cols, depth), jnp.int32),
            pltpu.SemaphoreType.DMA((6,)),
        ],
        compiler_params=params(56),
        cost_estimate=COST,
        name="first_rows",
    )(own, solid)


def first_columns_kernel(own, solid, even, odd):
    for start, out in zip(side_starts(own.shape[2]), (even, odd)):
        window = pl.ds(start, 2 * WIDE)
        for comp in range(2):
            out[comp] = jnp.where(solid[:, window] == 0, own[comp, :, window], 0.0)


def first_columns(own, solid):
    _, rows, _, depth = own.shape
    side = shape(2, rows, 2 * WIDE, depth)
    return pl.pallas_call(
        first_columns_kernel,
        out_shape=(side, side),
        in_specs=in_vmem(2),
        out_specs=tuple(in_vmem(2)),
        compiler_params=params(8),
        cost_estimate=COST,
        name="first_columns",
    )(own, solid)


def sides_kernel(after, value, even, odd, sems):
    copies = []
    for i, (start, out) in enumerate(zip(side_starts(value.shape[1]), (even, odd))):
        copies.append(pltpu.make_async_copy(value.at[:, pl.ds(start, 2 * WIDE)], out, sems.at[i]))
    for copy in copies:
        copy.start()
    for copy in copies:
        copy.wait()


def sides_pack(after, value):
    count, _, depth = value.shape
    side = shape(count, 2 * WIDE, depth)
    return pl.pallas_call(
        sides_kernel,
        out_shape=(side, side),
        in_specs=[pl.BlockSpec(memory_space=pl.ANY)] * 2,
        out_specs=tuple(in_vmem(2)),
        scratch_shapes=[pltpu.SemaphoreType.DMA((2,))],
        compiler_params=params(4),
        cost_estimate=COST,
        name="sides_pack",
    )(after, value)


def columns_kernel(value, even, odd):
    for start, out in zip(side_starts(value.shape[2]), (even, odd)):
        out[...] = value[:, :, pl.ds(start, 2 * WIDE)]


def columns_pack(value):
    _, count, _, depth = value.shape
    side = shape(2, count, 2 * WIDE, depth)
    return pl.pallas_call(
        columns_kernel,
        out_shape=(side, side),
        in_specs=in_vmem(1),
        out_specs=tuple(in_vmem(2)),
        compiler_params=params(8),
        cost_estimate=COST,
        name="columns_pack",
    )(value)


def joint_kernel(halo, value, even, odd):
    count, rows = halo.shape[0], value.shape[1]
    for start, out in zip(side_starts(halo.shape[1]), (even, odd)):
        window = pl.ds(start, 2 * WIDE)
        out[:count] = halo[:, window]
        for comp in range(2):
            out[count + comp * rows : count + (comp + 1) * rows] = value[comp, :, window]


def joint_pack(halo, value):
    _, rows, _, depth = value.shape
    side = shape(halo.shape[0] + 2 * rows, 2 * WIDE, depth)
    return pl.pallas_call(
        joint_kernel,
        out_shape=(side, side),
        in_specs=in_vmem(2),
        out_specs=tuple(in_vmem(2)),
        compiler_params=params(6),
        cost_estimate=COST,
        name="joint_pack",
    )(halo, value)


def ready_kernel(after, value, out):
    pass


def ready_after(after, value):
    return pl.pallas_call(
        ready_kernel,
        out_shape=shape(*value.shape),
        in_specs=[pl.BlockSpec(memory_space=pl.ANY)] * 2,
        out_specs=pl.BlockSpec(memory_space=pl.ANY),
        input_output_aliases={1: 0},
        compiler_params=params(2),
        cost_estimate=COST,
        name="ready_after",
    )(after, value)


def add_partners(sums, axis, first, end):
    count = lax.axis_size(axis)
    for bit in range(first, end):
        sums = sums + lax.ppermute(sums, axis, [(i, i ^ (1 << bit)) for i in range(count)])
    return sums


def spread_kernel(one, two, out):
    total = (one[...] + two[...]).sum(axis=1)
    out[...] = jnp.broadcast_to(total[None], out.shape)


def total_over_all(one, two):
    devices = lax.axis_size(AXES)
    copies = pl.pallas_call(
        spread_kernel,
        out_shape=shape(devices, 2, one.shape[2]),
        in_specs=in_vmem(2),
        out_specs=in_vmem(1)[0],
        compiler_params=params(4),
        cost_estimate=COST,
        name="spread",
    )(one, two)
    return lax.all_to_all(copies, AXES, 0, 0, tiled=True)


def last_kernel(total_cells, scales, loadings, totals, own, solid, old_top, old_bottom, top, bottom, out, ready, sems):
    half = top.shape[1]
    copies = []
    for comp in range(2):
        total = jnp.sum(totals[:, comp], keepdims=True)
        factor = DAMPING * loadings[comp] * total_cells / total
        for i, (old, new) in enumerate(((old_top, top), (old_bottom, bottom))):
            part = slice(i * half, (i + 1) * half)
            start = jnp.where(solid[part] == 0, own[comp, part], 0.0)
            kept = (1.0 - DAMPING) * blend(start, old[comp], scales[comp])
            ready[comp, part] = kept + factor[None] * new[comp]
            copies.append(pltpu.make_async_copy(ready.at[comp, part], out.at[comp, part], sems.at[2 * comp + i]))
            copies[-1].start()
    for copy in copies:
        copy.wait()


def last_update(total_cells, scalars, blocks):
    own = blocks[1]
    return pl.pallas_call(
        functools.partial(last_kernel, total_cells),
        out_shape=shape(*own.shape),
        in_specs=[pl.BlockSpec(memory_space=pltpu.SMEM)] * len(scalars) + in_vmem(len(blocks)),
        out_specs=pl.BlockSpec(memory_space=pl.ANY),
        scratch_shapes=[pltpu.VMEM(own.shape, F32), pltpu.SemaphoreType.DMA((4,))],
        compiler_params=params(4),
        cost_estimate=COST,
        name="last_update",
    )(*scalars, *blocks)


def bits(axis):
    count = lax.axis_size(axis)
    assert count & (count - 1) == 0
    return count.bit_length() - 1


def body(density_init, solid_mask, loadings):
    rows, cols, depth = solid_mask.shape
    total_cells = float(rows * lax.axis_size("gx") * cols * lax.axis_size("gy") * depth)
    table = jnp.asarray(packed_tables(cols, depth)[0])

    def scale_of(sums):
        return DAMPING * loadings * total_cells / sums.sum(axis=tuple(range(sums.ndim))[1:])

    above = shift(first_rows(density_init, solid_mask), "gx", 1)
    columns = swap_columns(*first_columns(density_init, solid_mask))
    near, far, upper = mid(False, [density_init, solid_mask, *columns], table)
    below = shift(ready_after(above, upper), "gx", -1)
    to_sides = sides_pack(far, above)
    top_sides = swap_columns(*to_sides)
    (y2,) = rest(False, to_sides[0], [near], table)
    top, top_sums, upper = edge(True, False, False, [], y2, [above, *top_sides, near, far, y2, solid_mask], table)
    below_new = shift(upper, "gx", -1)
    top_columns = swap_columns(*columns_pack(top))
    bottom_sides = swap_columns(*sides_pack(top_sums, below))
    near_top, far_top = mid(True, [top, *top_columns], table)
    blocks = [below, *bottom_sides, near, far, y2, solid_mask]
    bottom, bottom_sums, lower = edge(False, False, False, [], far_top, blocks, table)
    old = [density_init, solid_mask, top, bottom]
    sums = add_partners(top_sums + bottom_sums, "gy", 0, bits("gy"))
    sums = add_partners(ready_after(below_new, sums), "gx", 0, bits("gx"))
    above_new = shift(ready_after(sums, lower), "gx", 1)
    sides_new = swap_columns(*joint_pack(below_new, bottom))
    near_bottom, far_bottom = mid(True, [bottom, *sides_new], table)
    scale = scale_of(sums)
    y2, near, far = rest(True, scale, [near, far, near_top, far_top, near_bottom, far_bottom], table)
    common = [near, far, y2, solid_mask]
    bottom, bottom_sums = edge(False, True, True, [scale], y2, [below, *bottom_sides, below_new, *sides_new, *common], table)
    sides_new = swap_columns(*sides_pack(y2, above_new))
    top, top_sums = edge(True, True, True, [scale], y2, [above, *top_sides, above_new, *sides_new, *common], table)
    totals = total_over_all(top_sums, bottom_sums)
    return last_update(total_cells, [scale, loadings], [totals, *old, top, bottom])


def solution(mesh):
    in_specs = (P(None, "gx", "gy", None), P("gx", "gy", None), P())
    out_specs = P(None, "gx", "gy", None)
    return jax.shard_map(body, mesh=mesh, in_specs=in_specs, out_specs=out_specs, check_vma=False)
```

```python
import functools

import jax
import jax.numpy as jnp
import ml_dtypes
import numpy as np
from jax import lax
from jax.experimental import pallas as pl
from jax.experimental.pallas import tpu as pltpu
from jax.sharding import PartitionSpec as P

ITERS = 2
SEGMENTS = (1.5131, 1.0)
RADII = (6.0, 8.0)
CROSS = 0.25
DAMPING = 0.3
ATTRACT = ((0.3, 0.22), (0.22, 0.16))
REACH = (5, 7)
FAR = 8
DERIV = REACH[1]
DEEP = tuple(DERIV + r for r in REACH)
WIDE = 8
AXES = ("gx", "gy")
BF16 = jnp.bfloat16
F32 = jnp.float32


def raw_profile(kind, radius):
    offset = np.arange(17) - 8.0
    if kind == 0:
        return np.maximum(radius * radius - offset * offset, 0.0)
    if kind == 1:
        return offset * offset * np.maximum(radius * radius - offset * offset, 0.0)
    return np.exp(-np.abs(offset) / 4.0)


def split_bf16(table):
    high = table.astype(np.float32).astype(ml_dtypes.bfloat16)
    low = (table - high.astype(np.float64)).astype(np.float32).astype(ml_dtypes.bfloat16)
    return high, low


def column_band(kind, radius, count, columns, first):
    band = np.zeros((count, columns))
    for o in range(count):
        band[o, first + o : first + o + 17] = raw_profile(kind, radius)
    return band


def depth_band(kind, radius, depth):
    taps = raw_profile(kind, radius)
    band = np.zeros((depth, depth))
    for column in range(depth):
        for offset in range(17):
            source = column + offset - 8
            if 0 <= source < depth:
                band[source, column] = taps[offset]
    return band


def stage1_tables(comp, cols):
    wide = cols + 2 * WIDE
    pack = column_band(0, RADII[comp], wide, wide + 16, 0)
    rest = np.concatenate(
        [column_band(1, RADII[comp], wide, wide + 16, 0), column_band(2, 0.0, cols, wide + 16, WIDE)]
    )
    high, low = split_bf16(np.concatenate([pack, rest]))
    return {f"first{comp}": np.concatenate([high, high], axis=1), f"rest{comp}": low[wide:]}


def stage2_table(kind, cols):
    high, low = split_bf16(np.concatenate([column_band(kind, r, cols, cols + 16, 0) for r in RADII]))
    return np.concatenate([high, high] if kind == 0 else [high, high, low], axis=1)


def depth_table(kinds, depth):
    scale = lambda kind, comp: SEGMENTS[comp] / raw_profile(0, RADII[comp]).sum() ** 3 if kind == 0 else 1.0
    high, low = split_bf16(np.concatenate([scale(kind, c) * depth_band(kind, RADII[c], depth) for kind, c in kinds]))
    return np.concatenate([high, low], axis=1)


def attraction_tables(depth):
    band = depth_band(2, 0.0, depth)
    high, low = split_bf16(-np.concatenate([np.concatenate([ATTRACT[i][j] * band for i in range(2)], axis=1) for j in range(2)]))
    return {"pull_high": high, "pull_low": low}


@functools.lru_cache
def packed_tables(cols, depth):
    tables = {**stage1_tables(0, cols), **stage1_tables(1, cols), **attraction_tables(depth)}
    tables |= {f"depth{kind}": depth_table([(kind, comp) for comp in range(2)], depth) for kind in range(2)}
    tables |= {f"last{comp}": depth_table([(0, comp), (1, comp)], depth) for comp in range(2)}
    tables |= {f"second{kind}": stage2_table(kind, cols) for kind in range(2)}
    width = max(t.shape[1] for t in tables.values())
    places, start = {}, 0
    for name, table in tables.items():
        places[name] = (start, *table.shape)
        start += table.shape[0]
    whole = np.zeros((start, width), ml_dtypes.bfloat16)
    for name, table in tables.items():
        whole[places[name][0] : places[name][0] + table.shape[0], : table.shape[1]] = table
    return whole, places


class Tables:
    def __init__(self, ref, cols, depth):
        self.ref, self.places = ref, packed_tables(cols, depth)[1]

    def __getitem__(self, name):
        start, rows, columns = self.places[name]
        return self.ref[start : start + rows, :columns]


def row_taps(kind, radius, scale):
    taps = raw_profile(kind, radius)
    return [float(v) for v in taps * (scale / taps.sum() ** 3)]


def split(field):
    high = field.astype(BF16)
    return high, (field - high.astype(F32)).astype(BF16)


def smooth_rows(values, taps, count, reach):
    out = []
    for i in range(count):
        total = None
        for k in range(reach + 1):
            if taps[8 + k] == 0.0:
                continue
            pair = values[i + reach] if k == 0 else values[i + reach - k] + values[i + reach + k]
            term = taps[8 + k] * pair
            total = term if total is None else total + term
        out.append(total)
    return out


def smooth_rows_packing(values, radius, count):
    reach = radius - 1
    at = lambda x: values[x + reach]
    taps = raw_profile(0, radius)
    out = smooth_rows(values[: 2 + 2 * reach], [float(v) for v in taps], 2, reach)
    slope = out[1] - out[0]
    box = at(1)
    for j in range(1, radius):
        box = box + (at(1 - j) + at(1 + j))
    for x in range(1, count - 1):
        if x > 1:
            box = box + (at(x + reach) - at(x - radius))
        slope = slope + ((2 * radius - 1.0) * (at(x + radius) + at(x - radius)) - 2.0 * box)
        out.append(out[-1] + slope)
    return out


def smooth_rows_of(kind, comp, values, count):
    if kind == 0:
        return smooth_rows_packing(values, int(RADII[comp]), count)
    return smooth_rows(values, row_taps(kind, RADII[comp], 1.0), count, REACH[comp])


def smooth_rows_exp(values, scale, count):
    q = float(np.exp(-0.25))
    q9 = q**9
    up = values[0]
    for j in range(1, 9):
        up = up * q + values[j]
    ups = [up]
    for i in range(1, count):
        up = up * q + (values[i + 8] - q9 * values[i - 1])
        ups.append(up)
    down = values[count + 15]
    for j in range(1, 8):
        down = down * q + values[count + 15 - j]
    down = down * q
    out = [None] * count
    out[count - 1] = scale * (ups[count - 1] + down)
    for i in range(count - 2, -1, -1):
        down = down * q + (q * values[i + 9] - q9 * values[i + 17])
        out[i] = scale * (ups[i] + down)
    return out


def split_dot(pair, table):
    high, low = split(pair)
    width = table.shape[1] // 2
    both = jnp.dot(high, table, preferred_element_type=F32)
    rest = jnp.dot(low, table[:, :width], preferred_element_type=F32)
    return both[:, :width] + both[:, width:] + rest


def stage1_columns(load, pairs, comp, tables, near, far, cols, unroll, begin):
    wide = cols + 2 * WIDE

    @pl.loop(0, pairs, unroll=unroll)
    def _(i):
        high, low = split(jnp.concatenate([load(2 * i), load(2 * i + 1)], axis=1))
        first = jnp.dot(tables[f"first{comp}"], jnp.concatenate([high, low], axis=0), preferred_element_type=F32)
        rest = first[wide:] + jnp.dot(tables[f"rest{comp}"], high, preferred_element_type=F32)
        depth = high.shape[1] // 2
        for j in range(2):
            lanes = slice(j * depth, (j + 1) * depth)
            row = begin + 2 * i + j
            near[2 * comp, row] = first[:wide, lanes]
            near[2 * comp + 1, row] = rest[:wide, lanes]
            far[comp, row] = rest[wide:, lanes]


def stage1_rows(load, first, count, out):
    wide = out.shape[2]

    @pl.loop(0, wide // 8)
    def _(t):
        window = pl.ds(pl.multiple_of(t * 8, 8), 8)
        for comp in range(2):
            reach = REACH[comp]
            for kind in range(2):
                field = 2 * comp + kind
                values = [load(field, row, window) for row in range(first - reach, first + count + reach)]
                for i, value in enumerate(smooth_rows_of(kind, comp, values, count)):
                    out[field, i, window, :] = value


def stage1_depth(xs, count, step, tables, deriv, place, gates):
    wide, depth = xs.shape[2:]
    for i, start in enumerate(range(0, count, step)):
        rows = slice(start, start + step)
        pair = lambda p: jnp.concatenate([xs[q, rows].reshape(step * wide, depth) for q in (p, p + 2)], axis=1)
        n3 = split_dot(pair(0), tables["depth0"])
        n2 = split_dot(pair(1), tables["depth1"])
        one = 1.0 + n3
        two = (jnp.log(one) + 2.0 * CROSS * n2 * one).reshape(step, wide, depth)
        three = (n2 / one + CROSS * n2 * n2).reshape(step, wide, depth)
        for which, value in enumerate((two, three)):
            if gates[i] is not None:
                value = value * place[gates[i]].astype(F32)
            deriv[which, rows, :WIDE] = value[:, :WIDE] * place[2].astype(F32)
            deriv[which, rows, WIDE : wide - WIDE] = value[:, WIDE : wide - WIDE]
            deriv[which, rows, wide - WIDE :] = value[:, wide - WIDE :] * place[3].astype(F32)


def stage2_columns(deriv, count, tables, out, unroll):
    cols = out.shape[2]

    @pl.loop(0, count // 2, unroll=unroll)
    def _(i):
        for which, kind in ((0, 1), (1, 0)):
            high, low = split(jnp.concatenate([deriv[which, 2 * i], deriv[which, 2 * i + 1]], axis=1))
            stacked = [high, low, high] if which == 0 else [high, low]
            result = jnp.dot(tables[f"second{kind}"], jnp.concatenate(stacked, axis=0), preferred_element_type=F32)
            depth = high.shape[1] // 2
            for comp in range(2):
                for j in range(2):
                    out[2 * which + comp, 2 * i + j] = result[comp * cols : (comp + 1) * cols, j * depth : (j + 1) * depth]


def position():
    flags = []
    for axis in AXES:
        index = lax.axis_index(axis)
        flags += [(index > 0).astype(jnp.int32), (index + 1 < lax.axis_size(axis)).astype(jnp.int32)]
    return flags + [lax.rem(lax.axis_index("gy"), 2)]


def blend(first, second, scale):
    return first if scale is None else (1.0 - DAMPING) * first + scale * second


def pack_rows(strips, middle, base, value):
    cols, width = value.shape[1], 2 * WIDE
    part = slice(base, base + value.shape[0])
    strips[part, :width] = value[:, :width]
    strips[part, width:] = value[:, cols - width :]
    middle[part] = value[:, width : cols - width]


def packed_shapes(cols, depth):
    return [shape(sum(DEEP), 4 * WIDE, depth), shape(sum(DEEP), cols - 4 * WIDE, depth)]


def side_rows(pair, index, odd):
    one, two = pair[0][index], pair[1][index]
    return jnp.where(odd, one, two), jnp.where(odd, two, one)


def mid_kernel(later, own, *refs):
    if later:
        sides, table_ref, near, far = refs[:2], *refs[2:]
    else:
        solid, *sides, table_ref, near, far, upper = refs
        base = 0
        for comp in range(2):
            part = slice(0, DEEP[comp])
            upper[base : base + DEEP[comp]] = jnp.where(solid[part] == 0, own[comp, part], 0.0)
            base += DEEP[comp]
    rows, cols, depth = far.shape[1:]
    tables = Tables(table_ref, cols, depth)
    odd = position()[4] == 1
    for comp in range(2):

        def load(row):
            index = (comp, row) if len(sides[0].shape) == 4 else sum(DEEP) + comp * rows + row
            left, right = side_rows(sides, index, odd)
            value = own[comp, row] if later else jnp.where(solid[row] == 0, own[comp, row], 0.0)
            return jnp.concatenate([left, value, right], axis=0)

        stage1_columns(load, rows // 2, comp, tables, near, far, cols, rows // 2, 0)


def rest_kernel(later, *refs):
    if later:
        scales, near_old, far_old, near_top, far_top, near_bottom, far_bottom, table_ref, y2, near, far, xs, deriv = refs
        half = near_top.shape[1]
        for old, halves, out in ((near_old, (near_top, near_bottom), near), (far_old, (far_top, far_bottom), far)):
            fields = out.shape[0]

            @pl.loop(0, half)
            def _(row):
                for field in range(fields):
                    for i, new in enumerate(halves):
                        at = row + i * half
                        out[field, at] = blend(old[field, at], new[field, row], scales[2 * field // fields])
    else:
        after, near, table_ref, y2, xs, deriv = refs
    count, cols, depth = y2.shape[1:]
    tables, place = Tables(table_ref, cols, depth), position()
    stage1_rows(lambda field, row, window: near[field, row, window, :], DERIV, count, xs)
    stage1_depth(xs, count, count // 3, tables, deriv, place, [None] * 3)
    stage2_columns(deriv, count, tables, y2, count // 2)


def edge_kernel(top, later, last, *refs):
    if later:
        scales, after, *refs = refs
        halo, sides, halo_new, sides_new, refs = refs[:1], refs[1:3], refs[3:5], refs[5:7], refs[7:]
    else:
        after, *refs = refs
        halo, sides, refs = refs[:1], refs[1:3], refs[3:]
    near, far, y2, solid, table_ref, proposal, sums, *refs = refs
    if not last:
        strips, middle, *refs = refs
    near_h, far_h, xs, deriv, y2_h, xm, xa = refs
    _, rows, cols, depth = far.shape
    half = rows // 2
    tables = Tables(table_ref, cols, depth)
    place = position()
    odd = place[4] == 1

    def pieces(rows_in, columns_in, row):
        left, right = side_rows(columns_in, row, odd)
        if len(rows_in) == 1:
            whole = rows_in[0][row]
            return [left, whole[: 2 * WIDE], whole[2 * WIDE : cols - 2 * WIDE], whole[cols - 2 * WIDE :], right]
        outer, inner = rows_in
        return [left, outer[row, : 2 * WIDE], inner[row], outer[row, 2 * WIDE :], right]

    for comp in range(2):
        base = 0 if comp == 0 else DEEP[0]
        scale = scales[comp] if later else None

        def load(row):
            parts = pieces(halo, sides, base + row)
            if later:
                parts = [blend(old, new, scale) for old, new in zip(parts, pieces(halo_new, sides_new, base + row))]
            return jnp.concatenate(parts, axis=0)

        stage1_columns(load, DEEP[comp] // 2, comp, tables, near_h, far_h, cols, DEEP[comp] // 2, 0)

    def pick(own, edge, index, row, window):
        comp = index // 2 if own is near else index
        if 0 <= row < rows:
            return own[index, row, window, :]
        return edge[index, row + DEEP[comp] if top else row - rows, window, :]

    first = -DERIV if top else rows - DERIV
    stage1_rows(lambda f, row, window: pick(near, near_h, f, row, window), first, 2 * DERIV, xs)
    gates = [0, None] if top else [None, 1]
    stage1_depth(xs, 2 * DERIV, DERIV, tables, deriv, place, gates)
    stage2_columns(deriv, 2 * DERIV, tables, y2_h, 7)

    start = 0 if top else half

    @pl.loop(0, cols // 8)
    def _(t):
        window = pl.ds(pl.multiple_of(t * 8, 8), 8)

        def second(index, row):
            if DERIV <= row < rows - DERIV:
                return y2[index, row - DERIV, window, :]
            return y2_h[index, row - first, window, :]

        for which, kind in ((0, 1), (1, 0)):
            for comp in range(2):
                reach = REACH[comp]
                values = [second(2 * which + comp, row) for row in range(start - reach, start + half + reach)]
                for i, value in enumerate(smooth_rows_of(kind, comp, values, half)):
                    xm[2 * which + comp, i, window, :] = value
        scale = row_taps(2, 0.0, 1.0)[8]
        for comp in range(2):
            values = [pick(far, far_h, comp, row, window) for row in range(start - FAR, start + half + FAR)]
            for i, value in enumerate(smooth_rows_exp(values, scale, half)):
                xa[comp, i, window, :] = value

    sums[...] = jnp.zeros_like(sums)
    step = half // 2
    for i in range(0, half, step):
        part = slice(i, i + step)
        flat = lambda ref, p: ref[p, part].reshape(step * cols, depth)
        pore = solid[start + i : start + i + step].reshape(step * cols, depth) == 0
        high, low = split(jnp.concatenate([flat(xa, 0), flat(xa, 1)], axis=1))
        pull = jnp.dot(high, tables["pull_high"], preferred_element_type=F32)
        pull += jnp.dot(high, tables["pull_low"], preferred_element_type=F32)
        pull += jnp.dot(low, tables["pull_high"], preferred_element_type=F32)
        for comp in range(2):
            mu = split_dot(jnp.concatenate([flat(xm, 2 + comp), flat(xm, comp)], axis=1), tables[f"last{comp}"])
            mu = mu + pull[:, comp * depth : (comp + 1) * depth]
            value = jnp.where(pore, jnp.exp(-mu), 0.0)
            proposal[comp, part] = value.reshape(step, cols, depth)
            sums[comp] += value.reshape(step * cols // 8, 8, depth).sum(0)
    if not last:
        base = 0
        for comp in range(2):
            part = slice(0, DEEP[comp]) if top else slice(half - DEEP[comp], half)
            pack_rows(strips, middle, base, proposal[comp, part])
            base += DEEP[comp]


def in_vmem(count):
    return [pl.BlockSpec(memory_space=pltpu.VMEM)] * count


def params(mebibytes):
    return pltpu.CompilerParams(vmem_limit_bytes=mebibytes * 1024 * 1024)


def shape(*sizes):
    return jax.ShapeDtypeStruct(sizes, F32)


COST = pl.CostEstimate(flops=1000, bytes_accessed=1000, transcendentals=0)


def derivative_scratch(count, wide, depth):
    return [pltpu.VMEM((4, count, wide, depth), F32), pltpu.VMEM((2, count, wide, depth), F32)]


def mid(later, blocks, table):
    _, rows, cols, depth = blocks[0].shape
    outs = [shape(4, rows, cols + 2 * WIDE, depth), shape(2, rows, cols, depth)]
    if not later:
        outs += [shape(sum(DEEP), cols, depth)]
    return pl.pallas_call(
        functools.partial(mid_kernel, later),
        out_shape=tuple(outs),
        in_specs=in_vmem(len(blocks) + 1),
        out_specs=tuple(in_vmem(len(outs))),
        compiler_params=params(6),
        cost_estimate=COST,
        name="mid",
    )(*blocks, table)


def rest(later, first, blocks, table):
    _, rows, wide, depth = blocks[0].shape
    count, cols = rows - 2 * DERIV, wide - 2 * WIDE
    outs = [shape(4, count, cols, depth)]
    if later:
        outs += [shape(*block.shape) for block in blocks[:2]]
    return pl.pallas_call(
        functools.partial(rest_kernel, later),
        out_shape=tuple(outs),
        in_specs=[pl.BlockSpec(memory_space=pltpu.SMEM if later else pl.ANY)] + in_vmem(len(blocks) + 1),
        out_specs=tuple(in_vmem(len(outs))),
        scratch_shapes=[pltpu.VMEM((4, count, wide, depth), F32), pltpu.VMEM((2, count, wide, depth), F32)],
        compiler_params=params(8),
        cost_estimate=COST,
        name="rest",
    )(first, *blocks, table)


def edge(top, later, last, scalars, after, blocks, table):
    rows, cols, depth = blocks[-1].shape
    wide, half = cols + 2 * WIDE, rows // 2
    f32 = lambda *s: pltpu.VMEM(s, F32)
    outs = [shape(2, half, cols, depth), shape(2, 8, depth)]
    if not last:
        outs += packed_shapes(cols, depth)
    return pl.pallas_call(
        functools.partial(edge_kernel, top, later, last),
        out_shape=tuple(outs),
        in_specs=[pl.BlockSpec(memory_space=pltpu.SMEM)] * len(scalars) + [pl.BlockSpec(memory_space=pl.ANY)] + in_vmem(len(blocks) + 1),
        out_specs=tuple(in_vmem(len(outs))),
        scratch_shapes=[
            f32(4, DEEP[1], wide, depth),
            f32(2, DEEP[1], cols, depth),
            f32(4, 2 * DERIV, wide, depth),
            f32(2, 2 * DERIV, wide, depth),
            f32(4, 2 * DERIV, cols, depth),
            f32(4, half, cols, depth),
            f32(2, half, cols, depth),
        ],
        compiler_params=params(16),
        cost_estimate=COST,
        name="edge_top" if top else "edge_bottom",
    )(*scalars, after, *blocks, table)


def shift(value, axis, step):
    count = lax.axis_size(axis)
    return lax.ppermute(value, axis, [(i, i + step) for i in range(count) if 0 <= i + step < count])


def swap_columns(even, odd):
    count = lax.axis_size("gy")
    pairs = lambda first: [p for i in range(first, count - 1, 2) for p in ((i, i + 1), (i + 1, i))]
    return lax.ppermute(even, "gy", pairs(0)), lax.ppermute(odd, "gy", pairs(1))


def side_starts(cols):
    right, left = cols - 2 * WIDE, 0
    odd = position()[4]
    return pl.multiple_of(right * (1 - odd), 8), pl.multiple_of(right * odd, 8)


def first_rows_kernel(own, solid, out, density, mask, sems):
    rows = own.shape[1]
    most = max(DEEP)
    half = most // 2
    copies = []
    for part, begin in enumerate((0, half)):
        source, target = pl.ds(rows - most + begin, half), pl.ds(begin, half)
        copies.append(pltpu.make_async_copy(solid.at[source], mask.at[target], sems.at[part]))
        for comp in range(2):
            copies.append(pltpu.make_async_copy(own.at[comp, source], density.at[comp, target], sems.at[2 + 2 * part + comp]))
    for copy in copies:
        copy.start()
    for copy in copies:
        copy.wait()
    base = 0
    for comp in range(2):
        out[base : base + DEEP[comp]] = jnp.where(mask[most - DEEP[comp] :] == 0, density[comp, most - DEEP[comp] :], 0.0)
        base += DEEP[comp]


def first_rows(own, solid):
    _, _, cols, depth = own.shape
    return pl.pallas_call(
        first_rows_kernel,
        out_shape=shape(sum(DEEP), cols, depth),
        in_specs=[pl.BlockSpec(memory_space=pl.ANY)] * 2,
        out_specs=in_vmem(1)[0],
        scratch_shapes=[
            pltpu.VMEM((2, max(DEEP), cols, depth), F32),
            pltpu.VMEM((max(DEEP), cols, depth), jnp.int32),
            pltpu.SemaphoreType.DMA((6,)),
        ],
        compiler_params=params(56),
        cost_estimate=COST,
        name="first_rows",
    )(own, solid)


def first_columns_kernel(own, solid, even, odd):
    for start, out in zip(side_starts(own.shape[2]), (even, odd)):
        window = pl.ds(start, 2 * WIDE)
        for comp in range(2):
            out[comp] = jnp.where(solid[:, window] == 0, own[comp, :, window], 0.0)


def first_columns(own, solid):
    _, rows, _, depth = own.shape
    side = shape(2, rows, 2 * WIDE, depth)
    return pl.pallas_call(
        first_columns_kernel,
        out_shape=(side, side),
        in_specs=in_vmem(2),
        out_specs=tuple(in_vmem(2)),
        compiler_params=params(8),
        cost_estimate=COST,
        name="first_columns",
    )(own, solid)


def sides_kernel(after, value, even, odd, sems):
    copies = []
    for i, (start, out) in enumerate(zip(side_starts(value.shape[1]), (even, odd))):
        copies.append(pltpu.make_async_copy(value.at[:, pl.ds(start, 2 * WIDE)], out, sems.at[i]))
    for copy in copies:
        copy.start()
    for copy in copies:
        copy.wait()


def sides_pack(after, value):
    count, _, depth = value.shape
    side = shape(count, 2 * WIDE, depth)
    return pl.pallas_call(
        sides_kernel,
        out_shape=(side, side),
        in_specs=[pl.BlockSpec(memory_space=pl.ANY)] * 2,
        out_specs=tuple(in_vmem(2)),
        scratch_shapes=[pltpu.SemaphoreType.DMA((2,))],
        compiler_params=params(4),
        cost_estimate=COST,
        name="sides_pack",
    )(after, value)


def columns_kernel(value, even, odd):
    for start, out in zip(side_starts(value.shape[2]), (even, odd)):
        out[...] = value[:, :, pl.ds(start, 2 * WIDE)]


def columns_pack(value):
    _, count, _, depth = value.shape
    side = shape(2, count, 2 * WIDE, depth)
    return pl.pallas_call(
        columns_kernel,
        out_shape=(side, side),
        in_specs=in_vmem(1),
        out_specs=tuple(in_vmem(2)),
        compiler_params=params(8),
        cost_estimate=COST,
        name="columns_pack",
    )(value)


def joint_kernel(after, halo, value, even, odd):
    count, rows = halo.shape[0], value.shape[1]
    starts = zip(side_starts(halo.shape[1]), side_starts(value.shape[2]))
    for (start, own_start), out in zip(starts, (even, odd)):
        out[:count] = halo[:, pl.ds(start, 2 * WIDE)]
        window = pl.ds(own_start, 2 * WIDE)
        for comp in range(2):
            out[count + comp * rows : count + (comp + 1) * rows] = value[comp, :, window]


def joint_pack(after, halo, value):
    _, rows, _, depth = value.shape
    side = shape(halo.shape[0] + 2 * rows, 2 * WIDE, depth)
    return pl.pallas_call(
        joint_kernel,
        out_shape=(side, side),
        in_specs=[pl.BlockSpec(memory_space=pl.ANY)] + in_vmem(2),
        out_specs=tuple(in_vmem(2)),
        compiler_params=params(6),
        cost_estimate=COST,
        name="joint_pack",
    )(after, halo, value)


def ready_kernel(after, value, out):
    pass


def ready_after(after, value):
    return pl.pallas_call(
        ready_kernel,
        out_shape=shape(*value.shape),
        in_specs=[pl.BlockSpec(memory_space=pl.ANY)] * 2,
        out_specs=pl.BlockSpec(memory_space=pl.ANY),
        input_output_aliases={1: 0},
        compiler_params=params(2),
        cost_estimate=COST,
        name="ready_after",
    )(after, value)


def add_partners(sums, axis, first, end):
    count = lax.axis_size(axis)
    for bit in range(first, end):
        sums = sums + lax.ppermute(sums, axis, [(i, i ^ (1 << bit)) for i in range(count)])
    return sums


def spread_kernel(one, two, out):
    total = (one[...] + two[...]).sum(axis=1)
    out[...] = jnp.broadcast_to(total[None], out.shape)


def total_over_all(one, two):
    devices = lax.axis_size(AXES)
    copies = pl.pallas_call(
        spread_kernel,
        out_shape=shape(devices, 2, one.shape[2]),
        in_specs=in_vmem(2),
        out_specs=in_vmem(1)[0],
        compiler_params=params(4),
        cost_estimate=COST,
        name="spread",
    )(one, two)
    return lax.all_to_all(copies, AXES, 0, 0, tiled=True)


def last_kernel(total_cells, scales, loadings, totals, own, solid, old_top, old_bottom, top, bottom, out, ready, sems):
    half = top.shape[1]
    copies = []
    for comp in range(2):
        total = jnp.sum(totals[:, comp], keepdims=True)
        factor = DAMPING * loadings[comp] * total_cells / total
        for i, (old, new) in enumerate(((old_top, top), (old_bottom, bottom))):
            part = slice(i * half, (i + 1) * half)
            start = jnp.where(solid[part] == 0, own[comp, part], 0.0)
            kept = (1.0 - DAMPING) * blend(start, old[comp], scales[comp])
            ready[comp, part] = kept + factor[None] * new[comp]
            copies.append(pltpu.make_async_copy(ready.at[comp, part], out.at[comp, part], sems.at[2 * comp + i]))
            copies[-1].start()
    for copy in copies:
        copy.wait()


def last_update(total_cells, scalars, blocks):
    own = blocks[1]
    return pl.pallas_call(
        functools.partial(last_kernel, total_cells),
        out_shape=shape(*own.shape),
        in_specs=[pl.BlockSpec(memory_space=pltpu.SMEM)] * len(scalars) + in_vmem(len(blocks)),
        out_specs=pl.BlockSpec(memory_space=pl.ANY),
        scratch_shapes=[pltpu.VMEM(own.shape, F32), pltpu.SemaphoreType.DMA((4,))],
        compiler_params=params(4),
        cost_estimate=COST,
        name="last_update",
    )(*scalars, *blocks)


def bits(axis):
    count = lax.axis_size(axis)
    assert count & (count - 1) == 0
    return count.bit_length() - 1


def body(density_init, solid_mask, loadings):
    rows, cols, depth = solid_mask.shape
    total_cells = float(rows * lax.axis_size("gx") * cols * lax.axis_size("gy") * depth)
    table = jnp.asarray(packed_tables(cols, depth)[0])

    def scale_of(sums):
        return DAMPING * loadings * total_cells / sums.sum(axis=tuple(range(sums.ndim))[1:])

    both = lambda pair, step: [shift(part, "gx", step) for part in pair]
    above = shift(first_rows(density_init, solid_mask), "gx", 1)
    columns = swap_columns(*first_columns(density_init, solid_mask))
    near, far, upper = mid(False, [density_init, solid_mask, *columns], table)
    below = shift(ready_after(above, upper), "gx", -1)
    to_sides = sides_pack(far, above)
    top_sides = swap_columns(*to_sides)
    (y2,) = rest(False, to_sides[0], [near], table)
    top, top_sums, *upper = edge(True, False, False, [], y2, [above, *top_sides, near, far, y2, solid_mask], table)
    below_new = both(upper, -1)
    top_columns = swap_columns(*columns_pack(top))
    bottom_sides = swap_columns(*sides_pack(top_sums, below))
    near_top, far_top = mid(True, [top, *top_columns], table)
    blocks = [below, *bottom_sides, near, far, y2, solid_mask]
    bottom, bottom_sums, *lower = edge(False, False, False, [], far_top, blocks, table)
    old = [density_init, solid_mask, top, bottom]
    sums = add_partners(top_sums + bottom_sums, "gy", 0, bits("gy"))
    to_sides = joint_pack(sums, below_new[0], bottom)
    sides_new = swap_columns(*to_sides)
    sums = add_partners(ready_after(below_new[1], ready_after(to_sides[0], sums)), "gx", 0, bits("gx"))
    above_new = both([ready_after(sums, part) for part in lower], 1)
    near_bottom, far_bottom = mid(True, [bottom, *sides_new], table)
    scale = scale_of(sums)
    y2, near, far = rest(True, scale, [near, far, near_top, far_top, near_bottom, far_bottom], table)
    common = [near, far, y2, solid_mask]
    blocks = [below, *bottom_sides, *below_new, *sides_new, *common]
    bottom, bottom_sums = edge(False, True, True, [scale], y2, blocks, table)
    sides_new = swap_columns(*sides_pack(bottom_sums, above_new[0]))
    top, top_sums = edge(True, True, True, [scale], y2, [above, *top_sides, *above_new, *sides_new, *common], table)
    totals = total_over_all(top_sums, bottom_sums)
    return last_update(total_cells, [scale, loadings], [totals, *old, top, bottom])


def solution(mesh):
    in_specs = (P(None, "gx", "gy", None), P("gx", "gy", None), P())
    out_specs = P(None, "gx", "gy", None)
    return jax.shard_map(body, mesh=mesh, in_specs=in_specs, out_specs=out_specs, check_vma=False)
```

```python
import functools

import jax
import jax.numpy as jnp
import ml_dtypes
import numpy as np
from jax import lax
from jax.experimental import pallas as pl
from jax.experimental.pallas import tpu as pltpu
from jax.sharding import PartitionSpec as P

ITERS = 2
SEGMENTS = (1.5131, 1.0)
RADII = (6.0, 8.0)
CROSS = 0.25
DAMPING = 0.3
ATTRACT = ((0.3, 0.22), (0.22, 0.16))
REACH = (5, 7)
FAR = 8
DERIV = REACH[1]
DEEP = tuple(DERIV + r for r in REACH)
WIDE = 8
AXES = ("gx", "gy")
BF16 = jnp.bfloat16
F32 = jnp.float32


def raw_profile(kind, radius):
    offset = np.arange(17) - 8.0
    if kind == 0:
        return np.maximum(radius * radius - offset * offset, 0.0)
    if kind == 1:
        return offset * offset * np.maximum(radius * radius - offset * offset, 0.0)
    return np.exp(-np.abs(offset) / 4.0)


def split_bf16(table):
    high = table.astype(np.float32).astype(ml_dtypes.bfloat16)
    low = (table - high.astype(np.float64)).astype(np.float32).astype(ml_dtypes.bfloat16)
    return high, low


def column_band(kind, radius, count, columns, first):
    band = np.zeros((count, columns))
    for o in range(count):
        band[o, first + o : first + o + 17] = raw_profile(kind, radius)
    return band


def depth_band(kind, radius, depth):
    taps = raw_profile(kind, radius)
    band = np.zeros((depth, depth))
    for column in range(depth):
        for offset in range(17):
            source = column + offset - 8
            if 0 <= source < depth:
                band[source, column] = taps[offset]
    return band


def stage1_tables(comp, cols):
    wide = cols + 2 * WIDE
    pack = column_band(0, RADII[comp], wide, wide + 16, 0)
    rest = np.concatenate(
        [column_band(1, RADII[comp], wide, wide + 16, 0), column_band(2, 0.0, cols, wide + 16, WIDE)]
    )
    high, low = split_bf16(np.concatenate([pack, rest]))
    return {f"first{comp}": np.concatenate([high, high], axis=1), f"rest{comp}": low[wide:]}


def stage2_table(kind, cols):
    high, low = split_bf16(np.concatenate([column_band(kind, r, cols, cols + 16, 0) for r in RADII]))
    return np.concatenate([high, high] if kind == 0 else [high, high, low], axis=1)


def depth_table(kinds, depth):
    scale = lambda kind, comp: SEGMENTS[comp] / raw_profile(0, RADII[comp]).sum() ** 3 if kind == 0 else 1.0
    high, low = split_bf16(np.concatenate([scale(kind, c) * depth_band(kind, RADII[c], depth) for kind, c in kinds]))
    return np.concatenate([high, low], axis=1)


def attraction_tables(depth):
    band = depth_band(2, 0.0, depth)
    high, low = split_bf16(-np.concatenate([np.concatenate([ATTRACT[i][j] * band for i in range(2)], axis=1) for j in range(2)]))
    return {"pull_high": high, "pull_low": low}


@functools.lru_cache
def packed_tables(cols, depth):
    tables = {**stage1_tables(0, cols), **stage1_tables(1, cols), **attraction_tables(depth)}
    tables |= {f"depth{kind}": depth_table([(kind, comp) for comp in range(2)], depth) for kind in range(2)}
    tables |= {f"last{comp}": depth_table([(0, comp), (1, comp)], depth) for comp in range(2)}
    tables |= {f"second{kind}": stage2_table(kind, cols) for kind in range(2)}
    width = max(t.shape[1] for t in tables.values())
    places, start = {}, 0
    for name, table in tables.items():
        places[name] = (start, *table.shape)
        start += table.shape[0]
    whole = np.zeros((start, width), ml_dtypes.bfloat16)
    for name, table in tables.items():
        whole[places[name][0] : places[name][0] + table.shape[0], : table.shape[1]] = table
    return whole, places


class Tables:
    def __init__(self, ref, cols, depth):
        self.ref, self.places = ref, packed_tables(cols, depth)[1]

    def __getitem__(self, name):
        start, rows, columns = self.places[name]
        return self.ref[start : start + rows, :columns]


def row_taps(kind, radius, scale):
    taps = raw_profile(kind, radius)
    return [float(v) for v in taps * (scale / taps.sum() ** 3)]


def split(field):
    high = field.astype(BF16)
    return high, (field - high.astype(F32)).astype(BF16)


def smooth_rows(values, taps, count, reach):
    out = []
    for i in range(count):
        total = None
        for k in range(reach + 1):
            if taps[8 + k] == 0.0:
                continue
            pair = values[i + reach] if k == 0 else values[i + reach - k] + values[i + reach + k]
            term = taps[8 + k] * pair
            total = term if total is None else total + term
        out.append(total)
    return out


def smooth_rows_packing(values, radius, count):
    reach = radius - 1
    at = lambda x: values[x + reach]
    taps = raw_profile(0, radius)
    out = smooth_rows(values[: 2 + 2 * reach], [float(v) for v in taps], 2, reach)
    slope = out[1] - out[0]
    box = at(1)
    for j in range(1, radius):
        box = box + (at(1 - j) + at(1 + j))
    for x in range(1, count - 1):
        if x > 1:
            box = box + (at(x + reach) - at(x - radius))
        slope = slope + ((2 * radius - 1.0) * (at(x + radius) + at(x - radius)) - 2.0 * box)
        out.append(out[-1] + slope)
    return out


def smooth_rows_of(kind, comp, values, count):
    if kind == 0:
        return smooth_rows_packing(values, int(RADII[comp]), count)
    return smooth_rows(values, row_taps(kind, RADII[comp], 1.0), count, REACH[comp])


def smooth_rows_exp(values, scale, count):
    q = float(np.exp(-0.25))
    q9 = q**9
    up = values[0]
    for j in range(1, 9):
        up = up * q + values[j]
    ups = [up]
    for i in range(1, count):
        up = up * q + (values[i + 8] - q9 * values[i - 1])
        ups.append(up)
    down = values[count + 15]
    for j in range(1, 8):
        down = down * q + values[count + 15 - j]
    down = down * q
    out = [None] * count
    out[count - 1] = scale * (ups[count - 1] + down)
    for i in range(count - 2, -1, -1):
        down = down * q + (q * values[i + 9] - q9 * values[i + 17])
        out[i] = scale * (ups[i] + down)
    return out


def split_dot(pair, table):
    high, low = split(pair)
    width = table.shape[1] // 2
    both = jnp.dot(high, table, preferred_element_type=F32)
    rest = jnp.dot(low, table[:, :width], preferred_element_type=F32)
    return both[:, :width] + both[:, width:] + rest


def stage1_columns(load, pairs, comp, tables, near, far, cols, unroll, begin):
    wide = cols + 2 * WIDE

    @pl.loop(0, pairs, unroll=unroll)
    def _(i):
        high, low = split(jnp.concatenate([load(2 * i), load(2 * i + 1)], axis=1))
        first = jnp.dot(tables[f"first{comp}"], jnp.concatenate([high, low], axis=0), preferred_element_type=F32)
        rest = first[wide:] + jnp.dot(tables[f"rest{comp}"], high, preferred_element_type=F32)
        depth = high.shape[1] // 2
        for j in range(2):
            lanes = slice(j * depth, (j + 1) * depth)
            row = begin + 2 * i + j
            near[2 * comp, row] = first[:wide, lanes]
            near[2 * comp + 1, row] = rest[:wide, lanes]
            far[comp, row] = rest[wide:, lanes]


def stage1_rows(load, first, count, out):
    wide = out.shape[2]

    @pl.loop(0, wide // 8)
    def _(t):
        window = pl.ds(pl.multiple_of(t * 8, 8), 8)
        for comp in range(2):
            reach = REACH[comp]
            for kind in range(2):
                field = 2 * comp + kind
                values = [load(field, row, window) for row in range(first - reach, first + count + reach)]
                for i, value in enumerate(smooth_rows_of(kind, comp, values, count)):
                    out[field, i, window, :] = value


def stage1_depth(xs, count, step, tables, deriv, place, gates):
    wide, depth = xs.shape[2:]
    for i, start in enumerate(range(0, count, step)):
        rows = slice(start, start + step)
        pair = lambda p: jnp.concatenate([xs[q, rows].reshape(step * wide, depth) for q in (p, p + 2)], axis=1)
        n3 = split_dot(pair(0), tables["depth0"])
        n2 = split_dot(pair(1), tables["depth1"])
        one = 1.0 + n3
        two = (jnp.log(one) + 2.0 * CROSS * n2 * one).reshape(step, wide, depth)
        three = (n2 / one + CROSS * n2 * n2).reshape(step, wide, depth)
        for which, value in enumerate((two, three)):
            if gates[i] is not None:
                value = value * place[gates[i]].astype(F32)
            deriv[which, rows, :WIDE] = value[:, :WIDE] * place[2].astype(F32)
            deriv[which, rows, WIDE : wide - WIDE] = value[:, WIDE : wide - WIDE]
            deriv[which, rows, wide - WIDE :] = value[:, wide - WIDE :] * place[3].astype(F32)


def stage2_columns(deriv, count, tables, out, unroll):
    cols = out.shape[2]

    @pl.loop(0, count // 2, unroll=unroll)
    def _(i):
        for which, kind in ((0, 1), (1, 0)):
            high, low = split(jnp.concatenate([deriv[which, 2 * i], deriv[which, 2 * i + 1]], axis=1))
            stacked = [high, low, high] if which == 0 else [high, low]
            result = jnp.dot(tables[f"second{kind}"], jnp.concatenate(stacked, axis=0), preferred_element_type=F32)
            depth = high.shape[1] // 2
            for comp in range(2):
                for j in range(2):
                    out[2 * which + comp, 2 * i + j] = result[comp * cols : (comp + 1) * cols, j * depth : (j + 1) * depth]


def position():
    flags = []
    for axis in AXES:
        index = lax.axis_index(axis)
        flags += [(index > 0).astype(jnp.int32), (index + 1 < lax.axis_size(axis)).astype(jnp.int32)]
    return flags + [lax.rem(lax.axis_index("gy"), 2)]


def blend(first, second, scale):
    return first if scale is None else (1.0 - DAMPING) * first + scale * second


def pack_rows(strips, middle, base, value):
    cols, width = value.shape[1], 2 * WIDE
    part = slice(base, base + value.shape[0])
    strips[part, :width] = value[:, :width]
    strips[part, width:] = value[:, cols - width :]
    middle[part] = value[:, width : cols - width]


def packed_shapes(cols, depth):
    return [shape(sum(DEEP), 4 * WIDE, depth), shape(sum(DEEP), cols - 4 * WIDE, depth)]


def side_rows(pair, index, odd):
    one, two = pair[0][index], pair[1][index]
    return jnp.where(odd, one, two), jnp.where(odd, two, one)


def mid_kernel(later, own, *refs):
    if later:
        sides, table_ref, near, far = refs[:2], *refs[2:]
    else:
        solid, *sides, table_ref, near, far, upper = refs
        base = 0
        for comp in range(2):
            part = slice(0, DEEP[comp])
            upper[base : base + DEEP[comp]] = jnp.where(solid[part] == 0, own[comp, part], 0.0)
            base += DEEP[comp]
    rows, cols, depth = far.shape[1:]
    tables = Tables(table_ref, cols, depth)
    odd = position()[4] == 1
    for comp in range(2):

        def load(row):
            index = (comp, row) if len(sides[0].shape) == 4 else sum(DEEP) + comp * rows + row
            left, right = side_rows(sides, index, odd)
            value = own[comp, row] if later else jnp.where(solid[row] == 0, own[comp, row], 0.0)
            return jnp.concatenate([left, value, right], axis=0)

        stage1_columns(load, rows // 2, comp, tables, near, far, cols, rows // 2, 0)


def rest_kernel(later, *refs):
    if later:
        scales, near_old, far_old, near_top, far_top, near_bottom, far_bottom, table_ref, y2, near, far, xs, deriv = refs
        half = near_top.shape[1]
        for old, halves, out in ((near_old, (near_top, near_bottom), near), (far_old, (far_top, far_bottom), far)):
            fields = out.shape[0]

            @pl.loop(0, half)
            def _(row):
                for field in range(fields):
                    for i, new in enumerate(halves):
                        at = row + i * half
                        out[field, at] = blend(old[field, at], new[field, row], scales[2 * field // fields])
    else:
        after, near, table_ref, y2, xs, deriv = refs
    count, cols, depth = y2.shape[1:]
    tables, place = Tables(table_ref, cols, depth), position()
    stage1_rows(lambda field, row, window: near[field, row, window, :], DERIV, count, xs)
    stage1_depth(xs, count, count // 3, tables, deriv, place, [None] * 3)
    stage2_columns(deriv, count, tables, y2, count // 2)


def edge_kernel(top, later, last, *refs):
    if later:
        scales, after, *refs = refs
        halo, sides, halo_new, sides_new, refs = refs[:1], refs[1:3], refs[3:5], refs[5:7], refs[7:]
    else:
        after, *refs = refs
        halo, sides, refs = refs[:1], refs[1:3], refs[3:]
    near, far, y2, solid, table_ref, proposal, sums, *refs = refs
    if not last:
        strips, middle, *refs = refs
    near_h, far_h, xs, deriv, y2_h, xm, xa = refs
    _, rows, cols, depth = far.shape
    half = rows // 2
    tables = Tables(table_ref, cols, depth)
    place = position()
    odd = place[4] == 1

    def pieces(rows_in, columns_in, row):
        left, right = side_rows(columns_in, row, odd)
        if len(rows_in) == 1:
            whole = rows_in[0][row]
            return [left, whole[: 2 * WIDE], whole[2 * WIDE : cols - 2 * WIDE], whole[cols - 2 * WIDE :], right]
        outer, inner = rows_in
        return [left, outer[row, : 2 * WIDE], inner[row], outer[row, 2 * WIDE :], right]

    for comp in range(2):
        base = 0 if comp == 0 else DEEP[0]
        scale = scales[comp] if later else None

        def load(row):
            parts = pieces(halo, sides, base + row)
            if later:
                parts = [blend(old, new, scale) for old, new in zip(parts, pieces(halo_new, sides_new, base + row))]
            return jnp.concatenate(parts, axis=0)

        stage1_columns(load, DEEP[comp] // 2, comp, tables, near_h, far_h, cols, DEEP[comp] // 2, 0)

    def pick(own, edge, index, row, window):
        comp = index // 2 if own is near else index
        if 0 <= row < rows:
            return own[index, row, window, :]
        return edge[index, row + DEEP[comp] if top else row - rows, window, :]

    first = -DERIV if top else rows - DERIV
    stage1_rows(lambda f, row, window: pick(near, near_h, f, row, window), first, 2 * DERIV, xs)
    gates = [0, None] if top else [None, 1]
    stage1_depth(xs, 2 * DERIV, DERIV, tables, deriv, place, gates)
    stage2_columns(deriv, 2 * DERIV, tables, y2_h, 7)

    start = 0 if top else half

    @pl.loop(0, cols // 8)
    def _(t):
        window = pl.ds(pl.multiple_of(t * 8, 8), 8)

        def second(index, row):
            if DERIV <= row < rows - DERIV:
                return y2[index, row - DERIV, window, :]
            return y2_h[index, row - first, window, :]

        for which, kind in ((0, 1), (1, 0)):
            for comp in range(2):
                reach = REACH[comp]
                values = [second(2 * which + comp, row) for row in range(start - reach, start + half + reach)]
                for i, value in enumerate(smooth_rows_of(kind, comp, values, half)):
                    xm[2 * which + comp, i, window, :] = value
        scale = row_taps(2, 0.0, 1.0)[8]
        for comp in range(2):
            values = [pick(far, far_h, comp, row, window) for row in range(start - FAR, start + half + FAR)]
            for i, value in enumerate(smooth_rows_exp(values, scale, half)):
                xa[comp, i, window, :] = value

    sums[...] = jnp.zeros_like(sums)
    step = half // 2
    for i in range(0, half, step):
        part = slice(i, i + step)
        flat = lambda ref, p: ref[p, part].reshape(step * cols, depth)
        pore = solid[start + i : start + i + step].reshape(step * cols, depth) == 0
        high, low = split(jnp.concatenate([flat(xa, 0), flat(xa, 1)], axis=1))
        pull = jnp.dot(high, tables["pull_high"], preferred_element_type=F32)
        pull += jnp.dot(high, tables["pull_low"], preferred_element_type=F32)
        pull += jnp.dot(low, tables["pull_high"], preferred_element_type=F32)
        for comp in range(2):
            mu = split_dot(jnp.concatenate([flat(xm, 2 + comp), flat(xm, comp)], axis=1), tables[f"last{comp}"])
            mu = mu + pull[:, comp * depth : (comp + 1) * depth]
            value = jnp.where(pore, jnp.exp(-mu), 0.0)
            proposal[comp, part] = value.reshape(step, cols, depth)
            sums[comp] += value.reshape(step * cols // 8, 8, depth).sum(0)
    if not last:
        base = 0
        for comp in range(2):
            part = slice(0, DEEP[comp]) if top else slice(half - DEEP[comp], half)
            pack_rows(strips, middle, base, proposal[comp, part])
            base += DEEP[comp]


def in_vmem(count):
    return [pl.BlockSpec(memory_space=pltpu.VMEM)] * count


def params(mebibytes):
    return pltpu.CompilerParams(vmem_limit_bytes=mebibytes * 1024 * 1024)


def shape(*sizes):
    return jax.ShapeDtypeStruct(sizes, F32)


COST = pl.CostEstimate(flops=1000, bytes_accessed=1000, transcendentals=0)


def derivative_scratch(count, wide, depth):
    return [pltpu.VMEM((4, count, wide, depth), F32), pltpu.VMEM((2, count, wide, depth), F32)]


def mid(later, blocks, table):
    _, rows, cols, depth = blocks[0].shape
    outs = [shape(4, rows, cols + 2 * WIDE, depth), shape(2, rows, cols, depth)]
    if not later:
        outs += [shape(sum(DEEP), cols, depth)]
    return pl.pallas_call(
        functools.partial(mid_kernel, later),
        out_shape=tuple(outs),
        in_specs=in_vmem(len(blocks) + 1),
        out_specs=tuple(in_vmem(len(outs))),
        compiler_params=params(6),
        cost_estimate=COST,
        name="mid",
    )(*blocks, table)


def rest(later, first, blocks, table):
    _, rows, wide, depth = blocks[0].shape
    count, cols = rows - 2 * DERIV, wide - 2 * WIDE
    outs = [shape(4, count, cols, depth)]
    if later:
        outs += [shape(*block.shape) for block in blocks[:2]]
    return pl.pallas_call(
        functools.partial(rest_kernel, later),
        out_shape=tuple(outs),
        in_specs=[pl.BlockSpec(memory_space=pltpu.SMEM if later else pl.ANY)] + in_vmem(len(blocks) + 1),
        out_specs=tuple(in_vmem(len(outs))),
        scratch_shapes=[pltpu.VMEM((4, count, wide, depth), F32), pltpu.VMEM((2, count, wide, depth), F32)],
        compiler_params=params(8),
        cost_estimate=COST,
        name="rest",
    )(first, *blocks, table)


def edge(top, later, last, scalars, after, blocks, table):
    rows, cols, depth = blocks[-1].shape
    wide, half = cols + 2 * WIDE, rows // 2
    f32 = lambda *s: pltpu.VMEM(s, F32)
    outs = [shape(2, half, cols, depth), shape(2, 8, depth)]
    if not last:
        outs += packed_shapes(cols, depth)
    return pl.pallas_call(
        functools.partial(edge_kernel, top, later, last),
        out_shape=tuple(outs),
        in_specs=[pl.BlockSpec(memory_space=pltpu.SMEM)] * len(scalars) + [pl.BlockSpec(memory_space=pl.ANY)] + in_vmem(len(blocks) + 1),
        out_specs=tuple(in_vmem(len(outs))),
        scratch_shapes=[
            f32(4, DEEP[1], wide, depth),
            f32(2, DEEP[1], cols, depth),
            f32(4, 2 * DERIV, wide, depth),
            f32(2, 2 * DERIV, wide, depth),
            f32(4, 2 * DERIV, cols, depth),
            f32(4, half, cols, depth),
            f32(2, half, cols, depth),
        ],
        compiler_params=params(16),
        cost_estimate=COST,
        name="edge_top" if top else "edge_bottom",
    )(*scalars, after, *blocks, table)


def shift(value, axis, step):
    count = lax.axis_size(axis)
    return lax.ppermute(value, axis, [(i, i + step) for i in range(count) if 0 <= i + step < count])


def swap_columns(even, odd):
    count = lax.axis_size("gy")
    pairs = lambda first: [p for i in range(first, count - 1, 2) for p in ((i, i + 1), (i + 1, i))]
    return lax.ppermute(even, "gy", pairs(0)), lax.ppermute(odd, "gy", pairs(1))


def side_starts(cols):
    right, left = cols - 2 * WIDE, 0
    odd = position()[4]
    return pl.multiple_of(right * (1 - odd), 8), pl.multiple_of(right * odd, 8)


def first_rows_kernel(own, solid, out, density, mask, sems):
    rows = own.shape[1]
    most = max(DEEP)
    half = most // 2
    copies = []
    for part, begin in enumerate((0, half)):
        source, target = pl.ds(rows - most + begin, half), pl.ds(begin, half)
        copies.append(pltpu.make_async_copy(solid.at[source], mask.at[target], sems.at[part]))
        for comp in range(2):
            copies.append(pltpu.make_async_copy(own.at[comp, source], density.at[comp, target], sems.at[2 + 2 * part + comp]))
    for copy in copies:
        copy.start()
    for copy in copies:
        copy.wait()
    base = 0
    for comp in range(2):
        out[base : base + DEEP[comp]] = jnp.where(mask[most - DEEP[comp] :] == 0, density[comp, most - DEEP[comp] :], 0.0)
        base += DEEP[comp]


def first_rows(own, solid):
    _, _, cols, depth = own.shape
    return pl.pallas_call(
        first_rows_kernel,
        out_shape=shape(sum(DEEP), cols, depth),
        in_specs=[pl.BlockSpec(memory_space=pl.ANY)] * 2,
        out_specs=in_vmem(1)[0],
        scratch_shapes=[
            pltpu.VMEM((2, max(DEEP), cols, depth), F32),
            pltpu.VMEM((max(DEEP), cols, depth), jnp.int32),
            pltpu.SemaphoreType.DMA((6,)),
        ],
        compiler_params=params(56),
        cost_estimate=COST,
        name="first_rows",
    )(own, solid)


def first_columns_kernel(own, solid, even, odd):
    for start, out in zip(side_starts(own.shape[2]), (even, odd)):
        window = pl.ds(start, 2 * WIDE)
        for comp in range(2):
            out[comp] = jnp.where(solid[:, window] == 0, own[comp, :, window], 0.0)


def first_columns(own, solid):
    _, rows, _, depth = own.shape
    side = shape(2, rows, 2 * WIDE, depth)
    return pl.pallas_call(
        first_columns_kernel,
        out_shape=(side, side),
        in_specs=in_vmem(2),
        out_specs=tuple(in_vmem(2)),
        compiler_params=params(8),
        cost_estimate=COST,
        name="first_columns",
    )(own, solid)


def sides_kernel(after, value, even, odd, sems):
    copies = []
    for i, (start, out) in enumerate(zip(side_starts(value.shape[1]), (even, odd))):
        copies.append(pltpu.make_async_copy(value.at[:, pl.ds(start, 2 * WIDE)], out, sems.at[i]))
    for copy in copies:
        copy.start()
    for copy in copies:
        copy.wait()


def sides_pack(after, value):
    count, _, depth = value.shape
    side = shape(count, 2 * WIDE, depth)
    return pl.pallas_call(
        sides_kernel,
        out_shape=(side, side),
        in_specs=[pl.BlockSpec(memory_space=pl.ANY)] * 2,
        out_specs=tuple(in_vmem(2)),
        scratch_shapes=[pltpu.SemaphoreType.DMA((2,))],
        compiler_params=params(4),
        cost_estimate=COST,
        name="sides_pack",
    )(after, value)


def columns_kernel(value, even, odd):
    for start, out in zip(side_starts(value.shape[2]), (even, odd)):
        out[...] = value[:, :, pl.ds(start, 2 * WIDE)]


def columns_pack(value):
    _, count, _, depth = value.shape
    side = shape(2, count, 2 * WIDE, depth)
    return pl.pallas_call(
        columns_kernel,
        out_shape=(side, side),
        in_specs=in_vmem(1),
        out_specs=tuple(in_vmem(2)),
        compiler_params=params(8),
        cost_estimate=COST,
        name="columns_pack",
    )(value)


def joint_kernel(after, halo, value, even, odd):
    count, rows = halo.shape[0], value.shape[1]
    starts = zip(side_starts(halo.shape[1]), side_starts(value.shape[2]))
    for (start, own_start), out in zip(starts, (even, odd)):
        out[:count] = halo[:, pl.ds(start, 2 * WIDE)]
        window = pl.ds(own_start, 2 * WIDE)
        for comp in range(2):
            out[count + comp * rows : count + (comp + 1) * rows] = value[comp, :, window]


def joint_pack(after, halo, value):
    _, rows, _, depth = value.shape
    side = shape(halo.shape[0] + 2 * rows, 2 * WIDE, depth)
    return pl.pallas_call(
        joint_kernel,
        out_shape=(side, side),
        in_specs=[pl.BlockSpec(memory_space=pl.ANY)] + in_vmem(2),
        out_specs=tuple(in_vmem(2)),
        compiler_params=params(6),
        cost_estimate=COST,
        name="joint_pack",
    )(after, halo, value)


def ready_kernel(after, value, out):
    pass


def ready_after(after, value):
    return pl.pallas_call(
        ready_kernel,
        out_shape=shape(*value.shape),
        in_specs=[pl.BlockSpec(memory_space=pl.ANY)] * 2,
        out_specs=pl.BlockSpec(memory_space=pl.ANY),
        input_output_aliases={1: 0},
        compiler_params=params(2),
        cost_estimate=COST,
        name="ready_after",
    )(after, value)


def add_partners(sums, axis, first, end):
    count = lax.axis_size(axis)
    for bit in range(first, end):
        sums = sums + lax.ppermute(sums, axis, [(i, i ^ (1 << bit)) for i in range(count)])
    return sums


def spread_kernel(one, two, out):
    total = (one[...] + two[...]).sum(axis=1)
    out[...] = jnp.broadcast_to(total[None], out.shape)


def total_over_all(one, two):
    devices = lax.axis_size(AXES)
    copies = pl.pallas_call(
        spread_kernel,
        out_shape=shape(devices, 2, one.shape[2]),
        in_specs=in_vmem(2),
        out_specs=in_vmem(1)[0],
        compiler_params=params(4),
        cost_estimate=COST,
        name="spread",
    )(one, two)
    return lax.all_to_all(copies, AXES, 0, 0, tiled=True)


def last_kernel(total_cells, scales, loadings, totals, own, solid, old_top, old_bottom, top, bottom, out, ready, sems):
    half = top.shape[1]
    copies = []
    for comp in range(2):
        total = jnp.sum(totals[:, comp], keepdims=True)
        factor = DAMPING * loadings[comp] * total_cells / total
        for i, (old, new) in enumerate(((old_top, top), (old_bottom, bottom))):
            part = slice(i * half, (i + 1) * half)

            @pl.loop(0, half, unroll=4)
            def _(row):
                at = i * half + row
                start = jnp.where(solid[at] == 0, own[comp, at], 0.0)
                kept = (1.0 - DAMPING) * blend(start, old[comp, row], scales[comp])
                ready[comp, at] = kept + factor * new[comp, row]

            copies.append(pltpu.make_async_copy(ready.at[comp, part], out.at[comp, part], sems.at[2 * comp + i]))
            copies[-1].start()
    for copy in copies:
        copy.wait()


def last_update(total_cells, scalars, blocks):
    own = blocks[1]
    return pl.pallas_call(
        functools.partial(last_kernel, total_cells),
        out_shape=shape(*own.shape),
        in_specs=[pl.BlockSpec(memory_space=pltpu.SMEM)] * len(scalars) + in_vmem(len(blocks)),
        out_specs=pl.BlockSpec(memory_space=pl.ANY),
        scratch_shapes=[pltpu.VMEM(own.shape, F32), pltpu.SemaphoreType.DMA((4,))],
        compiler_params=params(4),
        cost_estimate=COST,
        name="last_update",
    )(*scalars, *blocks)


def bits(axis):
    count = lax.axis_size(axis)
    assert count & (count - 1) == 0
    return count.bit_length() - 1


def body(density_init, solid_mask, loadings):
    rows, cols, depth = solid_mask.shape
    total_cells = float(rows * lax.axis_size("gx") * cols * lax.axis_size("gy") * depth)
    table = jnp.asarray(packed_tables(cols, depth)[0])

    def scale_of(sums):
        return DAMPING * loadings * total_cells / sums.sum(axis=tuple(range(sums.ndim))[1:])

    both = lambda pair, step: [shift(part, "gx", step) for part in pair]
    above = shift(first_rows(density_init, solid_mask), "gx", 1)
    columns = swap_columns(*first_columns(density_init, solid_mask))
    near, far, upper = mid(False, [density_init, solid_mask, *columns], table)
    below = shift(ready_after(above, upper), "gx", -1)
    to_sides = sides_pack(far, above)
    top_sides = swap_columns(*to_sides)
    (y2,) = rest(False, to_sides[0], [near], table)
    top, top_sums, *upper = edge(True, False, False, [], y2, [above, *top_sides, near, far, y2, solid_mask], table)
    below_new = both(upper, -1)
    top_columns = swap_columns(*columns_pack(top))
    bottom_sides = swap_columns(*sides_pack(top_sums, below))
    near_top, far_top = mid(True, [top, *top_columns], table)
    blocks = [below, *bottom_sides, near, far, y2, solid_mask]
    bottom, bottom_sums, *lower = edge(False, False, False, [], far_top, blocks, table)
    old = [density_init, solid_mask, top, bottom]
    sums = add_partners(top_sums + bottom_sums, "gy", 0, bits("gy"))
    to_sides = joint_pack(sums, below_new[0], bottom)
    sides_new = swap_columns(*to_sides)
    sums = add_partners(ready_after(below_new[1], ready_after(to_sides[0], sums)), "gx", 0, bits("gx"))
    above_new = both([ready_after(sums, part) for part in lower], 1)
    near_bottom, far_bottom = mid(True, [bottom, *sides_new], table)
    scale = scale_of(sums)
    y2, near, far = rest(True, scale, [near, far, near_top, far_top, near_bottom, far_bottom], table)
    common = [near, far, y2, solid_mask]
    to_sides = sides_pack(y2, above_new[0])
    top_sides_new = swap_columns(*to_sides)
    blocks = [below, *bottom_sides, *below_new, *sides_new, *common]
    bottom, bottom_sums = edge(False, True, True, [scale], to_sides[0], blocks, table)
    blocks = [above, *top_sides, *above_new, *top_sides_new, *common]
    top, top_sums = edge(True, True, True, [scale], bottom_sums, blocks, table)
    totals = total_over_all(top_sums, bottom_sums)
    return last_update(total_cells, [scale, loadings], [totals, *old, top, bottom])


def solution(mesh):
    in_specs = (P(None, "gx", "gy", None), P("gx", "gy", None), P())
    out_specs = P(None, "gx", "gy", None)
    return jax.shard_map(body, mesh=mesh, in_specs=in_specs, out_specs=out_specs, check_vma=False)
```

```python
import functools

import jax
import jax.numpy as jnp
import ml_dtypes
import numpy as np
from jax import lax
from jax.experimental import pallas as pl
from jax.experimental.pallas import tpu as pltpu
from jax.sharding import PartitionSpec as P

ITERS = 2
SEGMENTS = (1.5131, 1.0)
RADII = (6.0, 8.0)
CROSS = 0.25
DAMPING = 0.3
ATTRACT = ((0.3, 0.22), (0.22, 0.16))
REACH = (5, 7)
FAR = 8
DERIV = REACH[1]
DEEP = tuple(DERIV + r for r in REACH)
WIDE = 8
AXES = ("gx", "gy")
BF16 = jnp.bfloat16
F32 = jnp.float32


def raw_profile(kind, radius):
    offset = np.arange(17) - 8.0
    if kind == 0:
        return np.maximum(radius * radius - offset * offset, 0.0)
    if kind == 1:
        return offset * offset * np.maximum(radius * radius - offset * offset, 0.0)
    return np.exp(-np.abs(offset) / 4.0)


def split_bf16(table):
    high = table.astype(np.float32).astype(ml_dtypes.bfloat16)
    low = (table - high.astype(np.float64)).astype(np.float32).astype(ml_dtypes.bfloat16)
    return high, low


def column_band(kind, radius, count, columns, first):
    band = np.zeros((count, columns))
    for o in range(count):
        band[o, first + o : first + o + 17] = raw_profile(kind, radius)
    return band


def depth_band(kind, radius, depth):
    taps = raw_profile(kind, radius)
    band = np.zeros((depth, depth))
    for column in range(depth):
        for offset in range(17):
            source = column + offset - 8
            if 0 <= source < depth:
                band[source, column] = taps[offset]
    return band


def stage1_tables(comp, cols):
    wide = cols + 2 * WIDE
    pack = column_band(0, RADII[comp], wide, wide + 16, 0)
    rest = np.concatenate(
        [column_band(1, RADII[comp], wide, wide + 16, 0), column_band(2, 0.0, cols, wide + 16, WIDE)]
    )
    high, low = split_bf16(np.concatenate([pack, rest]))
    return {f"first{comp}": np.concatenate([high, high], axis=1), f"rest{comp}": low[wide:]}


def stage2_table(kind, cols):
    high, low = split_bf16(np.concatenate([column_band(kind, r, cols, cols + 16, 0) for r in RADII]))
    return np.concatenate([high, high] if kind == 0 else [high, high, low], axis=1)


def depth_table(kinds, depth):
    scale = lambda kind, comp: SEGMENTS[comp] / raw_profile(0, RADII[comp]).sum() ** 3 if kind == 0 else 1.0
    high, low = split_bf16(np.concatenate([scale(kind, c) * depth_band(kind, RADII[c], depth) for kind, c in kinds]))
    return np.concatenate([high, low], axis=1)


def attraction_tables(depth):
    band = depth_band(2, 0.0, depth)
    high, low = split_bf16(-np.concatenate([np.concatenate([ATTRACT[i][j] * band for i in range(2)], axis=1) for j in range(2)]))
    return {"pull_high": high, "pull_low": low}


@functools.lru_cache
def packed_tables(cols, depth):
    tables = {**stage1_tables(0, cols), **stage1_tables(1, cols), **attraction_tables(depth)}
    tables |= {f"depth{kind}": depth_table([(kind, comp) for comp in range(2)], depth) for kind in range(2)}
    tables |= {f"last{comp}": depth_table([(0, comp), (1, comp)], depth) for comp in range(2)}
    tables |= {f"second{kind}": stage2_table(kind, cols) for kind in range(2)}
    width = max(t.shape[1] for t in tables.values())
    places, start = {}, 0
    for name, table in tables.items():
        places[name] = (start, *table.shape)
        start += table.shape[0]
    whole = np.zeros((start, width), ml_dtypes.bfloat16)
    for name, table in tables.items():
        whole[places[name][0] : places[name][0] + table.shape[0], : table.shape[1]] = table
    return whole, places


class Tables:
    def __init__(self, ref, cols, depth):
        self.ref, self.places = ref, packed_tables(cols, depth)[1]

    def __getitem__(self, name):
        start, rows, columns = self.places[name]
        return self.ref[start : start + rows, :columns]


def row_taps(kind, radius, scale):
    taps = raw_profile(kind, radius)
    return [float(v) for v in taps * (scale / taps.sum() ** 3)]


def split(field):
    high = field.astype(BF16)
    return high, (field - high.astype(F32)).astype(BF16)


def smooth_rows(values, taps, count, reach):
    out = []
    for i in range(count):
        total = None
        for k in range(reach + 1):
            if taps[8 + k] == 0.0:
                continue
            pair = values[i + reach] if k == 0 else values[i + reach - k] + values[i + reach + k]
            term = taps[8 + k] * pair
            total = term if total is None else total + term
        out.append(total)
    return out


def smooth_rows_packing(values, radius, count):
    reach = radius - 1
    at = lambda x: values[x + reach]
    taps = raw_profile(0, radius)
    out = smooth_rows(values[: 2 + 2 * reach], [float(v) for v in taps], 2, reach)
    slope = out[1] - out[0]
    box = at(1)
    for j in range(1, radius):
        box = box + (at(1 - j) + at(1 + j))
    for x in range(1, count - 1):
        if x > 1:
            box = box + (at(x + reach) - at(x - radius))
        slope = slope + ((2 * radius - 1.0) * (at(x + radius) + at(x - radius)) - 2.0 * box)
        out.append(out[-1] + slope)
    return out


def smooth_rows_of(kind, comp, values, count):
    if kind == 0:
        return smooth_rows_packing(values, int(RADII[comp]), count)
    return smooth_rows(values, row_taps(kind, RADII[comp], 1.0), count, REACH[comp])


def smooth_rows_exp(values, scale, count):
    q = float(np.exp(-0.25))
    q9 = q**9
    up = values[0]
    for j in range(1, 9):
        up = up * q + values[j]
    ups = [up]
    for i in range(1, count):
        up = up * q + (values[i + 8] - q9 * values[i - 1])
        ups.append(up)
    down = values[count + 15]
    for j in range(1, 8):
        down = down * q + values[count + 15 - j]
    down = down * q
    out = [None] * count
    out[count - 1] = scale * (ups[count - 1] + down)
    for i in range(count - 2, -1, -1):
        down = down * q + (q * values[i + 9] - q9 * values[i + 17])
        out[i] = scale * (ups[i] + down)
    return out


def split_dot(pair, table):
    high, low = split(pair)
    width = table.shape[1] // 2
    both = jnp.dot(high, table, preferred_element_type=F32)
    rest = jnp.dot(low, table[:, :width], preferred_element_type=F32)
    return both[:, :width] + both[:, width:] + rest


def stage1_columns(load, pairs, comp, tables, near, far, cols, unroll, begin):
    wide = cols + 2 * WIDE

    @pl.loop(0, pairs, unroll=unroll)
    def _(i):
        high, low = split(jnp.concatenate([load(2 * i), load(2 * i + 1)], axis=1))
        first = jnp.dot(tables[f"first{comp}"], jnp.concatenate([high, low], axis=0), preferred_element_type=F32)
        rest = first[wide:] + jnp.dot(tables[f"rest{comp}"], high, preferred_element_type=F32)
        depth = high.shape[1] // 2
        for j in range(2):
            lanes = slice(j * depth, (j + 1) * depth)
            row = begin + 2 * i + j
            near[2 * comp, row] = first[:wide, lanes]
            near[2 * comp + 1, row] = rest[:wide, lanes]
            far[comp, row] = rest[wide:, lanes]


def stage1_rows(load, first, count, out):
    wide = out.shape[2]

    @pl.loop(0, wide // 8)
    def _(t):
        window = pl.ds(pl.multiple_of(t * 8, 8), 8)
        for comp in range(2):
            reach = REACH[comp]
            for kind in range(2):
                field = 2 * comp + kind
                values = [load(field, row, window) for row in range(first - reach, first + count + reach)]
                for i, value in enumerate(smooth_rows_of(kind, comp, values, count)):
                    out[field, i, window, :] = value


def stage1_depth(xs, count, step, tables, deriv, place, gates):
    wide, depth = xs.shape[2:]
    for i, start in enumerate(range(0, count, step)):
        rows = slice(start, start + step)
        pair = lambda p: jnp.concatenate([xs[q, rows].reshape(step * wide, depth) for q in (p, p + 2)], axis=1)
        n3 = split_dot(pair(0), tables["depth0"])
        n2 = split_dot(pair(1), tables["depth1"])
        one = 1.0 + n3
        two = (jnp.log(one) + 2.0 * CROSS * n2 * one).reshape(step, wide, depth)
        three = (n2 / one + CROSS * n2 * n2).reshape(step, wide, depth)
        for which, value in enumerate((two, three)):
            if gates[i] is not None:
                value = value * place[gates[i]].astype(F32)
            deriv[which, rows, :WIDE] = value[:, :WIDE] * place[2].astype(F32)
            deriv[which, rows, WIDE : wide - WIDE] = value[:, WIDE : wide - WIDE]
            deriv[which, rows, wide - WIDE :] = value[:, wide - WIDE :] * place[3].astype(F32)


def stage2_columns(deriv, count, tables, out, unroll):
    cols = out.shape[2]

    @pl.loop(0, count // 2, unroll=unroll)
    def _(i):
        for which, kind in ((0, 1), (1, 0)):
            high, low = split(jnp.concatenate([deriv[which, 2 * i], deriv[which, 2 * i + 1]], axis=1))
            stacked = [high, low, high] if which == 0 else [high, low]
            result = jnp.dot(tables[f"second{kind}"], jnp.concatenate(stacked, axis=0), preferred_element_type=F32)
            depth = high.shape[1] // 2
            for comp in range(2):
                for j in range(2):
                    out[2 * which + comp, 2 * i + j] = result[comp * cols : (comp + 1) * cols, j * depth : (j + 1) * depth]


def position():
    flags = []
    for axis in AXES:
        index = lax.axis_index(axis)
        flags += [(index > 0).astype(jnp.int32), (index + 1 < lax.axis_size(axis)).astype(jnp.int32)]
    return flags + [lax.rem(lax.axis_index("gy"), 2)]


def blend(first, second, scale):
    return first if scale is None else (1.0 - DAMPING) * first + scale * second


def pack_rows(strips, middle, base, value):
    cols, width = value.shape[1], 2 * WIDE
    part = slice(base, base + value.shape[0])
    strips[part, :width] = value[:, :width]
    strips[part, width:] = value[:, cols - width :]
    middle[part] = value[:, width : cols - width]


def packed_shapes(cols, depth):
    return [shape(sum(DEEP), 4 * WIDE, depth), shape(sum(DEEP), cols - 4 * WIDE, depth)]


def side_rows(pair, index, odd):
    one, two = pair[0][index], pair[1][index]
    return jnp.where(odd, one, two), jnp.where(odd, two, one)


def mid_kernel(later, own, *refs):
    if later:
        sides, table_ref, near, far = refs[:2], *refs[2:]
    else:
        solid, *sides, table_ref, near, far, upper = refs
        base = 0
        for comp in range(2):
            part = slice(0, DEEP[comp])
            upper[base : base + DEEP[comp]] = jnp.where(solid[part] == 0, own[comp, part], 0.0)
            base += DEEP[comp]
    rows, cols, depth = far.shape[1:]
    tables = Tables(table_ref, cols, depth)
    odd = position()[4] == 1
    for comp in range(2):

        def load(row):
            index = (comp, row) if len(sides[0].shape) == 4 else sum(DEEP) + comp * rows + row
            left, right = side_rows(sides, index, odd)
            value = own[comp, row] if later else jnp.where(solid[row] == 0, own[comp, row], 0.0)
            return jnp.concatenate([left, value, right], axis=0)

        stage1_columns(load, rows // 2, comp, tables, near, far, cols, rows // 2, 0)


def rest_kernel(later, *refs):
    if later:
        scales, near_old, far_old, near_top, far_top, near_bottom, far_bottom, table_ref, y2, near, far, xs, deriv = refs
        half = near_top.shape[1]
        for old, halves, out in ((near_old, (near_top, near_bottom), near), (far_old, (far_top, far_bottom), far)):
            fields = out.shape[0]

            @pl.loop(0, half)
            def _(row):
                for field in range(fields):
                    for i, new in enumerate(halves):
                        at = row + i * half
                        out[field, at] = blend(old[field, at], new[field, row], scales[2 * field // fields])
    else:
        after, near, table_ref, y2, xs, deriv = refs
    count, cols, depth = y2.shape[1:]
    tables, place = Tables(table_ref, cols, depth), position()
    stage1_rows(lambda field, row, window: near[field, row, window, :], DERIV, count, xs)
    stage1_depth(xs, count, count // 3, tables, deriv, place, [None] * 3)
    stage2_columns(deriv, count, tables, y2, count // 2)


def edge_kernel(top, later, last, *refs):
    if later:
        scales, after, *refs = refs
        halo, sides, halo_new, sides_new, refs = refs[:1], refs[1:3], refs[3:5], refs[5:7], refs[7:]
    else:
        after, *refs = refs
        halo, sides, refs = refs[:1], refs[1:3], refs[3:]
    near, far, y2, solid, table_ref, proposal, sums, *refs = refs
    if not last:
        strips, middle, *refs = refs
    near_h, far_h, xs, deriv, y2_h, xm, xa = refs
    _, rows, cols, depth = far.shape
    half = rows // 2
    tables = Tables(table_ref, cols, depth)
    place = position()
    odd = place[4] == 1

    def pieces(rows_in, columns_in, row):
        left, right = side_rows(columns_in, row, odd)
        if len(rows_in) == 1:
            whole = rows_in[0][row]
            return [left, whole[: 2 * WIDE], whole[2 * WIDE : cols - 2 * WIDE], whole[cols - 2 * WIDE :], right]
        outer, inner = rows_in
        return [left, outer[row, : 2 * WIDE], inner[row], outer[row, 2 * WIDE :], right]

    for comp in range(2):
        base = 0 if comp == 0 else DEEP[0]
        scale = scales[comp] if later else None

        def load(row):
            parts = pieces(halo, sides, base + row)
            if later:
                parts = [blend(old, new, scale) for old, new in zip(parts, pieces(halo_new, sides_new, base + row))]
            return jnp.concatenate(parts, axis=0)

        stage1_columns(load, DEEP[comp] // 2, comp, tables, near_h, far_h, cols, DEEP[comp] // 2, 0)

    def pick(own, edge, index, row, window):
        comp = index // 2 if own is near else index
        if 0 <= row < rows:
            return own[index, row, window, :]
        return edge[index, row + DEEP[comp] if top else row - rows, window, :]

    first = -DERIV if top else rows - DERIV
    stage1_rows(lambda f, row, window: pick(near, near_h, f, row, window), first, 2 * DERIV, xs)
    gates = [0, None] if top else [None, 1]
    stage1_depth(xs, 2 * DERIV, DERIV, tables, deriv, place, gates)
    stage2_columns(deriv, 2 * DERIV, tables, y2_h, 7)

    start = 0 if top else half

    @pl.loop(0, cols // 8)
    def _(t):
        window = pl.ds(pl.multiple_of(t * 8, 8), 8)

        def second(index, row):
            if DERIV <= row < rows - DERIV:
                return y2[index, row - DERIV, window, :]
            return y2_h[index, row - first, window, :]

        for which, kind in ((0, 1), (1, 0)):
            for comp in range(2):
                reach = REACH[comp]
                values = [second(2 * which + comp, row) for row in range(start - reach, start + half + reach)]
                for i, value in enumerate(smooth_rows_of(kind, comp, values, half)):
                    xm[2 * which + comp, i, window, :] = value
        scale = row_taps(2, 0.0, 1.0)[8]
        for comp in range(2):
            values = [pick(far, far_h, comp, row, window) for row in range(start - FAR, start + half + FAR)]
            for i, value in enumerate(smooth_rows_exp(values, scale, half)):
                xa[comp, i, window, :] = value

    sums[...] = jnp.zeros_like(sums)
    step = half // 2
    for i in range(0, half, step):
        part = slice(i, i + step)
        flat = lambda ref, p: ref[p, part].reshape(step * cols, depth)
        pore = solid[start + i : start + i + step].reshape(step * cols, depth) == 0
        high, low = split(jnp.concatenate([flat(xa, 0), flat(xa, 1)], axis=1))
        pull = jnp.dot(high, tables["pull_high"], preferred_element_type=F32)
        pull += jnp.dot(high, tables["pull_low"], preferred_element_type=F32)
        pull += jnp.dot(low, tables["pull_high"], preferred_element_type=F32)
        for comp in range(2):
            mu = split_dot(jnp.concatenate([flat(xm, 2 + comp), flat(xm, comp)], axis=1), tables[f"last{comp}"])
            mu = mu + pull[:, comp * depth : (comp + 1) * depth]
            value = jnp.where(pore, jnp.exp(-mu), 0.0)
            proposal[comp, part] = value.reshape(step, cols, depth)
            sums[comp] += value.reshape(step * cols // 8, 8, depth).sum(0)
    if not last:
        base = 0
        for comp in range(2):
            part = slice(0, DEEP[comp]) if top else slice(half - DEEP[comp], half)
            pack_rows(strips, middle, base, proposal[comp, part])
            base += DEEP[comp]


def in_vmem(count):
    return [pl.BlockSpec(memory_space=pltpu.VMEM)] * count


def params(mebibytes):
    return pltpu.CompilerParams(vmem_limit_bytes=mebibytes * 1024 * 1024)


def shape(*sizes):
    return jax.ShapeDtypeStruct(sizes, F32)


COST = pl.CostEstimate(flops=1000, bytes_accessed=1000, transcendentals=0)


def derivative_scratch(count, wide, depth):
    return [pltpu.VMEM((4, count, wide, depth), F32), pltpu.VMEM((2, count, wide, depth), F32)]


def mid(later, blocks, table):
    _, rows, cols, depth = blocks[0].shape
    outs = [shape(4, rows, cols + 2 * WIDE, depth), shape(2, rows, cols, depth)]
    if not later:
        outs += [shape(sum(DEEP), cols, depth)]
    return pl.pallas_call(
        functools.partial(mid_kernel, later),
        out_shape=tuple(outs),
        in_specs=in_vmem(len(blocks) + 1),
        out_specs=tuple(in_vmem(len(outs))),
        compiler_params=params(6),
        cost_estimate=COST,
        name="mid",
    )(*blocks, table)


def rest(later, first, blocks, table):
    _, rows, wide, depth = blocks[0].shape
    count, cols = rows - 2 * DERIV, wide - 2 * WIDE
    outs = [shape(4, count, cols, depth)]
    if later:
        outs += [shape(*block.shape) for block in blocks[:2]]
    return pl.pallas_call(
        functools.partial(rest_kernel, later),
        out_shape=tuple(outs),
        in_specs=[pl.BlockSpec(memory_space=pltpu.SMEM if later else pl.ANY)] + in_vmem(len(blocks) + 1),
        out_specs=tuple(in_vmem(len(outs))),
        scratch_shapes=[pltpu.VMEM((4, count, wide, depth), F32), pltpu.VMEM((2, count, wide, depth), F32)],
        compiler_params=params(8),
        cost_estimate=COST,
        name="rest",
    )(first, *blocks, table)


def edge(top, later, last, scalars, after, blocks, table):
    rows, cols, depth = blocks[-1].shape
    wide, half = cols + 2 * WIDE, rows // 2
    f32 = lambda *s: pltpu.VMEM(s, F32)
    outs = [shape(2, half, cols, depth), shape(2, 8, depth)]
    if not last:
        outs += packed_shapes(cols, depth)
    return pl.pallas_call(
        functools.partial(edge_kernel, top, later, last),
        out_shape=tuple(outs),
        in_specs=[pl.BlockSpec(memory_space=pltpu.SMEM)] * len(scalars) + [pl.BlockSpec(memory_space=pl.ANY)] + in_vmem(len(blocks) + 1),
        out_specs=tuple(in_vmem(len(outs))),
        scratch_shapes=[
            f32(4, DEEP[1], wide, depth),
            f32(2, DEEP[1], cols, depth),
            f32(4, 2 * DERIV, wide, depth),
            f32(2, 2 * DERIV, wide, depth),
            f32(4, 2 * DERIV, cols, depth),
            f32(4, half, cols, depth),
            f32(2, half, cols, depth),
        ],
        compiler_params=params(16),
        cost_estimate=COST,
        name="edge_top" if top else "edge_bottom",
    )(*scalars, after, *blocks, table)


def shift(value, axis, step):
    count = lax.axis_size(axis)
    return lax.ppermute(value, axis, [(i, i + step) for i in range(count) if 0 <= i + step < count])


def swap_columns(even, odd):
    count = lax.axis_size("gy")
    pairs = lambda first: [p for i in range(first, count - 1, 2) for p in ((i, i + 1), (i + 1, i))]
    return lax.ppermute(even, "gy", pairs(0)), lax.ppermute(odd, "gy", pairs(1))


def side_starts(cols):
    right, left = cols - 2 * WIDE, 0
    odd = position()[4]
    return pl.multiple_of(right * (1 - odd), 8), pl.multiple_of(right * odd, 8)


def first_rows_kernel(own, solid, out, density, mask, sems):
    rows = own.shape[1]
    most = max(DEEP)
    half = most // 2
    copies = []
    for part, begin in enumerate((0, half)):
        source, target = pl.ds(rows - most + begin, half), pl.ds(begin, half)
        copies.append(pltpu.make_async_copy(solid.at[source], mask.at[target], sems.at[part]))
        for comp in range(2):
            copies.append(pltpu.make_async_copy(own.at[comp, source], density.at[comp, target], sems.at[2 + 2 * part + comp]))
    for copy in copies:
        copy.start()
    for copy in copies:
        copy.wait()
    base = 0
    for comp in range(2):
        out[base : base + DEEP[comp]] = jnp.where(mask[most - DEEP[comp] :] == 0, density[comp, most - DEEP[comp] :], 0.0)
        base += DEEP[comp]


def first_rows(own, solid):
    _, _, cols, depth = own.shape
    return pl.pallas_call(
        first_rows_kernel,
        out_shape=shape(sum(DEEP), cols, depth),
        in_specs=[pl.BlockSpec(memory_space=pl.ANY)] * 2,
        out_specs=in_vmem(1)[0],
        scratch_shapes=[
            pltpu.VMEM((2, max(DEEP), cols, depth), F32),
            pltpu.VMEM((max(DEEP), cols, depth), jnp.int32),
            pltpu.SemaphoreType.DMA((6,)),
        ],
        compiler_params=params(56),
        cost_estimate=COST,
        name="first_rows",
    )(own, solid)


def first_columns_kernel(own, solid, even, odd):
    for start, out in zip(side_starts(own.shape[2]), (even, odd)):
        window = pl.ds(start, 2 * WIDE)
        for comp in range(2):
            out[comp] = jnp.where(solid[:, window] == 0, own[comp, :, window], 0.0)


def first_columns(own, solid):
    _, rows, _, depth = own.shape
    side = shape(2, rows, 2 * WIDE, depth)
    return pl.pallas_call(
        first_columns_kernel,
        out_shape=(side, side),
        in_specs=in_vmem(2),
        out_specs=tuple(in_vmem(2)),
        compiler_params=params(8),
        cost_estimate=COST,
        name="first_columns",
    )(own, solid)


def sides_kernel(after, value, even, odd, sems):
    copies = []
    for i, (start, out) in enumerate(zip(side_starts(value.shape[1]), (even, odd))):
        copies.append(pltpu.make_async_copy(value.at[:, pl.ds(start, 2 * WIDE)], out, sems.at[i]))
    for copy in copies:
        copy.start()
    for copy in copies:
        copy.wait()


def sides_pack(after, value):
    count, _, depth = value.shape
    side = shape(count, 2 * WIDE, depth)
    return pl.pallas_call(
        sides_kernel,
        out_shape=(side, side),
        in_specs=[pl.BlockSpec(memory_space=pl.ANY)] * 2,
        out_specs=tuple(in_vmem(2)),
        scratch_shapes=[pltpu.SemaphoreType.DMA((2,))],
        compiler_params=params(4),
        cost_estimate=COST,
        name="sides_pack",
    )(after, value)


def columns_kernel(value, even, odd):
    for start, out in zip(side_starts(value.shape[2]), (even, odd)):
        out[...] = value[:, :, pl.ds(start, 2 * WIDE)]


def columns_pack(value):
    _, count, _, depth = value.shape
    side = shape(2, count, 2 * WIDE, depth)
    return pl.pallas_call(
        columns_kernel,
        out_shape=(side, side),
        in_specs=in_vmem(1),
        out_specs=tuple(in_vmem(2)),
        compiler_params=params(8),
        cost_estimate=COST,
        name="columns_pack",
    )(value)


def joint_kernel(after, halo, value, even, odd):
    count, rows = halo.shape[0], value.shape[1]
    starts = zip(side_starts(halo.shape[1]), side_starts(value.shape[2]))
    for (start, own_start), out in zip(starts, (even, odd)):
        out[:count] = halo[:, pl.ds(start, 2 * WIDE)]
        window = pl.ds(own_start, 2 * WIDE)
        for comp in range(2):
            out[count + comp * rows : count + (comp + 1) * rows] = value[comp, :, window]


def joint_pack(after, halo, value):
    _, rows, _, depth = value.shape
    side = shape(halo.shape[0] + 2 * rows, 2 * WIDE, depth)
    return pl.pallas_call(
        joint_kernel,
        out_shape=(side, side),
        in_specs=[pl.BlockSpec(memory_space=pl.ANY)] + in_vmem(2),
        out_specs=tuple(in_vmem(2)),
        compiler_params=params(6),
        cost_estimate=COST,
        name="joint_pack",
    )(after, halo, value)


def ready_kernel(after, value, out):
    pass


def ready_after(after, value):
    return pl.pallas_call(
        ready_kernel,
        out_shape=shape(*value.shape),
        in_specs=[pl.BlockSpec(memory_space=pl.ANY)] * 2,
        out_specs=pl.BlockSpec(memory_space=pl.ANY),
        input_output_aliases={1: 0},
        compiler_params=params(2),
        cost_estimate=COST,
        name="ready_after",
    )(after, value)


def spread_kernel(one, two, out):
    total = (one[...] + two[...]).sum(axis=1)
    out[...] = jnp.broadcast_to(total[None], out.shape)


def total_over_all(one, two):
    devices = lax.axis_size(AXES)
    copies = pl.pallas_call(
        spread_kernel,
        out_shape=shape(devices, 2, one.shape[2]),
        in_specs=in_vmem(2),
        out_specs=in_vmem(1)[0],
        compiler_params=params(4),
        cost_estimate=COST,
        name="spread",
    )(one, two)
    return lax.all_to_all(copies, AXES, 0, 0, tiled=True)


def last_kernel(total_cells, scales, loadings, totals, own, solid, old_top, old_bottom, top, bottom, out, ready, sems):
    half = top.shape[1]
    copies = []
    for comp in range(2):
        total = jnp.sum(totals[:, comp], keepdims=True)
        factor = DAMPING * loadings[comp] * total_cells / total
        for i, (old, new) in enumerate(((old_top, top), (old_bottom, bottom))):
            part = slice(i * half, (i + 1) * half)

            @pl.loop(0, half, unroll=4)
            def _(row):
                at = i * half + row
                start = jnp.where(solid[at] == 0, own[comp, at], 0.0)
                kept = (1.0 - DAMPING) * blend(start, old[comp, row], scales[comp])
                ready[comp, at] = kept + factor * new[comp, row]

            copies.append(pltpu.make_async_copy(ready.at[comp, part], out.at[comp, part], sems.at[2 * comp + i]))
            copies[-1].start()
    for copy in copies:
        copy.wait()


def last_update(total_cells, scalars, blocks):
    own = blocks[1]
    return pl.pallas_call(
        functools.partial(last_kernel, total_cells),
        out_shape=shape(*own.shape),
        in_specs=[pl.BlockSpec(memory_space=pltpu.SMEM)] * len(scalars) + in_vmem(len(blocks)),
        out_specs=pl.BlockSpec(memory_space=pl.ANY),
        scratch_shapes=[pltpu.VMEM(own.shape, F32), pltpu.SemaphoreType.DMA((4,))],
        compiler_params=params(4),
        cost_estimate=COST,
        name="last_update",
    )(*scalars, *blocks)


def body(density_init, solid_mask, loadings):
    rows, cols, depth = solid_mask.shape
    total_cells = float(rows * lax.axis_size("gx") * cols * lax.axis_size("gy") * depth)
    table = jnp.asarray(packed_tables(cols, depth)[0])

    both = lambda pair, step: [shift(part, "gx", step) for part in pair]
    above = shift(first_rows(density_init, solid_mask), "gx", 1)
    columns = swap_columns(*first_columns(density_init, solid_mask))
    near, far, upper = mid(False, [density_init, solid_mask, *columns], table)
    below = shift(ready_after(above, upper), "gx", -1)
    to_sides = sides_pack(far, above)
    top_sides = swap_columns(*to_sides)
    (y2,) = rest(False, to_sides[0], [near], table)
    top, top_sums, *upper = edge(True, False, False, [], y2, [above, *top_sides, near, far, y2, solid_mask], table)
    below_new = both(upper, -1)
    top_columns = swap_columns(*columns_pack(top))
    bottom_sides = swap_columns(*sides_pack(top_sums, below))
    near_top, far_top = mid(True, [top, *top_columns], table)
    blocks = [below, *bottom_sides, near, far, y2, solid_mask]
    bottom, bottom_sums, *lower = edge(False, False, False, [], far_top, blocks, table)
    old = [density_init, solid_mask, top, bottom]
    totals = total_over_all(top_sums, bottom_sums)
    above_new = both([ready_after(totals, part) for part in lower], 1)
    sides_new = swap_columns(*joint_pack(totals, below_new[0], bottom))
    near_bottom, far_bottom = mid(True, [bottom, *sides_new], table)
    scale = DAMPING * loadings * total_cells / totals.sum(axis=(0, 2))
    y2, near, far = rest(True, scale, [near, far, near_top, far_top, near_bottom, far_bottom], table)
    common = [near, far, y2, solid_mask]
    to_sides = sides_pack(y2, above_new[0])
    top_sides_new = swap_columns(*to_sides)
    blocks = [below, *bottom_sides, *below_new, *sides_new, *common]
    bottom, bottom_sums = edge(False, True, True, [scale], to_sides[0], blocks, table)
    blocks = [above, *top_sides, *above_new, *top_sides_new, *common]
    top, top_sums = edge(True, True, True, [scale], bottom_sums, blocks, table)
    totals = total_over_all(top_sums, bottom_sums)
    return last_update(total_cells, [scale, loadings], [totals, *old, top, bottom])


def solution(mesh):
    in_specs = (P(None, "gx", "gy", None), P("gx", "gy", None), P())
    out_specs = P(None, "gx", "gy", None)
    return jax.shard_map(body, mesh=mesh, in_specs=in_specs, out_specs=out_specs, check_vma=False)
```

```python
import functools

import jax
import jax.numpy as jnp
import ml_dtypes
import numpy as np
from jax import lax
from jax.experimental import pallas as pl
from jax.experimental.pallas import tpu as pltpu
from jax.sharding import PartitionSpec as P

ITERS = 2
SEGMENTS = (1.5131, 1.0)
RADII = (6.0, 8.0)
CROSS = 0.25
DAMPING = 0.3
ATTRACT = ((0.3, 0.22), (0.22, 0.16))
REACH = (5, 7)
FAR = 8
DERIV = REACH[1]
DEEP = tuple(DERIV + r for r in REACH)
WIDE = 8
AXES = ("gx", "gy")
CHUNKS = 4
BF16 = jnp.bfloat16
F32 = jnp.float32


def raw_profile(kind, radius):
    offset = np.arange(17) - 8.0
    if kind == 0:
        return np.maximum(radius * radius - offset * offset, 0.0)
    if kind == 1:
        return offset * offset * np.maximum(radius * radius - offset * offset, 0.0)
    return np.exp(-np.abs(offset) / 4.0)


def split_bf16(table):
    high = table.astype(np.float32).astype(ml_dtypes.bfloat16)
    low = (table - high.astype(np.float64)).astype(np.float32).astype(ml_dtypes.bfloat16)
    return high, low


def column_band(kind, radius, count, columns, first):
    band = np.zeros((count, columns))
    for o in range(count):
        band[o, first + o : first + o + 17] = raw_profile(kind, radius)
    return band


def depth_band(kind, radius, depth):
    taps = raw_profile(kind, radius)
    band = np.zeros((depth, depth))
    for column in range(depth):
        for offset in range(17):
            source = column + offset - 8
            if 0 <= source < depth:
                band[source, column] = taps[offset]
    return band


def stage1_tables(comp, cols):
    wide = cols + 2 * WIDE
    pack = column_band(0, RADII[comp], wide, wide + 16, 0)
    rest = np.concatenate(
        [column_band(1, RADII[comp], wide, wide + 16, 0), column_band(2, 0.0, cols, wide + 16, WIDE)]
    )
    high, low = split_bf16(np.concatenate([pack, rest]))
    return {f"first{comp}": np.concatenate([high, high], axis=1), f"rest{comp}": low[wide:]}


def stage2_table(kind, cols):
    high, low = split_bf16(np.concatenate([column_band(kind, r, cols, cols + 16, 0) for r in RADII]))
    return np.concatenate([high, high] if kind == 0 else [high, high, low], axis=1)


def depth_table(kinds, depth):
    scale = lambda kind, comp: SEGMENTS[comp] / raw_profile(0, RADII[comp]).sum() ** 3 if kind == 0 else 1.0
    high, low = split_bf16(np.concatenate([scale(kind, c) * depth_band(kind, RADII[c], depth) for kind, c in kinds]))
    return np.concatenate([high, low], axis=1)


def attraction_tables(depth):
    band = depth_band(2, 0.0, depth)
    high, low = split_bf16(-np.concatenate([np.concatenate([ATTRACT[i][j] * band for i in range(2)], axis=1) for j in range(2)]))
    return {"pull_high": high, "pull_low": low}


@functools.lru_cache
def packed_tables(cols, depth):
    tables = {**stage1_tables(0, cols), **stage1_tables(1, cols), **attraction_tables(depth)}
    tables |= {f"depth{kind}": depth_table([(kind, comp) for comp in range(2)], depth) for kind in range(2)}
    tables |= {f"last{comp}": depth_table([(0, comp), (1, comp)], depth) for comp in range(2)}
    tables |= {f"second{kind}": stage2_table(kind, cols) for kind in range(2)}
    width = max(t.shape[1] for t in tables.values())
    places, start = {}, 0
    for name, table in tables.items():
        places[name] = (start, *table.shape)
        start += table.shape[0]
    whole = np.zeros((start, width), ml_dtypes.bfloat16)
    for name, table in tables.items():
        whole[places[name][0] : places[name][0] + table.shape[0], : table.shape[1]] = table
    return whole, places


class Tables:
    def __init__(self, ref, cols, depth):
        self.ref, self.places = ref, packed_tables(cols, depth)[1]

    def __getitem__(self, name):
        start, rows, columns = self.places[name]
        return self.ref[start : start + rows, :columns]


def row_taps(kind, radius, scale):
    taps = raw_profile(kind, radius)
    return [float(v) for v in taps * (scale / taps.sum() ** 3)]


def split(field):
    high = field.astype(BF16)
    return high, (field - high.astype(F32)).astype(BF16)


def smooth_rows(values, taps, count, reach):
    out = []
    for i in range(count):
        total = None
        for k in range(reach + 1):
            if taps[8 + k] == 0.0:
                continue
            pair = values[i + reach] if k == 0 else values[i + reach - k] + values[i + reach + k]
            term = taps[8 + k] * pair
            total = term if total is None else total + term
        out.append(total)
    return out


def smooth_rows_packing(values, radius, count):
    reach = radius - 1
    at = lambda x: values[x + reach]
    taps = raw_profile(0, radius)
    out = smooth_rows(values[: 2 + 2 * reach], [float(v) for v in taps], 2, reach)
    slope = out[1] - out[0]
    box = at(1)
    for j in range(1, radius):
        box = box + (at(1 - j) + at(1 + j))
    for x in range(1, count - 1):
        if x > 1:
            box = box + (at(x + reach) - at(x - radius))
        slope = slope + ((2 * radius - 1.0) * (at(x + radius) + at(x - radius)) - 2.0 * box)
        out.append(out[-1] + slope)
    return out


def smooth_rows_of(kind, comp, values, count):
    if kind == 0:
        return smooth_rows_packing(values, int(RADII[comp]), count)
    return smooth_rows(values, row_taps(kind, RADII[comp], 1.0), count, REACH[comp])


def smooth_rows_exp(values, scale, count):
    q = float(np.exp(-0.25))
    q9 = q**9
    up = values[0]
    for j in range(1, 9):
        up = up * q + values[j]
    ups = [up]
    for i in range(1, count):
        up = up * q + (values[i + 8] - q9 * values[i - 1])
        ups.append(up)
    down = values[count + 15]
    for j in range(1, 8):
        down = down * q + values[count + 15 - j]
    down = down * q
    out = [None] * count
    out[count - 1] = scale * (ups[count - 1] + down)
    for i in range(count - 2, -1, -1):
        down = down * q + (q * values[i + 9] - q9 * values[i + 17])
        out[i] = scale * (ups[i] + down)
    return out


def split_dot(pair, table):
    high, low = split(pair)
    width = table.shape[1] // 2
    both = jnp.dot(high, table, preferred_element_type=F32)
    rest = jnp.dot(low, table[:, :width], preferred_element_type=F32)
    return both[:, :width] + both[:, width:] + rest


def stage1_columns(load, pairs, comp, tables, near, far, cols, unroll, begin):
    wide = cols + 2 * WIDE

    @pl.loop(0, pairs, unroll=unroll)
    def _(i):
        high, low = split(jnp.concatenate([load(2 * i), load(2 * i + 1)], axis=1))
        first = jnp.dot(tables[f"first{comp}"], jnp.concatenate([high, low], axis=0), preferred_element_type=F32)
        rest = first[wide:] + jnp.dot(tables[f"rest{comp}"], high, preferred_element_type=F32)
        depth = high.shape[1] // 2
        for j in range(2):
            lanes = slice(j * depth, (j + 1) * depth)
            row = begin + 2 * i + j
            near[2 * comp, row] = first[:wide, lanes]
            near[2 * comp + 1, row] = rest[:wide, lanes]
            far[comp, row] = rest[wide:, lanes]


def stage1_rows(load, first, count, out):
    wide = out.shape[2]

    @pl.loop(0, wide // 8)
    def _(t):
        window = pl.ds(pl.multiple_of(t * 8, 8), 8)
        for comp in range(2):
            reach = REACH[comp]
            for kind in range(2):
                field = 2 * comp + kind
                values = [load(field, row, window) for row in range(first - reach, first + count + reach)]
                for i, value in enumerate(smooth_rows_of(kind, comp, values, count)):
                    out[field, i, window, :] = value


def stage1_depth(xs, count, step, tables, deriv, place, gates):
    wide, depth = xs.shape[2:]
    for i, start in enumerate(range(0, count, step)):
        rows = slice(start, start + step)
        pair = lambda p: jnp.concatenate([xs[q, rows].reshape(step * wide, depth) for q in (p, p + 2)], axis=1)
        n3 = split_dot(pair(0), tables["depth0"])
        n2 = split_dot(pair(1), tables["depth1"])
        one = 1.0 + n3
        two = (jnp.log(one) + 2.0 * CROSS * n2 * one).reshape(step, wide, depth)
        three = (n2 / one + CROSS * n2 * n2).reshape(step, wide, depth)
        for which, value in enumerate((two, three)):
            if gates[i] is not None:
                value = value * place[gates[i]].astype(F32)
            deriv[which, rows, :WIDE] = value[:, :WIDE] * place[2].astype(F32)
            deriv[which, rows, WIDE : wide - WIDE] = value[:, WIDE : wide - WIDE]
            deriv[which, rows, wide - WIDE :] = value[:, wide - WIDE :] * place[3].astype(F32)


def stage2_columns(deriv, count, tables, out, unroll):
    cols = out.shape[2]

    @pl.loop(0, count // 2, unroll=unroll)
    def _(i):
        for which, kind in ((0, 1), (1, 0)):
            high, low = split(jnp.concatenate([deriv[which, 2 * i], deriv[which, 2 * i + 1]], axis=1))
            stacked = [high, low, high] if which == 0 else [high, low]
            result = jnp.dot(tables[f"second{kind}"], jnp.concatenate(stacked, axis=0), preferred_element_type=F32)
            depth = high.shape[1] // 2
            for comp in range(2):
                for j in range(2):
                    out[2 * which + comp, 2 * i + j] = result[comp * cols : (comp + 1) * cols, j * depth : (j + 1) * depth]


def position():
    flags = []
    for axis in AXES:
        index = lax.axis_index(axis)
        flags += [(index > 0).astype(jnp.int32), (index + 1 < lax.axis_size(axis)).astype(jnp.int32)]
    return flags + [lax.rem(lax.axis_index("gy"), 2)]


def blend(first, second, scale):
    return first if scale is None else (1.0 - DAMPING) * first + scale * second


def pack_rows(strips, middle, base, value):
    cols, width = value.shape[1], 2 * WIDE
    part = slice(base, base + value.shape[0])
    strips[part, :width] = value[:, :width]
    strips[part, width:] = value[:, cols - width :]
    middle[part] = value[:, width : cols - width]


def packed_shapes(cols, depth):
    return [shape(sum(DEEP), 4 * WIDE, depth), shape(sum(DEEP), cols - 4 * WIDE, depth)]


def side_rows(pair, index, odd):
    one, two = pair[0][index], pair[1][index]
    return jnp.where(odd, one, two), jnp.where(odd, two, one)


def mid_kernel(later, own, *refs):
    if later:
        sides, table_ref, near, far = refs[:2], *refs[2:]
    else:
        solid, *sides, table_ref, near, far, upper = refs
        base = 0
        for comp in range(2):
            part = slice(0, DEEP[comp])
            upper[base : base + DEEP[comp]] = jnp.where(solid[part] == 0, own[comp, part], 0.0)
            base += DEEP[comp]
    rows, cols, depth = far.shape[1:]
    tables = Tables(table_ref, cols, depth)
    odd = position()[4] == 1
    for comp in range(2):

        def load(row):
            index = (comp, row) if len(sides[0].shape) == 4 else sum(DEEP) + comp * rows + row
            left, right = side_rows(sides, index, odd)
            value = own[comp, row] if later else jnp.where(solid[row] == 0, own[comp, row], 0.0)
            return jnp.concatenate([left, value, right], axis=0)

        stage1_columns(load, rows // 2, comp, tables, near, far, cols, rows // 2, 0)


def rest_kernel(later, *refs):
    if later:
        scales, near_old, far_old, near_top, far_top, near_bottom, far_bottom, table_ref, y2, near, far, xs, deriv = refs
        half = near_top.shape[1]
        for old, halves, out in ((near_old, (near_top, near_bottom), near), (far_old, (far_top, far_bottom), far)):
            fields = out.shape[0]

            @pl.loop(0, half)
            def _(row):
                for field in range(fields):
                    for i, new in enumerate(halves):
                        at = row + i * half
                        out[field, at] = blend(old[field, at], new[field, row], scales[2 * field // fields])
    else:
        after, near, table_ref, y2, xs, deriv = refs
    count, cols, depth = y2.shape[1:]
    tables, place = Tables(table_ref, cols, depth), position()
    stage1_rows(lambda field, row, window: near[field, row, window, :], DERIV, count, xs)
    stage1_depth(xs, count, count // 3, tables, deriv, place, [None] * 3)
    stage2_columns(deriv, count, tables, y2, count // 2)


def edge_kernel(top, later, last, *refs):
    if later:
        scales, after, *refs = refs
        halo, sides, halo_new, sides_new, refs = refs[:1], refs[1:3], refs[3:5], refs[5:7], refs[7:]
    else:
        after, *refs = refs
        halo, sides, refs = refs[:1], refs[1:3], refs[3:]
    near, far, y2, solid, table_ref, proposal, sums, *refs = refs
    if not last:
        strips, middle, *refs = refs
    near_h, far_h, xs, deriv, y2_h, xm, xa = refs
    _, rows, cols, depth = far.shape
    half = rows // 2
    tables = Tables(table_ref, cols, depth)
    place = position()
    odd = place[4] == 1

    def pieces(rows_in, columns_in, row):
        left, right = side_rows(columns_in, row, odd)
        if len(rows_in) == 1:
            whole = rows_in[0][row]
            return [left, whole[: 2 * WIDE], whole[2 * WIDE : cols - 2 * WIDE], whole[cols - 2 * WIDE :], right]
        outer, inner = rows_in
        return [left, outer[row, : 2 * WIDE], inner[row], outer[row, 2 * WIDE :], right]

    for comp in range(2):
        base = 0 if comp == 0 else DEEP[0]
        scale = scales[comp] if later else None

        def load(row):
            parts = pieces(halo, sides, base + row)
            if later:
                parts = [blend(old, new, scale) for old, new in zip(parts, pieces(halo_new, sides_new, base + row))]
            return jnp.concatenate(parts, axis=0)

        stage1_columns(load, DEEP[comp] // 2, comp, tables, near_h, far_h, cols, DEEP[comp] // 2, 0)

    def pick(own, edge, index, row, window):
        comp = index // 2 if own is near else index
        if 0 <= row < rows:
            return own[index, row, window, :]
        return edge[index, row + DEEP[comp] if top else row - rows, window, :]

    first = -DERIV if top else rows - DERIV
    stage1_rows(lambda f, row, window: pick(near, near_h, f, row, window), first, 2 * DERIV, xs)
    gates = [0, None] if top else [None, 1]
    stage1_depth(xs, 2 * DERIV, DERIV, tables, deriv, place, gates)
    stage2_columns(deriv, 2 * DERIV, tables, y2_h, 7)

    start = 0 if top else half

    @pl.loop(0, cols // 8)
    def _(t):
        window = pl.ds(pl.multiple_of(t * 8, 8), 8)

        def second(index, row):
            if DERIV <= row < rows - DERIV:
                return y2[index, row - DERIV, window, :]
            return y2_h[index, row - first, window, :]

        for which, kind in ((0, 1), (1, 0)):
            for comp in range(2):
                reach = REACH[comp]
                values = [second(2 * which + comp, row) for row in range(start - reach, start + half + reach)]
                for i, value in enumerate(smooth_rows_of(kind, comp, values, half)):
                    xm[2 * which + comp, i, window, :] = value
        scale = row_taps(2, 0.0, 1.0)[8]
        for comp in range(2):
            values = [pick(far, far_h, comp, row, window) for row in range(start - FAR, start + half + FAR)]
            for i, value in enumerate(smooth_rows_exp(values, scale, half)):
                xa[comp, i, window, :] = value

    sums[...] = jnp.zeros_like(sums)
    step = half // 2
    for i in range(0, half, step):
        part = slice(i, i + step)
        flat = lambda ref, p: ref[p, part].reshape(step * cols, depth)
        pore = solid[start + i : start + i + step].reshape(step * cols, depth) == 0
        high, low = split(jnp.concatenate([flat(xa, 0), flat(xa, 1)], axis=1))
        pull = jnp.dot(high, tables["pull_high"], preferred_element_type=F32)
        pull += jnp.dot(high, tables["pull_low"], preferred_element_type=F32)
        pull += jnp.dot(low, tables["pull_high"], preferred_element_type=F32)
        for comp in range(2):
            mu = split_dot(jnp.concatenate([flat(xm, 2 + comp), flat(xm, comp)], axis=1), tables[f"last{comp}"])
            mu = mu + pull[:, comp * depth : (comp + 1) * depth]
            value = jnp.where(pore, jnp.exp(-mu), 0.0)
            proposal[comp, part] = value.reshape(step, cols, depth)
            sums[comp] += value.reshape(step * cols // 8, 8, depth).sum(0)
    if not last:
        base = 0
        for comp in range(2):
            part = slice(0, DEEP[comp]) if top else slice(half - DEEP[comp], half)
            pack_rows(strips, middle, base, proposal[comp, part])
            base += DEEP[comp]


def in_vmem(count):
    return [pl.BlockSpec(memory_space=pltpu.VMEM)] * count


def params(mebibytes):
    return pltpu.CompilerParams(vmem_limit_bytes=mebibytes * 1024 * 1024)


def shape(*sizes):
    return jax.ShapeDtypeStruct(sizes, F32)


COST = pl.CostEstimate(flops=1000, bytes_accessed=1000, transcendentals=0)


def derivative_scratch(count, wide, depth):
    return [pltpu.VMEM((4, count, wide, depth), F32), pltpu.VMEM((2, count, wide, depth), F32)]


def mid(later, blocks, table):
    _, rows, cols, depth = blocks[0].shape
    outs = [shape(4, rows, cols + 2 * WIDE, depth), shape(2, rows, cols, depth)]
    if not later:
        outs += [shape(sum(DEEP), cols, depth)]
    return pl.pallas_call(
        functools.partial(mid_kernel, later),
        out_shape=tuple(outs),
        in_specs=in_vmem(len(blocks) + 1),
        out_specs=tuple(in_vmem(len(outs))),
        compiler_params=params(6),
        cost_estimate=COST,
        name="mid",
    )(*blocks, table)


def rest(later, first, blocks, table):
    _, rows, wide, depth = blocks[0].shape
    count, cols = rows - 2 * DERIV, wide - 2 * WIDE
    outs = [shape(4, count, cols, depth)]
    if later:
        outs += [shape(*block.shape) for block in blocks[:2]]
    return pl.pallas_call(
        functools.partial(rest_kernel, later),
        out_shape=tuple(outs),
        in_specs=[pl.BlockSpec(memory_space=pltpu.SMEM if later else pl.ANY)] + in_vmem(len(blocks) + 1),
        out_specs=tuple(in_vmem(len(outs))),
        scratch_shapes=[pltpu.VMEM((4, count, wide, depth), F32), pltpu.VMEM((2, count, wide, depth), F32)],
        compiler_params=params(8),
        cost_estimate=COST,
        name="rest",
    )(first, *blocks, table)


def edge(top, later, last, scalars, after, blocks, table):
    rows, cols, depth = blocks[-1].shape
    wide, half = cols + 2 * WIDE, rows // 2
    f32 = lambda *s: pltpu.VMEM(s, F32)
    outs = [shape(2, half, cols, depth), shape(2, 8, depth)]
    if not last:
        outs += packed_shapes(cols, depth)
    return pl.pallas_call(
        functools.partial(edge_kernel, top, later, last),
        out_shape=tuple(outs),
        in_specs=[pl.BlockSpec(memory_space=pltpu.SMEM)] * len(scalars) + [pl.BlockSpec(memory_space=pl.ANY)] + in_vmem(len(blocks) + 1),
        out_specs=tuple(in_vmem(len(outs))),
        scratch_shapes=[
            f32(4, DEEP[1], wide, depth),
            f32(2, DEEP[1], cols, depth),
            f32(4, 2 * DERIV, wide, depth),
            f32(2, 2 * DERIV, wide, depth),
            f32(4, 2 * DERIV, cols, depth),
            f32(4, half, cols, depth),
            f32(2, half, cols, depth),
        ],
        compiler_params=params(16),
        cost_estimate=COST,
        name="edge_top" if top else "edge_bottom",
    )(*scalars, after, *blocks, table)


def shift(value, axis, step):
    count = lax.axis_size(axis)
    return lax.ppermute(value, axis, [(i, i + step) for i in range(count) if 0 <= i + step < count])


def swap_columns(even, odd):
    count = lax.axis_size("gy")
    pairs = lambda first: [p for i in range(first, count - 1, 2) for p in ((i, i + 1), (i + 1, i))]
    from_odd = lax.ppermute(odd, "gy", pairs(1))
    return lax.ppermute(even, "gy", pairs(0)), from_odd


def side_starts(cols):
    right, left = cols - 2 * WIDE, 0
    odd = position()[4]
    return pl.multiple_of(right * (1 - odd), 8), pl.multiple_of(right * odd, 8)


def first_rows_kernel(own, solid, out, density, mask, ready, sems, out_sems):
    rows = own.shape[1]
    most = max(DEEP)
    step = most // 7
    copies = []
    for part in range(7):
        source, target = pl.ds(rows - most + part * step, step), pl.ds(part * step, step)
        copies.append(pltpu.make_async_copy(solid.at[source], mask.at[target], sems.at[3 * part]))
        for comp in range(2):
            sem = sems.at[3 * part + 1 + comp]
            copies.append(pltpu.make_async_copy(own.at[comp, source], density.at[comp, target], sem))
    for copy in copies:
        copy.start()
    for copy in copies:
        copy.wait()
    base, sent = 0, []
    for comp in range(2):
        part = slice(base, base + DEEP[comp])
        ready[part] = jnp.where(mask[most - DEEP[comp] :] == 0, density[comp, most - DEEP[comp] :], 0.0)
        sent.append(pltpu.make_async_copy(ready.at[part], out.at[part], out_sems.at[comp]))
        sent[-1].start()
        base += DEEP[comp]
    for copy in sent:
        copy.wait()


def first_rows(own, solid):
    _, _, cols, depth = own.shape
    return pl.pallas_call(
        first_rows_kernel,
        out_shape=shape(sum(DEEP), cols, depth),
        in_specs=[pl.BlockSpec(memory_space=pl.ANY)] * 2,
        out_specs=pl.BlockSpec(memory_space=pl.ANY),
        scratch_shapes=[
            pltpu.VMEM((2, max(DEEP), cols, depth), F32),
            pltpu.VMEM((max(DEEP), cols, depth), jnp.int32),
            pltpu.VMEM((sum(DEEP), cols, depth), F32),
            pltpu.SemaphoreType.DMA((21,)),
            pltpu.SemaphoreType.DMA((2,)),
        ],
        compiler_params=params(56),
        cost_estimate=COST,
        name="first_rows",
    )(own, solid)


def first_columns_kernel(own, solid, even, odd):
    for start, out in zip(side_starts(own.shape[2]), (even, odd)):
        window = pl.ds(start, 2 * WIDE)
        for comp in range(2):
            out[comp] = jnp.where(solid[:, window] == 0, own[comp, :, window], 0.0)


def first_columns(own, solid):
    _, rows, _, depth = own.shape
    side = shape(2, rows, 2 * WIDE, depth)
    return pl.pallas_call(
        first_columns_kernel,
        out_shape=(side, side),
        in_specs=in_vmem(2),
        out_specs=tuple(in_vmem(2)),
        compiler_params=params(8),
        cost_estimate=COST,
        name="first_columns",
    )(own, solid)


def sides_kernel(after, value, even, odd, sems):
    copies = []
    for i, (start, out) in enumerate(zip(side_starts(value.shape[1]), (even, odd))):
        copies.append(pltpu.make_async_copy(value.at[:, pl.ds(start, 2 * WIDE)], out, sems.at[i]))
    for copy in copies:
        copy.start()
    for copy in copies:
        copy.wait()


def sides_pack(after, value):
    count, _, depth = value.shape
    side = shape(count, 2 * WIDE, depth)
    return pl.pallas_call(
        sides_kernel,
        out_shape=(side, side),
        in_specs=[pl.BlockSpec(memory_space=pl.ANY)] * 2,
        out_specs=tuple(in_vmem(2)),
        scratch_shapes=[pltpu.SemaphoreType.DMA((2,))],
        compiler_params=params(4),
        cost_estimate=COST,
        name="sides_pack",
    )(after, value)


def columns_kernel(value, even, odd):
    for start, out in zip(side_starts(value.shape[2]), (even, odd)):
        out[...] = value[:, :, pl.ds(start, 2 * WIDE)]


def columns_pack(value):
    _, count, _, depth = value.shape
    side = shape(2, count, 2 * WIDE, depth)
    return pl.pallas_call(
        columns_kernel,
        out_shape=(side, side),
        in_specs=in_vmem(1),
        out_specs=tuple(in_vmem(2)),
        compiler_params=params(8),
        cost_estimate=COST,
        name="columns_pack",
    )(value)


def joint_kernel(after, halo, value, even, odd):
    count, rows = halo.shape[0], value.shape[1]
    starts = zip(side_starts(halo.shape[1]), side_starts(value.shape[2]))
    for (start, own_start), out in zip(starts, (even, odd)):
        out[:count] = halo[:, pl.ds(start, 2 * WIDE)]
        window = pl.ds(own_start, 2 * WIDE)
        for comp in range(2):
            out[count + comp * rows : count + (comp + 1) * rows] = value[comp, :, window]


def joint_pack(after, halo, value):
    _, rows, _, depth = value.shape
    side = shape(halo.shape[0] + 2 * rows, 2 * WIDE, depth)
    return pl.pallas_call(
        joint_kernel,
        out_shape=(side, side),
        in_specs=[pl.BlockSpec(memory_space=pl.ANY)] + in_vmem(2),
        out_specs=tuple(in_vmem(2)),
        compiler_params=params(6),
        cost_estimate=COST,
        name="joint_pack",
    )(after, halo, value)


def ready_kernel(after, value, out):
    pass


def ready_after(after, value):
    return pl.pallas_call(
        ready_kernel,
        out_shape=shape(*value.shape),
        in_specs=[pl.BlockSpec(memory_space=pl.ANY)] * 2,
        out_specs=pl.BlockSpec(memory_space=pl.ANY),
        input_output_aliases={1: 0},
        compiler_params=params(2),
        cost_estimate=COST,
        name="ready_after",
    )(after, value)


def add_partners(sums, axis, first, end):
    count = lax.axis_size(axis)
    for bit in range(first, end):
        sums = sums + lax.ppermute(sums, axis, [(i, i ^ (1 << bit)) for i in range(count)])
    return sums


def spread_kernel(one, two, out):
    total = (one[...] + two[...]).sum(axis=1)
    out[...] = jnp.broadcast_to(total[None], out.shape)


def total_over_all(one, two):
    devices = lax.axis_size(AXES)
    copies = pl.pallas_call(
        spread_kernel,
        out_shape=shape(devices, 2, one.shape[2]),
        in_specs=in_vmem(2),
        out_specs=in_vmem(1)[0],
        compiler_params=params(4),
        cost_estimate=COST,
        name="spread",
    )(one, two)
    return lax.all_to_all(copies, AXES, 0, 0, tiled=True)


def last_kernel(total_cells, scales, loadings, totals, own, solid, old_top, old_bottom, top, bottom, out, ready, sems):
    half = top.shape[1]
    step = half // CHUNKS
    copies = []
    for comp in range(2):
        total = jnp.sum(totals[:, comp], keepdims=True)
        factor = DAMPING * loadings[comp] * total_cells / total
        for i, (old, new) in enumerate(((old_top, top), (old_bottom, bottom))):
            for chunk in range(CHUNKS):
                part = slice(i * half + chunk * step, i * half + (chunk + 1) * step)

                @pl.loop(chunk * step, (chunk + 1) * step)
                def _(row):
                    at = i * half + row
                    start = jnp.where(solid[at] == 0, own[comp, at], 0.0)
                    kept = (1.0 - DAMPING) * blend(start, old[comp, row], scales[comp])
                    ready[comp, at] = kept + factor * new[comp, row]

                sem = sems.at[(2 * comp + i) * CHUNKS + chunk]
                copies.append(pltpu.make_async_copy(ready.at[comp, part], out.at[comp, part], sem))
                copies[-1].start()
    for copy in copies:
        copy.wait()


def last_update(total_cells, scalars, blocks):
    own = blocks[1]
    return pl.pallas_call(
        functools.partial(last_kernel, total_cells),
        out_shape=shape(*own.shape),
        in_specs=[pl.BlockSpec(memory_space=pltpu.SMEM)] * len(scalars) + in_vmem(len(blocks)),
        out_specs=pl.BlockSpec(memory_space=pl.ANY),
        scratch_shapes=[pltpu.VMEM(own.shape, F32), pltpu.SemaphoreType.DMA((4 * CHUNKS,))],
        compiler_params=params(4),
        cost_estimate=COST,
        name="last_update",
    )(*scalars, *blocks)


def bits(axis):
    count = lax.axis_size(axis)
    assert count & (count - 1) == 0
    return count.bit_length() - 1


def body(density_init, solid_mask, loadings):
    rows, cols, depth = solid_mask.shape
    total_cells = float(rows * lax.axis_size("gx") * cols * lax.axis_size("gy") * depth)
    table = jnp.asarray(packed_tables(cols, depth)[0])

    def scale_of(sums):
        return DAMPING * loadings * total_cells / sums.sum(axis=tuple(range(sums.ndim))[1:])

    both = lambda pair, step: [shift(part, "gx", step) for part in pair]
    above = shift(first_rows(density_init, solid_mask), "gx", 1)
    columns = swap_columns(*first_columns(density_init, solid_mask))
    near, far, upper = mid(False, [density_init, solid_mask, *columns], table)
    below = shift(ready_after(above, upper), "gx", -1)
    to_sides = sides_pack(far, above)
    top_sides = swap_columns(*to_sides)
    (y2,) = rest(False, to_sides[0], [near], table)
    top, top_sums, *upper = edge(True, False, False, [], y2, [above, *top_sides, near, far, y2, solid_mask], table)
    below_new = both(upper, -1)
    top_columns = swap_columns(*columns_pack(top))
    bottom_sides = swap_columns(*sides_pack(top_sums, below))
    near_top, far_top = mid(True, [top, *top_columns], table)
    blocks = [below, *bottom_sides, near, far, y2, solid_mask]
    bottom, bottom_sums, *lower = edge(False, False, False, [], far_top, blocks, table)
    old = [density_init, solid_mask, top, bottom]
    sums = add_partners(top_sums + bottom_sums, "gy", 0, bits("gy"))
    to_sides = joint_pack(sums, below_new[0], bottom)
    sides_new = swap_columns(*to_sides)
    sums = add_partners(ready_after(below_new[1], ready_after(to_sides[0], sums)), "gx", 0, bits("gx"))
    above_new = both([ready_after(sums, part) for part in lower], 1)
    near_bottom, far_bottom = mid(True, [bottom, *sides_new], table)
    scale = scale_of(sums)
    y2, near, far = rest(True, scale, [near, far, near_top, far_top, near_bottom, far_bottom], table)
    common = [near, far, y2, solid_mask]
    to_sides = sides_pack(y2, above_new[0])
    top_sides_new = swap_columns(*to_sides)
    blocks = [below, *bottom_sides, *below_new, *sides_new, *common]
    bottom, bottom_sums = edge(False, True, True, [scale], to_sides[0], blocks, table)
    blocks = [above, *top_sides, *above_new, *top_sides_new, *common]
    top, top_sums = edge(True, True, True, [scale], bottom_sums, blocks, table)
    totals = total_over_all(top_sums, bottom_sums)
    return last_update(total_cells, [scale, loadings], [totals, *old, top, bottom])


def solution(mesh):
    in_specs = (P(None, "gx", "gy", None), P("gx", "gy", None), P())
    out_specs = P(None, "gx", "gy", None)
    return jax.shard_map(body, mesh=mesh, in_specs=in_specs, out_specs=out_specs, check_vma=False)
```

```python
import functools

import jax
import jax.numpy as jnp
import ml_dtypes
import numpy as np
from jax import lax
from jax.experimental import pallas as pl
from jax.experimental.pallas import tpu as pltpu
from jax.sharding import PartitionSpec as P

ITERS = 2
SEGMENTS = (1.5131, 1.0)
RADII = (6.0, 8.0)
CROSS = 0.25
DAMPING = 0.3
ATTRACT = ((0.3, 0.22), (0.22, 0.16))
REACH = (5, 7)
FAR = 8
DERIV = REACH[1]
DEEP = tuple(DERIV + r for r in REACH)
WIDE = 8
AXES = ("gx", "gy")
BF16 = jnp.bfloat16
F32 = jnp.float32


def raw_profile(kind, radius):
    offset = np.arange(17) - 8.0
    if kind == 0:
        return np.maximum(radius * radius - offset * offset, 0.0)
    if kind == 1:
        return offset * offset * np.maximum(radius * radius - offset * offset, 0.0)
    return np.exp(-np.abs(offset) / 4.0)


def split_bf16(table):
    high = table.astype(np.float32).astype(ml_dtypes.bfloat16)
    low = (table - high.astype(np.float64)).astype(np.float32).astype(ml_dtypes.bfloat16)
    return high, low


def column_band(kind, radius, count, columns, first):
    band = np.zeros((count, columns))
    for o in range(count):
        band[o, first + o : first + o + 17] = raw_profile(kind, radius)
    return band


def depth_band(kind, radius, depth):
    taps = raw_profile(kind, radius)
    band = np.zeros((depth, depth))
    for column in range(depth):
        for offset in range(17):
            source = column + offset - 8
            if 0 <= source < depth:
                band[source, column] = taps[offset]
    return band


def stage1_tables(comp, cols):
    wide = cols + 2 * WIDE
    pack = column_band(0, RADII[comp], wide, wide + 16, 0)
    rest = np.concatenate(
        [column_band(1, RADII[comp], wide, wide + 16, 0), column_band(2, 0.0, cols, wide + 16, WIDE)]
    )
    high, low = split_bf16(np.concatenate([pack, rest]))
    return {f"first{comp}": np.concatenate([high, high], axis=1), f"rest{comp}": low[wide:]}


def stage2_table(kind, cols):
    high, low = split_bf16(np.concatenate([column_band(kind, r, cols, cols + 16, 0) for r in RADII]))
    return np.concatenate([high, high] if kind == 0 else [high, high, low], axis=1)


def depth_table(kinds, depth):
    scale = lambda kind, comp: SEGMENTS[comp] / raw_profile(0, RADII[comp]).sum() ** 3 if kind == 0 else 1.0
    high, low = split_bf16(np.concatenate([scale(kind, c) * depth_band(kind, RADII[c], depth) for kind, c in kinds]))
    return np.concatenate([high, low], axis=1)


def attraction_tables(depth):
    band = depth_band(2, 0.0, depth)
    high, low = split_bf16(-np.concatenate([np.concatenate([ATTRACT[i][j] * band for i in range(2)], axis=1) for j in range(2)]))
    return {"pull_high": high, "pull_low": low}


@functools.lru_cache
def packed_tables(cols, depth):
    tables = {**stage1_tables(0, cols), **stage1_tables(1, cols), **attraction_tables(depth)}
    tables |= {f"depth{kind}": depth_table([(kind, comp) for comp in range(2)], depth) for kind in range(2)}
    tables |= {f"last{comp}": depth_table([(0, comp), (1, comp)], depth) for comp in range(2)}
    tables |= {f"second{kind}": stage2_table(kind, cols) for kind in range(2)}
    width = max(t.shape[1] for t in tables.values())
    places, start = {}, 0
    for name, table in tables.items():
        places[name] = (start, *table.shape)
        start += table.shape[0]
    whole = np.zeros((start, width), ml_dtypes.bfloat16)
    for name, table in tables.items():
        whole[places[name][0] : places[name][0] + table.shape[0], : table.shape[1]] = table
    return whole, places


class Tables:
    def __init__(self, ref, cols, depth):
        self.ref, self.places = ref, packed_tables(cols, depth)[1]

    def __getitem__(self, name):
        start, rows, columns = self.places[name]
        return self.ref[start : start + rows, :columns]


def row_taps(kind, radius, scale):
    taps = raw_profile(kind, radius)
    return [float(v) for v in taps * (scale / taps.sum() ** 3)]


def split(field):
    high = field.astype(BF16)
    return high, (field - high.astype(F32)).astype(BF16)


def smooth_rows(values, taps, count, reach):
    out = []
    for i in range(count):
        total = None
        for k in range(reach + 1):
            if taps[8 + k] == 0.0:
                continue
            pair = values[i + reach] if k == 0 else values[i + reach - k] + values[i + reach + k]
            term = taps[8 + k] * pair
            total = term if total is None else total + term
        out.append(total)
    return out


def smooth_rows_packing(values, radius, count):
    reach = radius - 1
    at = lambda x: values[x + reach]
    taps = raw_profile(0, radius)
    out = smooth_rows(values[: 2 + 2 * reach], [float(v) for v in taps], 2, reach)
    slope = out[1] - out[0]
    box = at(1)
    for j in range(1, radius):
        box = box + (at(1 - j) + at(1 + j))
    for x in range(1, count - 1):
        if x > 1:
            box = box + (at(x + reach) - at(x - radius))
        slope = slope + ((2 * radius - 1.0) * (at(x + radius) + at(x - radius)) - 2.0 * box)
        out.append(out[-1] + slope)
    return out


def smooth_rows_of(kind, comp, values, count):
    if kind == 0:
        return smooth_rows_packing(values, int(RADII[comp]), count)
    return smooth_rows(values, row_taps(kind, RADII[comp], 1.0), count, REACH[comp])


def smooth_rows_exp(values, scale, count):
    q = float(np.exp(-0.25))
    q9 = q**9
    up = values[0]
    for j in range(1, 9):
        up = up * q + values[j]
    ups = [up]
    for i in range(1, count):
        up = up * q + (values[i + 8] - q9 * values[i - 1])
        ups.append(up)
    down = values[count + 15]
    for j in range(1, 8):
        down = down * q + values[count + 15 - j]
    down = down * q
    out = [None] * count
    out[count - 1] = scale * (ups[count - 1] + down)
    for i in range(count - 2, -1, -1):
        down = down * q + (q * values[i + 9] - q9 * values[i + 17])
        out[i] = scale * (ups[i] + down)
    return out


def split_dot(pair, table):
    high, low = split(pair)
    width = table.shape[1] // 2
    both = jnp.dot(high, table, preferred_element_type=F32)
    rest = jnp.dot(low, table[:, :width], preferred_element_type=F32)
    return both[:, :width] + both[:, width:] + rest


def stage1_columns(load, pairs, comp, tables, near, far, cols, unroll, begin):
    wide = cols + 2 * WIDE

    @pl.loop(0, pairs, unroll=unroll)
    def _(i):
        high, low = split(jnp.concatenate([load(2 * i), load(2 * i + 1)], axis=1))
        first = jnp.dot(tables[f"first{comp}"], jnp.concatenate([high, low], axis=0), preferred_element_type=F32)
        rest = first[wide:] + jnp.dot(tables[f"rest{comp}"], high, preferred_element_type=F32)
        depth = high.shape[1] // 2
        for j in range(2):
            lanes = slice(j * depth, (j + 1) * depth)
            row = begin + 2 * i + j
            near[2 * comp, row] = first[:wide, lanes]
            near[2 * comp + 1, row] = rest[:wide, lanes]
            far[comp, row] = rest[wide:, lanes]


def stage1_rows(load, first, count, out):
    wide = out.shape[2]

    @pl.loop(0, wide // 8)
    def _(t):
        window = pl.ds(pl.multiple_of(t * 8, 8), 8)
        for comp in range(2):
            reach = REACH[comp]
            for kind in range(2):
                field = 2 * comp + kind
                values = [load(field, row, window) for row in range(first - reach, first + count + reach)]
                for i, value in enumerate(smooth_rows_of(kind, comp, values, count)):
                    out[field, i, window, :] = value


def stage1_depth(xs, count, step, tables, deriv, place, gates):
    wide, depth = xs.shape[2:]
    for i, start in enumerate(range(0, count, step)):
        rows = slice(start, start + step)
        pair = lambda p: jnp.concatenate([xs[q, rows].reshape(step * wide, depth) for q in (p, p + 2)], axis=1)
        n3 = split_dot(pair(0), tables["depth0"])
        n2 = split_dot(pair(1), tables["depth1"])
        one = 1.0 + n3
        two = (jnp.log(one) + 2.0 * CROSS * n2 * one).reshape(step, wide, depth)
        three = (n2 / one + CROSS * n2 * n2).reshape(step, wide, depth)
        for which, value in enumerate((two, three)):
            if gates[i] is not None:
                value = value * place[gates[i]].astype(F32)
            deriv[which, rows, :WIDE] = value[:, :WIDE] * place[2].astype(F32)
            deriv[which, rows, WIDE : wide - WIDE] = value[:, WIDE : wide - WIDE]
            deriv[which, rows, wide - WIDE :] = value[:, wide - WIDE :] * place[3].astype(F32)


def stage2_columns(deriv, count, tables, out, unroll):
    cols = out.shape[2]

    @pl.loop(0, count // 2, unroll=unroll)
    def _(i):
        for which, kind in ((0, 1), (1, 0)):
            high, low = split(jnp.concatenate([deriv[which, 2 * i], deriv[which, 2 * i + 1]], axis=1))
            stacked = [high, low, high] if which == 0 else [high, low]
            result = jnp.dot(tables[f"second{kind}"], jnp.concatenate(stacked, axis=0), preferred_element_type=F32)
            depth = high.shape[1] // 2
            for comp in range(2):
                for j in range(2):
                    out[2 * which + comp, 2 * i + j] = result[comp * cols : (comp + 1) * cols, j * depth : (j + 1) * depth]


def position():
    flags = []
    for axis in AXES:
        index = lax.axis_index(axis)
        flags += [(index > 0).astype(jnp.int32), (index + 1 < lax.axis_size(axis)).astype(jnp.int32)]
    return flags + [lax.rem(lax.axis_index("gy"), 2)]


def blend(first, second, scale):
    return first if scale is None else (1.0 - DAMPING) * first + scale * second


def pack_rows(strips, middle, base, value):
    cols, width = value.shape[1], 2 * WIDE
    part = slice(base, base + value.shape[0])
    strips[part, :width] = value[:, :width]
    strips[part, width:] = value[:, cols - width :]
    middle[part] = value[:, width : cols - width]


def packed_shapes(cols, depth):
    return [shape(sum(DEEP), 4 * WIDE, depth), shape(sum(DEEP), cols - 4 * WIDE, depth)]


def side_rows(pair, index, odd):
    one, two = pair[0][index], pair[1][index]
    return jnp.where(odd, one, two), jnp.where(odd, two, one)


def mid_kernel(later, own, *refs):
    if later:
        sides, table_ref, near, far = refs[:2], *refs[2:]
    else:
        solid, *sides, table_ref, near, far, upper = refs
        base = 0
        for comp in range(2):
            part = slice(0, DEEP[comp])
            upper[base : base + DEEP[comp]] = jnp.where(solid[part] == 0, own[comp, part], 0.0)
            base += DEEP[comp]
    rows, cols, depth = far.shape[1:]
    tables = Tables(table_ref, cols, depth)
    odd = position()[4] == 1
    for comp in range(2):

        def load(row):
            index = (comp, row) if len(sides[0].shape) == 4 else sum(DEEP) + comp * rows + row
            left, right = side_rows(sides, index, odd)
            value = own[comp, row] if later else jnp.where(solid[row] == 0, own[comp, row], 0.0)
            return jnp.concatenate([left, value, right], axis=0)

        stage1_columns(load, rows // 2, comp, tables, near, far, cols, rows // 2, 0)


def rest_kernel(later, *refs):
    if later:
        scales, near_old, far_old, near_top, far_top, near_bottom, far_bottom, table_ref, y2, near, far, xs, deriv = refs
        half = near_top.shape[1]
        for old, halves, out in ((near_old, (near_top, near_bottom), near), (far_old, (far_top, far_bottom), far)):
            fields = out.shape[0]

            @pl.loop(0, half)
            def _(row):
                for field in range(fields):
                    for i, new in enumerate(halves):
                        at = row + i * half
                        out[field, at] = blend(old[field, at], new[field, row], scales[2 * field // fields])
    else:
        after, near, table_ref, y2, xs, deriv = refs
    count, cols, depth = y2.shape[1:]
    tables, place = Tables(table_ref, cols, depth), position()
    stage1_rows(lambda field, row, window: near[field, row, window, :], DERIV, count, xs)
    stage1_depth(xs, count, count // 3, tables, deriv, place, [None] * 3)
    stage2_columns(deriv, count, tables, y2, count // 2)


def edge_kernel(top, later, last, *refs):
    if later:
        scales, after, *refs = refs
        end = 5 if top else 4
        halo, sides, halo_new, sides_new, refs = refs[:1], refs[1:3], refs[3:end], refs[end : end + 2], refs[end + 2 :]
    else:
        after, *refs = refs
        halo, sides, refs = refs[:1], refs[1:3], refs[3:]
    near, far, y2, solid, table_ref, proposal, sums, *refs = refs
    *packed, near_h, far_h, xs, deriv, y2_h, xm, xa = refs
    _, rows, cols, depth = far.shape
    half = rows // 2
    tables = Tables(table_ref, cols, depth)
    place = position()
    odd = place[4] == 1

    def pieces(rows_in, columns_in, row):
        left, right = side_rows(columns_in, row, odd)
        if len(rows_in) == 1:
            whole = rows_in[0][row]
            return [left, whole[: 2 * WIDE], whole[2 * WIDE : cols - 2 * WIDE], whole[cols - 2 * WIDE :], right]
        outer, inner = rows_in
        return [left, outer[row, : 2 * WIDE], inner[row], outer[row, 2 * WIDE :], right]

    for comp in range(2):
        base = 0 if comp == 0 else DEEP[0]
        scale = scales[comp] if later else None

        def load(row):
            parts = pieces(halo, sides, base + row)
            if later:
                parts = [blend(old, new, scale) for old, new in zip(parts, pieces(halo_new, sides_new, base + row))]
            return jnp.concatenate(parts, axis=0)

        stage1_columns(load, DEEP[comp] // 2, comp, tables, near_h, far_h, cols, DEEP[comp] // 2, 0)

    def pick(own, edge, index, row, window):
        comp = index // 2 if own is near else index
        if 0 <= row < rows:
            return own[index, row, window, :]
        return edge[index, row + DEEP[comp] if top else row - rows, window, :]

    first = -DERIV if top else rows - DERIV
    stage1_rows(lambda f, row, window: pick(near, near_h, f, row, window), first, 2 * DERIV, xs)
    gates = [0, None] if top else [None, 1]
    stage1_depth(xs, 2 * DERIV, DERIV, tables, deriv, place, gates)
    stage2_columns(deriv, 2 * DERIV, tables, y2_h, 7)

    start = 0 if top else half

    @pl.loop(0, cols // 8)
    def _(t):
        window = pl.ds(pl.multiple_of(t * 8, 8), 8)

        def second(index, row):
            if DERIV <= row < rows - DERIV:
                return y2[index, row - DERIV, window, :]
            return y2_h[index, row - first, window, :]

        for which, kind in ((0, 1), (1, 0)):
            for comp in range(2):
                reach = REACH[comp]
                values = [second(2 * which + comp, row) for row in range(start - reach, start + half + reach)]
                for i, value in enumerate(smooth_rows_of(kind, comp, values, half)):
                    xm[2 * which + comp, i, window, :] = value
        scale = row_taps(2, 0.0, 1.0)[8]
        for comp in range(2):
            values = [pick(far, far_h, comp, row, window) for row in range(start - FAR, start + half + FAR)]
            for i, value in enumerate(smooth_rows_exp(values, scale, half)):
                xa[comp, i, window, :] = value

    sums[...] = jnp.zeros_like(sums)
    step = half // 2
    for i in range(0, half, step):
        part = slice(i, i + step)
        flat = lambda ref, p: ref[p, part].reshape(step * cols, depth)
        pore = solid[start + i : start + i + step].reshape(step * cols, depth) == 0
        high, low = split(jnp.concatenate([flat(xa, 0), flat(xa, 1)], axis=1))
        pull = jnp.dot(high, tables["pull_high"], preferred_element_type=F32)
        pull += jnp.dot(high, tables["pull_low"], preferred_element_type=F32)
        pull += jnp.dot(low, tables["pull_high"], preferred_element_type=F32)
        for comp in range(2):
            mu = split_dot(jnp.concatenate([flat(xm, 2 + comp), flat(xm, comp)], axis=1), tables[f"last{comp}"])
            mu = mu + pull[:, comp * depth : (comp + 1) * depth]
            value = jnp.where(pore, jnp.exp(-mu), 0.0)
            proposal[comp, part] = value.reshape(step, cols, depth)
            sums[comp] += value.reshape(step * cols // 8, 8, depth).sum(0)
    if not last:
        base = 0
        for comp in range(2):
            part = slice(0, DEEP[comp]) if top else slice(half - DEEP[comp], half)
            if top:
                packed[0][base : base + DEEP[comp]] = proposal[comp, part]
            else:
                pack_rows(*packed, base, proposal[comp, part])
            base += DEEP[comp]


def in_vmem(count):
    return [pl.BlockSpec(memory_space=pltpu.VMEM)] * count


def params(mebibytes):
    return pltpu.CompilerParams(vmem_limit_bytes=mebibytes * 1024 * 1024)


def shape(*sizes):
    return jax.ShapeDtypeStruct(sizes, F32)


COST = pl.CostEstimate(flops=1000, bytes_accessed=1000, transcendentals=0)


def derivative_scratch(count, wide, depth):
    return [pltpu.VMEM((4, count, wide, depth), F32), pltpu.VMEM((2, count, wide, depth), F32)]


def mid(later, blocks, table):
    _, rows, cols, depth = blocks[0].shape
    outs = [shape(4, rows, cols + 2 * WIDE, depth), shape(2, rows, cols, depth)]
    if not later:
        outs += [shape(sum(DEEP), cols, depth)]
    return pl.pallas_call(
        functools.partial(mid_kernel, later),
        out_shape=tuple(outs),
        in_specs=in_vmem(len(blocks) + 1),
        out_specs=tuple(in_vmem(len(outs))),
        compiler_params=params(6),
        cost_estimate=COST,
        name="mid",
    )(*blocks, table)


def rest(later, first, blocks, table):
    _, rows, wide, depth = blocks[0].shape
    count, cols = rows - 2 * DERIV, wide - 2 * WIDE
    outs = [shape(4, count, cols, depth)]
    if later:
        outs += [shape(*block.shape) for block in blocks[:2]]
    return pl.pallas_call(
        functools.partial(rest_kernel, later),
        out_shape=tuple(outs),
        in_specs=[pl.BlockSpec(memory_space=pltpu.SMEM if later else pl.ANY)] + in_vmem(len(blocks) + 1),
        out_specs=tuple(in_vmem(len(outs))),
        scratch_shapes=[pltpu.VMEM((4, count, wide, depth), F32), pltpu.VMEM((2, count, wide, depth), F32)],
        compiler_params=params(8),
        cost_estimate=COST,
        name="rest",
    )(first, *blocks, table)


def edge(top, later, last, scalars, after, blocks, table):
    rows, cols, depth = blocks[-1].shape
    wide, half = cols + 2 * WIDE, rows // 2
    f32 = lambda *s: pltpu.VMEM(s, F32)
    outs = [shape(2, half, cols, depth), shape(2, 8, depth)]
    if not last:
        outs += [shape(sum(DEEP), cols, depth)] if top else packed_shapes(cols, depth)
    return pl.pallas_call(
        functools.partial(edge_kernel, top, later, last),
        out_shape=tuple(outs),
        in_specs=[pl.BlockSpec(memory_space=pltpu.SMEM)] * len(scalars) + [pl.BlockSpec(memory_space=pl.ANY)] + in_vmem(len(blocks) + 1),
        out_specs=tuple(in_vmem(len(outs))),
        scratch_shapes=[
            f32(4, DEEP[1], wide, depth),
            f32(2, DEEP[1], cols, depth),
            f32(4, 2 * DERIV, wide, depth),
            f32(2, 2 * DERIV, wide, depth),
            f32(4, 2 * DERIV, cols, depth),
            f32(4, half, cols, depth),
            f32(2, half, cols, depth),
        ],
        compiler_params=params(16),
        cost_estimate=COST,
        name="edge_top" if top else "edge_bottom",
    )(*scalars, after, *blocks, table)


def shift(value, axis, step):
    count = lax.axis_size(axis)
    return lax.ppermute(value, axis, [(i, i + step) for i in range(count) if 0 <= i + step < count])


def swap_columns(even, odd):
    count = lax.axis_size("gy")
    pairs = lambda first: [p for i in range(first, count - 1, 2) for p in ((i, i + 1), (i + 1, i))]
    return lax.ppermute(even, "gy", pairs(0)), lax.ppermute(odd, "gy", pairs(1))


def side_starts(cols):
    right, left = cols - 2 * WIDE, 0
    odd = position()[4]
    return pl.multiple_of(right * (1 - odd), 8), pl.multiple_of(right * odd, 8)


def first_rows_kernel(own, solid, out, density, mask, sems):
    rows = own.shape[1]
    most = max(DEEP)
    half = most // 2
    copies = []
    for part, begin in enumerate((0, half)):
        source, target = pl.ds(rows - most + begin, half), pl.ds(begin, half)
        copies.append(pltpu.make_async_copy(solid.at[source], mask.at[target], sems.at[part]))
        for comp in range(2):
            copies.append(pltpu.make_async_copy(own.at[comp, source], density.at[comp, target], sems.at[2 + 2 * part + comp]))
    for copy in copies:
        copy.start()
    for copy in copies:
        copy.wait()
    base = 0
    for comp in range(2):
        out[base : base + DEEP[comp]] = jnp.where(mask[most - DEEP[comp] :] == 0, density[comp, most - DEEP[comp] :], 0.0)
        base += DEEP[comp]


def first_rows(own, solid):
    _, _, cols, depth = own.shape
    return pl.pallas_call(
        first_rows_kernel,
        out_shape=shape(sum(DEEP), cols, depth),
        in_specs=[pl.BlockSpec(memory_space=pl.ANY)] * 2,
        out_specs=in_vmem(1)[0],
        scratch_shapes=[
            pltpu.VMEM((2, max(DEEP), cols, depth), F32),
            pltpu.VMEM((max(DEEP), cols, depth), jnp.int32),
            pltpu.SemaphoreType.DMA((6,)),
        ],
        compiler_params=params(56),
        cost_estimate=COST,
        name="first_rows",
    )(own, solid)


def first_columns_kernel(own, solid, even, odd):
    for start, out in zip(side_starts(own.shape[2]), (even, odd)):
        window = pl.ds(start, 2 * WIDE)
        for comp in range(2):
            out[comp] = jnp.where(solid[:, window] == 0, own[comp, :, window], 0.0)


def first_columns(own, solid):
    _, rows, _, depth = own.shape
    side = shape(2, rows, 2 * WIDE, depth)
    return pl.pallas_call(
        first_columns_kernel,
        out_shape=(side, side),
        in_specs=in_vmem(2),
        out_specs=tuple(in_vmem(2)),
        compiler_params=params(8),
        cost_estimate=COST,
        name="first_columns",
    )(own, solid)


def sides_kernel(after, value, even, odd, sems):
    copies = []
    for i, (start, out) in enumerate(zip(side_starts(value.shape[1]), (even, odd))):
        copies.append(pltpu.make_async_copy(value.at[:, pl.ds(start, 2 * WIDE)], out, sems.at[i]))
    for copy in copies:
        copy.start()
    for copy in copies:
        copy.wait()


def sides_pack(after, value):
    count, _, depth = value.shape
    side = shape(count, 2 * WIDE, depth)
    return pl.pallas_call(
        sides_kernel,
        out_shape=(side, side),
        in_specs=[pl.BlockSpec(memory_space=pl.ANY)] * 2,
        out_specs=tuple(in_vmem(2)),
        scratch_shapes=[pltpu.SemaphoreType.DMA((2,))],
        compiler_params=params(4),
        cost_estimate=COST,
        name="sides_pack",
    )(after, value)


def columns_kernel(value, even, odd):
    for start, out in zip(side_starts(value.shape[2]), (even, odd)):
        out[...] = value[:, :, pl.ds(start, 2 * WIDE)]


def columns_pack(value):
    _, count, _, depth = value.shape
    side = shape(2, count, 2 * WIDE, depth)
    return pl.pallas_call(
        columns_kernel,
        out_shape=(side, side),
        in_specs=in_vmem(1),
        out_specs=tuple(in_vmem(2)),
        compiler_params=params(8),
        cost_estimate=COST,
        name="columns_pack",
    )(value)


def joint_kernel(after, halo, value, even, odd):
    count, rows = halo.shape[0], value.shape[1]
    starts = zip(side_starts(halo.shape[1]), side_starts(value.shape[2]))
    for (start, own_start), out in zip(starts, (even, odd)):
        out[:count] = halo[:, pl.ds(start, 2 * WIDE)]
        window = pl.ds(own_start, 2 * WIDE)
        for comp in range(2):
            out[count + comp * rows : count + (comp + 1) * rows] = value[comp, :, window]


def joint_pack(after, halo, value):
    _, rows, _, depth = value.shape
    side = shape(halo.shape[0] + 2 * rows, 2 * WIDE, depth)
    return pl.pallas_call(
        joint_kernel,
        out_shape=(side, side),
        in_specs=[pl.BlockSpec(memory_space=pl.ANY)] + in_vmem(2),
        out_specs=tuple(in_vmem(2)),
        compiler_params=params(6),
        cost_estimate=COST,
        name="joint_pack",
    )(after, halo, value)


def ready_kernel(after, value, out):
    pass


def ready_after(after, value):
    return pl.pallas_call(
        ready_kernel,
        out_shape=shape(*value.shape),
        in_specs=[pl.BlockSpec(memory_space=pl.ANY)] * 2,
        out_specs=pl.BlockSpec(memory_space=pl.ANY),
        input_output_aliases={1: 0},
        compiler_params=params(2),
        cost_estimate=COST,
        name="ready_after",
    )(after, value)


def add_partners(sums, axis, first, end):
    count = lax.axis_size(axis)
    for bit in range(first, end):
        sums = sums + lax.ppermute(sums, axis, [(i, i ^ (1 << bit)) for i in range(count)])
    return sums


def spread_kernel(one, two, out):
    total = (one[...] + two[...]).sum(axis=1)
    out[...] = jnp.broadcast_to(total[None], out.shape)


def total_over_all(one, two):
    devices = lax.axis_size(AXES)
    copies = pl.pallas_call(
        spread_kernel,
        out_shape=shape(devices, 2, one.shape[2]),
        in_specs=in_vmem(2),
        out_specs=in_vmem(1)[0],
        compiler_params=params(4),
        cost_estimate=COST,
        name="spread",
    )(one, two)
    return lax.all_to_all(copies, AXES, 0, 0, tiled=True)


def last_kernel(total_cells, scales, loadings, totals, own, solid, old_top, old_bottom, top, bottom, out, ready, sems):
    half = top.shape[1]
    copies = []
    for comp in range(2):
        total = jnp.sum(totals[:, comp], keepdims=True)
        factor = DAMPING * loadings[comp] * total_cells / total
        for i, (old, new) in enumerate(((old_top, top), (old_bottom, bottom))):
            part = slice(i * half, (i + 1) * half)

            @pl.loop(0, half, unroll=4)
            def _(row):
                at = i * half + row
                start = jnp.where(solid[at] == 0, own[comp, at], 0.0)
                kept = (1.0 - DAMPING) * blend(start, old[comp, row], scales[comp])
                ready[comp, at] = kept + factor * new[comp, row]

            copies.append(pltpu.make_async_copy(ready.at[comp, part], out.at[comp, part], sems.at[2 * comp + i]))
            copies[-1].start()
    for copy in copies:
        copy.wait()


def last_update(total_cells, scalars, blocks):
    own = blocks[1]
    return pl.pallas_call(
        functools.partial(last_kernel, total_cells),
        out_shape=shape(*own.shape),
        in_specs=[pl.BlockSpec(memory_space=pltpu.SMEM)] * len(scalars) + in_vmem(len(blocks)),
        out_specs=pl.BlockSpec(memory_space=pl.ANY),
        scratch_shapes=[pltpu.VMEM(own.shape, F32), pltpu.SemaphoreType.DMA((4,))],
        compiler_params=params(4),
        cost_estimate=COST,
        name="last_update",
    )(*scalars, *blocks)


def bits(axis):
    count = lax.axis_size(axis)
    assert count & (count - 1) == 0
    return count.bit_length() - 1


def body(density_init, solid_mask, loadings):
    rows, cols, depth = solid_mask.shape
    total_cells = float(rows * lax.axis_size("gx") * cols * lax.axis_size("gy") * depth)
    table = jnp.asarray(packed_tables(cols, depth)[0])

    def scale_of(sums):
        return DAMPING * loadings * total_cells / sums.sum(axis=tuple(range(sums.ndim))[1:])

    above = shift(first_rows(density_init, solid_mask), "gx", 1)
    columns = swap_columns(*first_columns(density_init, solid_mask))
    near, far, upper = mid(False, [density_init, solid_mask, *columns], table)
    below = shift(ready_after(above, upper), "gx", -1)
    to_sides = sides_pack(far, above)
    top_sides = swap_columns(*to_sides)
    (y2,) = rest(False, to_sides[0], [near], table)
    top, top_sums, upper = edge(True, False, False, [], y2, [above, *top_sides, near, far, y2, solid_mask], table)
    below_new = shift(upper, "gx", -1)
    top_columns = swap_columns(*columns_pack(top))
    bottom_sides = swap_columns(*sides_pack(top_sums, below))
    near_top, far_top = mid(True, [top, *top_columns], table)
    blocks = [below, *bottom_sides, near, far, y2, solid_mask]
    bottom, bottom_sums, *lower = edge(False, False, False, [], far_top, blocks, table)
    old = [density_init, solid_mask, top, bottom]
    sums = add_partners(top_sums + bottom_sums, "gy", 0, bits("gy"))
    to_sides = joint_pack(sums, below_new, bottom)
    sides_new = swap_columns(*to_sides)
    sums = add_partners(ready_after(below_new, ready_after(to_sides[0], sums)), "gx", 0, bits("gx"))
    above_new = [shift(ready_after(sums, part), "gx", 1) for part in lower]
    near_bottom, far_bottom = mid(True, [bottom, *sides_new], table)
    scale = scale_of(sums)
    y2, near, far = rest(True, scale, [near, far, near_top, far_top, near_bottom, far_bottom], table)
    common = [near, far, y2, solid_mask]
    to_sides = sides_pack(y2, above_new[0])
    top_sides_new = swap_columns(*to_sides)
    blocks = [below, *bottom_sides, below_new, *sides_new, *common]
    bottom, bottom_sums = edge(False, True, True, [scale], to_sides[0], blocks, table)
    blocks = [above, *top_sides, *above_new, *top_sides_new, *common]
    top, top_sums = edge(True, True, True, [scale], bottom_sums, blocks, table)
    totals = total_over_all(top_sums, bottom_sums)
    return last_update(total_cells, [scale, loadings], [totals, *old, top, bottom])


def solution(mesh):
    in_specs = (P(None, "gx", "gy", None), P("gx", "gy", None), P())
    out_specs = P(None, "gx", "gy", None)
    return jax.shard_map(body, mesh=mesh, in_specs=in_specs, out_specs=out_specs, check_vma=False)
```

```python
import functools

import jax
import jax.numpy as jnp
import ml_dtypes
import numpy as np
from jax import lax
from jax.experimental import pallas as pl
from jax.experimental.pallas import tpu as pltpu
from jax.sharding import PartitionSpec as P

ITERS = 2
SEGMENTS = (1.5131, 1.0)
RADII = (6.0, 8.0)
CROSS = 0.25
DAMPING = 0.3
ATTRACT = ((0.3, 0.22), (0.22, 0.16))
REACH = (5, 7)
FAR = 8
DERIV = REACH[1]
DEEP = tuple(DERIV + r for r in REACH)
WIDE = 8
AXES = ("gx", "gy")
BF16 = jnp.bfloat16
F32 = jnp.float32


def raw_profile(kind, radius):
    offset = np.arange(17) - 8.0
    if kind == 0:
        return np.maximum(radius * radius - offset * offset, 0.0)
    if kind == 1:
        return offset * offset * np.maximum(radius * radius - offset * offset, 0.0)
    return np.exp(-np.abs(offset) / 4.0)


def split_bf16(table):
    high = table.astype(np.float32).astype(ml_dtypes.bfloat16)
    low = (table - high.astype(np.float64)).astype(np.float32).astype(ml_dtypes.bfloat16)
    return high, low


def column_band(kind, radius, count, columns, first):
    band = np.zeros((count, columns))
    for o in range(count):
        band[o, first + o : first + o + 17] = raw_profile(kind, radius)
    return band


def depth_band(kind, radius, depth):
    taps = raw_profile(kind, radius)
    band = np.zeros((depth, depth))
    for column in range(depth):
        for offset in range(17):
            source = column + offset - 8
            if 0 <= source < depth:
                band[source, column] = taps[offset]
    return band


def stage1_tables(comp, cols):
    wide = cols + 2 * WIDE
    pack = column_band(0, RADII[comp], wide, wide + 16, 0)
    rest = np.concatenate(
        [column_band(1, RADII[comp], wide, wide + 16, 0), column_band(2, 0.0, cols, wide + 16, WIDE)]
    )
    high, low = split_bf16(np.concatenate([pack, rest]))
    return {f"first{comp}": np.concatenate([high, high], axis=1), f"rest{comp}": low[wide:]}


def stage2_table(kind, cols):
    high, low = split_bf16(np.concatenate([column_band(kind, r, cols, cols + 16, 0) for r in RADII]))
    return np.concatenate([high, high] if kind == 0 else [high, high, low], axis=1)


def depth_table(kinds, depth):
    scale = lambda kind, comp: SEGMENTS[comp] / raw_profile(0, RADII[comp]).sum() ** 3 if kind == 0 else 1.0
    high, low = split_bf16(np.concatenate([scale(kind, c) * depth_band(kind, RADII[c], depth) for kind, c in kinds]))
    return np.concatenate([high, low], axis=1)


def attraction_tables(depth):
    band = depth_band(2, 0.0, depth)
    high, low = split_bf16(-np.concatenate([np.concatenate([ATTRACT[i][j] * band for i in range(2)], axis=1) for j in range(2)]))
    return {"pull_high": high, "pull_low": low}


@functools.lru_cache
def packed_tables(cols, depth):
    tables = {**stage1_tables(0, cols), **stage1_tables(1, cols), **attraction_tables(depth)}
    tables |= {f"depth{kind}": depth_table([(kind, comp) for comp in range(2)], depth) for kind in range(2)}
    tables |= {f"last{comp}": depth_table([(0, comp), (1, comp)], depth) for comp in range(2)}
    tables |= {f"second{kind}": stage2_table(kind, cols) for kind in range(2)}
    width = max(t.shape[1] for t in tables.values())
    places, start = {}, 0
    for name, table in tables.items():
        places[name] = (start, *table.shape)
        start += table.shape[0]
    whole = np.zeros((start, width), ml_dtypes.bfloat16)
    for name, table in tables.items():
        whole[places[name][0] : places[name][0] + table.shape[0], : table.shape[1]] = table
    return whole, places


class Tables:
    def __init__(self, ref, cols, depth):
        self.ref, self.places = ref, packed_tables(cols, depth)[1]

    def __getitem__(self, name):
        start, rows, columns = self.places[name]
        return self.ref[start : start + rows, :columns]


def row_taps(kind, radius, scale):
    taps = raw_profile(kind, radius)
    return [float(v) for v in taps * (scale / taps.sum() ** 3)]


def split(field):
    high = field.astype(BF16)
    return high, (field - high.astype(F32)).astype(BF16)


def smooth_rows(values, taps, count, reach):
    out = []
    for i in range(count):
        total = None
        for k in range(reach + 1):
            if taps[8 + k] == 0.0:
                continue
            pair = values[i + reach] if k == 0 else values[i + reach - k] + values[i + reach + k]
            term = taps[8 + k] * pair
            total = term if total is None else total + term
        out.append(total)
    return out


def smooth_rows_packing(values, radius, count):
    reach = radius - 1
    at = lambda x: values[x + reach]
    taps = raw_profile(0, radius)
    out = smooth_rows(values[: 2 + 2 * reach], [float(v) for v in taps], 2, reach)
    slope = out[1] - out[0]
    box = at(1)
    for j in range(1, radius):
        box = box + (at(1 - j) + at(1 + j))
    for x in range(1, count - 1):
        if x > 1:
            box = box + (at(x + reach) - at(x - radius))
        slope = slope + ((2 * radius - 1.0) * (at(x + radius) + at(x - radius)) - 2.0 * box)
        out.append(out[-1] + slope)
    return out


def smooth_rows_of(kind, comp, values, count):
    if kind == 0:
        return smooth_rows_packing(values, int(RADII[comp]), count)
    return smooth_rows(values, row_taps(kind, RADII[comp], 1.0), count, REACH[comp])


def smooth_rows_exp(values, scale, count):
    q = float(np.exp(-0.25))
    q9 = q**9
    up = values[0]
    for j in range(1, 9):
        up = up * q + values[j]
    ups = [up]
    for i in range(1, count):
        up = up * q + (values[i + 8] - q9 * values[i - 1])
        ups.append(up)
    down = values[count + 15]
    for j in range(1, 8):
        down = down * q + values[count + 15 - j]
    down = down * q
    out = [None] * count
    out[count - 1] = scale * (ups[count - 1] + down)
    for i in range(count - 2, -1, -1):
        down = down * q + (q * values[i + 9] - q9 * values[i + 17])
        out[i] = scale * (ups[i] + down)
    return out


def split_dot(pair, table):
    high, low = split(pair)
    width = table.shape[1] // 2
    both = jnp.dot(high, table, preferred_element_type=F32)
    rest = jnp.dot(low, table[:, :width], preferred_element_type=F32)
    return both[:, :width] + both[:, width:] + rest


def stage1_columns(load, pairs, comp, tables, near, far, cols, unroll, begin):
    wide = cols + 2 * WIDE

    @pl.loop(0, pairs, unroll=unroll)
    def _(i):
        high, low = split(jnp.concatenate([load(2 * i), load(2 * i + 1)], axis=1))
        first = jnp.dot(tables[f"first{comp}"], jnp.concatenate([high, low], axis=0), preferred_element_type=F32)
        rest = first[wide:] + jnp.dot(tables[f"rest{comp}"], high, preferred_element_type=F32)
        depth = high.shape[1] // 2
        for j in range(2):
            lanes = slice(j * depth, (j + 1) * depth)
            row = begin + 2 * i + j
            near[2 * comp, row] = first[:wide, lanes]
            near[2 * comp + 1, row] = rest[:wide, lanes]
            far[comp, row] = rest[wide:, lanes]


def stage1_rows(load, first, count, out):
    wide = out.shape[2]

    @pl.loop(0, wide // 8)
    def _(t):
        window = pl.ds(pl.multiple_of(t * 8, 8), 8)
        for comp in range(2):
            reach = REACH[comp]
            for kind in range(2):
                field = 2 * comp + kind
                values = [load(field, row, window) for row in range(first - reach, first + count + reach)]
                for i, value in enumerate(smooth_rows_of(kind, comp, values, count)):
                    out[field, i, window, :] = value


def stage1_depth(xs, count, step, tables, deriv, place, gates):
    wide, depth = xs.shape[2:]
    for i, start in enumerate(range(0, count, step)):
        rows = slice(start, start + step)
        pair = lambda p: jnp.concatenate([xs[q, rows].reshape(step * wide, depth) for q in (p, p + 2)], axis=1)
        n3 = split_dot(pair(0), tables["depth0"])
        n2 = split_dot(pair(1), tables["depth1"])
        one = 1.0 + n3
        two = (jnp.log(one) + 2.0 * CROSS * n2 * one).reshape(step, wide, depth)
        three = (n2 / one + CROSS * n2 * n2).reshape(step, wide, depth)
        for which, value in enumerate((two, three)):
            if gates[i] is not None:
                value = value * place[gates[i]].astype(F32)
            deriv[which, rows, :WIDE] = value[:, :WIDE] * place[2].astype(F32)
            deriv[which, rows, WIDE : wide - WIDE] = value[:, WIDE : wide - WIDE]
            deriv[which, rows, wide - WIDE :] = value[:, wide - WIDE :] * place[3].astype(F32)


def stage2_columns(deriv, count, tables, out, unroll):
    cols = out.shape[2]

    @pl.loop(0, count // 2, unroll=unroll)
    def _(i):
        for which, kind in ((0, 1), (1, 0)):
            high, low = split(jnp.concatenate([deriv[which, 2 * i], deriv[which, 2 * i + 1]], axis=1))
            stacked = [high, low, high] if which == 0 else [high, low]
            result = jnp.dot(tables[f"second{kind}"], jnp.concatenate(stacked, axis=0), preferred_element_type=F32)
            depth = high.shape[1] // 2
            for comp in range(2):
                for j in range(2):
                    out[2 * which + comp, 2 * i + j] = result[comp * cols : (comp + 1) * cols, j * depth : (j + 1) * depth]


def position():
    flags = []
    for axis in AXES:
        index = lax.axis_index(axis)
        flags += [(index > 0).astype(jnp.int32), (index + 1 < lax.axis_size(axis)).astype(jnp.int32)]
    return flags + [lax.rem(lax.axis_index("gy"), 2)]


def blend(first, second, scale):
    return first if scale is None else (1.0 - DAMPING) * first + scale * second


def pack_rows(strips, middle, base, value):
    cols, width = value.shape[1], 2 * WIDE
    part = slice(base, base + value.shape[0])
    strips[part, :width] = value[:, :width]
    strips[part, width:] = value[:, cols - width :]
    middle[part] = value[:, width : cols - width]


def packed_shapes(cols, depth):
    return [shape(sum(DEEP), 4 * WIDE, depth), shape(sum(DEEP), cols - 4 * WIDE, depth)]


def side_rows(pair, index, odd):
    one, two = pair[0][index], pair[1][index]
    return jnp.where(odd, one, two), jnp.where(odd, two, one)


def mid_kernel(later, own, *refs):
    if later:
        sides, table_ref, near, far = refs[:2], *refs[2:]
    else:
        solid, *sides, table_ref, near, far, upper = refs
        base = 0
        for comp in range(2):
            part = slice(0, DEEP[comp])
            upper[base : base + DEEP[comp]] = jnp.where(solid[part] == 0, own[comp, part], 0.0)
            base += DEEP[comp]
    rows, cols, depth = far.shape[1:]
    tables = Tables(table_ref, cols, depth)
    odd = position()[4] == 1
    for comp in range(2):

        def load(row):
            index = (comp, row) if len(sides[0].shape) == 4 else sum(DEEP) + comp * rows + row
            left, right = side_rows(sides, index, odd)
            value = own[comp, row] if later else jnp.where(solid[row] == 0, own[comp, row], 0.0)
            return jnp.concatenate([left, value, right], axis=0)

        stage1_columns(load, rows // 2, comp, tables, near, far, cols, rows // 2, 0)


def rest_kernel(later, total_cells, *refs):
    if later:
        loadings, sums, near_old, far_old, near_top, far_top, near_bottom, far_bottom, table_ref, *refs = refs
        y2, near, far, scales, xs, deriv = refs
        half = near_top.shape[1]
        factors = []
        for comp in range(2):
            total = jnp.sum(sums[comp], keepdims=True)
            factors.append((DAMPING * loadings[comp] * total_cells / total)[0, 0])
            scales[comp] = factors[comp]
        for old, halves, out in ((near_old, (near_top, near_bottom), near), (far_old, (far_top, far_bottom), far)):
            fields = out.shape[0]

            @pl.loop(0, half)
            def _(row):
                for field in range(fields):
                    for i, new in enumerate(halves):
                        at = row + i * half
                        out[field, at] = blend(old[field, at], new[field, row], factors[2 * field // fields])
    else:
        after, near, table_ref, y2, xs, deriv = refs
    count, cols, depth = y2.shape[1:]
    tables, place = Tables(table_ref, cols, depth), position()
    stage1_rows(lambda field, row, window: near[field, row, window, :], DERIV, count, xs)
    stage1_depth(xs, count, count // 3, tables, deriv, place, [None] * 3)
    stage2_columns(deriv, count, tables, y2, count // 2)


def edge_kernel(top, later, last, *refs):
    if later:
        scales, after, *refs = refs
        end = 5 if top else 4
        halo, sides, halo_new, sides_new, refs = refs[:1], refs[1:3], refs[3:end], refs[end : end + 2], refs[end + 2 :]
    else:
        after, *refs = refs
        halo, sides, refs = refs[:1], refs[1:3], refs[3:]
    near, far, y2, solid, table_ref, proposal, sums, *refs = refs
    *packed, near_h, far_h, xs, deriv, y2_h, xm, xa = refs
    _, rows, cols, depth = far.shape
    half = rows // 2
    tables = Tables(table_ref, cols, depth)
    place = position()
    odd = place[4] == 1

    def pieces(rows_in, columns_in, row):
        left, right = side_rows(columns_in, row, odd)
        if len(rows_in) == 1:
            whole = rows_in[0][row]
            return [left, whole[: 2 * WIDE], whole[2 * WIDE : cols - 2 * WIDE], whole[cols - 2 * WIDE :], right]
        outer, inner = rows_in
        return [left, outer[row, : 2 * WIDE], inner[row], outer[row, 2 * WIDE :], right]

    for comp in range(2):
        base = 0 if comp == 0 else DEEP[0]
        scale = scales[comp] if later else None

        def load(row):
            parts = pieces(halo, sides, base + row)
            if later:
                parts = [blend(old, new, scale) for old, new in zip(parts, pieces(halo_new, sides_new, base + row))]
            return jnp.concatenate(parts, axis=0)

        stage1_columns(load, DEEP[comp] // 2, comp, tables, near_h, far_h, cols, DEEP[comp] // 2, 0)

    def pick(own, edge, index, row, window):
        comp = index // 2 if own is near else index
        if 0 <= row < rows:
            return own[index, row, window, :]
        return edge[index, row + DEEP[comp] if top else row - rows, window, :]

    first = -DERIV if top else rows - DERIV
    stage1_rows(lambda f, row, window: pick(near, near_h, f, row, window), first, 2 * DERIV, xs)
    gates = [0, None] if top else [None, 1]
    stage1_depth(xs, 2 * DERIV, DERIV, tables, deriv, place, gates)
    stage2_columns(deriv, 2 * DERIV, tables, y2_h, 7)

    start = 0 if top else half

    @pl.loop(0, cols // 8)
    def _(t):
        window = pl.ds(pl.multiple_of(t * 8, 8), 8)

        def second(index, row):
            if DERIV <= row < rows - DERIV:
                return y2[index, row - DERIV, window, :]
            return y2_h[index, row - first, window, :]

        for which, kind in ((0, 1), (1, 0)):
            for comp in range(2):
                reach = REACH[comp]
                values = [second(2 * which + comp, row) for row in range(start - reach, start + half + reach)]
                for i, value in enumerate(smooth_rows_of(kind, comp, values, half)):
                    xm[2 * which + comp, i, window, :] = value
        scale = row_taps(2, 0.0, 1.0)[8]
        for comp in range(2):
            values = [pick(far, far_h, comp, row, window) for row in range(start - FAR, start + half + FAR)]
            for i, value in enumerate(smooth_rows_exp(values, scale, half)):
                xa[comp, i, window, :] = value

    sums[...] = jnp.zeros_like(sums)
    step = half // 2
    for i in range(0, half, step):
        part = slice(i, i + step)
        flat = lambda ref, p: ref[p, part].reshape(step * cols, depth)
        pore = solid[start + i : start + i + step].reshape(step * cols, depth) == 0
        high, low = split(jnp.concatenate([flat(xa, 0), flat(xa, 1)], axis=1))
        pull = jnp.dot(high, tables["pull_high"], preferred_element_type=F32)
        pull += jnp.dot(high, tables["pull_low"], preferred_element_type=F32)
        pull += jnp.dot(low, tables["pull_high"], preferred_element_type=F32)
        for comp in range(2):
            mu = split_dot(jnp.concatenate([flat(xm, 2 + comp), flat(xm, comp)], axis=1), tables[f"last{comp}"])
            mu = mu + pull[:, comp * depth : (comp + 1) * depth]
            value = jnp.where(pore, jnp.exp(-mu), 0.0)
            proposal[comp, part] = value.reshape(step, cols, depth)
            sums[comp] += value.reshape(step * cols // 8, 8, depth).sum(0)
    if not last:
        base = 0
        for comp in range(2):
            part = slice(0, DEEP[comp]) if top else slice(half - DEEP[comp], half)
            if top:
                packed[0][base : base + DEEP[comp]] = proposal[comp, part]
            else:
                pack_rows(*packed, base, proposal[comp, part])
            base += DEEP[comp]


def in_vmem(count):
    return [pl.BlockSpec(memory_space=pltpu.VMEM)] * count


def params(mebibytes):
    return pltpu.CompilerParams(vmem_limit_bytes=mebibytes * 1024 * 1024)


def shape(*sizes):
    return jax.ShapeDtypeStruct(sizes, F32)


COST = pl.CostEstimate(flops=1000, bytes_accessed=1000, transcendentals=0)


def derivative_scratch(count, wide, depth):
    return [pltpu.VMEM((4, count, wide, depth), F32), pltpu.VMEM((2, count, wide, depth), F32)]


def mid(later, blocks, table):
    _, rows, cols, depth = blocks[0].shape
    outs = [shape(4, rows, cols + 2 * WIDE, depth), shape(2, rows, cols, depth)]
    if not later:
        outs += [shape(sum(DEEP), cols, depth)]
    return pl.pallas_call(
        functools.partial(mid_kernel, later),
        out_shape=tuple(outs),
        in_specs=in_vmem(len(blocks) + 1),
        out_specs=tuple(in_vmem(len(outs))),
        compiler_params=params(6),
        cost_estimate=COST,
        name="mid",
    )(*blocks, table)


def rest(later, total_cells, first, blocks, table):
    _, rows, wide, depth = blocks[later].shape
    count, cols = rows - 2 * DERIV, wide - 2 * WIDE
    outs = [shape(4, count, cols, depth)]
    if later:
        outs += [shape(*block.shape) for block in blocks[1:3]] + [shape(2)]
    out_specs = in_vmem(len(outs))
    if later:
        out_specs[-1] = pl.BlockSpec(memory_space=pltpu.SMEM)
    return pl.pallas_call(
        functools.partial(rest_kernel, later, total_cells),
        out_shape=tuple(outs),
        in_specs=[pl.BlockSpec(memory_space=pltpu.SMEM if later else pl.ANY)] + in_vmem(len(blocks) + 1),
        out_specs=tuple(out_specs),
        scratch_shapes=[pltpu.VMEM((4, count, wide, depth), F32), pltpu.VMEM((2, count, wide, depth), F32)],
        compiler_params=params(8),
        cost_estimate=COST,
        name="rest",
    )(first, *blocks, table)


def edge(top, later, last, scalars, after, blocks, table):
    rows, cols, depth = blocks[-1].shape
    wide, half = cols + 2 * WIDE, rows // 2
    f32 = lambda *s: pltpu.VMEM(s, F32)
    outs = [shape(2, half, cols, depth), shape(2, 8, depth)]
    if not last:
        outs += [shape(sum(DEEP), cols, depth)] if top else packed_shapes(cols, depth)
    return pl.pallas_call(
        functools.partial(edge_kernel, top, later, last),
        out_shape=tuple(outs),
        in_specs=[pl.BlockSpec(memory_space=pltpu.SMEM)] * len(scalars) + [pl.BlockSpec(memory_space=pl.ANY)] + in_vmem(len(blocks) + 1),
        out_specs=tuple(in_vmem(len(outs))),
        scratch_shapes=[
            f32(4, DEEP[1], wide, depth),
            f32(2, DEEP[1], cols, depth),
            f32(4, 2 * DERIV, wide, depth),
            f32(2, 2 * DERIV, wide, depth),
            f32(4, 2 * DERIV, cols, depth),
            f32(4, half, cols, depth),
            f32(2, half, cols, depth),
        ],
        compiler_params=params(16),
        cost_estimate=COST,
        name="edge_top" if top else "edge_bottom",
    )(*scalars, after, *blocks, table)


def shift(value, axis, step):
    count = lax.axis_size(axis)
    return lax.ppermute(value, axis, [(i, i + step) for i in range(count) if 0 <= i + step < count])


def swap_columns(even, odd):
    count = lax.axis_size("gy")
    pairs = lambda first: [p for i in range(first, count - 1, 2) for p in ((i, i + 1), (i + 1, i))]
    return lax.ppermute(even, "gy", pairs(0)), lax.ppermute(odd, "gy", pairs(1))


def side_starts(cols):
    right, left = cols - 2 * WIDE, 0
    odd = position()[4]
    return pl.multiple_of(right * (1 - odd), 8), pl.multiple_of(right * odd, 8)


def first_rows_kernel(own, solid, out, density, mask, sems):
    rows = own.shape[1]
    most = max(DEEP)
    half = most // 2
    copies = []
    for part, begin in enumerate((0, half)):
        source, target = pl.ds(rows - most + begin, half), pl.ds(begin, half)
        copies.append(pltpu.make_async_copy(solid.at[source], mask.at[target], sems.at[part]))
        for comp in range(2):
            copies.append(pltpu.make_async_copy(own.at[comp, source], density.at[comp, target], sems.at[2 + 2 * part + comp]))
    for copy in copies:
        copy.start()
    for copy in copies:
        copy.wait()
    base = 0
    for comp in range(2):
        out[base : base + DEEP[comp]] = jnp.where(mask[most - DEEP[comp] :] == 0, density[comp, most - DEEP[comp] :], 0.0)
        base += DEEP[comp]


def first_rows(own, solid):
    _, _, cols, depth = own.shape
    return pl.pallas_call(
        first_rows_kernel,
        out_shape=shape(sum(DEEP), cols, depth),
        in_specs=[pl.BlockSpec(memory_space=pl.ANY)] * 2,
        out_specs=in_vmem(1)[0],
        scratch_shapes=[
            pltpu.VMEM((2, max(DEEP), cols, depth), F32),
            pltpu.VMEM((max(DEEP), cols, depth), jnp.int32),
            pltpu.SemaphoreType.DMA((6,)),
        ],
        compiler_params=params(56),
        cost_estimate=COST,
        name="first_rows",
    )(own, solid)


def first_columns_kernel(own, solid, even, odd):
    for start, out in zip(side_starts(own.shape[2]), (even, odd)):
        window = pl.ds(start, 2 * WIDE)
        for comp in range(2):
            out[comp] = jnp.where(solid[:, window] == 0, own[comp, :, window], 0.0)


def first_columns(own, solid):
    _, rows, _, depth = own.shape
    side = shape(2, rows, 2 * WIDE, depth)
    return pl.pallas_call(
        first_columns_kernel,
        out_shape=(side, side),
        in_specs=in_vmem(2),
        out_specs=tuple(in_vmem(2)),
        compiler_params=params(8),
        cost_estimate=COST,
        name="first_columns",
    )(own, solid)


def sides_kernel(after, value, even, odd, sems):
    copies = []
    for i, (start, out) in enumerate(zip(side_starts(value.shape[1]), (even, odd))):
        copies.append(pltpu.make_async_copy(value.at[:, pl.ds(start, 2 * WIDE)], out, sems.at[i]))
    for copy in copies:
        copy.start()
    for copy in copies:
        copy.wait()


def sides_pack(after, value):
    count, _, depth = value.shape
    side = shape(count, 2 * WIDE, depth)
    return pl.pallas_call(
        sides_kernel,
        out_shape=(side, side),
        in_specs=[pl.BlockSpec(memory_space=pl.ANY)] * 2,
        out_specs=tuple(in_vmem(2)),
        scratch_shapes=[pltpu.SemaphoreType.DMA((2,))],
        compiler_params=params(4),
        cost_estimate=COST,
        name="sides_pack",
    )(after, value)


def columns_kernel(value, even, odd):
    for start, out in zip(side_starts(value.shape[2]), (even, odd)):
        out[...] = value[:, :, pl.ds(start, 2 * WIDE)]


def columns_pack(value):
    _, count, _, depth = value.shape
    side = shape(2, count, 2 * WIDE, depth)
    return pl.pallas_call(
        columns_kernel,
        out_shape=(side, side),
        in_specs=in_vmem(1),
        out_specs=tuple(in_vmem(2)),
        compiler_params=params(8),
        cost_estimate=COST,
        name="columns_pack",
    )(value)


def joint_kernel(after, halo, value, even, odd):
    count, rows = halo.shape[0], value.shape[1]
    starts = zip(side_starts(halo.shape[1]), side_starts(value.shape[2]))
    for (start, own_start), out in zip(starts, (even, odd)):
        out[:count] = halo[:, pl.ds(start, 2 * WIDE)]
        window = pl.ds(own_start, 2 * WIDE)
        for comp in range(2):
            out[count + comp * rows : count + (comp + 1) * rows] = value[comp, :, window]


def joint_pack(after, halo, value):
    _, rows, _, depth = value.shape
    side = shape(halo.shape[0] + 2 * rows, 2 * WIDE, depth)
    return pl.pallas_call(
        joint_kernel,
        out_shape=(side, side),
        in_specs=[pl.BlockSpec(memory_space=pl.ANY)] + in_vmem(2),
        out_specs=tuple(in_vmem(2)),
        compiler_params=params(6),
        cost_estimate=COST,
        name="joint_pack",
    )(after, halo, value)


def ready_kernel(after, value, out):
    pass


def ready_after(after, value):
    return pl.pallas_call(
        ready_kernel,
        out_shape=shape(*value.shape),
        in_specs=[pl.BlockSpec(memory_space=pl.ANY)] * 2,
        out_specs=pl.BlockSpec(memory_space=pl.ANY),
        input_output_aliases={1: 0},
        compiler_params=params(2),
        cost_estimate=COST,
        name="ready_after",
    )(after, value)


def add_partners(sums, axis, first, end):
    count = lax.axis_size(axis)
    for bit in range(first, end):
        sums = sums + lax.ppermute(sums, axis, [(i, i ^ (1 << bit)) for i in range(count)])
    return sums


def spread_kernel(one, two, out):
    total = (one[...] + two[...]).sum(axis=1)
    out[...] = jnp.broadcast_to(total[None], out.shape)


def total_over_all(one, two):
    devices = lax.axis_size(AXES)
    copies = pl.pallas_call(
        spread_kernel,
        out_shape=shape(devices, 2, one.shape[2]),
        in_specs=in_vmem(2),
        out_specs=in_vmem(1)[0],
        compiler_params=params(4),
        cost_estimate=COST,
        name="spread",
    )(one, two)
    return lax.all_to_all(copies, AXES, 0, 0, tiled=True)


def last_kernel(total_cells, scales, loadings, totals, own, solid, old_top, old_bottom, top, bottom, out, ready, sems):
    half = top.shape[1]
    copies = []
    for comp in range(2):
        total = jnp.sum(totals[:, comp], keepdims=True)
        factor = DAMPING * loadings[comp] * total_cells / total
        for i, (old, new) in enumerate(((old_top, top), (old_bottom, bottom))):
            part = slice(i * half, (i + 1) * half)

            @pl.loop(0, half, unroll=4)
            def _(row):
                at = i * half + row
                start = jnp.where(solid[at] == 0, own[comp, at], 0.0)
                kept = (1.0 - DAMPING) * blend(start, old[comp, row], scales[comp])
                ready[comp, at] = kept + factor * new[comp, row]

            copies.append(pltpu.make_async_copy(ready.at[comp, part], out.at[comp, part], sems.at[2 * comp + i]))
            copies[-1].start()
    for copy in copies:
        copy.wait()


def last_update(total_cells, scalars, blocks):
    own = blocks[1]
    return pl.pallas_call(
        functools.partial(last_kernel, total_cells),
        out_shape=shape(*own.shape),
        in_specs=[pl.BlockSpec(memory_space=pltpu.SMEM)] * len(scalars) + in_vmem(len(blocks)),
        out_specs=pl.BlockSpec(memory_space=pl.ANY),
        scratch_shapes=[pltpu.VMEM(own.shape, F32), pltpu.SemaphoreType.DMA((4,))],
        compiler_params=params(4),
        cost_estimate=COST,
        name="last_update",
    )(*scalars, *blocks)


def bits(axis):
    count = lax.axis_size(axis)
    assert count & (count - 1) == 0
    return count.bit_length() - 1


def body(density_init, solid_mask, loadings):
    rows, cols, depth = solid_mask.shape
    total_cells = float(rows * lax.axis_size("gx") * cols * lax.axis_size("gy") * depth)
    table = jnp.asarray(packed_tables(cols, depth)[0])

    above = shift(first_rows(density_init, solid_mask), "gx", 1)
    columns = swap_columns(*first_columns(density_init, solid_mask))
    near, far, upper = mid(False, [density_init, solid_mask, *columns], table)
    below = shift(ready_after(above, upper), "gx", -1)
    to_sides = sides_pack(far, above)
    top_sides = swap_columns(*to_sides)
    (y2,) = rest(False, total_cells, to_sides[0], [near], table)
    top, top_sums, upper = edge(True, False, False, [], y2, [above, *top_sides, near, far, y2, solid_mask], table)
    below_new = shift(upper, "gx", -1)
    top_columns = swap_columns(*columns_pack(top))
    bottom_sides = swap_columns(*sides_pack(top_sums, below))
    near_top, far_top = mid(True, [top, *top_columns], table)
    blocks = [below, *bottom_sides, near, far, y2, solid_mask]
    bottom, bottom_sums, *lower = edge(False, False, False, [], far_top, blocks, table)
    old = [density_init, solid_mask, top, bottom]
    sums = add_partners(top_sums + bottom_sums, "gy", 0, bits("gy"))
    to_sides = joint_pack(sums, below_new, bottom)
    sides_new = swap_columns(*to_sides)
    sums = add_partners(ready_after(below_new, ready_after(to_sides[0], sums)), "gx", 0, bits("gx"))
    above_new = [shift(ready_after(sums, part), "gx", 1) for part in lower]
    near_bottom, far_bottom = mid(True, [bottom, *sides_new], table)
    blocks = [sums, near, far, near_top, far_top, near_bottom, far_bottom]
    y2, near, far, scale = rest(True, total_cells, loadings, blocks, table)
    common = [near, far, y2, solid_mask]
    to_sides = sides_pack(y2, above_new[0])
    top_sides_new = swap_columns(*to_sides)
    blocks = [below, *bottom_sides, below_new, *sides_new, *common]
    bottom, bottom_sums = edge(False, True, True, [scale], to_sides[0], blocks, table)
    blocks = [above, *top_sides, *above_new, *top_sides_new, *common]
    top, top_sums = edge(True, True, True, [scale], bottom_sums, blocks, table)
    totals = total_over_all(top_sums, bottom_sums)
    return last_update(total_cells, [scale, loadings], [totals, *old, top, bottom])


def solution(mesh):
    in_specs = (P(None, "gx", "gy", None), P("gx", "gy", None), P())
    out_specs = P(None, "gx", "gy", None)
    return jax.shard_map(body, mesh=mesh, in_specs=in_specs, out_specs=out_specs, check_vma=False)
```
